32 devices in a mesh: batch: 8 (over z, x), seq: 4 (over y, core).
Axes of the slice: x: 2, y: 2, z: 4, core: 2. Of those that a mesh axis runs over, the one named last changes fastest.
Arguments:
- tokens_in: bfloat16 [16, 2048, 768], P('batch', 'seq'), may hold values from -6 to 6
- doc_starts: int32 [16, 6], P('batch'), may hold values from 0 to 2047, as said below
- mixer_in: bfloat16 [2, 768, 1920], P(None, 'batch'), may hold values from -0.21875 to 0.21875
- mixer_out: bfloat16 [2, 768, 768], P(None, 'batch'), may hold values from -0.21875 to 0.21875
- ffn_in: bfloat16 [2, 768, 3072], P(None, 'batch'), may hold values from -0.21875 to 0.21875
- ffn_out: bfloat16 [2, 1536, 768], P(None, 'batch'), may hold values from -0.15625 to 0.15625
- gains: float32 [2, 3, 768], replicated, may hold values from 0.5 to 1.5
- gate_params: float32 [2, 2, 384], replicated, as said below
- cotangent: bfloat16 [16, 2048, 768], P('batch', 'seq'), may hold values from -6 to 6
Outputs:
- block_out: bfloat16 [16, 2048, 768], P('batch', 'seq')
- d_tokens: float32 [16, 2048, 768], P('batch', 'seq')
- d_mixer_in: float32 [2, 768, 1920], P(None, 'batch')
- d_mixer_out: float32 [2, 768, 768], P(None, 'batch')
- d_ffn_in: float32 [2, 768, 3072], P(None, 'batch')
- d_ffn_out: float32 [2, 1536, 768], P(None, 'batch')
- d_gains: float32 [2, 3, 768], replicated
- d_gate_params: float32 [2, 2, 384], replicated
The draws below stay inside these ranges and needn't reach their ends.
Inputs may be any that keep to these rules, and one draw needn't show every extreme that they name: `doc_starts`: along each row the starts do not fall and the first is 0; equal starts mark empty documents. gate_params[l, 0] are angles, gate_params[l, 1] lower bounds of the forget gates between 0 and 1.
All inputs are finite; a program needn't handle non-finite values.
Results may differ from the reference program's by a relative error of at most 0.02.
Values may be sent and summed in bfloat16 or wider, within the bound.
A program may use at most 256 MiB of HBM per device.

```python
import math
import jax
import jax.numpy as jnp
from jax import lax

D = 768
C = 384
FF = 1536
LAYERS = 2
LENGTH = 2048
DOCS = 6
ROWS_DEV = 2
ROWS = 16
N_BATCH = 8
N_SEQ = 4


def draw_doc_starts(key, part):
    key = jax.random.fold_in(key, 7)
    keys = jax.random.split(key, 5)
    span = LENGTH // N_SEQ
    generic = jnp.sort(jax.random.randint(keys[0], (ROWS, DOCS - 1), 1, LENGTH), axis=1)
    first_end = jax.random.randint(keys[1], (ROWS, 1), 1, span)
    tail = jnp.sort(jax.random.randint(keys[2], (ROWS, DOCS - 2), LENGTH - span, LENGTH), axis=1)
    special = jnp.concatenate([first_end, tail], axis=1)
    picked = jax.random.randint(keys[3], (N_BATCH, 1), 0, ROWS_DEV)
    row_in_group = jnp.tile(jnp.arange(ROWS_DEV)[None, :], (N_BATCH, 1))
    chosen = (row_in_group == picked).reshape(ROWS, 1)
    remaining = jnp.where(chosen, special, generic)
    starts = jnp.concatenate([jnp.zeros((ROWS, 1), jnp.int32), remaining.astype(jnp.int32)], axis=1)
    target_row = jax.random.randint(keys[4], (), 0, ROWS)
    last_column = jnp.where(jnp.arange(ROWS) == target_row, LENGTH - 1, starts[:, DOCS - 1])
    return starts.at[:, DOCS - 1].set(last_column.astype(jnp.int32))


def draw_gate_params(key, part):
    key = jax.random.fold_in(key, 11)
    keys = jax.random.split(key, 3)
    theta = jax.random.uniform(keys[0], (LAYERS, C), jnp.float32, -math.pi, math.pi)
    spread = jax.random.uniform(keys[1], (LAYERS, C), jnp.float32)
    slowly = jax.random.bernoulli(keys[2], 0.5, (LAYERS, C))
    slow_bound = 1.0 - 0.0002 * jnp.exp(1.6 * spread)
    fast_bound = 0.9 + 0.07 * spread
    lower = jnp.where(slowly, slow_bound, fast_bound)
    return jnp.stack([theta, lower], axis=1).astype(jnp.float32)


def level_of(rng, dims, cuts, smallest, high):
    loudness, own = 1.0, jax.random.fold_in(rng, 6)
    for axis_at, shards_of in cuts:
        heights = jnp.exp(jax.random.uniform(jax.random.fold_in(own, axis_at), (shards_of,), jnp.float32, smallest / len(cuts), high / len(cuts)))
        loudness = loudness * jnp.repeat(heights, dims[axis_at] // shards_of).reshape([-1 if axis == axis_at else 1 for axis in range(len(dims))])
    return loudness


def centred(stream_key, dims, scale, most, cuts=(), kind=jnp.bfloat16):
    loudness = level_of(stream_key, dims, cuts, -0.22, 0.18) if cuts else 1.0
    entries = jax.random.normal(stream_key, dims, jnp.float32) * scale * loudness
    return jnp.minimum(jnp.maximum(entries, -most), most).astype(kind)


def setup_inputs(seed: int = 0) -> dict:
    seeds = jax.random.split(jax.random.key(seed), 10)
    tokens_in = centred(seeds[0], (ROWS, LENGTH, D), 1.0, 6.0, ((0, 8), (1, 4)))
    doc_starts = draw_doc_starts(jax.random.fold_in(seeds[9], 71), 0)
    mixer_in = centred(seeds[2], (LAYERS, D, 3 * C + D), D ** -0.5, 0.21875, ((1, 8),))
    mixer_out = centred(seeds[3], (LAYERS, 2 * C, D), (2 * C) ** -0.5, 0.21875, ((1, 8),))
    ffn_in = centred(seeds[4], (LAYERS, D, 2 * FF), D ** -0.5, 0.21875, ((1, 8),))
    ffn_out = centred(seeds[5], (LAYERS, FF, D), FF ** -0.5, 0.15625, ((1, 8),))
    gains = jnp.clip(1.0 + 0.1 * jax.random.normal(seeds[6], (LAYERS, 3, D), jnp.float32), 0.5, 1.5)
    gate_params = draw_gate_params(jax.random.fold_in(seeds[9], 71), 0)
    cotangent = centred(seeds[8], (ROWS, LENGTH, D), 1.0, 6.0, ((0, 8), (1, 4)))
    return dict(tokens_in=tokens_in, doc_starts=doc_starts, mixer_in=mixer_in, mixer_out=mixer_out, ffn_in=ffn_in, ffn_out=ffn_out, gains=gains, gate_params=gate_params, cotangent=cotangent)


EPS = 1e-06
HIGH = lax.Precision.HIGHEST

@jax.custom_vjp
def low(v):
    return lax.optimization_barrier(v.astype(jnp.bfloat16)).astype(jnp.float32)

@jax.custom_vjp
def low_back(v):
    return v

def low_keep(v):
    return (low(v), None)

def low_pass(kept, grad):
    return (grad,)

def back_keep(v):
    return (v, None)

def back_low(kept, grad):
    return (low(grad),)
low.defvjp(low_keep, low_pass)
low_back.defvjp(back_keep, back_low)

def complex_combine(earlier, later_segment):
    earlier_acc_real, earlier_acc_imaginary, earlier_source_real, earlier_source_imaginary = earlier
    later_term_real, later_term_imaginary, later_source_real, later_source_imaginary = later_segment
    return (later_term_real * earlier_acc_real - later_term_imaginary * earlier_acc_imaginary, later_term_real * earlier_acc_imaginary + later_term_imaginary * earlier_acc_real, later_term_real * earlier_source_real - later_term_imaginary * earlier_source_imaginary + later_source_real, later_term_real * earlier_source_imaginary + later_term_imaginary * earlier_source_real + later_source_imaginary)

def rms_scale(values):
    return lax.rsqrt(lax.optimization_barrier(jnp.mean(values * values, axis=-1, keepdims=True)) + EPS)

def swish(values):
    return values * jax.nn.sigmoid(values)

def mixer_layer(stream, weight_in, weight_out, weight_ffn, weight_down, gain_rows, gate_pair, keep):
    chan = gate_pair.shape[1]
    hidden_units = weight_down.shape[0]
    normed = low(stream * rms_scale(stream) * gain_rows[0])
    projected = low_back(jnp.einsum('bld,de->ble', normed, weight_in, precision=HIGH))
    part_r = projected[..., :chan]
    part_i = projected[..., chan:2 * chan]
    part_f = projected[..., 2 * chan:3 * chan]
    part_g = projected[..., 3 * chan:]
    theta = gate_pair[0]
    lower = gate_pair[1]
    forget = jax.nn.sigmoid(part_f)
    retain = keep[..., None] * (lower + (1.0 - lower) * forget)
    decay_r = retain * jnp.cos(theta)
    decay_i = retain * jnp.sin(theta)
    source_r = (1.0 - retain) * swish(part_r)
    source_i = (1.0 - retain) * swish(part_i)
    scanned = lax.associative_scan(complex_combine, (decay_r, decay_i, source_r, source_i), axis=1)
    state = jnp.concatenate([scanned[2], scanned[3]], axis=-1)
    mixed = low(state * rms_scale(state) * gain_rows[1] * swish(part_g))
    branch = low_back(jnp.einsum('ble,ed->bld', mixed, weight_out, precision=HIGH))
    middle = stream + branch
    normed2 = low(middle * rms_scale(middle) * gain_rows[2])
    gate_up = low_back(jnp.einsum('bld,df->blf', normed2, weight_ffn, precision=HIGH))
    hidden = low(swish(gate_up[..., :hidden_units]) * gate_up[..., hidden_units:])
    down = low_back(jnp.einsum('blf,fd->bld', hidden, weight_down, precision=HIGH))
    return middle + down

def reference(tokens_in, doc_starts, mixer_in, mixer_out, ffn_in, ffn_out, gains, gate_params, cotangent):
    params = (mixer_in.astype(jnp.float32), mixer_out.astype(jnp.float32), ffn_in.astype(jnp.float32), ffn_out.astype(jnp.float32), gains, gate_params)
    positions = jnp.arange(LENGTH).astype(jnp.int32)
    group_rows = 2

    def whole_block(stream, weights, keep):
        for which_layer in range(LAYERS):
            stream = mixer_layer(stream, weights[0][which_layer], weights[1][which_layer], weights[2][which_layer], weights[3][which_layer], weights[4][which_layer], weights[5][which_layer], keep)
        return stream

    def group_step(grads, group_index):
        start = (group_index * group_rows).astype(jnp.int32)
        stream = lax.dynamic_slice_in_dim(tokens_in, start, group_rows, 0).astype(jnp.float32)
        seed_grad = lax.dynamic_slice_in_dim(cotangent, start, group_rows, 0).astype(jnp.float32)
        starts = lax.dynamic_slice_in_dim(doc_starts, start, group_rows, 0)
        resets = jnp.any(starts[:, :, None] == positions[None, None, :], axis=1)
        keep = 1.0 - resets.astype(jnp.float32)
        result, pull = jax.vjp(lambda s, w: whole_block(s, w, keep), stream, params)
        grad_stream, grad_params = pull(seed_grad)
        grads = jax.tree.map(jnp.add, grads, grad_params)
        return (grads, (result.astype(jnp.bfloat16), grad_stream))
    initial = tuple((jnp.zeros_like(p) for p in params))
    grads, outputs = lax.scan(group_step, initial, jnp.arange(ROWS // group_rows).astype(jnp.int32))
    block_out = outputs[0].reshape(ROWS, LENGTH, D)
    d_tokens = outputs[1].reshape(ROWS, LENGTH, D)
    return (block_out, d_tokens, grads[0], grads[1], grads[2], grads[3], grads[4], grads[5])
```

```python
import functools

import jax
import jax.numpy as jnp
from jax import lax
from jax.experimental import pallas as pl
from jax.experimental.pallas import tpu as pltpu
from jax.sharding import PartitionSpec as P

LAYERS = 2
EPS = 1e-06
F32 = jnp.float32
BF16 = jnp.bfloat16
LANES = 128
MESH = pl.DeviceIdType.MESH


def sigmoid(values):
    return 1.0 / (1.0 + jnp.exp(-values))


def rms_scale(values):
    return lax.rsqrt(jnp.mean(values * values, axis=-1, keepdims=True) + EPS)


def dot(left, right):
    return jnp.dot(left, right, preferred_element_type=F32)


def dot_t(left, right):
    return lax.dot_general(left, right, (((1,), (1,)), ((), ())), preferred_element_type=F32)


def eight_sum(values):
    rows, cols = values.shape
    return jnp.sum(values.reshape(rows // 8, 8, cols), axis=0)


def wide(ref, first, last):
    return jnp.concatenate([ref[g] for g in range(first, last)], axis=-1)


def split_store(ref, first, values):
    for g in range(values.shape[1] // LANES):
        ref[first + g] = values[:, g * LANES : (g + 1) * LANES]


def lanes(values):
    return [values[:, g * LANES : (g + 1) * LANES] for g in range(values.shape[1] // LANES)]


def keep_mask(rel_ref, row, first, shape):
    pos = lax.broadcasted_iota(jnp.int32, shape, 0) + first
    hit = pos == rel_ref[row, 0]
    for k in range(1, rel_ref.shape[1]):
        hit = hit | (pos == rel_ref[row, k])
    return hit


def enter_kernel(rel_ref, x_ref, w_ref, gain_ref, gate_ref, proj_ref, normed_ref, lam_ref, h_ref,
                 cum_ref, ends_ref, tot_ref, src):
    row, tile = pl.program_id(0), pl.program_id(1)
    tokens, width = x_ref.shape
    chan = width // 2
    seg = tokens // 8
    x = x_ref[...].astype(F32)
    normed = (x * rms_scale(x) * gain_ref[0:1, :]).astype(BF16)
    normed_ref[...] = normed
    proj = dot(normed, w_ref[...])
    proj_ref[...] = proj.astype(BF16)
    cos, sin, lower = gate_ref[0:1, :], gate_ref[1:2, :], gate_ref[2:3, :]
    seg_cos, seg_sin = gate_ref[3:4, :], gate_ref[4:5, :]
    p_r, p_i, p_f = proj[:, :chan], proj[:, chan : 2 * chan], proj[:, 2 * chan : 3 * chan]
    hit = keep_mask(rel_ref, row, tile * tokens, (tokens, chan))
    lam = jnp.where(hit, 0.0, lower + (1.0 - lower) * sigmoid(p_f))
    groups = chan // LANES
    split_store(lam_ref, 0, lam)
    split_store(src, 0, (1.0 - lam) * (p_r * sigmoid(p_r)))
    split_store(src, groups, (1.0 - lam) * (p_i * sigmoid(p_i)))
    cos_l, sin_l = lanes(cos), lanes(sin)

    def step(s, state):
        at = pl.ds(s, 8, stride=seg)
        after = []
        for k, (h_r, h_i, cum) in enumerate(state):
            lam_s = lam_ref[k, at, :]
            a_r, a_i = lam_s * cos_l[k], lam_s * sin_l[k]
            n_r = a_r * h_r - a_i * h_i + src[k, at, :]
            n_i = a_r * h_i + a_i * h_r + src[groups + k, at, :]
            cum = cum * lam_s
            h_ref[k, at, :] = n_r
            h_ref[groups + k, at, :] = n_i
            cum_ref[k, at, :] = cum
            after.append((n_r, n_i, cum))
        return tuple(after)

    zero = lam_ref[0, 0:8, :] * 0.0
    last = lax.fori_loop(0, seg, step, ((zero, zero, zero + 1.0),) * groups, unroll=8)
    e_r, e_i, e_c = (jnp.concatenate([v[i] for v in last], axis=-1) for i in range(3))
    ends_ref[0, 0:8, :] = e_r
    ends_ref[0, 8:16, :] = e_i
    ends_ref[0, 16:24, :] = e_c

    @pl.when(tile == 0)
    def _():
        tot_ref[0, 0:2, :] = jnp.zeros((2, chan), F32)
        tot_ref[0, 2:3, :] = jnp.ones((1, chan), F32)

    c_r, c_i, c_l = tot_ref[0, 0:1, :], tot_ref[0, 1:2, :], tot_ref[0, 2:3, :]
    for j in range(8):
        m = e_c[j : j + 1, :]
        a_r, a_i = m * seg_cos, m * seg_sin
        c_r, c_i = a_r * c_r - a_i * c_i + e_r[j : j + 1, :], a_r * c_i + a_i * c_r + e_i[j : j + 1, :]
        c_l = c_l * m
    tot_ref[0, 0:1, :] = c_r
    tot_ref[0, 1:2, :] = c_i
    tot_ref[0, 2:3, :] = c_l


def leave_kernel(x_ref, proj_ref, h_ref, cum_ref, ends_ref, carry_ref, wo_ref, wf_ref, wd_ref,
                 gain_ref, gate_ref, state_ref, prior_ref, mixed_ref, mid_ref, normed_ref, gu_ref,
                 hid_ref, out_ref, run):
    tile = pl.program_id(1)
    tokens, width = x_ref.shape
    chan = width // 2
    seg = tokens // 8
    cos, sin = gate_ref[0:1, :], gate_ref[1:2, :]
    seg_cos, seg_sin = gate_ref[3:4, :], gate_ref[4:5, :]

    @pl.when(tile == 0)
    def _():
        run[0:2, :] = carry_ref[0, 0:2, :]

    c_r, c_i = run[0:1, :], run[1:2, :]
    l_r, l_i = [], []
    for j in range(8):
        l_r.append(c_r)
        l_i.append(c_i)
        m = ends_ref[0, 16 + j : 17 + j, :]
        a_r, a_i = m * seg_cos, m * seg_sin
        c_r, c_i = (
            a_r * c_r - a_i * c_i + ends_ref[0, j : j + 1, :],
            a_r * c_i + a_i * c_r + ends_ref[0, 8 + j : 9 + j, :],
        )
    run[0:1, :] = c_r
    run[1:2, :] = c_i
    groups = chan // LANES
    start_r, start_i = lanes(jnp.concatenate(l_r, axis=0)), lanes(jnp.concatenate(l_i, axis=0))
    cos_l, sin_l = lanes(cos), lanes(sin)

    def step(s, state):
        at = pl.ds(s, 8, stride=seg)
        after = []
        for k, (w_r, w_i, q_r, q_i) in enumerate(state):
            w_r, w_i = w_r * cos_l[k] - w_i * sin_l[k], w_r * sin_l[k] + w_i * cos_l[k]
            cum = cum_ref[k, at, :]
            s_r = h_ref[k, at, :] + cum * w_r
            s_i = h_ref[groups + k, at, :] + cum * w_i
            state_ref[k, at, :] = s_r
            state_ref[groups + k, at, :] = s_i
            prior_ref[k, at, :] = q_r
            prior_ref[groups + k, at, :] = q_i
            after.append((w_r, w_i, s_r, s_i))
        return tuple(after)

    lax.fori_loop(0, seg, step, tuple(zip(start_r, start_i, start_r, start_i)), unroll=8)
    state = wide(state_ref, 0, 2 * groups)
    p_g = proj_ref[...].astype(F32)
    mixed = (state * rms_scale(state) * gain_ref[1:2, :] * (p_g * sigmoid(p_g))).astype(BF16)
    mixed_ref[...] = mixed
    mid = x_ref[...].astype(F32) + dot(mixed, wo_ref[...])
    mid_ref[...] = mid
    normed = (mid * rms_scale(mid) * gain_ref[2:3, :]).astype(BF16)
    normed_ref[...] = normed
    gu = dot(normed, wf_ref[...])
    gu_ref[...] = gu.astype(BF16)
    hidden = gu.shape[1] // 2
    gate = gu[:, :hidden]
    hid = (gate * sigmoid(gate) * gu[:, hidden:]).astype(BF16)
    hid_ref[...] = hid
    out_ref[...] = (mid + dot(hid, wd_ref[...])).astype(out_ref.dtype)


def back_out_kernel(dx_ref, gu_ref, mid_ref, state_ref, proj_ref, lam_ref, wo_ref, wf_ref, wd_ref,
                    gain_ref, gate_ref, dz_ref, dgu_ref, dmid_ref, dy_ref, dpg_ref, g_ref, cum_ref,
                    ends_ref, tot_ref, dgain_ref, grad):
    row, tile = pl.program_id(0), pl.program_id(1)
    tokens, width = dx_ref.shape
    chan = width // 2
    seg = tokens // 8
    cos, sin = gate_ref[0:1, :], gate_ref[1:2, :]
    seg_cos, seg_sin = gate_ref[3:4, :], gate_ref[4:5, :]
    dx = dx_ref[...].astype(F32)
    dz = dx.astype(BF16)
    dz_ref[...] = dz
    d_hid = dot_t(dz, wd_ref[...])
    hidden = d_hid.shape[1]
    gate = gu_ref[:, :hidden].astype(F32)
    up = gu_ref[:, hidden:].astype(F32)
    sg = sigmoid(gate)
    silu = gate * sg
    d_gu = jnp.concatenate(
        [(d_hid * up * (sg + silu * (1.0 - sg))).astype(BF16), (d_hid * silu).astype(BF16)], axis=1
    )
    dgu_ref[...] = d_gu
    d_n = dot_t(d_gu, wf_ref[...])
    mid = mid_ref[...]
    scale = rms_scale(mid)
    hat = mid * scale
    d_hat = d_n * gain_ref[2:3, :]

    @pl.when((row == 0) & (tile == 0))
    def _():
        dgain_ref[...] = jnp.zeros_like(dgain_ref)

    dgain_ref[8:16, :] += eight_sum(d_n * hat)
    d_mid = dx + scale * (d_hat - hat * jnp.mean(d_hat * hat, axis=-1, keepdims=True))
    dmid_ref[...] = d_mid
    dy = d_mid.astype(BF16)
    dy_ref[...] = dy
    d_mixed = dot_t(dy, wo_ref[...])
    p_g = proj_ref[...].astype(F32)
    sg = sigmoid(p_g)
    silu = p_g * sg
    groups = chan // LANES
    state = wide(state_ref, 0, 2 * groups)
    scale = rms_scale(state)
    hat = state * scale
    g1 = gain_ref[1:2, :]
    dpg_ref[...] = (d_mixed * hat * g1 * (sg + silu * (1.0 - sg))).astype(BF16)
    d_n = d_mixed * silu
    dgain_ref[0:8, :] += eight_sum(d_n * hat)
    d_hat = d_n * g1
    split_store(grad, 0, scale * (d_hat - hat * jnp.mean(d_hat * hat, axis=-1, keepdims=True)))
    cos_l, sin_l = lanes(cos), lanes(sin)

    def step(s, state):
        at = pl.ds(seg - 1 - s, 8, stride=seg)
        after = []
        for k, (g_r, g_i, cum, lam_n) in enumerate(state):
            a_r, a_i = lam_n * cos_l[k], lam_n * sin_l[k]
            n_r = grad[k, at, :] + a_r * g_r + a_i * g_i
            n_i = grad[groups + k, at, :] + a_r * g_i - a_i * g_r
            cum = cum * lam_n
            g_ref[k, at, :] = n_r
            g_ref[groups + k, at, :] = n_i
            cum_ref[k, at, :] = cum
            after.append((n_r, n_i, cum, lam_ref[k, at, :]))
        return tuple(after)

    zero = lam_ref[0, 0:8, :] * 0.0
    last = lax.fori_loop(0, seg, step, ((zero, zero, zero + 1.0, zero + 1.0),) * groups, unroll=8)
    g_r, g_i, cum, lam_0 = (jnp.concatenate([v[i] for v in last], axis=-1) for i in range(4))
    e_r = lam_0 * (cos * g_r + sin * g_i)
    e_i = lam_0 * (cos * g_i - sin * g_r)
    e_c = lam_0 * cum
    ends_ref[0, 0:8, :] = e_r
    ends_ref[0, 8:16, :] = e_i
    ends_ref[0, 16:24, :] = e_c

    @pl.when(tile == 0)
    def _():
        tot_ref[0, 0:2, :] = jnp.zeros((2, chan), F32)
        tot_ref[0, 2:3, :] = jnp.ones((1, chan), F32)

    c_r, c_i, c_l = tot_ref[0, 0:1, :], tot_ref[0, 1:2, :], tot_ref[0, 2:3, :]
    for j in reversed(range(8)):
        m = e_c[j : j + 1, :]
        a_r, a_i = m * seg_cos, m * seg_sin
        c_r, c_i = a_r * c_r + a_i * c_i + e_r[j : j + 1, :], a_r * c_i - a_i * c_r + e_i[j : j + 1, :]
        c_l = c_l * m
    tot_ref[0, 0:1, :] = c_r
    tot_ref[0, 1:2, :] = c_i
    tot_ref[0, 2:3, :] = c_l


def back_in_kernel(rel_ref, x_ref, dmid_ref, proj_ref, dpg_ref, lam_ref, prior_ref, g_ref, cum_ref,
                   ends_ref, carry_ref, w_ref, gain_ref, gate_ref, dproj_ref, dx_ref, dgain_ref,
                   dgate_ref, run, tot):
    row, tile = pl.program_id(0), pl.program_id(1)
    tokens, width = x_ref.shape
    chan = width // 2
    seg = tokens // 8
    cos, sin, lower = gate_ref[0:1, :], gate_ref[1:2, :], gate_ref[2:3, :]
    seg_cos, seg_sin = gate_ref[3:4, :], gate_ref[4:5, :]

    @pl.when(tile == 0)
    def _():
        run[0:2, :] = carry_ref[0, 0:2, :]

    c_r, c_i = run[0:1, :], run[1:2, :]
    l_r, l_i = [None] * 8, [None] * 8
    for j in reversed(range(8)):
        l_r[j], l_i[j] = c_r, c_i
        m = ends_ref[0, 16 + j : 17 + j, :]
        a_r, a_i = m * seg_cos, m * seg_sin
        c_r, c_i = (
            a_r * c_r + a_i * c_i + ends_ref[0, j : j + 1, :],
            a_r * c_i - a_i * c_r + ends_ref[0, 8 + j : 9 + j, :],
        )
    run[0:1, :] = c_r
    run[1:2, :] = c_i

    groups = chan // LANES
    start_r, start_i = lanes(jnp.concatenate(l_r, axis=0)), lanes(jnp.concatenate(l_i, axis=0))
    cos_l, sin_l = lanes(cos), lanes(sin)

    def step(s, state):
        at = pl.ds(seg - 1 - s, 8, stride=seg)
        after = []
        for k, (w_r, w_i) in enumerate(state):
            cum = cum_ref[k, at, :]
            tot[k, at, :] = g_ref[k, at, :] + cum * w_r
            tot[groups + k, at, :] = g_ref[groups + k, at, :] + cum * w_i
            after.append((w_r * cos_l[k] + w_i * sin_l[k], w_i * cos_l[k] - w_r * sin_l[k]))
        return tuple(after)

    lax.fori_loop(0, seg, step, tuple(zip(start_r, start_i)), unroll=8)
    g_r, g_i = wide(tot, 0, groups), wide(tot, groups, 2 * groups)
    q_r, q_i = wide(prior_ref, 0, groups), wide(prior_ref, groups, 2 * groups)
    p_r = proj_ref[:, :chan].astype(F32)
    p_i = proj_ref[:, chan : 2 * chan].astype(F32)
    forget = sigmoid(proj_ref[:, 2 * chan : 3 * chan].astype(F32))
    lam = wide(lam_ref, 0, groups)
    d_ar = g_r * q_r + g_i * q_i
    d_ai = g_i * q_r - g_r * q_i
    s_r, s_i = sigmoid(p_r), sigmoid(p_i)
    in_r, in_i = p_r * s_r, p_i * s_i
    d_lam = d_ar * cos + d_ai * sin - (g_r * in_r + g_i * in_i)

    @pl.when((row == 0) & (tile == 0))
    def _():
        dgain_ref[...] = jnp.zeros_like(dgain_ref)
        dgate_ref[...] = jnp.zeros_like(dgate_ref)

    dgate_ref[0:8, :] += eight_sum(lam * (d_ai * cos - d_ar * sin))
    first = (pl.num_programs(1) - 1 - tile) * tokens
    hit = keep_mask(rel_ref, row, first, (tokens, chan))
    d_f = jnp.where(hit, 0.0, d_lam) * (1.0 - forget)
    dgate_ref[8:16, :] += eight_sum(d_f)
    rest = 1.0 - lam
    d_proj = jnp.concatenate(
        [
            (rest * g_r * (s_r + in_r * (1.0 - s_r))).astype(BF16),
            (rest * g_i * (s_i + in_i * (1.0 - s_i))).astype(BF16),
            (d_f * (1.0 - lower) * forget).astype(BF16),
            dpg_ref[...],
        ],
        axis=1,
    )
    dproj_ref[...] = d_proj
    d_n = dot_t(d_proj, w_ref[...])
    x = x_ref[...].astype(F32)
    scale = rms_scale(x)
    hat = x * scale
    dgain_ref[...] += eight_sum(d_n * hat)
    d_hat = d_n * gain_ref[0:1, :]
    dx_ref[...] = dmid_ref[...] + scale * (d_hat - hat * jnp.mean(d_hat * hat, axis=-1, keepdims=True))


def carry_kernel(axis, count, forward, tot_ref, rot_ref, out_ref, buf, send_sem, recv_sem):
    me = lax.axis_index(axis)
    barrier = pltpu.get_barrier_semaphore()
    peers = [lax.rem(me + k, count) for k in range(1, count)]
    for peer in peers:
        pl.semaphore_signal(barrier, inc=1, device_id={axis: peer}, device_id_type=MESH)
    pl.semaphore_wait(barrier, count - 1)
    copies = []
    for k, peer in enumerate(peers):
        copy = pltpu.make_async_remote_copy(
            src_ref=tot_ref,
            dst_ref=buf.at[k],
            send_sem=send_sem.at[k],
            recv_sem=recv_sem.at[k],
            device_id={axis: peer},
            device_id_type=MESH,
        )
        copy.start()
        copies.append(copy)
    for copy in copies:
        copy.wait()
    cos, sin = rot_ref[0:1, :], rot_ref[1:2, :]
    rows = tot_ref.shape[0]
    for r in range(rows):
        c_r = jnp.zeros_like(cos)
        c_i = jnp.zeros_like(cos)
        for k in range(count - 1, 0, -1):
            slot = k - 1 if forward else count - k - 1
            valid = me >= k if forward else me + k < count
            e_r, e_i, m = buf[slot, r, 0:1, :], buf[slot, r, 1:2, :], buf[slot, r, 2:3, :]
            a_r = m * cos
            a_i = m * sin if forward else -m * sin
            n_r = a_r * c_r - a_i * c_i + e_r
            n_i = a_r * c_i + a_i * c_r + e_i
            keep = jnp.where(valid, 1.0, 0.0)
            c_r, c_i = n_r * keep, n_i * keep
        out_ref[r, 0:1, :] = c_r
        out_ref[r, 1:2, :] = c_i


def vmem(bytes_):
    return pltpu.CompilerParams(vmem_limit_bytes=bytes_)


def whole(*shape):
    return pl.BlockSpec(shape, lambda *_: (0,) * len(shape), pipeline_mode=pl.Buffered(1))


def make_carry(count, rows, chan, forward):
    return pl.pallas_call(
        functools.partial(carry_kernel, "seq", count, forward),
        out_shape=jax.ShapeDtypeStruct((rows, 8, chan), F32),
        in_specs=[pl.BlockSpec(memory_space=pltpu.VMEM)] * 2,
        out_specs=pl.BlockSpec(memory_space=pltpu.VMEM),
        scratch_shapes=[
            pltpu.VMEM((count - 1, rows, 8, chan), F32),
            pltpu.SemaphoreType.DMA((count - 1,)),
            pltpu.SemaphoreType.DMA((count - 1,)),
        ],
        compiler_params=pltpu.CompilerParams(
            collective_id=1 if forward else 2, has_side_effects=True
        ),
    )


LIMIT = 48 * 1024 * 1024


def layer_calls(rows, length, width, hidden, cols, n_seq, tokens):
    chan = width // 2
    tiles = length // tokens
    total = rows * length
    grid = (rows, tiles)
    shape = jax.ShapeDtypeStruct
    smem = pl.BlockSpec(memory_space=pltpu.SMEM)

    def fwd(w, col=0):
        return pl.BlockSpec((tokens, w), lambda r, t: (r * tiles + t, col))

    def fwd_l(w):
        return pl.BlockSpec((w // LANES, tokens, LANES), lambda r, t: (0, r * tiles + t, 0))

    def bwd_l(w):
        return pl.BlockSpec(
            (w // LANES, tokens, LANES), lambda r, t: (0, r * tiles + tiles - 1 - t, 0)
        )

    def split(w):
        return shape((w // LANES, total, LANES), F32)

    def bwd(w, col=0):
        return pl.BlockSpec((tokens, w), lambda r, t: (r * tiles + tiles - 1 - t, col))

    ends_f = pl.BlockSpec((1, 24, chan), lambda r, t: (r * tiles + t, 0, 0))
    ends_b = pl.BlockSpec((1, 24, chan), lambda r, t: (r * tiles + tiles - 1 - t, 0, 0))
    per_row = pl.BlockSpec((1, 8, chan), lambda r, t: (r, 0, 0))
    ends_s = shape((rows * tiles, 24, chan), F32)
    row_s = shape((rows, 8, chan), F32)

    enter = pl.pallas_call(
        enter_kernel,
        grid=grid,
        in_specs=[smem, fwd(width), whole(width, cols), whole(8, width), whole(8, chan)],
        out_specs=[fwd(cols), fwd(width), fwd_l(chan), fwd_l(width), fwd_l(chan), ends_f, per_row],
        out_shape=[
            shape((total, cols), BF16),
            shape((total, width), BF16),
            split(chan),
            split(width),
            split(chan),
            ends_s,
            row_s,
        ],
        scratch_shapes=[pltpu.VMEM((width // LANES, tokens, LANES), F32)],
        compiler_params=vmem(LIMIT),
    )

    def leave(out_type):
        return pl.pallas_call(
            leave_kernel,
            grid=grid,
            in_specs=[
                fwd(width),
                fwd(width),
                fwd_l(width),
                fwd_l(chan),
                ends_f,
                per_row,
                whole(width, width),
                whole(width, 2 * hidden),
                whole(hidden, width),
                whole(8, width),
                whole(8, chan),
            ],
            out_specs=[
                fwd_l(width),
                fwd_l(width),
                fwd(width),
                fwd(width),
                fwd(width),
                fwd(2 * hidden),
                fwd(hidden),
                fwd(width),
            ],
            out_shape=[
                split(width),
                split(width),
                shape((total, width), BF16),
                shape((total, width), F32),
                shape((total, width), BF16),
                shape((total, 2 * hidden), BF16),
                shape((total, hidden), BF16),
                shape((total, width), out_type),
            ],
            scratch_shapes=[pltpu.VMEM((8, chan), F32)],
            compiler_params=vmem(LIMIT),
        )

    back_out = pl.pallas_call(
        back_out_kernel,
        grid=grid,
        in_specs=[
            bwd(width),
            bwd(2 * hidden),
            bwd(width),
            bwd_l(width),
            bwd(width),
            bwd_l(chan),
            whole(width, width),
            whole(width, 2 * hidden),
            whole(hidden, width),
            whole(8, width),
            whole(8, chan),
        ],
        out_specs=[
            bwd(width),
            bwd(2 * hidden),
            bwd(width),
            bwd(width),
            bwd(width),
            bwd_l(width),
            bwd_l(chan),
            ends_b,
            per_row,
            pl.BlockSpec((16, width), lambda r, t: (0, 0)),
        ],
        out_shape=[
            shape((total, width), BF16),
            shape((total, 2 * hidden), BF16),
            shape((total, width), F32),
            shape((total, width), BF16),
            shape((total, width), BF16),
            split(width),
            split(chan),
            ends_s,
            row_s,
            shape((16, width), F32),
        ],
        scratch_shapes=[pltpu.VMEM((width // LANES, tokens, LANES), F32)],
        compiler_params=vmem(LIMIT),
    )

    back_in = pl.pallas_call(
        back_in_kernel,
        grid=grid,
        in_specs=[
            smem,
            bwd(width),
            bwd(width),
            bwd(3 * chan),
            bwd(width),
            bwd_l(chan),
            bwd_l(width),
            bwd_l(width),
            bwd_l(chan),
            ends_b,
            per_row,
            whole(width, cols),
            whole(8, width),
            whole(8, chan),
        ],
        out_specs=[
            bwd(cols),
            bwd(width),
            pl.BlockSpec((8, width), lambda r, t: (0, 0)),
            pl.BlockSpec((16, chan), lambda r, t: (0, 0)),
        ],
        out_shape=[
            shape((total, cols), BF16),
            shape((total, width), F32),
            shape((8, width), F32),
            shape((16, chan), F32),
        ],
        scratch_shapes=[
            pltpu.VMEM((8, chan), F32),
            pltpu.VMEM((width // LANES, tokens, LANES), F32),
        ],
        compiler_params=vmem(LIMIT),
    )
    carry_f = make_carry(n_seq, rows, chan, True)
    carry_b = make_carry(n_seq, rows, chan, False)
    return enter, carry_f, leave, back_out, carry_b, back_in


def contract_rows(left, right):
    return lax.dot_general(
        left, right, (((0,), (0,)), ((), ())), preferred_element_type=F32
    ).astype(BF16)


def shards(
    tokens_in, doc_starts, mixer_in, mixer_out, ffn_in, ffn_out, gains, gate_params, cotangent
):
    rows, length, width = tokens_in.shape
    chan = width // 2
    n_seq = lax.axis_size("seq")
    hidden = ffn_in.shape[2] // 2
    cols = mixer_in.shape[2]
    total = rows * length
    tokens = min(length, 256)
    seg = tokens // 8
    enter, carry_f, leave, back_out, carry_b, back_in = layer_calls(
        rows, length, width, hidden, cols, n_seq, tokens
    )
    rel = doc_starts - lax.axis_index("seq") * length
    gain_rows = jnp.pad(gains, ((0, 0), (0, 5), (0, 0)))
    theta, lower = gate_params[:, 0], gate_params[:, 1]
    gate_rows = jnp.stack(
        [jnp.cos(theta), jnp.sin(theta), lower, jnp.cos(theta * seg), jnp.sin(theta * seg),
         jnp.cos(theta * length), jnp.sin(theta * length), lower], axis=1
    )
    x = tokens_in.reshape(total, width)
    saved = []
    for k in range(LAYERS):
        w_in = lax.all_gather(mixer_in[k], "batch", axis=0, tiled=True)
        w_out = lax.all_gather(mixer_out[k], "batch", axis=0, tiled=True)
        w_ffn = lax.all_gather(ffn_in[k], "batch", axis=0, tiled=True)
        w_down = lax.all_gather(ffn_out[k], "batch", axis=0, tiled=True)
        proj, normed, lam, h, cum, ends, tot = enter(rel, x, w_in, gain_rows[k], gate_rows[k])
        carry = carry_f(tot, gate_rows[k, 5:8])
        state, prior, mixed, mid, normed2, gu, hid, nxt = leave(F32 if k + 1 < LAYERS else BF16)(
            x, proj[:, 3 * chan :], h, cum, ends, carry, w_out, w_ffn, w_down, gain_rows[k], gate_rows[k]
        )
        saved.append((w_in, w_out, w_ffn, w_down, x, proj, normed, lam, state, prior, mixed, mid,
                      normed2, gu, hid))
        x = nxt
    block_out = x.reshape(rows, length, width)
    dx = cotangent.reshape(total, width)
    big, small_gain, small_gate = [None] * LAYERS, [None] * LAYERS, [None] * LAYERS
    for k in reversed(range(LAYERS)):
        (w_in, w_out, w_ffn, w_down, x, proj, normed, lam, state, prior, mixed, mid,
         normed2, gu, hid) = saved[k]
        dz, d_gu, d_mid, dy, d_pg, g, cum, ends, tot, dg_a = back_out(
            dx, gu, mid, state, proj[:, 3 * chan :], lam, w_out, w_ffn, w_down, gain_rows[k], gate_rows[k]
        )
        carry = carry_b(tot, gate_rows[k, 5:8])
        d_proj, dx, dg_b, dgate = back_in(
            rel, x, d_mid, proj, d_pg, lam, prior, g, cum, ends, carry, w_in, gain_rows[k], gate_rows[k]
        )
        big[k] = (
            contract_rows(normed, d_proj),
            contract_rows(mixed, dy),
            contract_rows(normed2, d_gu),
            contract_rows(hid, dz),
        )
        small_gain[k] = jnp.stack(
            [jnp.sum(dg_b, axis=0), jnp.sum(dg_a[:8], axis=0), jnp.sum(dg_a[8:], axis=0)]
        )
        small_gate[k] = jnp.stack([jnp.sum(dgate[:8], axis=0), jnp.sum(dgate[8:], axis=0)])
    d_gains, d_gate_params = lax.psum(
        (jnp.stack(small_gain), jnp.stack(small_gate)), ("batch", "seq")
    )
    outs = []
    for m in range(4):
        parts = []
        for k in range(LAYERS):
            part = lax.psum_scatter(big[k][m], "batch", scatter_dimension=0, tiled=True)
            parts.append(lax.psum(part, "seq").astype(F32))
        outs.append(jnp.stack(parts))
    return (block_out, dx.reshape(rows, length, width), *outs, d_gains, d_gate_params)


def solution(mesh):
    tok = P("batch", "seq", None)
    mat = P(None, "batch", None)
    return jax.shard_map(
        shards,
        mesh=mesh,
        in_specs=(tok, P("batch", None), mat, mat, mat, mat, P(), P(), tok),
        out_specs=(tok, tok, mat, mat, mat, mat, P(), P()),
        check_vma=False,
    )
```

```python
import functools

import jax
import jax.numpy as jnp
from jax import lax
from jax.experimental import pallas as pl
from jax.experimental.pallas import tpu as pltpu
from jax.sharding import PartitionSpec as P

LAYERS = 2
EPS = 1e-06
F32 = jnp.float32
BF16 = jnp.bfloat16
LANES = 128
MESH = pl.DeviceIdType.MESH


def sigmoid(values):
    return 1.0 / (1.0 + jnp.exp(-values))


def rms_scale(values):
    return lax.rsqrt(jnp.mean(values * values, axis=-1, keepdims=True) + EPS)


def dot(left, right):
    return jnp.dot(left, right, preferred_element_type=F32)


def dot_t(left, right):
    return lax.dot_general(left, right, (((1,), (1,)), ((), ())), preferred_element_type=F32)


def eight_sum(values):
    rows, cols = values.shape
    return jnp.sum(values.reshape(rows // 8, 8, cols), axis=0)


def wide(ref, first, last):
    return jnp.concatenate([ref[g] for g in range(first, last)], axis=-1)


def split_store(ref, first, values):
    for g in range(values.shape[1] // LANES):
        ref[first + g] = values[:, g * LANES : (g + 1) * LANES]


def lanes(values):
    return [values[:, g * LANES : (g + 1) * LANES] for g in range(values.shape[1] // LANES)]


def keep_mask(rel_ref, row, first, shape):
    pos = lax.broadcasted_iota(jnp.int32, shape, 0) + first
    hit = pos == rel_ref[row, 0]
    for k in range(1, rel_ref.shape[1]):
        hit = hit | (pos == rel_ref[row, k])
    return hit


def enter_kernel(rel_ref, x_ref, w_ref, gain_ref, gate_ref, proj_ref, normed_ref, lam_ref, h_ref,
                 cum_ref, ends_ref, tot_ref, src):
    row, tile = pl.program_id(0), pl.program_id(1)
    tokens, width = x_ref.shape
    chan = width // 2
    seg = tokens // 8
    x = x_ref[...].astype(F32)
    normed = (x * rms_scale(x) * gain_ref[0:1, :]).astype(BF16)
    normed_ref[...] = normed
    proj = dot(normed, w_ref[...])
    proj_ref[...] = proj.astype(BF16)
    cos, sin, lower = gate_ref[0:1, :], gate_ref[1:2, :], gate_ref[2:3, :]
    seg_cos, seg_sin = gate_ref[3:4, :], gate_ref[4:5, :]
    p_r, p_i, p_f = proj[:, :chan], proj[:, chan : 2 * chan], proj[:, 2 * chan : 3 * chan]
    hit = keep_mask(rel_ref, row, tile * tokens, (tokens, chan))
    lam = jnp.where(hit, 0.0, lower + (1.0 - lower) * sigmoid(p_f))
    groups = chan // LANES
    split_store(lam_ref, 0, lam)
    split_store(src, 0, (1.0 - lam) * (p_r * sigmoid(p_r)))
    split_store(src, groups, (1.0 - lam) * (p_i * sigmoid(p_i)))
    cos_l, sin_l = lanes(cos), lanes(sin)

    def step(s, state):
        at = pl.ds(s, 8, stride=seg)
        after = []
        for k, (h_r, h_i, cum) in enumerate(state):
            lam_s = lam_ref[k, at, :]
            a_r, a_i = lam_s * cos_l[k], lam_s * sin_l[k]
            n_r = a_r * h_r - a_i * h_i + src[k, at, :]
            n_i = a_r * h_i + a_i * h_r + src[groups + k, at, :]
            cum = cum * lam_s
            h_ref[k, at, :] = n_r
            h_ref[groups + k, at, :] = n_i
            cum_ref[k, at, :] = cum
            after.append((n_r, n_i, cum))
        return tuple(after)

    zero = lam_ref[0, 0:8, :] * 0.0
    last = lax.fori_loop(0, seg, step, ((zero, zero, zero + 1.0),) * groups, unroll=8)
    e_r, e_i, e_c = (jnp.concatenate([v[i] for v in last], axis=-1) for i in range(3))
    ends_ref[0, 0:8, :] = e_r
    ends_ref[0, 8:16, :] = e_i
    ends_ref[0, 16:24, :] = e_c

    @pl.when(tile == 0)
    def _():
        tot_ref[0, 0:2, :] = jnp.zeros((2, chan), F32)
        tot_ref[0, 2:3, :] = jnp.ones((1, chan), F32)

    c_r, c_i, c_l = tot_ref[0, 0:1, :], tot_ref[0, 1:2, :], tot_ref[0, 2:3, :]
    for j in range(8):
        m = e_c[j : j + 1, :]
        a_r, a_i = m * seg_cos, m * seg_sin
        c_r, c_i = a_r * c_r - a_i * c_i + e_r[j : j + 1, :], a_r * c_i + a_i * c_r + e_i[j : j + 1, :]
        c_l = c_l * m
    tot_ref[0, 0:1, :] = c_r
    tot_ref[0, 1:2, :] = c_i
    tot_ref[0, 2:3, :] = c_l


def leave_kernel(x_ref, proj_ref, h_ref, cum_ref, ends_ref, carry_ref, wo_ref, wf_ref, wd_ref,
                 gain_ref, gate_ref, state_ref, prior_ref, mixed_ref, mid_ref, normed_ref, gu_ref,
                 hid_ref, out_ref, run):
    tile = pl.program_id(1)
    tokens, width = x_ref.shape
    chan = width // 2
    seg = tokens // 8
    cos, sin = gate_ref[0:1, :], gate_ref[1:2, :]
    seg_cos, seg_sin = gate_ref[3:4, :], gate_ref[4:5, :]

    @pl.when(tile == 0)
    def _():
        run[0:2, :] = carry_ref[0, 0:2, :]

    c_r, c_i = run[0:1, :], run[1:2, :]
    l_r, l_i = [], []
    for j in range(8):
        l_r.append(c_r)
        l_i.append(c_i)
        m = ends_ref[0, 16 + j : 17 + j, :]
        a_r, a_i = m * seg_cos, m * seg_sin
        c_r, c_i = (
            a_r * c_r - a_i * c_i + ends_ref[0, j : j + 1, :],
            a_r * c_i + a_i * c_r + ends_ref[0, 8 + j : 9 + j, :],
        )
    run[0:1, :] = c_r
    run[1:2, :] = c_i
    groups = chan // LANES
    start_r, start_i = lanes(jnp.concatenate(l_r, axis=0)), lanes(jnp.concatenate(l_i, axis=0))
    cos_l, sin_l = lanes(cos), lanes(sin)

    def step(s, state):
        at = pl.ds(s, 8, stride=seg)
        after = []
        for k, (w_r, w_i, q_r, q_i) in enumerate(state):
            w_r, w_i = w_r * cos_l[k] - w_i * sin_l[k], w_r * sin_l[k] + w_i * cos_l[k]
            cum = cum_ref[k, at, :]
            s_r = h_ref[k, at, :] + cum * w_r
            s_i = h_ref[groups + k, at, :] + cum * w_i
            state_ref[k, at, :] = s_r
            state_ref[groups + k, at, :] = s_i
            prior_ref[k, at, :] = q_r
            prior_ref[groups + k, at, :] = q_i
            after.append((w_r, w_i, s_r, s_i))
        return tuple(after)

    lax.fori_loop(0, seg, step, tuple(zip(start_r, start_i, start_r, start_i)), unroll=8)
    state = wide(state_ref, 0, 2 * groups)
    p_g = proj_ref[...].astype(F32)
    mixed = (state * rms_scale(state) * gain_ref[1:2, :] * (p_g * sigmoid(p_g))).astype(BF16)
    mixed_ref[...] = mixed
    mid = x_ref[...].astype(F32) + dot(mixed, wo_ref[...])
    mid_ref[...] = mid
    normed = (mid * rms_scale(mid) * gain_ref[2:3, :]).astype(BF16)
    normed_ref[...] = normed
    gu = dot(normed, wf_ref[...])
    gu_ref[...] = gu.astype(BF16)
    hidden = gu.shape[1] // 2
    gate = gu[:, :hidden]
    hid = (gate * sigmoid(gate) * gu[:, hidden:]).astype(BF16)
    hid_ref[...] = hid
    out_ref[...] = (mid + dot(hid, wd_ref[...])).astype(out_ref.dtype)


def back_out_kernel(dx_ref, gu_ref, mid_ref, state_ref, proj_ref, lam_ref, wo_ref, wf_ref, wd_ref,
                    gain_ref, gate_ref, dz_ref, dgu_ref, dmid_ref, dy_ref, dpg_ref, g_ref, cum_ref,
                    ends_ref, tot_ref, dgain_ref, grad):
    row, tile = pl.program_id(0), pl.program_id(1)
    tokens, width = dx_ref.shape
    chan = width // 2
    seg = tokens // 8
    cos, sin = gate_ref[0:1, :], gate_ref[1:2, :]
    seg_cos, seg_sin = gate_ref[3:4, :], gate_ref[4:5, :]
    dx = dx_ref[...].astype(F32)
    dz = dx.astype(BF16)
    dz_ref[...] = dz
    d_hid = dot_t(dz, wd_ref[...])
    hidden = d_hid.shape[1]
    gate = gu_ref[:, :hidden].astype(F32)
    up = gu_ref[:, hidden:].astype(F32)
    sg = sigmoid(gate)
    silu = gate * sg
    d_gu = jnp.concatenate(
        [(d_hid * up * (sg + silu * (1.0 - sg))).astype(BF16), (d_hid * silu).astype(BF16)], axis=1
    )
    dgu_ref[...] = d_gu
    d_n = dot_t(d_gu, wf_ref[...])
    mid = mid_ref[...]
    scale = rms_scale(mid)
    hat = mid * scale
    d_hat = d_n * gain_ref[2:3, :]

    @pl.when((row == 0) & (tile == 0))
    def _():
        dgain_ref[...] = jnp.zeros_like(dgain_ref)

    dgain_ref[8:16, :] += eight_sum(d_n * hat)
    d_mid = dx + scale * (d_hat - hat * jnp.mean(d_hat * hat, axis=-1, keepdims=True))
    dmid_ref[...] = d_mid
    dy = d_mid.astype(BF16)
    dy_ref[...] = dy
    d_mixed = dot_t(dy, wo_ref[...])
    p_g = proj_ref[...].astype(F32)
    sg = sigmoid(p_g)
    silu = p_g * sg
    groups = chan // LANES
    state = wide(state_ref, 0, 2 * groups)
    scale = rms_scale(state)
    hat = state * scale
    g1 = gain_ref[1:2, :]
    dpg_ref[...] = (d_mixed * hat * g1 * (sg + silu * (1.0 - sg))).astype(BF16)
    d_n = d_mixed * silu
    dgain_ref[0:8, :] += eight_sum(d_n * hat)
    d_hat = d_n * g1
    split_store(grad, 0, scale * (d_hat - hat * jnp.mean(d_hat * hat, axis=-1, keepdims=True)))
    cos_l, sin_l = lanes(cos), lanes(sin)

    def step(s, state):
        at = pl.ds(seg - 1 - s, 8, stride=seg)
        after = []
        for k, (g_r, g_i, cum, lam_n) in enumerate(state):
            a_r, a_i = lam_n * cos_l[k], lam_n * sin_l[k]
            n_r = grad[k, at, :] + a_r * g_r + a_i * g_i
            n_i = grad[groups + k, at, :] + a_r * g_i - a_i * g_r
            cum = cum * lam_n
            g_ref[k, at, :] = n_r
            g_ref[groups + k, at, :] = n_i
            cum_ref[k, at, :] = cum
            after.append((n_r, n_i, cum, lam_ref[k, at, :]))
        return tuple(after)

    zero = lam_ref[0, 0:8, :] * 0.0
    last = lax.fori_loop(0, seg, step, ((zero, zero, zero + 1.0, zero + 1.0),) * groups, unroll=8)
    g_r, g_i, cum, lam_0 = (jnp.concatenate([v[i] for v in last], axis=-1) for i in range(4))
    e_r = lam_0 * (cos * g_r + sin * g_i)
    e_i = lam_0 * (cos * g_i - sin * g_r)
    e_c = lam_0 * cum
    ends_ref[0, 0:8, :] = e_r
    ends_ref[0, 8:16, :] = e_i
    ends_ref[0, 16:24, :] = e_c

    @pl.when(tile == 0)
    def _():
        tot_ref[0, 0:2, :] = jnp.zeros((2, chan), F32)
        tot_ref[0, 2:3, :] = jnp.ones((1, chan), F32)

    c_r, c_i, c_l = tot_ref[0, 0:1, :], tot_ref[0, 1:2, :], tot_ref[0, 2:3, :]
    for j in reversed(range(8)):
        m = e_c[j : j + 1, :]
        a_r, a_i = m * seg_cos, m * seg_sin
        c_r, c_i = a_r * c_r + a_i * c_i + e_r[j : j + 1, :], a_r * c_i - a_i * c_r + e_i[j : j + 1, :]
        c_l = c_l * m
    tot_ref[0, 0:1, :] = c_r
    tot_ref[0, 1:2, :] = c_i
    tot_ref[0, 2:3, :] = c_l


def back_in_kernel(rel_ref, x_ref, dmid_ref, proj_ref, dpg_ref, lam_ref, prior_ref, g_ref, cum_ref,
                   ends_ref, carry_ref, w_ref, gain_ref, gate_ref, dproj_ref, dx_ref, dgain_ref,
                   dgate_ref, run, tot):
    row, tile = pl.program_id(0), pl.program_id(1)
    tokens, width = x_ref.shape
    chan = width // 2
    seg = tokens // 8
    cos, sin, lower = gate_ref[0:1, :], gate_ref[1:2, :], gate_ref[2:3, :]
    seg_cos, seg_sin = gate_ref[3:4, :], gate_ref[4:5, :]

    @pl.when(tile == 0)
    def _():
        run[0:2, :] = carry_ref[0, 0:2, :]

    c_r, c_i = run[0:1, :], run[1:2, :]
    l_r, l_i = [None] * 8, [None] * 8
    for j in reversed(range(8)):
        l_r[j], l_i[j] = c_r, c_i
        m = ends_ref[0, 16 + j : 17 + j, :]
        a_r, a_i = m * seg_cos, m * seg_sin
        c_r, c_i = (
            a_r * c_r + a_i * c_i + ends_ref[0, j : j + 1, :],
            a_r * c_i - a_i * c_r + ends_ref[0, 8 + j : 9 + j, :],
        )
    run[0:1, :] = c_r
    run[1:2, :] = c_i

    groups = chan // LANES
    start_r, start_i = lanes(jnp.concatenate(l_r, axis=0)), lanes(jnp.concatenate(l_i, axis=0))
    cos_l, sin_l = lanes(cos), lanes(sin)

    def step(s, state):
        at = pl.ds(seg - 1 - s, 8, stride=seg)
        after = []
        for k, (w_r, w_i) in enumerate(state):
            cum = cum_ref[k, at, :]
            tot[k, at, :] = g_ref[k, at, :] + cum * w_r
            tot[groups + k, at, :] = g_ref[groups + k, at, :] + cum * w_i
            after.append((w_r * cos_l[k] + w_i * sin_l[k], w_i * cos_l[k] - w_r * sin_l[k]))
        return tuple(after)

    lax.fori_loop(0, seg, step, tuple(zip(start_r, start_i)), unroll=8)
    g_r, g_i = wide(tot, 0, groups), wide(tot, groups, 2 * groups)
    q_r, q_i = wide(prior_ref, 0, groups), wide(prior_ref, groups, 2 * groups)
    p_r = proj_ref[:, :chan].astype(F32)
    p_i = proj_ref[:, chan : 2 * chan].astype(F32)
    forget = sigmoid(proj_ref[:, 2 * chan : 3 * chan].astype(F32))
    lam = wide(lam_ref, 0, groups)
    d_ar = g_r * q_r + g_i * q_i
    d_ai = g_i * q_r - g_r * q_i
    s_r, s_i = sigmoid(p_r), sigmoid(p_i)
    in_r, in_i = p_r * s_r, p_i * s_i
    d_lam = d_ar * cos + d_ai * sin - (g_r * in_r + g_i * in_i)

    @pl.when((row == 0) & (tile == 0))
    def _():
        dgain_ref[...] = jnp.zeros_like(dgain_ref)
        dgate_ref[...] = jnp.zeros_like(dgate_ref)

    dgate_ref[0:8, :] += eight_sum(lam * (d_ai * cos - d_ar * sin))
    first = (pl.num_programs(1) - 1 - tile) * tokens
    hit = keep_mask(rel_ref, row, first, (tokens, chan))
    d_f = jnp.where(hit, 0.0, d_lam) * (1.0 - forget)
    dgate_ref[8:16, :] += eight_sum(d_f)
    rest = 1.0 - lam
    d_proj = jnp.concatenate(
        [
            (rest * g_r * (s_r + in_r * (1.0 - s_r))).astype(BF16),
            (rest * g_i * (s_i + in_i * (1.0 - s_i))).astype(BF16),
            (d_f * (1.0 - lower) * forget).astype(BF16),
            dpg_ref[...],
        ],
        axis=1,
    )
    dproj_ref[...] = d_proj
    d_n = dot_t(d_proj, w_ref[...])
    x = x_ref[...].astype(F32)
    scale = rms_scale(x)
    hat = x * scale
    dgain_ref[...] += eight_sum(d_n * hat)
    d_hat = d_n * gain_ref[0:1, :]
    dx_ref[...] = dmid_ref[...] + scale * (d_hat - hat * jnp.mean(d_hat * hat, axis=-1, keepdims=True))


def carry_kernel(axis, count, forward, tot_ref, rot_ref, out_ref, buf, send_sem, recv_sem):
    me = lax.axis_index(axis)
    barrier = pltpu.get_barrier_semaphore()
    peers = [lax.rem(me + k, count) for k in range(1, count)]
    for peer in peers:
        pl.semaphore_signal(barrier, inc=1, device_id={axis: peer}, device_id_type=MESH)
    pl.semaphore_wait(barrier, count - 1)
    copies = []
    for k, peer in enumerate(peers):
        copy = pltpu.make_async_remote_copy(
            src_ref=tot_ref,
            dst_ref=buf.at[k],
            send_sem=send_sem.at[k],
            recv_sem=recv_sem.at[k],
            device_id={axis: peer},
            device_id_type=MESH,
        )
        copy.start()
        copies.append(copy)
    for copy in copies:
        copy.wait()
    cos, sin = rot_ref[0:1, :], rot_ref[1:2, :]
    rows = tot_ref.shape[0]
    for r in range(rows):
        c_r = jnp.zeros_like(cos)
        c_i = jnp.zeros_like(cos)
        for k in range(count - 1, 0, -1):
            slot = k - 1 if forward else count - k - 1
            valid = me >= k if forward else me + k < count
            e_r, e_i, m = buf[slot, r, 0:1, :], buf[slot, r, 1:2, :], buf[slot, r, 2:3, :]
            a_r = m * cos
            a_i = m * sin if forward else -m * sin
            n_r = a_r * c_r - a_i * c_i + e_r
            n_i = a_r * c_i + a_i * c_r + e_i
            keep = jnp.where(valid, 1.0, 0.0)
            c_r, c_i = n_r * keep, n_i * keep
        out_ref[r, 0:1, :] = c_r
        out_ref[r, 1:2, :] = c_i


class Ring:
    def __init__(self, n):
        self.n = n
        self.batch, self.seq = lax.axis_index("batch"), lax.axis_index("seq")
        z, x = self.batch // 2, self.batch % 2
        self.pos = z + x * (n - 1 - 2 * z)
        self.core, self.y = self.seq % 2, self.seq // 2
        self.sign = 1 - 2 * self.core
        self.core_peer = self.seq + self.sign
        self.y_peer = self.seq + 2 * (1 - 2 * self.y)

    def at(self, distance):
        p = (self.pos + distance + 2 * self.n) % self.n
        h = p // (self.n // 2)
        return 2 * (p + h * (self.n - 1 - 2 * p)) + h

    def ahead(self, hops):
        return self.at(self.sign * hops)


def remote(src, dst, send, recv, device):
    return pltpu.make_async_remote_copy(
        src_ref=src, dst_ref=dst, send_sem=send, recv_sem=recv, device_id=device, device_id_type=MESH
    )


def meet(devices):
    barrier = pltpu.get_barrier_semaphore()
    for device in devices:
        pl.semaphore_signal(barrier, inc=1, device_id=device, device_id_type=MESH)
    pl.semaphore_wait(barrier, len(devices))


def gather_kernel(n, layers, mats, *refs):
    srcs, dsts = refs[:mats], refs[mats : mats + layers * mats]
    own_sem, ring_send, ring_recv, y_send, y_recv, core_send, core_recv = refs[mats + layers * mats :]
    ring = Ring(n)
    far, near = n // 2, n - 1 - n // 2
    meet([{"batch": ring.ahead(1)}, {"batch": ring.ahead(-1)}, {"seq": ring.y_peer}, {"seq": ring.core_peer}])
    jobs = []
    for k in range(layers):
        for m in range(mats):
            jobs.append((srcs[m].at[k], dsts[k * mats + m], srcs[m].shape[1] // 6))

    def rows_of(u):
        base = ring.core * (3 * u)
        mine = pl.ds(pl.multiple_of(base + ring.y * u, 16), 2 * u)
        give = pl.ds(pl.multiple_of(base + ring.y * (2 * u), 16), u)
        take = pl.ds(pl.multiple_of(base + (1 - ring.y) * (2 * u), 16), u)
        return mine, give, take

    owns = []
    for j, (src, dst, u) in enumerate(jobs):
        mine, give, take = rows_of(u)
        for way, hops in ((1, far), (-1, near)):
            slot = 0 if way == 1 else far
            remote(
                src.at[mine], dst.at[ring.batch, mine], ring_send.at[j], ring_recv.at[j, slot],
                {"batch": ring.ahead(way)},
            ).start()
        own = pltpu.make_async_copy(src, dst.at[ring.batch], own_sem.at[j])
        own.start()
        owns.append(own)

    def arrived(j, way, h):
        src, dst, u = jobs[j]
        mine, give, take = rows_of(u)
        hops = far if way == 1 else near
        slot = h if way == 1 else far + h
        origin = ring.ahead(-way * (h + 1))
        piece = dst.at[origin, mine]
        remote(piece, piece, ring_send.at[j], ring_recv.at[j, slot], {"batch": ring.ahead(way)}).wait_recv()
        if h + 1 < hops:
            remote(piece, piece, ring_send.at[j], ring_recv.at[j, slot + 1], {"batch": ring.ahead(way)}).start()
        half = dst.at[origin, give]
        remote(half, half, y_send.at[j], y_recv.at[j, slot], {"seq": ring.y_peer}).start()
        remote(piece, piece, core_send.at[j], core_recv.at[j], {"seq": ring.core_peer}).start()

    def crossed(j, way, h):
        src, dst, u = jobs[j]
        mine, give, take = rows_of(u)
        slot = h if way == 1 else far + h
        origin = ring.ahead(-way * (h + 1))
        half = dst.at[origin, take]
        remote(half, half, y_send.at[j], y_recv.at[j, slot], {"seq": ring.y_peer}).wait_recv()
        remote(half, half, core_send.at[j], core_recv.at[j], {"seq": ring.core_peer}).start()

    for h in range(far + 1):
        for j in range(len(jobs)):
            for way, hops in ((1, far), (-1, near)):
                if h < hops:
                    arrived(j, way, h)
                if 0 <= h - 1 < hops:
                    crossed(j, way, h - 1)
    for j, (src, dst, u) in enumerate(jobs):
        owns[j].wait()
        for rows, send in ((2 * u, ring_send), (u, y_send), (3 * u, core_send)):
            view = dst.at[0 : n - 1, 0:rows]
            remote(view, view, send.at[j], core_recv.at[j], {"seq": ring.core_peer}).wait_send()
        view = dst.at[0 : n - 1, 0 : 3 * u]
        remote(view, view, core_send.at[j], core_recv.at[j], {"seq": ring.core_peer}).wait_recv()


def gather(n, *srcs):
    layers = srcs[0].shape[0]
    mats = len(srcs)
    jobs = layers * mats
    any_ = pl.BlockSpec(memory_space=pl.ANY)
    dma = pltpu.SemaphoreType.DMA
    outs = pl.pallas_call(
        functools.partial(gather_kernel, n, layers, mats),
        out_shape=[jax.ShapeDtypeStruct((n,) + s.shape[1:], BF16) for _ in range(layers) for s in srcs],
        in_specs=[any_] * mats,
        out_specs=[any_] * jobs,
        scratch_shapes=[dma((jobs,)), dma((jobs,)), dma((jobs, n - 1)), dma((jobs,)), dma((jobs, n - 1)),
                        dma((jobs,)), dma((jobs,))],
        compiler_params=pltpu.CompilerParams(collective_id=3, has_side_effects=True),
    )(*srcs)
    return [o.reshape(n * o.shape[1], o.shape[2]) for o in outs]


def add_rows(dst, dst_row, parts, rows):
    def block(i, _):
        step = pl.multiple_of(i * 16, 16)
        total = None
        for ref, first in parts:
            value = ref[pl.ds(pl.multiple_of(first + step, 16), 16), :].astype(F32)
            total = value if total is None else total + value
        dst[pl.ds(pl.multiple_of(dst_row + step, 16), 16), :] = total.astype(dst.dtype)
        return 0

    lax.fori_loop(0, rows // 16, block, 0)


def scatter_kernel(n, mats, *refs):
    grads, small = refs[:mats], refs[mats]
    outs, small_out = refs[mats + 1 : 2 * mats + 1], refs[2 * mats + 1]
    rest = refs[2 * mats + 2 :]
    core_buf, y_out, y_buf, ring_out, ring_buf = (rest[i * mats : (i + 1) * mats] for i in range(5))
    fin, fin_buf, half, half_buf = (rest[(5 + i) * mats : (6 + i) * mats] for i in range(4))
    small_buf, core_send, core_recv, y_send, y_recv, ring_send, ring_recv, end_send, end_recv, small_send, small_recv = rest[9 * mats :]
    ring = Ring(n)
    far, near = n // 2, n - 1 - n // 2
    core_dev, y_dev = {"seq": ring.core_peer}, {"seq": ring.y_peer}
    rounds = [core_dev, y_dev]
    d = 1
    while d < n:
        rounds.append({"batch": ring.batch + d * (1 - 2 * ((ring.batch // d) % 2))})
        d *= 2
    meet([{"batch": ring.ahead(1)}, {"batch": ring.ahead(-1)}] + rounds)
    us = [g.shape[1] // 6 for g in grads]

    order = []
    for h in range(far):
        order.append((1, h, far - h))
        if h < near:
            order.append((-1, h, near - h))
    order.append((0, 0, 0))

    def core_copy(m, slot, piece):
        u = us[m]
        return remote(
            grads[m].at[piece, pl.ds(pl.multiple_of((1 - ring.core) * (3 * u), 16), 3 * u)],
            core_buf[m].at[slot], core_send.at[m], core_recv.at[m, slot], core_dev,
        )

    def y_copy(m, slot):
        return remote(y_out[m].at[slot], y_buf[m].at[slot], y_send.at[m], y_recv.at[m, slot], y_dev)

    def ring_copy(m, slot, way):
        return remote(ring_out[m].at[slot], ring_buf[m].at[slot], ring_send.at[m], ring_recv.at[m, slot],
                      {"batch": ring.ahead(way)})

    for slot, (way, h, dist) in enumerate(order):
        for m in range(mats):
            core_copy(m, slot, ring.ahead(-way * dist)).start()
    small_buf[0] = small[...]

    def small_round(r):
        return remote(small_buf.at[2 * r], small_buf.at[2 * r + 1], small_send.at[r], small_recv.at[r], rounds[r])

    small_round(0).start()

    def cross(slot):
        way, h, dist = order[slot]
        piece = ring.ahead(way * dist)
        for m in range(mats):
            u = us[m]
            core_copy(m, slot, piece).wait_recv()
            give = 2 * (1 - ring.y) * u
            add_rows(y_out[m].at[slot], 0, [(grads[m].at[piece], ring.core * (3 * u) + give),
                                            (core_buf[m].at[slot], give)], u)
            y_copy(m, slot).start()

    def hop(slot):
        way, h, dist = order[slot]
        piece = ring.ahead(way * dist)
        for m in range(mats):
            u = us[m]
            y_copy(m, slot).wait_recv()
            extra = []
            if way == 0:
                prior = [i for i, o in enumerate(order) if o[2] == 1]
            elif h:
                prior = [i for i, o in enumerate(order) if o[0] == way and o[1] == h - 1]
            else:
                prior = []
            for i in prior:
                ring_copy(m, i, order[i][0]).wait_recv()
            target = fin[m] if way == 0 else ring_out[m].at[slot]
            own = ring.y * u
            rest_ = (1 - ring.y) * u
            base = [(grads[m].at[piece], ring.core * (3 * u) + ring.y * u), (core_buf[m].at[slot], ring.y * u)]
            more = [(ring_buf[m].at[i], 0) for i in prior]
            shift = lambda parts, by: [(r, f + by) for r, f in parts]
            add_rows(target, own, shift(base + more, own) + [(y_buf[m].at[slot], 0)], u)
            add_rows(target, rest_, shift(base + more, rest_), u)
            if way:
                ring_copy(m, slot, way).start()

    def end_copy(m, kind):
        src, dst, device = ((fin[m], fin_buf[m], y_dev), (half[m], half_buf[m], core_dev))[kind]
        return remote(src, dst, end_send.at[m, kind], end_recv.at[m, kind], device)

    last = len(order)
    small_at = 0
    for t in range(last + 1):
        if t < last:
            cross(t)
        if t >= 1:
            hop(t - 1)
        if t >= 1 and small_at < len(rounds):
            small_round(small_at).wait_recv()
            total = small_buf[2 * small_at] + small_buf[2 * small_at + 1]
            small_at += 1
            if small_at < len(rounds):
                small_buf[2 * small_at] = total
                small_round(small_at).start()
            else:
                small_out[...] = total
    for m in range(mats):
        end_copy(m, 0).start()
    for m in range(mats):
        u = us[m]
        y = ring.y
        end_copy(m, 0).wait_recv()
        add_rows(half[m], 2 * y * u, [(fin[m], y * u)], u)
        add_rows(half[m], 2 * (1 - y) * u, [(fin_buf[m], (1 - y) * u)], u)
        add_rows(half[m], u, [(fin[m], (1 - y) * u), (fin_buf[m], y * u)], u)
        end_copy(m, 1).start()
        add_rows(outs[m], ring.core * (3 * u), [(half[m], 0)], 3 * u)
    for m in range(mats):
        u = us[m]
        end_copy(m, 1).wait_recv()
        add_rows(outs[m], (1 - ring.core) * (3 * u), [(half_buf[m], 0)], 3 * u)
    for m in range(mats):
        end_copy(m, 0).wait_send()
        end_copy(m, 1).wait_send()
        remote(core_buf[m], core_buf[m], core_send.at[m], core_recv.at[m, 0], core_dev).wait_send()
        remote(y_out[m], y_buf[m], y_send.at[m], y_recv.at[m, 0], y_dev).wait_send()
        remote(ring_out[m], ring_buf[m], ring_send.at[m], ring_recv.at[m, 0], core_dev).wait_send()
    for r in range(len(rounds)):
        small_round(r).wait_send()


def scatter(n, grads, small):
    mats = len(grads)
    grads = [g.reshape(n, g.shape[0] // n, g.shape[1]) for g in grads]
    us = [(g.shape[1] // 6, g.shape[2]) for g in grads]
    dma = pltpu.SemaphoreType.DMA
    vm = pl.BlockSpec(memory_space=pltpu.VMEM)
    rounds = 2 + (n - 1).bit_length()

    def bufs(f):
        return [pltpu.VMEM(f(u, w), BF16) for u, w in us]

    outs = pl.pallas_call(
        functools.partial(scatter_kernel, n, mats),
        out_shape=[jax.ShapeDtypeStruct(g.shape[1:], F32) for g in grads]
        + [jax.ShapeDtypeStruct(small.shape, F32)],
        in_specs=[vm] * (mats + 1),
        out_specs=[vm] * (mats + 1),
        scratch_shapes=bufs(lambda u, w: (n, 3 * u, w))
        + bufs(lambda u, w: (n, u, w))
        + bufs(lambda u, w: (n, u, w))
        + bufs(lambda u, w: (n - 1, 2 * u, w))
        + bufs(lambda u, w: (n - 1, 2 * u, w))
        + bufs(lambda u, w: (2 * u, w))
        + bufs(lambda u, w: (2 * u, w))
        + bufs(lambda u, w: (3 * u, w))
        + bufs(lambda u, w: (3 * u, w))
        + [
            pltpu.VMEM((2 * rounds,) + small.shape, F32),
            dma((mats,)), dma((mats, n)), dma((mats,)), dma((mats, n)), dma((mats,)), dma((mats, n)),
            dma((mats, 2)), dma((mats, 2)), dma((rounds,)), dma((rounds,)),
        ],
        compiler_params=pltpu.CompilerParams(
            collective_id=4, has_side_effects=True, vmem_limit_bytes=52 * 1024 * 1024
        ),
    )(*grads, small)
    return outs[:-1], outs[-1]


def vmem(bytes_):
    return pltpu.CompilerParams(vmem_limit_bytes=bytes_)


def whole(*shape):
    return pl.BlockSpec(shape, lambda *_: (0,) * len(shape), pipeline_mode=pl.Buffered(1))


def make_carry(count, rows, chan, forward):
    return pl.pallas_call(
        functools.partial(carry_kernel, "seq", count, forward),
        out_shape=jax.ShapeDtypeStruct((rows, 8, chan), F32),
        in_specs=[pl.BlockSpec(memory_space=pltpu.VMEM)] * 2,
        out_specs=pl.BlockSpec(memory_space=pltpu.VMEM),
        scratch_shapes=[
            pltpu.VMEM((count - 1, rows, 8, chan), F32),
            pltpu.SemaphoreType.DMA((count - 1,)),
            pltpu.SemaphoreType.DMA((count - 1,)),
        ],
        compiler_params=pltpu.CompilerParams(
            collective_id=1 if forward else 2, has_side_effects=True
        ),
    )


LIMIT = 48 * 1024 * 1024


def layer_calls(rows, length, width, hidden, cols, n_seq, tokens):
    chan = width // 2
    tiles = length // tokens
    total = rows * length
    grid = (rows, tiles)
    shape = jax.ShapeDtypeStruct
    smem = pl.BlockSpec(memory_space=pltpu.SMEM)

    def fwd(w, col=0):
        return pl.BlockSpec((tokens, w), lambda r, t: (r * tiles + t, col))

    def fwd_l(w):
        return pl.BlockSpec((w // LANES, tokens, LANES), lambda r, t: (0, r * tiles + t, 0))

    def bwd_l(w):
        return pl.BlockSpec(
            (w // LANES, tokens, LANES), lambda r, t: (0, r * tiles + tiles - 1 - t, 0)
        )

    def split(w):
        return shape((w // LANES, total, LANES), F32)

    def bwd(w, col=0):
        return pl.BlockSpec((tokens, w), lambda r, t: (r * tiles + tiles - 1 - t, col))

    ends_f = pl.BlockSpec((1, 24, chan), lambda r, t: (r * tiles + t, 0, 0))
    ends_b = pl.BlockSpec((1, 24, chan), lambda r, t: (r * tiles + tiles - 1 - t, 0, 0))
    per_row = pl.BlockSpec((1, 8, chan), lambda r, t: (r, 0, 0))
    ends_s = shape((rows * tiles, 24, chan), F32)
    row_s = shape((rows, 8, chan), F32)

    enter = pl.pallas_call(
        enter_kernel,
        grid=grid,
        in_specs=[smem, fwd(width), whole(width, cols), whole(8, width), whole(8, chan)],
        out_specs=[fwd(cols), fwd(width), fwd_l(chan), fwd_l(width), fwd_l(chan), ends_f, per_row],
        out_shape=[
            shape((total, cols), BF16),
            shape((total, width), BF16),
            split(chan),
            split(width),
            split(chan),
            ends_s,
            row_s,
        ],
        scratch_shapes=[pltpu.VMEM((width // LANES, tokens, LANES), F32)],
        compiler_params=vmem(LIMIT),
    )

    def leave(out_type):
        return pl.pallas_call(
            leave_kernel,
            grid=grid,
            in_specs=[
                fwd(width),
                fwd(width),
                fwd_l(width),
                fwd_l(chan),
                ends_f,
                per_row,
                whole(width, width),
                whole(width, 2 * hidden),
                whole(hidden, width),
                whole(8, width),
                whole(8, chan),
            ],
            out_specs=[
                fwd_l(width),
                fwd_l(width),
                fwd(width),
                fwd(width),
                fwd(width),
                fwd(2 * hidden),
                fwd(hidden),
                fwd(width),
            ],
            out_shape=[
                split(width),
                split(width),
                shape((total, width), BF16),
                shape((total, width), F32),
                shape((total, width), BF16),
                shape((total, 2 * hidden), BF16),
                shape((total, hidden), BF16),
                shape((total, width), out_type),
            ],
            scratch_shapes=[pltpu.VMEM((8, chan), F32)],
            compiler_params=vmem(LIMIT),
        )

    back_out = pl.pallas_call(
        back_out_kernel,
        grid=grid,
        in_specs=[
            bwd(width),
            bwd(2 * hidden),
            bwd(width),
            bwd_l(width),
            bwd(width),
            bwd_l(chan),
            whole(width, width),
            whole(width, 2 * hidden),
            whole(hidden, width),
            whole(8, width),
            whole(8, chan),
        ],
        out_specs=[
            bwd(width),
            bwd(2 * hidden),
            bwd(width),
            bwd(width),
            bwd(width),
            bwd_l(width),
            bwd_l(chan),
            ends_b,
            per_row,
            pl.BlockSpec((16, width), lambda r, t: (0, 0)),
        ],
        out_shape=[
            shape((total, width), BF16),
            shape((total, 2 * hidden), BF16),
            shape((total, width), F32),
            shape((total, width), BF16),
            shape((total, width), BF16),
            split(width),
            split(chan),
            ends_s,
            row_s,
            shape((16, width), F32),
        ],
        scratch_shapes=[pltpu.VMEM((width // LANES, tokens, LANES), F32)],
        compiler_params=vmem(LIMIT),
    )

    back_in = pl.pallas_call(
        back_in_kernel,
        grid=grid,
        in_specs=[
            smem,
            bwd(width),
            bwd(width),
            bwd(3 * chan),
            bwd(width),
            bwd_l(chan),
            bwd_l(width),
            bwd_l(width),
            bwd_l(chan),
            ends_b,
            per_row,
            whole(width, cols),
            whole(8, width),
            whole(8, chan),
        ],
        out_specs=[
            bwd(cols),
            bwd(width),
            pl.BlockSpec((8, width), lambda r, t: (0, 0)),
            pl.BlockSpec((16, chan), lambda r, t: (0, 0)),
        ],
        out_shape=[
            shape((total, cols), BF16),
            shape((total, width), F32),
            shape((8, width), F32),
            shape((16, chan), F32),
        ],
        scratch_shapes=[
            pltpu.VMEM((8, chan), F32),
            pltpu.VMEM((width // LANES, tokens, LANES), F32),
        ],
        compiler_params=vmem(LIMIT),
    )
    carry_f = make_carry(n_seq, rows, chan, True)
    carry_b = make_carry(n_seq, rows, chan, False)
    return enter, carry_f, leave, back_out, carry_b, back_in


def contract_rows(left, right):
    return lax.dot_general(
        left, right, (((0,), (0,)), ((), ())), preferred_element_type=F32
    ).astype(BF16)


def shards(
    tokens_in, doc_starts, mixer_in, mixer_out, ffn_in, ffn_out, gains, gate_params, cotangent
):
    rows, length, width = tokens_in.shape
    chan = width // 2
    n_seq = lax.axis_size("seq")
    hidden = ffn_in.shape[2] // 2
    cols = mixer_in.shape[2]
    total = rows * length
    tokens = min(length, 256)
    seg = tokens // 8
    enter, carry_f, leave, back_out, carry_b, back_in = layer_calls(
        rows, length, width, hidden, cols, n_seq, tokens
    )
    rel = doc_starts - lax.axis_index("seq") * length
    gain_rows = jnp.pad(gains, ((0, 0), (0, 5), (0, 0)))
    theta, lower = gate_params[:, 0], gate_params[:, 1]
    gate_rows = jnp.stack(
        [jnp.cos(theta), jnp.sin(theta), lower, jnp.cos(theta * seg), jnp.sin(theta * seg),
         jnp.cos(theta * length), jnp.sin(theta * length), lower], axis=1
    )
    n = lax.axis_size("batch")
    paired = n_seq == 4 and n % 4 == 0 and all(
        w.shape[1] % 96 == 0 for w in (mixer_in, mixer_out, ffn_in, ffn_out)
    )
    sources = (mixer_in, mixer_out, ffn_in, ffn_out)
    if paired:
        gathered = gather(n, *sources)
    else:
        gathered = [
            lax.all_gather(w[k], "batch", axis=0, tiled=True) for k in range(LAYERS) for w in sources
        ]
    x = tokens_in.reshape(total, width)
    saved = []
    for k in range(LAYERS):
        w_in, w_out, w_ffn, w_down = gathered[4 * k : 4 * k + 4]
        proj, normed, lam, h, cum, ends, tot = enter(rel, x, w_in, gain_rows[k], gate_rows[k])
        carry = carry_f(tot, gate_rows[k, 5:8])
        state, prior, mixed, mid, normed2, gu, hid, nxt = leave(F32 if k + 1 < LAYERS else BF16)(
            x, proj[:, 3 * chan :], h, cum, ends, carry, w_out, w_ffn, w_down, gain_rows[k], gate_rows[k]
        )
        saved.append((w_in, w_out, w_ffn, w_down, x, proj, normed, lam, state, prior, mixed, mid,
                      normed2, gu, hid))
        x = nxt
    block_out = x.reshape(rows, length, width)
    dx = cotangent.reshape(total, width)
    big, small = [None] * LAYERS, [None] * LAYERS
    for k in reversed(range(LAYERS)):
        (w_in, w_out, w_ffn, w_down, x, proj, normed, lam, state, prior, mixed, mid,
         normed2, gu, hid) = saved[k]
        dz, d_gu, d_mid, dy, d_pg, g, cum, ends, tot, dg_a = back_out(
            dx, gu, mid, state, proj[:, 3 * chan :], lam, w_out, w_ffn, w_down, gain_rows[k], gate_rows[k]
        )
        carry = carry_b(tot, gate_rows[k, 5:8])
        d_proj, dx, dg_b, dgate = back_in(
            rel, x, d_mid, proj, d_pg, lam, prior, g, cum, ends, carry, w_in, gain_rows[k], gate_rows[k]
        )
        big[k] = (
            contract_rows(normed, d_proj),
            contract_rows(mixed, dy),
            contract_rows(normed2, d_gu),
            contract_rows(hid, dz),
        )
        small[k] = jnp.stack(
            [
                jnp.sum(dg_b, axis=0),
                jnp.sum(dg_a[:8], axis=0),
                jnp.sum(dg_a[8:], axis=0),
                jnp.concatenate([jnp.sum(dgate[:8], axis=0), jnp.sum(dgate[8:], axis=0)]),
            ]
        )
        if paired:
            big[k], rows_8 = scatter(n, big[k], jnp.pad(small[k], ((0, 4), (0, 0))))
            small[k] = rows_8[:4]
        else:
            parts = [lax.psum_scatter(g, "batch", scatter_dimension=0, tiled=True) for g in big[k]]
            big[k] = [lax.psum(part, "seq").astype(F32) for part in parts]
            small[k] = lax.psum(small[k], ("batch", "seq"))
    totals = jnp.stack(small)
    d_gains = totals[:, :3]
    d_gate_params = totals[:, 3].reshape(LAYERS, 2, chan)
    outs = [jnp.stack([big[k][m] for k in range(LAYERS)]) for m in range(4)]
    return (block_out, dx.reshape(rows, length, width), *outs, d_gains, d_gate_params)


def solution(mesh):
    tok = P("batch", "seq", None)
    mat = P(None, "batch", None)
    return jax.shard_map(
        shards,
        mesh=mesh,
        in_specs=(tok, P("batch", None), mat, mat, mat, mat, P(), P(), tok),
        out_specs=(tok, tok, mat, mat, mat, mat, P(), P()),
        check_vma=False,
    )
```

```python
import functools

import jax
import jax.numpy as jnp
from jax import lax
from jax.experimental import pallas as pl
from jax.experimental.pallas import tpu as pltpu
from jax.sharding import PartitionSpec as P

LAYERS = 2
EPS = 1e-06
F32 = jnp.float32
BF16 = jnp.bfloat16
LANES = 128
CHUNK = 768
MESH = pl.DeviceIdType.MESH


def sigmoid(values):
    return 1.0 / (1.0 + jnp.exp(-values))


def rms_scale(values):
    return lax.rsqrt(jnp.mean(values * values, axis=-1, keepdims=True) + EPS)


def dot(left, right):
    return jnp.dot(left, right, preferred_element_type=F32)


def dot_t(left, right):
    return lax.dot_general(left, right, (((1,), (1,)), ((), ())), preferred_element_type=F32)


def eight_sum(values):
    rows, cols = values.shape
    return jnp.sum(values.reshape(rows // 8, 8, cols), axis=0)


def wide(ref, first, last):
    return jnp.concatenate([ref[g] for g in range(first, last)], axis=-1)


def split_store(ref, first, values):
    for g in range(values.shape[1] // LANES):
        ref[first + g] = values[:, g * LANES : (g + 1) * LANES]


def lanes(values):
    return [values[:, g * LANES : (g + 1) * LANES] for g in range(values.shape[1] // LANES)]


def keep_mask(rel_ref, row, first, shape):
    pos = lax.broadcasted_iota(jnp.int32, shape, 0) + first
    hit = pos == rel_ref[row, 0]
    for k in range(1, rel_ref.shape[1]):
        hit = hit | (pos == rel_ref[row, k])
    return hit


def enter_kernel(rel_ref, x_ref, w_ref, gain_ref, gate_ref, proj_ref, normed_ref, lam_ref, h_ref,
                 cum_ref, ends_ref, tot_ref, src):
    row, tile = pl.program_id(0), pl.program_id(1)
    tokens, width = x_ref.shape
    chan = width // 2
    seg = tokens // 8
    x = x_ref[...].astype(F32)
    normed = (x * rms_scale(x) * gain_ref[0:1, :]).astype(BF16)
    normed_ref[...] = normed
    proj = dot(normed, w_ref[...])
    proj_ref[...] = proj.astype(BF16)
    cos, sin, lower = gate_ref[0:1, :], gate_ref[1:2, :], gate_ref[2:3, :]
    seg_cos, seg_sin = gate_ref[3:4, :], gate_ref[4:5, :]
    p_r, p_i, p_f = proj[:, :chan], proj[:, chan : 2 * chan], proj[:, 2 * chan : 3 * chan]
    hit = keep_mask(rel_ref, row, tile * tokens, (tokens, chan))
    lam = jnp.where(hit, 0.0, lower + (1.0 - lower) * sigmoid(p_f))
    groups = chan // LANES
    split_store(lam_ref, 0, lam)
    split_store(src, 0, (1.0 - lam) * (p_r * sigmoid(p_r)))
    split_store(src, groups, (1.0 - lam) * (p_i * sigmoid(p_i)))
    cos_l, sin_l = lanes(cos), lanes(sin)

    def step(s, state):
        at = pl.ds(s, 8, stride=seg)
        after = []
        for k, (h_r, h_i, cum) in enumerate(state):
            lam_s = lam_ref[k, at, :]
            a_r, a_i = lam_s * cos_l[k], lam_s * sin_l[k]
            n_r = a_r * h_r - a_i * h_i + src[k, at, :]
            n_i = a_r * h_i + a_i * h_r + src[groups + k, at, :]
            cum = cum * lam_s
            h_ref[k, at, :] = n_r
            h_ref[groups + k, at, :] = n_i
            cum_ref[k, at, :] = cum
            after.append((n_r, n_i, cum))
        return tuple(after)

    zero = lam_ref[0, 0:8, :] * 0.0
    last = lax.fori_loop(0, seg, step, ((zero, zero, zero + 1.0),) * groups, unroll=8)
    e_r, e_i, e_c = (jnp.concatenate([v[i] for v in last], axis=-1) for i in range(3))
    ends_ref[0, 0:8, :] = e_r
    ends_ref[0, 8:16, :] = e_i
    ends_ref[0, 16:24, :] = e_c

    @pl.when(tile == 0)
    def _():
        tot_ref[0, 0:2, :] = jnp.zeros((2, chan), F32)
        tot_ref[0, 2:3, :] = jnp.ones((1, chan), F32)

    c_r, c_i, c_l = tot_ref[0, 0:1, :], tot_ref[0, 1:2, :], tot_ref[0, 2:3, :]
    for j in range(8):
        m = e_c[j : j + 1, :]
        a_r, a_i = m * seg_cos, m * seg_sin
        c_r, c_i = a_r * c_r - a_i * c_i + e_r[j : j + 1, :], a_r * c_i + a_i * c_r + e_i[j : j + 1, :]
        c_l = c_l * m
    tot_ref[0, 0:1, :] = c_r
    tot_ref[0, 1:2, :] = c_i
    tot_ref[0, 2:3, :] = c_l


def leave_kernel(x_ref, proj_ref, h_ref, cum_ref, ends_ref, carry_ref, wo_ref, wf_ref, wd_ref,
                 gain_ref, gate_ref, state_ref, prior_ref, mixed_ref, mid_ref, normed_ref, gu_ref,
                 hid_ref, out_ref, run):
    tile = pl.program_id(1)
    tokens, width = x_ref.shape
    chan = width // 2
    seg = tokens // 8
    cos, sin = gate_ref[0:1, :], gate_ref[1:2, :]
    seg_cos, seg_sin = gate_ref[3:4, :], gate_ref[4:5, :]

    @pl.when(tile == 0)
    def _():
        run[0:2, :] = carry_ref[0, 0:2, :]

    c_r, c_i = run[0:1, :], run[1:2, :]
    l_r, l_i = [], []
    for j in range(8):
        l_r.append(c_r)
        l_i.append(c_i)
        m = ends_ref[0, 16 + j : 17 + j, :]
        a_r, a_i = m * seg_cos, m * seg_sin
        c_r, c_i = (
            a_r * c_r - a_i * c_i + ends_ref[0, j : j + 1, :],
            a_r * c_i + a_i * c_r + ends_ref[0, 8 + j : 9 + j, :],
        )
    run[0:1, :] = c_r
    run[1:2, :] = c_i
    groups = chan // LANES
    start_r, start_i = lanes(jnp.concatenate(l_r, axis=0)), lanes(jnp.concatenate(l_i, axis=0))
    cos_l, sin_l = lanes(cos), lanes(sin)

    def step(s, state):
        at = pl.ds(s, 8, stride=seg)
        after = []
        for k, (w_r, w_i, q_r, q_i) in enumerate(state):
            w_r, w_i = w_r * cos_l[k] - w_i * sin_l[k], w_r * sin_l[k] + w_i * cos_l[k]
            cum = cum_ref[k, at, :]
            s_r = h_ref[k, at, :] + cum * w_r
            s_i = h_ref[groups + k, at, :] + cum * w_i
            state_ref[k, at, :] = s_r
            state_ref[groups + k, at, :] = s_i
            prior_ref[k, at, :] = q_r
            prior_ref[groups + k, at, :] = q_i
            after.append((w_r, w_i, s_r, s_i))
        return tuple(after)

    lax.fori_loop(0, seg, step, tuple(zip(start_r, start_i, start_r, start_i)), unroll=8)
    state = wide(state_ref, 0, 2 * groups)
    p_g = proj_ref[...].astype(F32)
    mixed = (state * rms_scale(state) * gain_ref[1:2, :] * (p_g * sigmoid(p_g))).astype(BF16)
    mixed_ref[...] = mixed
    mid = x_ref[...].astype(F32) + dot(mixed, wo_ref[...])
    mid_ref[...] = mid
    normed = (mid * rms_scale(mid) * gain_ref[2:3, :]).astype(BF16)
    normed_ref[...] = normed
    gu = dot(normed, wf_ref[...])
    gu_ref[...] = gu.astype(BF16)
    hidden = gu.shape[1] // 2
    gate = gu[:, :hidden]
    hid = (gate * sigmoid(gate) * gu[:, hidden:]).astype(BF16)
    hid_ref[...] = hid
    out_ref[...] = (mid + dot(hid, wd_ref[...])).astype(out_ref.dtype)


def back_out_kernel(dx_ref, gu_ref, mid_ref, state_ref, proj_ref, lam_ref, wo_ref, wf_ref, wd_ref,
                    gain_ref, gate_ref, dz_ref, dgu_ref, dmid_ref, dy_ref, dpg_ref, g_ref, cum_ref,
                    ends_ref, tot_ref, dgain_ref, grad):
    row, tile = pl.program_id(0), pl.program_id(1)
    tokens, width = dx_ref.shape
    chan = width // 2
    seg = tokens // 8
    cos, sin = gate_ref[0:1, :], gate_ref[1:2, :]
    seg_cos, seg_sin = gate_ref[3:4, :], gate_ref[4:5, :]
    dx = dx_ref[...].astype(F32)
    dz = dx.astype(BF16)
    dz_ref[...] = dz
    d_hid = dot_t(dz, wd_ref[...])
    hidden = d_hid.shape[1]
    gate = gu_ref[:, :hidden].astype(F32)
    up = gu_ref[:, hidden:].astype(F32)
    sg = sigmoid(gate)
    silu = gate * sg
    d_gu = jnp.concatenate(
        [(d_hid * up * (sg + silu * (1.0 - sg))).astype(BF16), (d_hid * silu).astype(BF16)], axis=1
    )
    dgu_ref[...] = d_gu
    d_n = dot_t(d_gu, wf_ref[...])
    mid = mid_ref[...]
    scale = rms_scale(mid)
    hat = mid * scale
    d_hat = d_n * gain_ref[2:3, :]

    @pl.when((row == 0) & (tile == 0))
    def _():
        dgain_ref[...] = jnp.zeros_like(dgain_ref)

    dgain_ref[8:16, :] += eight_sum(d_n * hat)
    d_mid = dx + scale * (d_hat - hat * jnp.mean(d_hat * hat, axis=-1, keepdims=True))
    dmid_ref[...] = d_mid
    dy = d_mid.astype(BF16)
    dy_ref[...] = dy
    d_mixed = dot_t(dy, wo_ref[...])
    p_g = proj_ref[...].astype(F32)
    sg = sigmoid(p_g)
    silu = p_g * sg
    groups = chan // LANES
    state = wide(state_ref, 0, 2 * groups)
    scale = rms_scale(state)
    hat = state * scale
    g1 = gain_ref[1:2, :]
    dpg_ref[...] = (d_mixed * hat * g1 * (sg + silu * (1.0 - sg))).astype(BF16)
    d_n = d_mixed * silu
    dgain_ref[0:8, :] += eight_sum(d_n * hat)
    d_hat = d_n * g1
    split_store(grad, 0, scale * (d_hat - hat * jnp.mean(d_hat * hat, axis=-1, keepdims=True)))
    cos_l, sin_l = lanes(cos), lanes(sin)

    def step(s, state):
        at = pl.ds(seg - 1 - s, 8, stride=seg)
        after = []
        for k, (g_r, g_i, cum, lam_n) in enumerate(state):
            a_r, a_i = lam_n * cos_l[k], lam_n * sin_l[k]
            n_r = grad[k, at, :] + a_r * g_r + a_i * g_i
            n_i = grad[groups + k, at, :] + a_r * g_i - a_i * g_r
            cum = cum * lam_n
            g_ref[k, at, :] = n_r
            g_ref[groups + k, at, :] = n_i
            cum_ref[k, at, :] = cum
            after.append((n_r, n_i, cum, lam_ref[k, at, :]))
        return tuple(after)

    zero = lam_ref[0, 0:8, :] * 0.0
    last = lax.fori_loop(0, seg, step, ((zero, zero, zero + 1.0, zero + 1.0),) * groups, unroll=8)
    g_r, g_i, cum, lam_0 = (jnp.concatenate([v[i] for v in last], axis=-1) for i in range(4))
    e_r = lam_0 * (cos * g_r + sin * g_i)
    e_i = lam_0 * (cos * g_i - sin * g_r)
    e_c = lam_0 * cum
    ends_ref[0, 0:8, :] = e_r
    ends_ref[0, 8:16, :] = e_i
    ends_ref[0, 16:24, :] = e_c

    @pl.when(tile == 0)
    def _():
        tot_ref[0, 0:2, :] = jnp.zeros((2, chan), F32)
        tot_ref[0, 2:3, :] = jnp.ones((1, chan), F32)

    c_r, c_i, c_l = tot_ref[0, 0:1, :], tot_ref[0, 1:2, :], tot_ref[0, 2:3, :]
    for j in reversed(range(8)):
        m = e_c[j : j + 1, :]
        a_r, a_i = m * seg_cos, m * seg_sin
        c_r, c_i = a_r * c_r + a_i * c_i + e_r[j : j + 1, :], a_r * c_i - a_i * c_r + e_i[j : j + 1, :]
        c_l = c_l * m
    tot_ref[0, 0:1, :] = c_r
    tot_ref[0, 1:2, :] = c_i
    tot_ref[0, 2:3, :] = c_l


def back_in_kernel(rel_ref, x_ref, dmid_ref, proj_ref, dpg_ref, lam_ref, prior_ref, g_ref, cum_ref,
                   ends_ref, carry_ref, w_ref, gain_ref, gate_ref, dproj_ref, dx_ref, dgain_ref,
                   dgate_ref, run, tot):
    row, tile = pl.program_id(0), pl.program_id(1)
    tokens, width = x_ref.shape
    chan = width // 2
    seg = tokens // 8
    cos, sin, lower = gate_ref[0:1, :], gate_ref[1:2, :], gate_ref[2:3, :]
    seg_cos, seg_sin = gate_ref[3:4, :], gate_ref[4:5, :]

    @pl.when(tile == 0)
    def _():
        run[0:2, :] = carry_ref[0, 0:2, :]

    c_r, c_i = run[0:1, :], run[1:2, :]
    l_r, l_i = [None] * 8, [None] * 8
    for j in reversed(range(8)):
        l_r[j], l_i[j] = c_r, c_i
        m = ends_ref[0, 16 + j : 17 + j, :]
        a_r, a_i = m * seg_cos, m * seg_sin
        c_r, c_i = (
            a_r * c_r + a_i * c_i + ends_ref[0, j : j + 1, :],
            a_r * c_i - a_i * c_r + ends_ref[0, 8 + j : 9 + j, :],
        )
    run[0:1, :] = c_r
    run[1:2, :] = c_i

    groups = chan // LANES
    start_r, start_i = lanes(jnp.concatenate(l_r, axis=0)), lanes(jnp.concatenate(l_i, axis=0))
    cos_l, sin_l = lanes(cos), lanes(sin)

    def step(s, state):
        at = pl.ds(seg - 1 - s, 8, stride=seg)
        after = []
        for k, (w_r, w_i) in enumerate(state):
            cum = cum_ref[k, at, :]
            tot[k, at, :] = g_ref[k, at, :] + cum * w_r
            tot[groups + k, at, :] = g_ref[groups + k, at, :] + cum * w_i
            after.append((w_r * cos_l[k] + w_i * sin_l[k], w_i * cos_l[k] - w_r * sin_l[k]))
        return tuple(after)

    lax.fori_loop(0, seg, step, tuple(zip(start_r, start_i)), unroll=8)
    g_r, g_i = wide(tot, 0, groups), wide(tot, groups, 2 * groups)
    q_r, q_i = wide(prior_ref, 0, groups), wide(prior_ref, groups, 2 * groups)
    p_r = proj_ref[:, :chan].astype(F32)
    p_i = proj_ref[:, chan : 2 * chan].astype(F32)
    forget = sigmoid(proj_ref[:, 2 * chan : 3 * chan].astype(F32))
    lam = wide(lam_ref, 0, groups)
    d_ar = g_r * q_r + g_i * q_i
    d_ai = g_i * q_r - g_r * q_i
    s_r, s_i = sigmoid(p_r), sigmoid(p_i)
    in_r, in_i = p_r * s_r, p_i * s_i
    d_lam = d_ar * cos + d_ai * sin - (g_r * in_r + g_i * in_i)

    @pl.when((row == 0) & (tile == 0))
    def _():
        dgain_ref[...] = jnp.zeros_like(dgain_ref)
        dgate_ref[...] = jnp.zeros_like(dgate_ref)

    dgate_ref[0:8, :] += eight_sum(lam * (d_ai * cos - d_ar * sin))
    first = (pl.num_programs(1) - 1 - tile) * tokens
    hit = keep_mask(rel_ref, row, first, (tokens, chan))
    d_f = jnp.where(hit, 0.0, d_lam) * (1.0 - forget)
    dgate_ref[8:16, :] += eight_sum(d_f)
    rest = 1.0 - lam
    d_proj = jnp.concatenate(
        [
            (rest * g_r * (s_r + in_r * (1.0 - s_r))).astype(BF16),
            (rest * g_i * (s_i + in_i * (1.0 - s_i))).astype(BF16),
            (d_f * (1.0 - lower) * forget).astype(BF16),
            dpg_ref[...],
        ],
        axis=1,
    )
    dproj_ref[...] = d_proj
    d_n = dot_t(d_proj, w_ref[...])
    x = x_ref[...].astype(F32)
    scale = rms_scale(x)
    hat = x * scale
    dgain_ref[...] += eight_sum(d_n * hat)
    d_hat = d_n * gain_ref[0:1, :]
    dx_ref[...] = dmid_ref[...] + scale * (d_hat - hat * jnp.mean(d_hat * hat, axis=-1, keepdims=True))


def carry_kernel(axis, count, forward, tot_ref, rot_ref, out_ref, buf, send_sem, recv_sem):
    me = lax.axis_index(axis)
    barrier = pltpu.get_barrier_semaphore()
    peers = [lax.rem(me + k, count) for k in range(1, count)]
    for peer in peers:
        pl.semaphore_signal(barrier, inc=1, device_id={axis: peer}, device_id_type=MESH)
    pl.semaphore_wait(barrier, count - 1)
    copies = []
    for k, peer in enumerate(peers):
        copy = pltpu.make_async_remote_copy(
            src_ref=tot_ref,
            dst_ref=buf.at[k],
            send_sem=send_sem.at[k],
            recv_sem=recv_sem.at[k],
            device_id={axis: peer},
            device_id_type=MESH,
        )
        copy.start()
        copies.append(copy)
    for copy in copies:
        copy.wait()
    cos, sin = rot_ref[0:1, :], rot_ref[1:2, :]
    rows = tot_ref.shape[0]
    for r in range(rows):
        c_r = jnp.zeros_like(cos)
        c_i = jnp.zeros_like(cos)
        for k in range(count - 1, 0, -1):
            slot = k - 1 if forward else count - k - 1
            valid = me >= k if forward else me + k < count
            e_r, e_i, m = buf[slot, r, 0:1, :], buf[slot, r, 1:2, :], buf[slot, r, 2:3, :]
            a_r = m * cos
            a_i = m * sin if forward else -m * sin
            n_r = a_r * c_r - a_i * c_i + e_r
            n_i = a_r * c_i + a_i * c_r + e_i
            keep = jnp.where(valid, 1.0, 0.0)
            c_r, c_i = n_r * keep, n_i * keep
        out_ref[r, 0:1, :] = c_r
        out_ref[r, 1:2, :] = c_i


class Ring:
    def __init__(self, n):
        self.n = n
        self.batch, self.seq = lax.axis_index("batch"), lax.axis_index("seq")
        z, x = self.batch // 2, self.batch % 2
        self.pos = z + x * (n - 1 - 2 * z)
        self.core, self.y = self.seq % 2, self.seq // 2
        self.sign = 1 - 2 * self.core
        self.core_peer = self.seq + self.sign
        self.y_peer = self.seq + 2 * (1 - 2 * self.y)

    def at(self, distance):
        p = (self.pos + distance + 2 * self.n) % self.n
        h = p // (self.n // 2)
        return 2 * (p + h * (self.n - 1 - 2 * p)) + h

    def ahead(self, hops):
        return self.at(self.sign * hops)


def remote(src, dst, send, recv, device):
    return pltpu.make_async_remote_copy(
        src_ref=src, dst_ref=dst, send_sem=send, recv_sem=recv, device_id=device, device_id_type=MESH
    )


def meet(devices):
    barrier = pltpu.get_barrier_semaphore()
    for device in devices:
        pl.semaphore_signal(barrier, inc=1, device_id=device, device_id_type=MESH)
    pl.semaphore_wait(barrier, len(devices))


def gather_kernel(n, layers, mats, *refs):
    srcs, dsts = refs[:mats], refs[mats : mats + layers * mats]
    own_sem, ring_send, ring_recv, y_send, y_recv, core_send, core_recv = refs[mats + layers * mats :]
    ring = Ring(n)
    far, near = n // 2, n - 1 - n // 2
    meet([{"batch": ring.ahead(1)}, {"batch": ring.ahead(-1)}, {"seq": ring.y_peer}, {"seq": ring.core_peer}])
    jobs = []
    for k in range(layers):
        for m in range(mats):
            jobs.append((srcs[m].at[k], dsts[k * mats + m], srcs[m].shape[1] // 6))

    def rows_of(u):
        base = ring.core * (3 * u)
        mine = pl.ds(pl.multiple_of(base + ring.y * u, 16), 2 * u)
        give = pl.ds(pl.multiple_of(base + ring.y * (2 * u), 16), u)
        take = pl.ds(pl.multiple_of(base + (1 - ring.y) * (2 * u), 16), u)
        return mine, give, take

    owns = []
    for j, (src, dst, u) in enumerate(jobs):
        mine, give, take = rows_of(u)
        for way, hops in ((1, far), (-1, near)):
            slot = 0 if way == 1 else far
            remote(
                src.at[mine], dst.at[ring.batch, mine], ring_send.at[j], ring_recv.at[j, slot],
                {"batch": ring.ahead(way)},
            ).start()
        own = pltpu.make_async_copy(src, dst.at[ring.batch], own_sem.at[j])
        own.start()
        owns.append(own)

    def arrived(j, way, h):
        src, dst, u = jobs[j]
        mine, give, take = rows_of(u)
        hops = far if way == 1 else near
        slot = h if way == 1 else far + h
        origin = ring.ahead(-way * (h + 1))
        piece = dst.at[origin, mine]
        remote(piece, piece, ring_send.at[j], ring_recv.at[j, slot], {"batch": ring.ahead(way)}).wait_recv()
        if h + 1 < hops:
            remote(piece, piece, ring_send.at[j], ring_recv.at[j, slot + 1], {"batch": ring.ahead(way)}).start()
        half = dst.at[origin, give]
        remote(half, half, y_send.at[j], y_recv.at[j, slot], {"seq": ring.y_peer}).start()
        remote(piece, piece, core_send.at[j], core_recv.at[j], {"seq": ring.core_peer}).start()

    def crossed(j, way, h):
        src, dst, u = jobs[j]
        mine, give, take = rows_of(u)
        slot = h if way == 1 else far + h
        origin = ring.ahead(-way * (h + 1))
        half = dst.at[origin, take]
        remote(half, half, y_send.at[j], y_recv.at[j, slot], {"seq": ring.y_peer}).wait_recv()
        remote(half, half, core_send.at[j], core_recv.at[j], {"seq": ring.core_peer}).start()

    for h in range(far + 1):
        for j in range(len(jobs)):
            for way, hops in ((1, far), (-1, near)):
                if h < hops:
                    arrived(j, way, h)
                if 0 <= h - 1 < hops:
                    crossed(j, way, h - 1)
    for j, (src, dst, u) in enumerate(jobs):
        owns[j].wait()
        for rows, send in ((2 * u, ring_send), (u, y_send), (3 * u, core_send)):
            view = dst.at[0 : n - 1, 0:rows]
            remote(view, view, send.at[j], core_recv.at[j], {"seq": ring.core_peer}).wait_send()
        view = dst.at[0 : n - 1, 0 : 3 * u]
        remote(view, view, core_send.at[j], core_recv.at[j], {"seq": ring.core_peer}).wait_recv()


def gather(n, *srcs):
    layers = srcs[0].shape[0]
    mats = len(srcs)
    jobs = layers * mats
    any_ = pl.BlockSpec(memory_space=pl.ANY)
    dma = pltpu.SemaphoreType.DMA
    outs = pl.pallas_call(
        functools.partial(gather_kernel, n, layers, mats),
        out_shape=[jax.ShapeDtypeStruct((n,) + s.shape[1:], BF16) for _ in range(layers) for s in srcs],
        in_specs=[any_] * mats,
        out_specs=[any_] * jobs,
        scratch_shapes=[dma((jobs,)), dma((jobs,)), dma((jobs, n - 1)), dma((jobs,)), dma((jobs, n - 1)),
                        dma((jobs,)), dma((jobs,))],
        compiler_params=pltpu.CompilerParams(collective_id=3, has_side_effects=True),
    )(*srcs)
    return [o.reshape(n * o.shape[1], o.shape[2]) for o in outs]


def add_rows(dst, dst_row, parts, rows):
    def block(i, _):
        step = pl.multiple_of(i * 16, 16)
        total = None
        for ref, first in parts:
            value = ref[pl.ds(pl.multiple_of(first + step, 16), 16), :].astype(F32)
            total = value if total is None else total + value
        dst[pl.ds(pl.multiple_of(dst_row + step, 16), 16), :] = total.astype(dst.dtype)
        return 0

    lax.fori_loop(0, rows // 16, block, 0)


def grads_kernel(n, plan, *refs):
    jobs = len(plan)
    lefts, rights, small = refs[:jobs], refs[jobs : 2 * jobs], refs[2 * jobs]
    outs_count = 1 + max(p[0] for p in plan)
    outs, small_out = refs[2 * jobs + 1 : 2 * jobs + 1 + outs_count], refs[2 * jobs + 1 + outs_count]
    rest = refs[2 * jobs + 2 + outs_count :]
    grads, core_buf, y_buf, ring_buf, fin_buf = (rest[i * jobs : (i + 1) * jobs] for i in range(5))
    (left_big, left_small, right_buf, small_buf, left_sem, right_sem, core_send, core_recv, y_send, y_recv,
     ring_send, ring_recv, end_send, end_recv, small_send, small_recv) = rest[5 * jobs :]
    ring = Ring(n)
    far, near = n // 2, n - 1 - n // 2
    core_dev, y_dev = {"seq": ring.core_peer}, {"seq": ring.y_peer}
    y, core = ring.y, ring.core
    rounds = [core_dev, y_dev]
    d = 1
    while d < n:
        rounds.append({"batch": ring.batch + d * (1 - 2 * ((ring.batch // d) % 2))})
        d *= 2
    us = [g.shape[0] // n // 6 for g in grads]
    split = [p[2] for p in plan]
    own_rows = [(2 if s else 3) * u for s, u in zip(split, us)]

    def left_copy(j):
        buf = (left_big, left_small)[j % 2]
        return pltpu.make_async_copy(lefts[j], buf.at[:, 0 : plan[j][3]], left_sem.at[j % 2])

    chunks = []
    for j, (_, _, _, rows, cols) in enumerate(plan):
        first = 0
        while first < cols:
            size = min(CHUNK, cols - first)
            chunks.append((j, first, size, first + size == cols))
            first += size

    def right_copy(i):
        j, first, size, _ = chunks[i]
        return pltpu.make_async_copy(
            rights[j].at[:, first : first + size], right_buf.at[i % 2, :, 0:size], right_sem.at[i % 2]
        )

    left_copy(0).start()
    right_copy(0).start()
    right_copy(1).start()
    left_copy(1).start()
    meet([{"batch": ring.ahead(1)}, {"batch": ring.ahead(-1)}] + rounds)

    order = []
    for h in range(far):
        order.append((1, h, far - h))
        if h < near:
            order.append((-1, h, near - h))
    order.append((0, 0, 0))
    last = len(order)

    def rows_at(ref, first, rows):
        return ref.at[pl.ds(pl.multiple_of(first, 16), rows)]

    def core_copy(j, slot, piece):
        u = us[j]
        return remote(rows_at(grads[j], piece * (6 * u) + (1 - core) * (3 * u), 3 * u),
                      core_buf[j].at[slot], core_send.at[j], core_recv.at[j, slot], core_dev)

    def y_copy(j, slot, piece):
        u = us[j]
        src = rows_at(grads[j], piece * (6 * u) + core * (3 * u) + 2 * (1 - y) * u, u)
        return remote(src, y_buf[j].at[slot], y_send.at[j], y_recv.at[j, slot], y_dev)

    def mine(j, piece):
        u = us[j]
        return piece * (6 * u) + core * (3 * u) + (y * u if split[j] else 0)

    def ring_copy(j, slot, way, piece):
        return remote(rows_at(grads[j], mine(j, piece), own_rows[j]), ring_buf[j].at[slot], ring_send.at[j],
                      ring_recv.at[j, slot], {"batch": ring.ahead(way)})

    def small_round(r):
        return remote(small_buf.at[2 * r], small_buf.at[2 * r + 1], small_send.at[r], small_recv.at[r], rounds[r])

    small_buf[0] = small[...]
    small_round(0).start()

    def small_step(r):
        small_round(r).wait_recv()
        total = small_buf[2 * r] + small_buf[2 * r + 1]
        if r + 1 < len(rounds):
            small_buf[2 * r + 2] = total
            small_round(r + 1).start()
        else:
            small_out[...] = total

    def begin(j):
        for slot, (way, h, dist) in enumerate(order):
            core_copy(j, slot, ring.ahead(-way * dist)).start()

    def cross(j, slot):
        way, h, dist = order[slot]
        piece = ring.ahead(way * dist)
        u = us[j]
        core_copy(j, slot, piece).wait_recv()
        if not split[j]:
            return
        give = 2 * (1 - y) * u
        at = piece * (6 * u) + core * (3 * u) + give
        add_rows(grads[j], at, [(grads[j], at), (core_buf[j].at[slot], give)], u)
        y_copy(j, slot, piece).start()

    def hop(j, slot):
        way, h, dist = order[slot]
        piece = ring.ahead(way * dist)
        u = us[j]
        if split[j]:
            y_copy(j, slot, piece).wait_recv()
        if way == 0:
            prior = [i for i, o in enumerate(order) if o[2] == 1]
        elif h:
            prior = [i for i, o in enumerate(order) if o[0] == way and o[1] == h - 1]
        else:
            prior = []
        for i in prior:
            ring_copy(j, i, order[i][0], piece).wait_recv()
        at = mine(j, piece)
        base = [(grads[j], at), (core_buf[j].at[slot], y * u if split[j] else 0)]
        base += [(ring_buf[j].at[i], 0) for i in prior]
        if split[j]:
            for by, more in ((y * u, [(y_buf[j].at[slot], 0)]), ((1 - y) * u, [])):
                add_rows(grads[j], at + by, [(r, f + by) for r, f in base] + more, u)
        else:
            add_rows(grads[j], at, base, 3 * u)
        if way:
            ring_copy(j, slot, way, piece).start()

    def fin_copy(j):
        return remote(rows_at(grads[j], mine(j, ring.batch), own_rows[j]), fin_buf[j], end_send.at[j, 0],
                      end_recv.at[j, 0], y_dev)

    def half_copy(j):
        half = outs[plan[j][0]].at[plan[j][1], pl.ds(pl.multiple_of(core * (3 * us[j]), 16), 3 * us[j])]
        return remote(half, half, end_send.at[j, 1], end_recv.at[j, 1], core_dev)

    def finish(j):
        u = us[j]
        fin_copy(j).wait_recv()
        out = outs[plan[j][0]].at[plan[j][1]]
        at, to = mine(j, ring.batch), core * (3 * u)
        if split[j]:
            add_rows(out, to + 2 * y * u, [(grads[j], at + y * u)], u)
            add_rows(out, to + 2 * (1 - y) * u, [(fin_buf[j], (1 - y) * u)], u)
            add_rows(out, to + u, [(grads[j], at + (1 - y) * u), (fin_buf[j], y * u)], u)
        else:
            add_rows(out, to, [(grads[j], at), (fin_buf[j], 0)], 3 * u)
        half_copy(j).start()

    steps = far + 4

    def advance(j, t):
        now = [i for i, o in enumerate(order) if o[0] and o[1] == t]
        before = [i for i, o in enumerate(order) if o[0] and o[1] == t - 1]
        for slot in before:
            hop(j, slot)
        for slot in now:
            cross(j, slot)
        if t == far - 1:
            cross(j, last - 1)
        if t == far + 1:
            hop(j, last - 1)
            fin_copy(j).start()
        if t == far + 2:
            finish(j)
        if t == far + 3:
            half_copy(j).wait_recv()

    stage = {}

    def advance_all(turn):
        for j in list(stage):
            if j % 2 == turn:
                advance(j, stage[j])
                stage[j] += 1
                if stage[j] == steps:
                    del stage[j]

    small_at = 0
    for i, (j, first, size, done) in enumerate(chunks):
        if first == 0:
            left_copy(j).wait()
        right_copy(i).wait()
        left = (left_big, left_small)[j % 2]

        def multiply(b, _, i=i, j=j, first=first, size=size, left=left):
            at = pl.multiple_of(b * 256, 256)
            part = lax.dot_general(
                left[:, pl.ds(at, 256)], right_buf[i % 2, :, 0:size], (((0,), (0,)), ((), ())),
                preferred_element_type=F32,
            )
            grads[j][pl.ds(at, 256), first : first + size] = part.astype(BF16)
            return 0

        lax.fori_loop(0, plan[j][3] // 256, multiply, 0)
        if i + 2 < len(chunks):
            right_copy(i + 2).start()
        if done and j + 2 < jobs:
            left_copy(j + 2).start()
        advance_all(i % 2)
        if done:
            begin(j)
            stage[j] = 0
        if small_at < len(rounds):
            small_step(small_at)
            small_at += 1
    i = 0
    while stage:
        advance_all(i % 2)
        i += 1
    while small_at < len(rounds):
        small_step(small_at)
        small_at += 1
    for j in range(jobs):
        u = us[j]
        fin_copy(j).wait_send()
        half_copy(j).wait_send()
        remote(core_buf[j], core_buf[j], core_send.at[j], core_recv.at[j, 0], core_dev).wait_send()
        if split[j]:
            remote(y_buf[j], y_buf[j], y_send.at[j], y_recv.at[j, 0], y_dev).wait_send()
        remote(ring_buf[j], ring_buf[j], ring_send.at[j], ring_recv.at[j, 0], core_dev).wait_send()
    for r in range(len(rounds)):
        small_round(r).wait_send()


def grads_and_scatter(n, plan, lefts, rights, small):
    jobs = len(plan)
    plan = [p + (a.shape[1], b.shape[1]) for p, a, b in zip(plan, lefts, rights)]
    tokens = lefts[0].shape[0]
    layers = 1 + max(p[1] for p in plan)
    dma = pltpu.SemaphoreType.DMA
    rounds = 2 + (n - 1).bit_length()
    sizes = [(p[3] // n // 6, p[4], p[2]) for p in plan]
    outs = {p[0]: jax.ShapeDtypeStruct((layers, p[3] // n, p[4]), BF16) for p in plan}
    vm = pl.BlockSpec(memory_space=pltpu.VMEM)
    any_ = pl.BlockSpec(memory_space=pl.ANY)

    def bufs(f):
        return [pltpu.VMEM(f(u, w, s), BF16) for u, w, s in sizes]

    return pl.pallas_call(
        functools.partial(grads_kernel, n, plan),
        out_shape=[outs[m] for m in sorted(outs)] + [jax.ShapeDtypeStruct(small.shape, F32)],
        in_specs=[any_] * (2 * jobs) + [vm],
        out_specs=[vm] * (len(outs) + 1),
        scratch_shapes=bufs(lambda u, w, s: (6 * u * n, w))
        + bufs(lambda u, w, s: (n, 3 * u, w))
        + bufs(lambda u, w, s: (n if s else 1, u, w))
        + bufs(lambda u, w, s: (n - 1, 2 * u if s else 3 * u, w))
        + bufs(lambda u, w, s: (2 * u if s else 3 * u, w))
        + [
            pltpu.VMEM((tokens, max(p[3] for p in plan[0::2])), BF16),
            pltpu.VMEM((tokens, max(p[3] for p in plan[1::2])), BF16),
            pltpu.VMEM((2, tokens, CHUNK), BF16),
            pltpu.VMEM((2 * rounds,) + small.shape, F32),
            dma((2,)), dma((2,)), dma((jobs,)), dma((jobs, n)), dma((jobs,)), dma((jobs, n)), dma((jobs,)),
            dma((jobs, n)), dma((jobs, 2)), dma((jobs, 2)), dma((rounds,)), dma((rounds,)),
        ],
        compiler_params=pltpu.CompilerParams(
            collective_id=4, has_side_effects=True, vmem_limit_bytes=63 * 1024 * 1024
        ),
    )(*lefts, *rights, small)


def vmem(bytes_):
    return pltpu.CompilerParams(vmem_limit_bytes=bytes_)


def whole(*shape):
    return pl.BlockSpec(shape, lambda *_: (0,) * len(shape), pipeline_mode=pl.Buffered(1))


def make_carry(count, rows, chan, forward):
    return pl.pallas_call(
        functools.partial(carry_kernel, "seq", count, forward),
        out_shape=jax.ShapeDtypeStruct((rows, 8, chan), F32),
        in_specs=[pl.BlockSpec(memory_space=pltpu.VMEM)] * 2,
        out_specs=pl.BlockSpec(memory_space=pltpu.VMEM),
        scratch_shapes=[
            pltpu.VMEM((count - 1, rows, 8, chan), F32),
            pltpu.SemaphoreType.DMA((count - 1,)),
            pltpu.SemaphoreType.DMA((count - 1,)),
        ],
        compiler_params=pltpu.CompilerParams(
            collective_id=1 if forward else 2, has_side_effects=True
        ),
    )


LIMIT = 48 * 1024 * 1024


def layer_calls(rows, length, width, hidden, cols, n_seq, tokens):
    chan = width // 2
    tiles = length // tokens
    total = rows * length
    grid = (rows, tiles)
    shape = jax.ShapeDtypeStruct
    smem = pl.BlockSpec(memory_space=pltpu.SMEM)

    def fwd(w, col=0):
        return pl.BlockSpec((tokens, w), lambda r, t: (r * tiles + t, col))

    def fwd_l(w):
        return pl.BlockSpec((w // LANES, tokens, LANES), lambda r, t: (0, r * tiles + t, 0))

    def bwd_l(w):
        return pl.BlockSpec(
            (w // LANES, tokens, LANES), lambda r, t: (0, r * tiles + tiles - 1 - t, 0)
        )

    def split(w):
        return shape((w // LANES, total, LANES), F32)

    def bwd(w, col=0):
        return pl.BlockSpec((tokens, w), lambda r, t: (r * tiles + tiles - 1 - t, col))

    ends_f = pl.BlockSpec((1, 24, chan), lambda r, t: (r * tiles + t, 0, 0))
    ends_b = pl.BlockSpec((1, 24, chan), lambda r, t: (r * tiles + tiles - 1 - t, 0, 0))
    per_row = pl.BlockSpec((1, 8, chan), lambda r, t: (r, 0, 0))
    ends_s = shape((rows * tiles, 24, chan), F32)
    row_s = shape((rows, 8, chan), F32)

    enter = pl.pallas_call(
        enter_kernel,
        grid=grid,
        in_specs=[smem, fwd(width), whole(width, cols), whole(8, width), whole(8, chan)],
        out_specs=[fwd(cols), fwd(width), fwd_l(chan), fwd_l(width), fwd_l(chan), ends_f, per_row],
        out_shape=[
            shape((total, cols), BF16),
            shape((total, width), BF16),
            split(chan),
            split(width),
            split(chan),
            ends_s,
            row_s,
        ],
        scratch_shapes=[pltpu.VMEM((width // LANES, tokens, LANES), F32)],
        compiler_params=vmem(LIMIT),
    )

    def leave(out_type):
        return pl.pallas_call(
            leave_kernel,
            grid=grid,
            in_specs=[
                fwd(width),
                fwd(width),
                fwd_l(width),
                fwd_l(chan),
                ends_f,
                per_row,
                whole(width, width),
                whole(width, 2 * hidden),
                whole(hidden, width),
                whole(8, width),
                whole(8, chan),
            ],
            out_specs=[
                fwd_l(width),
                fwd_l(width),
                fwd(width),
                fwd(width),
                fwd(width),
                fwd(2 * hidden),
                fwd(hidden),
                fwd(width),
            ],
            out_shape=[
                split(width),
                split(width),
                shape((total, width), BF16),
                shape((total, width), F32),
                shape((total, width), BF16),
                shape((total, 2 * hidden), BF16),
                shape((total, hidden), BF16),
                shape((total, width), out_type),
            ],
            scratch_shapes=[pltpu.VMEM((8, chan), F32)],
            compiler_params=vmem(LIMIT),
        )

    back_out = pl.pallas_call(
        back_out_kernel,
        grid=grid,
        in_specs=[
            bwd(width),
            bwd(2 * hidden),
            bwd(width),
            bwd_l(width),
            bwd(width),
            bwd_l(chan),
            whole(width, width),
            whole(width, 2 * hidden),
            whole(hidden, width),
            whole(8, width),
            whole(8, chan),
        ],
        out_specs=[
            bwd(width),
            bwd(2 * hidden),
            bwd(width),
            bwd(width),
            bwd(width),
            bwd_l(width),
            bwd_l(chan),
            ends_b,
            per_row,
            pl.BlockSpec((16, width), lambda r, t: (0, 0)),
        ],
        out_shape=[
            shape((total, width), BF16),
            shape((total, 2 * hidden), BF16),
            shape((total, width), F32),
            shape((total, width), BF16),
            shape((total, width), BF16),
            split(width),
            split(chan),
            ends_s,
            row_s,
            shape((16, width), F32),
        ],
        scratch_shapes=[pltpu.VMEM((width // LANES, tokens, LANES), F32)],
        compiler_params=vmem(LIMIT),
    )

    back_in = pl.pallas_call(
        back_in_kernel,
        grid=grid,
        in_specs=[
            smem,
            bwd(width),
            bwd(width),
            bwd(3 * chan),
            bwd(width),
            bwd_l(chan),
            bwd_l(width),
            bwd_l(width),
            bwd_l(chan),
            ends_b,
            per_row,
            whole(width, cols),
            whole(8, width),
            whole(8, chan),
        ],
        out_specs=[
            bwd(cols),
            bwd(width),
            pl.BlockSpec((8, width), lambda r, t: (0, 0)),
            pl.BlockSpec((16, chan), lambda r, t: (0, 0)),
        ],
        out_shape=[
            shape((total, cols), BF16),
            shape((total, width), F32),
            shape((8, width), F32),
            shape((16, chan), F32),
        ],
        scratch_shapes=[
            pltpu.VMEM((8, chan), F32),
            pltpu.VMEM((width // LANES, tokens, LANES), F32),
        ],
        compiler_params=vmem(LIMIT),
    )
    carry_f = make_carry(n_seq, rows, chan, True)
    carry_b = make_carry(n_seq, rows, chan, False)
    return enter, carry_f, leave, back_out, carry_b, back_in


def contract_rows(left, right):
    return lax.dot_general(
        left, right, (((0,), (0,)), ((), ())), preferred_element_type=F32
    ).astype(BF16)


def shards(
    tokens_in, doc_starts, mixer_in, mixer_out, ffn_in, ffn_out, gains, gate_params, cotangent
):
    rows, length, width = tokens_in.shape
    chan = width // 2
    n_seq = lax.axis_size("seq")
    hidden = ffn_in.shape[2] // 2
    cols = mixer_in.shape[2]
    total = rows * length
    tokens = min(length, 256)
    seg = tokens // 8
    enter, carry_f, leave, back_out, carry_b, back_in = layer_calls(
        rows, length, width, hidden, cols, n_seq, tokens
    )
    rel = doc_starts - lax.axis_index("seq") * length
    gain_rows = jnp.pad(gains, ((0, 0), (0, 5), (0, 0)))
    theta, lower = gate_params[:, 0], gate_params[:, 1]
    gate_rows = jnp.stack(
        [jnp.cos(theta), jnp.sin(theta), lower, jnp.cos(theta * seg), jnp.sin(theta * seg),
         jnp.cos(theta * length), jnp.sin(theta * length), lower], axis=1
    )
    n = lax.axis_size("batch")
    paired = n_seq == 4 and n % 4 == 0 and all(
        w.shape[1] % 96 == 0 for w in (mixer_in, mixer_out, ffn_in, ffn_out)
    )
    sources = (mixer_in, mixer_out, ffn_in, ffn_out)
    if paired:
        gathered = gather(n, *sources)
    else:
        gathered = [
            lax.all_gather(w[k], "batch", axis=0, tiled=True) for k in range(LAYERS) for w in sources
        ]
    x = tokens_in.reshape(total, width)
    saved = []
    for k in range(LAYERS):
        w_in, w_out, w_ffn, w_down = gathered[4 * k : 4 * k + 4]
        proj, normed, lam, h, cum, ends, tot = enter(rel, x, w_in, gain_rows[k], gate_rows[k])
        carry = carry_f(tot, gate_rows[k, 5:8])
        state, prior, mixed, mid, normed2, gu, hid, nxt = leave(F32 if k + 1 < LAYERS else BF16)(
            x, proj[:, 3 * chan :], h, cum, ends, carry, w_out, w_ffn, w_down, gain_rows[k], gate_rows[k]
        )
        saved.append((w_in, w_out, w_ffn, w_down, x, proj, normed, lam, state, prior, mixed, mid,
                      normed2, gu, hid))
        x = nxt
    block_out = x.reshape(rows, length, width)
    dx = cotangent.reshape(total, width)
    pairs, small = [None] * LAYERS, [None] * LAYERS
    for k in reversed(range(LAYERS)):
        (w_in, w_out, w_ffn, w_down, x, proj, normed, lam, state, prior, mixed, mid,
         normed2, gu, hid) = saved[k]
        dz, d_gu, d_mid, dy, d_pg, g, cum, ends, tot, dg_a = back_out(
            dx, gu, mid, state, proj[:, 3 * chan :], lam, w_out, w_ffn, w_down, gain_rows[k], gate_rows[k]
        )
        carry = carry_b(tot, gate_rows[k, 5:8])
        d_proj, dx, dg_b, dgate = back_in(
            rel, x, d_mid, proj, d_pg, lam, prior, g, cum, ends, carry, w_in, gain_rows[k], gate_rows[k]
        )
        pairs[k] = ((normed, d_proj), (mixed, dy), (normed2, d_gu), (hid, dz))
        small[k] = jnp.stack(
            [
                jnp.sum(dg_b, axis=0),
                jnp.sum(dg_a[:8], axis=0),
                jnp.sum(dg_a[8:], axis=0),
                jnp.concatenate([jnp.sum(dgate[:8], axis=0), jnp.sum(dgate[8:], axis=0)]),
            ]
        )
    if paired:
        plan = []
        for k, mats in ((LAYERS - 1, (1, 2, 3, 0)),) + tuple(
            (k, (3, 2, 0, 1)) for k in reversed(range(LAYERS - 1))
        ):
            plan += [(m, k, m != 0) for m in mats]
        *outs, totals = grads_and_scatter(
            n, plan, [pairs[k][m][0] for m, k, _ in plan], [pairs[k][m][1] for m, k, _ in plan],
            jnp.concatenate(small),
        )
        totals = totals.reshape(LAYERS, 4, width)
    else:
        outs = []
        for m in range(4):
            parts = [
                lax.psum_scatter(contract_rows(*pairs[k][m]), "batch", scatter_dimension=0, tiled=True)
                for k in range(LAYERS)
            ]
            outs.append(jnp.stack([lax.psum(part, "seq") for part in parts]))
        totals = lax.psum(jnp.stack(small), ("batch", "seq"))
    outs = [o.astype(F32) for o in outs]
    d_gains = totals[:, :3]
    d_gate_params = totals[:, 3].reshape(LAYERS, 2, chan)
    return (block_out, dx.reshape(rows, length, width), *outs, d_gains, d_gate_params)


def solution(mesh):
    tok = P("batch", "seq", None)
    mat = P(None, "batch", None)
    return jax.shard_map(
        shards,
        mesh=mesh,
        in_specs=(tok, P("batch", None), mat, mat, mat, mat, P(), P(), tok),
        out_specs=(tok, tok, mat, mat, mat, mat, P(), P()),
        check_vma=False,
    )
```

```python
import functools

import jax
import jax.numpy as jnp
from jax import lax
from jax.experimental import pallas as pl
from jax.experimental.pallas import tpu as pltpu
from jax.sharding import PartitionSpec as P

LAYERS = 2
EPS = 1e-06
F32 = jnp.float32
BF16 = jnp.bfloat16
LANES = 128
CHUNK = 768
MESH = pl.DeviceIdType.MESH


def sigmoid(values):
    return 1.0 / (1.0 + jnp.exp(-values))


def rms_scale(values):
    return lax.rsqrt(jnp.mean(values * values, axis=-1, keepdims=True) + EPS)


def dot(left, right):
    return jnp.dot(left, right, preferred_element_type=F32)


def dot_t(left, right):
    return lax.dot_general(left, right, (((1,), (1,)), ((), ())), preferred_element_type=F32)


def eight_sum(values):
    rows, cols = values.shape
    return jnp.sum(values.reshape(rows // 8, 8, cols), axis=0)


def wide(ref, first, last):
    return jnp.concatenate([ref[g] for g in range(first, last)], axis=-1)


def split_store(ref, first, values):
    for g in range(values.shape[1] // LANES):
        ref[first + g] = values[:, g * LANES : (g + 1) * LANES]


def lanes(values):
    return [values[:, g * LANES : (g + 1) * LANES] for g in range(values.shape[1] // LANES)]


def keep_mask(rel_ref, row, first, shape):
    pos = lax.broadcasted_iota(jnp.int32, shape, 0) + first
    hit = pos == rel_ref[row, 0]
    for k in range(1, rel_ref.shape[1]):
        hit = hit | (pos == rel_ref[row, k])
    return hit


def enter_tile(rel_ref, row, tile, x, w_ref, gain_ref, gate_ref, proj_ref, pg_ref, normed_ref, lam_ref,
               h_ref, cum_ref, ends_ref, tot_ref, src):
    tokens, width = x.shape
    chan = width // 2
    seg = tokens // 8
    normed = (x * rms_scale(x) * gain_ref[0:1, :]).astype(BF16)
    normed_ref[...] = normed
    proj = dot(normed, w_ref[...])
    proj_ref[...] = proj[:, : 3 * chan].astype(BF16)
    pg_ref[...] = proj[:, 3 * chan :].astype(BF16)
    cos, sin, lower = gate_ref[0:1, :], gate_ref[1:2, :], gate_ref[2:3, :]
    seg_cos, seg_sin = gate_ref[3:4, :], gate_ref[4:5, :]
    p_r, p_i, p_f = proj[:, :chan], proj[:, chan : 2 * chan], proj[:, 2 * chan : 3 * chan]
    hit = keep_mask(rel_ref, row, tile * tokens, (tokens, chan))
    lam = jnp.where(hit, 0.0, lower + (1.0 - lower) * sigmoid(p_f))
    groups = chan // LANES
    split_store(lam_ref, 0, lam)
    split_store(src, 0, (1.0 - lam) * (p_r * sigmoid(p_r)))
    split_store(src, groups, (1.0 - lam) * (p_i * sigmoid(p_i)))
    cos_l, sin_l = lanes(cos), lanes(sin)

    def step(s, state):
        at = pl.ds(s, 8, stride=seg)
        after = []
        for k, (h_r, h_i, cum) in enumerate(state):
            lam_s = lam_ref[k, at, :]
            a_r, a_i = lam_s * cos_l[k], lam_s * sin_l[k]
            n_r = a_r * h_r - a_i * h_i + src[k, at, :]
            n_i = a_r * h_i + a_i * h_r + src[groups + k, at, :]
            cum = cum * lam_s
            h_ref[k, at, :] = n_r
            h_ref[groups + k, at, :] = n_i
            cum_ref[k, at, :] = cum
            after.append((n_r, n_i, cum))
        return tuple(after)

    zero = lam_ref[0, 0:8, :] * 0.0
    last = lax.fori_loop(0, seg, step, ((zero, zero, zero + 1.0),) * groups, unroll=8)
    e_r, e_i, e_c = (jnp.concatenate([v[i] for v in last], axis=-1) for i in range(3))
    ends_ref[0:8, :] = e_r
    ends_ref[8:16, :] = e_i
    ends_ref[16:24, :] = e_c

    @pl.when(tile == 0)
    def _():
        tot_ref[0:2, :] = jnp.zeros((2, chan), F32)
        tot_ref[2:3, :] = jnp.ones((1, chan), F32)

    c_r, c_i, c_l = tot_ref[0:1, :], tot_ref[1:2, :], tot_ref[2:3, :]
    for j in range(8):
        m = e_c[j : j + 1, :]
        a_r, a_i = m * seg_cos, m * seg_sin
        c_r, c_i = a_r * c_r - a_i * c_i + e_r[j : j + 1, :], a_r * c_i + a_i * c_r + e_i[j : j + 1, :]
        c_l = c_l * m
    tot_ref[0:1, :] = c_r
    tot_ref[1:2, :] = c_i
    tot_ref[2:3, :] = c_l


def leave_tile(tile, x, pg_ref, h_ref, cum_ref, ends_ref, carry_ref, wo_ref, wf_ref, wd_ref, gain_ref,
               gate_ref, state_ref, prior_ref, mixed_ref, mid_ref, normed_ref, gu_ref, hid_ref, run):
    tokens, width = x.shape
    chan = width // 2
    seg = tokens // 8
    cos, sin = gate_ref[0:1, :], gate_ref[1:2, :]
    seg_cos, seg_sin = gate_ref[3:4, :], gate_ref[4:5, :]

    @pl.when(tile == 0)
    def _():
        run[0:2, :] = carry_ref[0:2, :]

    c_r, c_i = run[0:1, :], run[1:2, :]
    l_r, l_i = [], []
    for j in range(8):
        l_r.append(c_r)
        l_i.append(c_i)
        m = ends_ref[16 + j : 17 + j, :]
        a_r, a_i = m * seg_cos, m * seg_sin
        c_r, c_i = (
            a_r * c_r - a_i * c_i + ends_ref[j : j + 1, :],
            a_r * c_i + a_i * c_r + ends_ref[8 + j : 9 + j, :],
        )
    run[0:1, :] = c_r
    run[1:2, :] = c_i
    groups = chan // LANES
    start_r, start_i = lanes(jnp.concatenate(l_r, axis=0)), lanes(jnp.concatenate(l_i, axis=0))
    cos_l, sin_l = lanes(cos), lanes(sin)

    def step(s, state):
        at = pl.ds(s, 8, stride=seg)
        after = []
        for k, (w_r, w_i, q_r, q_i) in enumerate(state):
            w_r, w_i = w_r * cos_l[k] - w_i * sin_l[k], w_r * sin_l[k] + w_i * cos_l[k]
            cum = cum_ref[k, at, :]
            s_r = h_ref[k, at, :] + cum * w_r
            s_i = h_ref[groups + k, at, :] + cum * w_i
            state_ref[k, at, :] = s_r
            state_ref[groups + k, at, :] = s_i
            prior_ref[k, at, :] = q_r
            prior_ref[groups + k, at, :] = q_i
            after.append((w_r, w_i, s_r, s_i))
        return tuple(after)

    lax.fori_loop(0, seg, step, tuple(zip(start_r, start_i, start_r, start_i)), unroll=8)
    state = wide(state_ref, 0, 2 * groups)
    p_g = pg_ref[...].astype(F32)
    mixed = (state * rms_scale(state) * gain_ref[1:2, :] * (p_g * sigmoid(p_g))).astype(BF16)
    mixed_ref[...] = mixed
    mid = x + dot(mixed, wo_ref[...])
    mid_ref[...] = mid
    normed = (mid * rms_scale(mid) * gain_ref[2:3, :]).astype(BF16)
    normed_ref[...] = normed
    gu = dot(normed, wf_ref[...])
    gu_ref[...] = gu.astype(BF16)
    hidden = gu.shape[1] // 2
    gate = gu[:, :hidden]
    hid = (gate * sigmoid(gate) * gu[:, hidden:]).astype(BF16)
    hid_ref[...] = hid
    return mid + dot(hid, wd_ref[...])


def enter_kernel(rel_ref, x_ref, w_ref, gain_ref, gate_ref, proj_ref, pg_ref, normed_ref, lam_ref, h_ref,
                 cum_ref, ends_ref, tot_ref, src):
    enter_tile(rel_ref, pl.program_id(0), pl.program_id(1), x_ref[...].astype(F32), w_ref, gain_ref, gate_ref,
               proj_ref, pg_ref, normed_ref, lam_ref, h_ref, cum_ref, ends_ref.at[0], tot_ref.at[0], src)


def leave_kernel(x_ref, pg_ref, h_ref, cum_ref, ends_ref, carry_ref, wo_ref, wf_ref, wd_ref, gain_ref, gate_ref,
                 state_ref, prior_ref, mixed_ref, mid_ref, normed_ref, gu_ref, hid_ref, out_ref, run):
    out = leave_tile(pl.program_id(1), x_ref[...].astype(F32), pg_ref, h_ref, cum_ref, ends_ref.at[0],
                     carry_ref.at[0], wo_ref, wf_ref, wd_ref, gain_ref, gate_ref, state_ref, prior_ref, mixed_ref,
                     mid_ref, normed_ref, gu_ref, hid_ref, run)
    out_ref[...] = out.astype(out_ref.dtype)


def back_out_kernel(dx_ref, gu_ref, mid_ref, state_ref, pg_ref, lam_ref, wo_ref, wf_ref, wd_ref,
                    gain_ref, gate_ref, dz_ref, dgu_ref, dmid_ref, dy_ref, dpg_ref, g_ref, cum_ref,
                    ends_ref, tot_ref, dgain_ref, grad):
    row, tile = pl.program_id(0), pl.program_id(1)
    tokens, width = dx_ref.shape
    chan = width // 2
    seg = tokens // 8
    cos, sin = gate_ref[0:1, :], gate_ref[1:2, :]
    seg_cos, seg_sin = gate_ref[3:4, :], gate_ref[4:5, :]
    dx = dx_ref[...].astype(F32)
    dz = dx.astype(BF16)
    dz_ref[...] = dz
    d_hid = dot_t(dz, wd_ref[...])
    hidden = d_hid.shape[1]
    gate = gu_ref[:, :hidden].astype(F32)
    up = gu_ref[:, hidden:].astype(F32)
    sg = sigmoid(gate)
    silu = gate * sg
    d_gu = jnp.concatenate(
        [(d_hid * up * (sg + silu * (1.0 - sg))).astype(BF16), (d_hid * silu).astype(BF16)], axis=1
    )
    dgu_ref[...] = d_gu
    d_n = dot_t(d_gu, wf_ref[...])
    mid = mid_ref[...]
    scale = rms_scale(mid)
    hat = mid * scale
    d_hat = d_n * gain_ref[2:3, :]

    @pl.when((row == 0) & (tile == 0))
    def _():
        dgain_ref[...] = jnp.zeros_like(dgain_ref)

    dgain_ref[8:16, :] += eight_sum(d_n * hat)
    d_mid = dx + scale * (d_hat - hat * jnp.mean(d_hat * hat, axis=-1, keepdims=True))
    dmid_ref[...] = d_mid
    dy = d_mid.astype(BF16)
    dy_ref[...] = dy
    d_mixed = dot_t(dy, wo_ref[...])
    p_g = pg_ref[...].astype(F32)
    sg = sigmoid(p_g)
    silu = p_g * sg
    groups = chan // LANES
    state = wide(state_ref, 0, 2 * groups)
    scale = rms_scale(state)
    hat = state * scale
    g1 = gain_ref[1:2, :]
    dpg_ref[...] = (d_mixed * hat * g1 * (sg + silu * (1.0 - sg))).astype(BF16)
    d_n = d_mixed * silu
    dgain_ref[0:8, :] += eight_sum(d_n * hat)
    d_hat = d_n * g1
    split_store(grad, 0, scale * (d_hat - hat * jnp.mean(d_hat * hat, axis=-1, keepdims=True)))
    cos_l, sin_l = lanes(cos), lanes(sin)

    def step(s, state):
        at = pl.ds(seg - 1 - s, 8, stride=seg)
        after = []
        for k, (g_r, g_i, cum, lam_n) in enumerate(state):
            a_r, a_i = lam_n * cos_l[k], lam_n * sin_l[k]
            n_r = grad[k, at, :] + a_r * g_r + a_i * g_i
            n_i = grad[groups + k, at, :] + a_r * g_i - a_i * g_r
            cum = cum * lam_n
            g_ref[k, at, :] = n_r
            g_ref[groups + k, at, :] = n_i
            cum_ref[k, at, :] = cum
            after.append((n_r, n_i, cum, lam_ref[k, at, :]))
        return tuple(after)

    zero = lam_ref[0, 0:8, :] * 0.0
    last = lax.fori_loop(0, seg, step, ((zero, zero, zero + 1.0, zero + 1.0),) * groups, unroll=8)
    g_r, g_i, cum, lam_0 = (jnp.concatenate([v[i] for v in last], axis=-1) for i in range(4))
    e_r = lam_0 * (cos * g_r + sin * g_i)
    e_i = lam_0 * (cos * g_i - sin * g_r)
    e_c = lam_0 * cum
    ends_ref[0, 0:8, :] = e_r
    ends_ref[0, 8:16, :] = e_i
    ends_ref[0, 16:24, :] = e_c

    @pl.when(tile == 0)
    def _():
        tot_ref[0, 0:2, :] = jnp.zeros((2, chan), F32)
        tot_ref[0, 2:3, :] = jnp.ones((1, chan), F32)

    c_r, c_i, c_l = tot_ref[0, 0:1, :], tot_ref[0, 1:2, :], tot_ref[0, 2:3, :]
    for j in reversed(range(8)):
        m = e_c[j : j + 1, :]
        a_r, a_i = m * seg_cos, m * seg_sin
        c_r, c_i = a_r * c_r + a_i * c_i + e_r[j : j + 1, :], a_r * c_i - a_i * c_r + e_i[j : j + 1, :]
        c_l = c_l * m
    tot_ref[0, 0:1, :] = c_r
    tot_ref[0, 1:2, :] = c_i
    tot_ref[0, 2:3, :] = c_l


def back_in_kernel(rel_ref, x_ref, dmid_ref, proj_ref, dpg_ref, lam_ref, prior_ref, g_ref, cum_ref,
                   ends_ref, carry_ref, w_ref, gain_ref, gate_ref, dproj_ref, dx_ref, dgain_ref,
                   dgate_ref, run, tot):
    row, tile = pl.program_id(0), pl.program_id(1)
    tokens, width = x_ref.shape
    chan = width // 2
    seg = tokens // 8
    cos, sin, lower = gate_ref[0:1, :], gate_ref[1:2, :], gate_ref[2:3, :]
    seg_cos, seg_sin = gate_ref[3:4, :], gate_ref[4:5, :]

    @pl.when(tile == 0)
    def _():
        run[0:2, :] = carry_ref[0, 0:2, :]

    c_r, c_i = run[0:1, :], run[1:2, :]
    l_r, l_i = [None] * 8, [None] * 8
    for j in reversed(range(8)):
        l_r[j], l_i[j] = c_r, c_i
        m = ends_ref[0, 16 + j : 17 + j, :]
        a_r, a_i = m * seg_cos, m * seg_sin
        c_r, c_i = (
            a_r * c_r + a_i * c_i + ends_ref[0, j : j + 1, :],
            a_r * c_i - a_i * c_r + ends_ref[0, 8 + j : 9 + j, :],
        )
    run[0:1, :] = c_r
    run[1:2, :] = c_i

    groups = chan // LANES
    start_r, start_i = lanes(jnp.concatenate(l_r, axis=0)), lanes(jnp.concatenate(l_i, axis=0))
    cos_l, sin_l = lanes(cos), lanes(sin)

    def step(s, state):
        at = pl.ds(seg - 1 - s, 8, stride=seg)
        after = []
        for k, (w_r, w_i) in enumerate(state):
            cum = cum_ref[k, at, :]
            tot[k, at, :] = g_ref[k, at, :] + cum * w_r
            tot[groups + k, at, :] = g_ref[groups + k, at, :] + cum * w_i
            after.append((w_r * cos_l[k] + w_i * sin_l[k], w_i * cos_l[k] - w_r * sin_l[k]))
        return tuple(after)

    lax.fori_loop(0, seg, step, tuple(zip(start_r, start_i)), unroll=8)
    g_r, g_i = wide(tot, 0, groups), wide(tot, groups, 2 * groups)
    q_r, q_i = wide(prior_ref, 0, groups), wide(prior_ref, groups, 2 * groups)
    p_r = proj_ref[:, :chan].astype(F32)
    p_i = proj_ref[:, chan : 2 * chan].astype(F32)
    forget = sigmoid(proj_ref[:, 2 * chan : 3 * chan].astype(F32))
    lam = wide(lam_ref, 0, groups)
    d_ar = g_r * q_r + g_i * q_i
    d_ai = g_i * q_r - g_r * q_i
    s_r, s_i = sigmoid(p_r), sigmoid(p_i)
    in_r, in_i = p_r * s_r, p_i * s_i
    d_lam = d_ar * cos + d_ai * sin - (g_r * in_r + g_i * in_i)

    @pl.when((row == 0) & (tile == 0))
    def _():
        dgain_ref[...] = jnp.zeros_like(dgain_ref)
        dgate_ref[...] = jnp.zeros_like(dgate_ref)

    dgate_ref[0:8, :] += eight_sum(lam * (d_ai * cos - d_ar * sin))
    first = (pl.num_programs(1) - 1 - tile) * tokens
    hit = keep_mask(rel_ref, row, first, (tokens, chan))
    d_f = jnp.where(hit, 0.0, d_lam) * (1.0 - forget)
    dgate_ref[8:16, :] += eight_sum(d_f)
    rest = 1.0 - lam
    d_proj = jnp.concatenate(
        [
            (rest * g_r * (s_r + in_r * (1.0 - s_r))).astype(BF16),
            (rest * g_i * (s_i + in_i * (1.0 - s_i))).astype(BF16),
            (d_f * (1.0 - lower) * forget).astype(BF16),
            dpg_ref[...],
        ],
        axis=1,
    )
    dproj_ref[...] = d_proj
    d_n = dot_t(d_proj, w_ref[...])
    x = x_ref[...].astype(F32)
    scale = rms_scale(x)
    hat = x * scale
    dgain_ref[...] += eight_sum(d_n * hat)
    d_hat = d_n * gain_ref[0:1, :]
    dx_ref[...] = dmid_ref[...] + scale * (d_hat - hat * jnp.mean(d_hat * hat, axis=-1, keepdims=True))


def combine(count, me, forward, buf, rot_ref, out_ref):
    cos, sin = rot_ref[0:1, :], rot_ref[1:2, :]
    for r in range(buf.shape[1]):
        c_r = jnp.zeros_like(cos)
        c_i = jnp.zeros_like(cos)
        for k in range(count - 1, 0, -1):
            slot = k - 1 if forward else count - k - 1
            valid = me >= k if forward else me + k < count
            e_r, e_i, m = buf[slot, r, 0:1, :], buf[slot, r, 1:2, :], buf[slot, r, 2:3, :]
            a_r = m * cos
            a_i = m * sin if forward else -m * sin
            n_r = a_r * c_r - a_i * c_i + e_r
            n_i = a_r * c_i + a_i * c_r + e_i
            keep = jnp.where(valid, 1.0, 0.0)
            c_r, c_i = n_r * keep, n_i * keep
        out_ref[r, 0:1, :] = c_r
        out_ref[r, 1:2, :] = c_i


def carry_copies(count, me, tot_ref, buf, send_sem, recv_sem):
    return [
        remote(tot_ref, buf.at[k - 1], send_sem.at[k - 1], recv_sem.at[k - 1], {"seq": lax.rem(me + k, count)})
        for k in range(1, count)
    ]


def carry_kernel(count, forward, tot_ref, rot_ref, out_ref, buf, send_sem, recv_sem):
    me = lax.axis_index("seq")
    meet([{"seq": lax.rem(me + k, count)} for k in range(1, count)])
    copies = carry_copies(count, me, tot_ref, buf, send_sem, recv_sem)
    for copy in copies:
        copy.start()
    for copy in copies:
        copy.wait()
    combine(count, me, forward, buf, rot_ref, out_ref)


class Ring:
    def __init__(self, n):
        self.n = n
        self.batch, self.seq = lax.axis_index("batch"), lax.axis_index("seq")
        z, x = self.batch // 2, self.batch % 2
        self.pos = z + x * (n - 1 - 2 * z)
        self.core, self.y = self.seq % 2, self.seq // 2
        self.sign = 1 - 2 * self.core
        self.core_peer = self.seq + self.sign
        self.y_peer = self.seq + 2 * (1 - 2 * self.y)

    def at(self, distance):
        p = (self.pos + distance + 2 * self.n) % self.n
        h = p // (self.n // 2)
        return 2 * (p + h * (self.n - 1 - 2 * p)) + h

    def ahead(self, hops):
        return self.at(self.sign * hops)


def remote(src, dst, send, recv, device):
    return pltpu.make_async_remote_copy(
        src_ref=src, dst_ref=dst, send_sem=send, recv_sem=recv, device_id=device, device_id_type=MESH
    )


def meet(devices):
    barrier = pltpu.get_barrier_semaphore()
    for device in devices:
        pl.semaphore_signal(barrier, inc=1, device_id=device, device_id_type=MESH)
    pl.semaphore_wait(barrier, len(devices))


class Gather:
    def __init__(self, ring, jobs, sems):
        self.ring, self.jobs = ring, jobs
        (self.own_sem, self.ring_send, self.ring_recv, self.y_send, self.y_recv, self.core_send,
         self.core_recv) = sems
        n = ring.n
        self.hops = ((1, n // 2, 0), (-1, n - 1 - n // 2, n // 2))

    def rows(self, j, piece):
        src, dst, u = self.jobs[j]
        ring = self.ring
        base = ring.core * (3 * u)
        whole = piece * (6 * u)
        view = lambda first, rows: dst.at[pl.ds(pl.multiple_of(whole + base + first, 16), rows)]
        return view(ring.y * u, 2 * u), view(2 * ring.y * u, u), view(2 * (1 - ring.y) * u, u)

    def own_copy(self, j):
        src, dst, u = self.jobs[j]
        return pltpu.make_async_copy(
            src, dst.at[pl.ds(pl.multiple_of(self.ring.batch * (6 * u), 16), 6 * u)], self.own_sem.at[j]
        )

    def own(self, j):
        src, dst, u = self.jobs[j]
        ring = self.ring
        mine, _, _ = self.rows(j, ring.batch)
        piece = src.at[pl.ds(pl.multiple_of(ring.core * (3 * u) + ring.y * u, 16), 2 * u)]
        for way, hops, first in self.hops:
            remote(piece, mine, self.ring_send.at[j], self.ring_recv.at[j, first],
                   {"batch": ring.ahead(way)}).start()
        self.own_copy(j).start()

    def arrived(self, j, h):
        ring = self.ring
        for way, hops, first in self.hops:
            if h < hops:
                mine, give, _ = self.rows(j, ring.ahead(-way * (h + 1)))
                on = lambda slot: remote(mine, mine, self.ring_send.at[j], self.ring_recv.at[j, first + slot],
                                         {"batch": ring.ahead(way)})
                on(h).wait_recv()
                if h + 1 < hops:
                    on(h + 1).start()
                remote(give, give, self.y_send.at[j], self.y_recv.at[j, first + h], {"seq": ring.y_peer}).start()
                remote(mine, mine, self.core_send.at[j], self.core_recv.at[j], {"seq": ring.core_peer}).start()

    def crossed(self, j, h):
        ring = self.ring
        for way, hops, first in self.hops:
            if h < hops:
                _, _, take = self.rows(j, ring.ahead(-way * (h + 1)))
                remote(take, take, self.y_send.at[j], self.y_recv.at[j, first + h], {"seq": ring.y_peer}).wait_recv()
                remote(take, take, self.core_send.at[j], self.core_recv.at[j], {"seq": ring.core_peer}).start()

    def swapped(self, j):
        src, dst, u = self.jobs[j]
        view = dst.at[0 : (self.ring.n - 1) * 3 * u]
        remote(view, view, self.core_send.at[j], self.core_recv.at[j], {"seq": self.ring.core_peer}).wait_recv()
        self.own_copy(j).wait()

    def sent(self, j):
        src, dst, u = self.jobs[j]
        for rows, send in ((2 * u, self.ring_send), (u, self.y_send), (3 * u, self.core_send)):
            view = dst.at[0 : (self.ring.n - 1) * rows]
            remote(view, view, send.at[j], self.core_recv.at[j], {"seq": self.ring.core_peer}).wait_send()


def forward_kernel(n, n_seq, layers, rows, *refs):
    rel_ref, tok_ref = refs[:2]
    sources, (gain_ref, gate_ref) = refs[2:6], refs[6:8]
    mats = len(sources)
    gathered = refs[8 : 8 + layers * mats]
    (proj_ref, pg_ref, normed_ref, lam_ref, state_ref, prior_ref, mixed_ref, mid_ref, normed2_ref, gu_ref, hid_ref,
     next_ref, out_ref) = refs[8 + layers * mats : 21 + layers * mats]
    (xs, hs, cum, pg, ends, tot, src, run, carry, buf, *rest) = refs[21 + layers * mats :]
    weights, (load_sem, carry_send, carry_recv), sems = rest[:mats], rest[mats : mats + 3], rest[mats + 3 :]
    layer, step = pl.program_id(0), pl.program_id(1)
    tokens = tok_ref.shape[0]
    count = xs.shape[0]
    tiles = count // rows
    now = layer * (2 * count) + step
    ring = Ring(n)
    jobs = [
        (sources[m].at[k], gathered[k * mats + m], sources[m].shape[1] // 6)
        for k in range(layers) for m in range(mats)
    ]
    net = Gather(ring, jobs, sems)
    far = n // 2

    def load(j):
        return pltpu.make_async_copy(gathered[j], weights[j % mats], load_sem.at[j % mats])

    def exchange():
        return carry_copies(n_seq, ring.seq, tot, buf.at[layer], carry_send.at[layer], carry_recv.at[layer])

    agenda = {}

    def at(when, *calls):
        agenda.setdefault(when, []).extend(calls)

    def do(f, *args):
        return lambda: f(*args)

    def complete(j):
        net.swapped(j)
        load(j).start()

    def hop(j, h):
        if h < far:
            net.arrived(j, h)
        if h >= 1:
            net.crossed(j, h - 1)

    at(0, lambda: meet([{"batch": ring.ahead(1)}, {"batch": ring.ahead(-1)}]
                       + [{"seq": lax.rem(ring.seq + k, n_seq)} for k in range(1, n_seq)]))
    at(0, do(net.own, 0), do(net.own, 1))
    for h in range(far + 1):
        at(0, do(hop, 0, h))
        if h == 0:
            at(0, do(net.own, 3))
        if h == 1:
            at(0, do(net.own, 2))
    at(0, do(complete, 0), lambda: load(0).wait())
    for h in range(far + 1):
        for j in (1, 3, 2):
            at(min(1 + h, count), do(hop, j, h))
    at(count - 2, *[do(net.own, j) for j in range(mats, layers * mats)])
    for j in (1, 3, 2):
        at(count, do(complete, j))
    for j in (1, 3, 2):
        at(count, lambda j=j: load(j).wait())
    for k in range(1, layers):
        start = (2 * k - 1) * count
        for h in range(far + 1):
            for j in range(k * mats, k * mats + mats):
                at(start + 1 + min(h, count - 1), do(hop, j, h))
        at(start + count, do(complete, k * mats), lambda k=k: load(k * mats).wait())
        for j in range(k * mats + 1, k * mats + mats):
            at(start + count + 1, do(complete, j))
        for j in range(k * mats + 1, k * mats + mats):
            at(start + 2 * count, lambda j=j: load(j).wait())
    for when, calls in sorted(agenda.items()):

        @pl.when(now == when)
        def _(calls=calls):
            for call in calls:
                call()

    tile = lax.rem(step, count)
    row, at_row = tile // tiles, lax.rem(tile, tiles)
    gains, gate = gain_ref.at[layer], gate_ref.at[layer]

    @pl.when((layer == 0) & (step < count))
    def _():
        xs[tile] = tok_ref[...].astype(F32)

    @pl.when(step < count)
    def _():
        enter_tile(rel_ref, row, at_row, xs[tile], weights[0], gains, gate, proj_ref, pg.at[tile], normed_ref,
                   lam_ref, hs.at[tile], cum.at[tile], ends.at[tile], tot.at[row], src)
        pg_ref[...] = pg[tile]

    @pl.when(step == count - 1)
    def _():
        for copy in exchange():
            copy.start()

    @pl.when(step == count)
    def _():
        for copy in exchange():
            copy.wait()
        combine(n_seq, ring.seq, True, buf.at[layer], gate.at[5:8], carry)

    @pl.when(step >= count)
    def _():
        out = leave_tile(at_row, xs[tile], pg.at[tile], hs.at[tile], cum.at[tile], ends.at[tile], carry.at[row],
                         weights[1], weights[2], weights[3], gains, gate, state_ref, prior_ref, mixed_ref, mid_ref,
                         normed2_ref, gu_ref, hid_ref, run)
        xs[tile] = out

        @pl.when(layer < layers - 1)
        def _():
            next_ref[...] = out

        @pl.when(layer == layers - 1)
        def _():
            out_ref[...] = out.astype(out_ref.dtype)

    @pl.when(now == layers * 2 * count - 1)
    def _():
        for j in range(layers * mats):
            net.sent(j)


def run_forward(n, n_seq, rows, tokens, rel, x, sources, gain_rows, gate_rows):
    layers = sources[0].shape[0]
    total, width = x.shape
    chan = width // 2
    hidden = sources[2].shape[2] // 2
    count = total // tokens
    mats = len(sources)
    jobs = layers * mats
    shape = jax.ShapeDtypeStruct
    dma = pltpu.SemaphoreType.DMA
    any_ = pl.BlockSpec(memory_space=pl.ANY)

    def first(step):
        return jnp.minimum(step, count - 1)

    def second(step):
        return jnp.maximum(step - count, 0)

    def flat(w, when):
        return pl.BlockSpec((None, tokens, w), lambda k, s: (k, when(s), 0))

    def split(w, when):
        return pl.BlockSpec((None, w // LANES, tokens, LANES), lambda k, s: (k, 0, when(s), 0))

    def flat_s(w, kind=BF16):
        return shape((layers, total, w), kind)

    def split_s(w):
        return shape((layers, w // LANES, total, LANES), F32)

    full = [(n * w.shape[1], w.shape[2]) for w in sources]
    last = layers - 1
    outs = pl.pallas_call(
        functools.partial(forward_kernel, n, n_seq, layers, rows),
        grid=(layers, 2 * count),
        in_specs=[
            pl.BlockSpec(memory_space=pltpu.SMEM),
            pl.BlockSpec((tokens, width), lambda k, s: (jnp.where(k == 0, first(s), count - 1), 0)),
        ]
        + [any_] * mats
        + [whole(layers, 8, width), whole(layers, 8, chan)],
        out_specs=[any_] * jobs
        + [
            flat(3 * chan, first),
            flat(width, first),
            flat(width, first),
            split(chan, first),
            split(width, second),
            split(width, second),
            flat(width, second),
            flat(width, second),
            flat(width, second),
            flat(2 * hidden, second),
            flat(hidden, second),
            pl.BlockSpec(
                (None, tokens, width),
                lambda k, s: (jnp.minimum(k, last - 1), jnp.where(k < last, second(s), count - 1), 0),
            ),
            pl.BlockSpec((tokens, width), lambda k, s: (jnp.where(k == last, second(s), 0), 0)),
        ],
        out_shape=[shape(f, BF16) for _ in range(layers) for f in full]
        + [
            flat_s(3 * chan),
            flat_s(width),
            flat_s(width),
            split_s(chan),
            split_s(width),
            split_s(width),
            flat_s(width),
            flat_s(width, F32),
            flat_s(width),
            flat_s(2 * hidden),
            flat_s(hidden),
            shape((last, total, width), F32),
            shape((total, width), BF16),
        ],
        scratch_shapes=[
            pltpu.VMEM((count, tokens, width), F32),
            pltpu.VMEM((count, width // LANES, tokens, LANES), F32),
            pltpu.VMEM((count, chan // LANES, tokens, LANES), F32),
            pltpu.VMEM((count, tokens, width), BF16),
            pltpu.VMEM((count, 24, chan), F32),
            pltpu.VMEM((rows, 8, chan), F32),
            pltpu.VMEM((width // LANES, tokens, LANES), F32),
            pltpu.VMEM((8, chan), F32),
            pltpu.VMEM((rows, 8, chan), F32),
            pltpu.VMEM((layers, n_seq - 1, rows, 8, chan), F32),
        ]
        + [pltpu.VMEM(f, BF16) for f in full]
        + [dma((mats,)), dma((layers, n_seq - 1)), dma((layers, n_seq - 1))]
        + [dma((jobs,)), dma((jobs,)), dma((jobs, n - 1)), dma((jobs,)), dma((jobs, n - 1)), dma((jobs,)),
           dma((jobs,))],
        compiler_params=pltpu.CompilerParams(
            collective_id=3, has_side_effects=True, vmem_limit_bytes=LIMIT
        ),
    )(rel, x, *sources, gain_rows, gate_rows)
    return outs[:jobs], outs[jobs:]


def add_rows(dst, dst_row, parts, rows):
    def block(i, _):
        step = pl.multiple_of(i * 16, 16)
        total = None
        for ref, first in parts:
            value = ref[pl.ds(pl.multiple_of(first + step, 16), 16), :].astype(F32)
            total = value if total is None else total + value
        dst[pl.ds(pl.multiple_of(dst_row + step, 16), 16), :] = total.astype(dst.dtype)
        return 0

    lax.fori_loop(0, rows // 16, block, 0)


def grads_kernel(n, plan, *refs):
    jobs = len(plan)
    lefts, rights, small = refs[:jobs], refs[jobs : 2 * jobs], refs[2 * jobs]
    outs_count = 1 + max(p[0] for p in plan)
    outs, small_out = refs[2 * jobs + 1 : 2 * jobs + 1 + outs_count], refs[2 * jobs + 1 + outs_count]
    rest = refs[2 * jobs + 2 + outs_count :]
    grads, core_buf, y_buf, ring_buf, fin_buf = (rest[i * jobs : (i + 1) * jobs] for i in range(5))
    (left_big, left_small, right_buf, small_buf, left_sem, right_sem, core_send, core_recv, y_send, y_recv,
     ring_send, ring_recv, end_send, end_recv, small_send, small_recv) = rest[5 * jobs :]
    ring = Ring(n)
    far, near = n // 2, n - 1 - n // 2
    core_dev, y_dev = {"seq": ring.core_peer}, {"seq": ring.y_peer}
    y, core = ring.y, ring.core
    rounds = [core_dev, y_dev]
    d = 1
    while d < n:
        rounds.append({"batch": ring.batch + d * (1 - 2 * ((ring.batch // d) % 2))})
        d *= 2
    us = [g.shape[0] // n // 6 for g in grads]
    split = [p[2] for p in plan]
    own_rows = [(2 if s else 3) * u for s, u in zip(split, us)]

    def left_copy(j):
        buf = (left_big, left_small)[j % 2]
        return pltpu.make_async_copy(lefts[j].at[plan[j][1]], buf.at[:, 0 : plan[j][3]], left_sem.at[j % 2])

    chunks = []
    for j, (_, _, _, rows, cols) in enumerate(plan):
        first = 0
        while first < cols:
            size = min(CHUNK, cols - first)
            chunks.append((j, first, size, first + size == cols))
            first += size

    def right_copy(i):
        j, first, size, _ = chunks[i]
        return pltpu.make_async_copy(
            rights[j].at[:, first : first + size], right_buf.at[i % 2, :, 0:size], right_sem.at[i % 2]
        )

    left_copy(0).start()
    right_copy(0).start()
    right_copy(1).start()
    left_copy(1).start()
    meet([{"batch": ring.ahead(1)}, {"batch": ring.ahead(-1)}] + rounds)

    order = []
    for h in range(far):
        order.append((1, h, far - h))
        if h < near:
            order.append((-1, h, near - h))
    order.append((0, 0, 0))
    last = len(order)

    def rows_at(ref, first, rows):
        return ref.at[pl.ds(pl.multiple_of(first, 16), rows)]

    def core_copy(j, slot, piece):
        u = us[j]
        return remote(rows_at(grads[j], piece * (6 * u) + (1 - core) * (3 * u), 3 * u),
                      core_buf[j].at[slot], core_send.at[j], core_recv.at[j, slot], core_dev)

    def y_copy(j, slot, piece):
        u = us[j]
        src = rows_at(grads[j], piece * (6 * u) + core * (3 * u) + 2 * (1 - y) * u, u)
        return remote(src, y_buf[j].at[slot], y_send.at[j], y_recv.at[j, slot], y_dev)

    def mine(j, piece):
        u = us[j]
        return piece * (6 * u) + core * (3 * u) + (y * u if split[j] else 0)

    def ring_copy(j, slot, way, piece):
        return remote(rows_at(grads[j], mine(j, piece), own_rows[j]), ring_buf[j].at[slot], ring_send.at[j],
                      ring_recv.at[j, slot], {"batch": ring.ahead(way)})

    def small_round(r):
        return remote(small_buf.at[2 * r], small_buf.at[2 * r + 1], small_send.at[r], small_recv.at[r], rounds[r])

    small_buf[0] = small[...]
    small_round(0).start()

    def small_step(r):
        small_round(r).wait_recv()
        total = small_buf[2 * r] + small_buf[2 * r + 1]
        if r + 1 < len(rounds):
            small_buf[2 * r + 2] = total
            small_round(r + 1).start()
        else:
            small_out[...] = total

    def begin(j):
        for slot, (way, h, dist) in enumerate(order):
            core_copy(j, slot, ring.ahead(-way * dist)).start()

    def cross(j, slot):
        way, h, dist = order[slot]
        piece = ring.ahead(way * dist)
        u = us[j]
        core_copy(j, slot, piece).wait_recv()
        if not split[j]:
            return
        give = 2 * (1 - y) * u
        at = piece * (6 * u) + core * (3 * u) + give
        add_rows(grads[j], at, [(grads[j], at), (core_buf[j].at[slot], give)], u)
        y_copy(j, slot, piece).start()

    def hop(j, slot):
        way, h, dist = order[slot]
        piece = ring.ahead(way * dist)
        u = us[j]
        if split[j]:
            y_copy(j, slot, piece).wait_recv()
        if way == 0:
            prior = [i for i, o in enumerate(order) if o[2] == 1]
        elif h:
            prior = [i for i, o in enumerate(order) if o[0] == way and o[1] == h - 1]
        else:
            prior = []
        for i in prior:
            ring_copy(j, i, order[i][0], piece).wait_recv()
        at = mine(j, piece)
        base = [(grads[j], at), (core_buf[j].at[slot], y * u if split[j] else 0)]
        base += [(ring_buf[j].at[i], 0) for i in prior]
        if split[j]:
            for by, more in ((y * u, [(y_buf[j].at[slot], 0)]), ((1 - y) * u, [])):
                add_rows(grads[j], at + by, [(r, f + by) for r, f in base] + more, u)
        else:
            add_rows(grads[j], at, base, 3 * u)
        if way:
            ring_copy(j, slot, way, piece).start()

    def fin_copy(j):
        return remote(rows_at(grads[j], mine(j, ring.batch), own_rows[j]), fin_buf[j], end_send.at[j, 0],
                      end_recv.at[j, 0], y_dev)

    def half_copy(j):
        half = outs[plan[j][0]].at[plan[j][1], pl.ds(pl.multiple_of(core * (3 * us[j]), 16), 3 * us[j])]
        return remote(half, half, end_send.at[j, 1], end_recv.at[j, 1], core_dev)

    def finish(j):
        u = us[j]
        fin_copy(j).wait_recv()
        out = outs[plan[j][0]].at[plan[j][1]]
        at, to = mine(j, ring.batch), core * (3 * u)
        if split[j]:
            add_rows(out, to + 2 * y * u, [(grads[j], at + y * u)], u)
            add_rows(out, to + 2 * (1 - y) * u, [(fin_buf[j], (1 - y) * u)], u)
            add_rows(out, to + u, [(grads[j], at + (1 - y) * u), (fin_buf[j], y * u)], u)
        else:
            add_rows(out, to, [(grads[j], at), (fin_buf[j], 0)], 3 * u)
        half_copy(j).start()

    steps = far + 4

    def advance(j, t):
        now = [i for i, o in enumerate(order) if o[0] and o[1] == t]
        before = [i for i, o in enumerate(order) if o[0] and o[1] == t - 1]
        for slot in before:
            hop(j, slot)
        for slot in now:
            cross(j, slot)
        if t == far - 1:
            cross(j, last - 1)
        if t == far + 1:
            hop(j, last - 1)
            fin_copy(j).start()
        if t == far + 2:
            finish(j)
        if t == far + 3:
            half_copy(j).wait_recv()

    stage = {}

    def advance_all(turn):
        for j in list(stage):
            if j % 2 == turn:
                advance(j, stage[j])
                stage[j] += 1
                if stage[j] == steps:
                    del stage[j]

    small_at = 0
    for i, (j, first, size, done) in enumerate(chunks):
        if first == 0:
            left_copy(j).wait()
        right_copy(i).wait()
        left = (left_big, left_small)[j % 2]

        def multiply(b, _, i=i, j=j, first=first, size=size, left=left):
            at = pl.multiple_of(b * 256, 256)
            part = lax.dot_general(
                left[:, pl.ds(at, 256)], right_buf[i % 2, :, 0:size], (((0,), (0,)), ((), ())),
                preferred_element_type=F32,
            )
            grads[j][pl.ds(at, 256), first : first + size] = part.astype(BF16)
            return 0

        lax.fori_loop(0, plan[j][3] // 256, multiply, 0)
        if i + 2 < len(chunks):
            right_copy(i + 2).start()
        if done and j + 2 < jobs:
            left_copy(j + 2).start()
        advance_all(i % 2)
        if done:
            begin(j)
            stage[j] = 0
        if small_at < len(rounds):
            small_step(small_at)
            small_at += 1
    i = 0
    while stage:
        advance_all(i % 2)
        i += 1
    while small_at < len(rounds):
        small_step(small_at)
        small_at += 1
    for j in range(jobs):
        u = us[j]
        fin_copy(j).wait_send()
        half_copy(j).wait_send()
        remote(core_buf[j], core_buf[j], core_send.at[j], core_recv.at[j, 0], core_dev).wait_send()
        if split[j]:
            remote(y_buf[j], y_buf[j], y_send.at[j], y_recv.at[j, 0], y_dev).wait_send()
        remote(ring_buf[j], ring_buf[j], ring_send.at[j], ring_recv.at[j, 0], core_dev).wait_send()
    for r in range(len(rounds)):
        small_round(r).wait_send()


def grads_and_scatter(n, plan, lefts, rights, small):
    jobs = len(plan)
    plan = [p + (a.shape[2], b.shape[1]) for p, a, b in zip(plan, lefts, rights)]
    tokens = lefts[0].shape[1]
    layers = 1 + max(p[1] for p in plan)
    dma = pltpu.SemaphoreType.DMA
    rounds = 2 + (n - 1).bit_length()
    sizes = [(p[3] // n // 6, p[4], p[2]) for p in plan]
    outs = {p[0]: jax.ShapeDtypeStruct((layers, p[3] // n, p[4]), BF16) for p in plan}
    vm = pl.BlockSpec(memory_space=pltpu.VMEM)
    any_ = pl.BlockSpec(memory_space=pl.ANY)

    def bufs(f):
        return [pltpu.VMEM(f(u, w, s), BF16) for u, w, s in sizes]

    return pl.pallas_call(
        functools.partial(grads_kernel, n, plan),
        out_shape=[outs[m] for m in sorted(outs)] + [jax.ShapeDtypeStruct(small.shape, F32)],
        in_specs=[any_] * (2 * jobs) + [vm],
        out_specs=[vm] * (len(outs) + 1),
        scratch_shapes=bufs(lambda u, w, s: (6 * u * n, w))
        + bufs(lambda u, w, s: (n, 3 * u, w))
        + bufs(lambda u, w, s: (n if s else 1, u, w))
        + bufs(lambda u, w, s: (n - 1, 2 * u if s else 3 * u, w))
        + bufs(lambda u, w, s: (2 * u if s else 3 * u, w))
        + [
            pltpu.VMEM((tokens, max(p[3] for p in plan[0::2])), BF16),
            pltpu.VMEM((tokens, max(p[3] for p in plan[1::2])), BF16),
            pltpu.VMEM((2, tokens, CHUNK), BF16),
            pltpu.VMEM((2 * rounds,) + small.shape, F32),
            dma((2,)), dma((2,)), dma((jobs,)), dma((jobs, n)), dma((jobs,)), dma((jobs, n)), dma((jobs,)),
            dma((jobs, n)), dma((jobs, 2)), dma((jobs, 2)), dma((rounds,)), dma((rounds,)),
        ],
        compiler_params=pltpu.CompilerParams(
            collective_id=4, has_side_effects=True, vmem_limit_bytes=63 * 1024 * 1024
        ),
    )(*lefts, *rights, small)


def vmem(bytes_):
    return pltpu.CompilerParams(vmem_limit_bytes=bytes_)


def whole(*shape):
    return pl.BlockSpec(shape, lambda *_: (0,) * len(shape), pipeline_mode=pl.Buffered(1))


def make_carry(count, rows, chan, forward):
    return pl.pallas_call(
        functools.partial(carry_kernel, count, forward),
        out_shape=jax.ShapeDtypeStruct((rows, 8, chan), F32),
        in_specs=[pl.BlockSpec(memory_space=pltpu.VMEM)] * 2,
        out_specs=pl.BlockSpec(memory_space=pltpu.VMEM),
        scratch_shapes=[
            pltpu.VMEM((count - 1, rows, 8, chan), F32),
            pltpu.SemaphoreType.DMA((count - 1,)),
            pltpu.SemaphoreType.DMA((count - 1,)),
        ],
        compiler_params=pltpu.CompilerParams(
            collective_id=1 if forward else 2, has_side_effects=True
        ),
    )


LIMIT = 60 * 1024 * 1024


def layer_calls(rows, length, width, hidden, cols, n_seq, tokens):
    chan = width // 2
    tiles = length // tokens
    total = rows * length
    grid = (rows, tiles)
    shape = jax.ShapeDtypeStruct
    smem = pl.BlockSpec(memory_space=pltpu.SMEM)

    def fwd(w, col=0):
        return pl.BlockSpec((tokens, w), lambda r, t: (r * tiles + t, col))

    def fwd_l(w):
        return pl.BlockSpec((w // LANES, tokens, LANES), lambda r, t: (0, r * tiles + t, 0))

    def bwd_l(w):
        return pl.BlockSpec(
            (w // LANES, tokens, LANES), lambda r, t: (0, r * tiles + tiles - 1 - t, 0)
        )

    def split(w):
        return shape((w // LANES, total, LANES), F32)

    def bwd(w, col=0):
        return pl.BlockSpec((tokens, w), lambda r, t: (r * tiles + tiles - 1 - t, col))

    ends_f = pl.BlockSpec((1, 24, chan), lambda r, t: (r * tiles + t, 0, 0))
    ends_b = pl.BlockSpec((1, 24, chan), lambda r, t: (r * tiles + tiles - 1 - t, 0, 0))
    per_row = pl.BlockSpec((1, 8, chan), lambda r, t: (r, 0, 0))
    ends_s = shape((rows * tiles, 24, chan), F32)
    row_s = shape((rows, 8, chan), F32)

    enter = pl.pallas_call(
        enter_kernel,
        grid=grid,
        in_specs=[smem, fwd(width), whole(width, cols), whole(8, width), whole(8, chan)],
        out_specs=[
            fwd(3 * chan), fwd(width), fwd(width), fwd_l(chan), fwd_l(width), fwd_l(chan), ends_f, per_row
        ],
        out_shape=[
            shape((total, 3 * chan), BF16),
            shape((total, width), BF16),
            shape((total, width), BF16),
            split(chan),
            split(width),
            split(chan),
            ends_s,
            row_s,
        ],
        scratch_shapes=[pltpu.VMEM((width // LANES, tokens, LANES), F32)],
        compiler_params=vmem(LIMIT),
    )

    def leave(out_type):
        return pl.pallas_call(
            leave_kernel,
            grid=grid,
            in_specs=[
                fwd(width),
                fwd(width),
                fwd_l(width),
                fwd_l(chan),
                ends_f,
                per_row,
                whole(width, width),
                whole(width, 2 * hidden),
                whole(hidden, width),
                whole(8, width),
                whole(8, chan),
            ],
            out_specs=[
                fwd_l(width),
                fwd_l(width),
                fwd(width),
                fwd(width),
                fwd(width),
                fwd(2 * hidden),
                fwd(hidden),
                fwd(width),
            ],
            out_shape=[
                split(width),
                split(width),
                shape((total, width), BF16),
                shape((total, width), F32),
                shape((total, width), BF16),
                shape((total, 2 * hidden), BF16),
                shape((total, hidden), BF16),
                shape((total, width), out_type),
            ],
            scratch_shapes=[pltpu.VMEM((8, chan), F32)],
            compiler_params=vmem(LIMIT),
        )

    def back(k):
        def kept(w):
            return pl.BlockSpec((None, tokens, w), lambda r, t: (k, r * tiles + tiles - 1 - t, 0))

        def kept_l(w):
            return pl.BlockSpec(
                (None, w // LANES, tokens, LANES), lambda r, t: (k, 0, r * tiles + tiles - 1 - t, 0)
            )

        back_out = pl.pallas_call(
            back_out_kernel,
            grid=grid,
            in_specs=[
                bwd(width),
                kept(2 * hidden),
                kept(width),
                kept_l(width),
                kept(width),
                kept_l(chan),
                whole(width, width),
                whole(width, 2 * hidden),
                whole(hidden, width),
                whole(8, width),
                whole(8, chan),
            ],
            out_specs=[
                bwd(width),
                bwd(2 * hidden),
                bwd(width),
                bwd(width),
                bwd(width),
                bwd_l(width),
                bwd_l(chan),
                ends_b,
                per_row,
                pl.BlockSpec((16, width), lambda r, t: (0, 0)),
            ],
            out_shape=[
                shape((total, width), BF16),
                shape((total, 2 * hidden), BF16),
                shape((total, width), F32),
                shape((total, width), BF16),
                shape((total, width), BF16),
                split(width),
                split(chan),
                ends_s,
                row_s,
                shape((16, width), F32),
            ],
            scratch_shapes=[pltpu.VMEM((width // LANES, tokens, LANES), F32)],
            compiler_params=vmem(LIMIT),
        )

        back_in = pl.pallas_call(
            back_in_kernel,
            grid=grid,
            in_specs=[
                smem,
                bwd(width),
                bwd(width),
                kept(3 * chan),
                bwd(width),
                kept_l(chan),
                kept_l(width),
                bwd_l(width),
                bwd_l(chan),
                ends_b,
                per_row,
                whole(width, cols),
                whole(8, width),
                whole(8, chan),
            ],
            out_specs=[
                bwd(cols),
                bwd(width),
                pl.BlockSpec((8, width), lambda r, t: (0, 0)),
                pl.BlockSpec((16, chan), lambda r, t: (0, 0)),
            ],
            out_shape=[
                shape((total, cols), BF16),
                shape((total, width), F32),
                shape((8, width), F32),
                shape((16, chan), F32),
            ],
            scratch_shapes=[
                pltpu.VMEM((8, chan), F32),
                pltpu.VMEM((width // LANES, tokens, LANES), F32),
            ],
            compiler_params=vmem(LIMIT),
        )
        return back_out, back_in

    carry_f = make_carry(n_seq, rows, chan, True)
    carry_b = make_carry(n_seq, rows, chan, False)
    return enter, carry_f, leave, carry_b, back


def contract_rows(left, right):
    return lax.dot_general(
        left, right, (((0,), (0,)), ((), ())), preferred_element_type=F32
    ).astype(BF16)


def shards(
    tokens_in, doc_starts, mixer_in, mixer_out, ffn_in, ffn_out, gains, gate_params, cotangent
):
    rows, length, width = tokens_in.shape
    chan = width // 2
    n_seq = lax.axis_size("seq")
    hidden = ffn_in.shape[2] // 2
    cols = mixer_in.shape[2]
    total = rows * length
    tokens = min(length, 256)
    seg = tokens // 8
    enter, carry_f, leave, carry_b, back = layer_calls(rows, length, width, hidden, cols, n_seq, tokens)
    rel = doc_starts - lax.axis_index("seq") * length
    gain_rows = jnp.pad(gains, ((0, 0), (0, 5), (0, 0)))
    theta, lower = gate_params[:, 0], gate_params[:, 1]
    gate_rows = jnp.stack(
        [jnp.cos(theta), jnp.sin(theta), lower, jnp.cos(theta * seg), jnp.sin(theta * seg),
         jnp.cos(theta * length), jnp.sin(theta * length), lower], axis=1
    )
    n = lax.axis_size("batch")
    sources = (mixer_in, mixer_out, ffn_in, ffn_out)
    paired = n_seq == 4 and n % 4 == 0 and all(w.shape[1] % 96 == 0 for w in sources)
    x = tokens_in.reshape(total, width)
    if paired:
        gathered, kept = run_forward(n, n_seq, rows, tokens, rel, x, sources, gain_rows, gate_rows)
        *kept, between, x_end = kept
        streams = [x] + [between[k] for k in range(LAYERS - 1)]
    else:
        gathered = [
            lax.all_gather(w[k], "batch", axis=0, tiled=True) for k in range(LAYERS) for w in sources
        ]
        streams, lists = [x], []
        for k in range(LAYERS):
            w_in, w_out, w_ffn, w_down = gathered[4 * k : 4 * k + 4]
            proj, p_g, normed, lam, h, cum, ends, tot = enter(rel, x, w_in, gain_rows[k], gate_rows[k])
            carry = carry_f(tot, gate_rows[k, 5:8])
            *after, x = leave(F32 if k + 1 < LAYERS else BF16)(
                x, p_g, h, cum, ends, carry, w_out, w_ffn, w_down, gain_rows[k], gate_rows[k]
            )
            streams.append(x)
            lists.append((proj, p_g, normed, lam, *after))
        kept, x_end = [jnp.stack(parts) for parts in zip(*lists)], x
    proj, p_g, normed, lam, state, prior, mixed, mid, normed2, gu, hid = kept
    block_out = x_end.reshape(rows, length, width)
    dx = cotangent.reshape(total, width)
    pairs, small = [None] * LAYERS, [None] * LAYERS
    for k in reversed(range(LAYERS)):
        w_in, w_out, w_ffn, w_down = gathered[4 * k : 4 * k + 4]
        back_out, back_in = back(k)
        dz, d_gu, d_mid, dy, d_pg, g, cum, ends, tot, dg_a = back_out(
            dx, gu, mid, state, p_g, lam, w_out, w_ffn, w_down, gain_rows[k], gate_rows[k]
        )
        carry = carry_b(tot, gate_rows[k, 5:8])
        d_proj, dx, dg_b, dgate = back_in(
            rel, streams[k], d_mid, proj, d_pg, lam, prior, g, cum, ends, carry, w_in, gain_rows[k], gate_rows[k]
        )
        pairs[k] = ((normed, d_proj), (mixed, dy), (normed2, d_gu), (hid, dz))
        small[k] = jnp.stack(
            [
                jnp.sum(dg_b, axis=0),
                jnp.sum(dg_a[:8], axis=0),
                jnp.sum(dg_a[8:], axis=0),
                jnp.concatenate([jnp.sum(dgate[:8], axis=0), jnp.sum(dgate[8:], axis=0)]),
            ]
        )
    if paired:
        plan = []
        for k, mats in ((LAYERS - 1, (1, 2, 3, 0)),) + tuple(
            (k, (3, 2, 0, 1)) for k in reversed(range(LAYERS - 1))
        ):
            plan += [(m, k, m != 0) for m in mats]
        *outs, totals = grads_and_scatter(
            n, plan, [pairs[k][m][0] for m, k, _ in plan], [pairs[k][m][1] for m, k, _ in plan],
            jnp.concatenate(small),
        )
        totals = totals.reshape(LAYERS, 4, width)
    else:
        outs = []
        for m in range(4):
            parts = [
                lax.psum_scatter(contract_rows(pairs[k][m][0][k], pairs[k][m][1]), "batch", scatter_dimension=0, tiled=True)
                for k in range(LAYERS)
            ]
            outs.append(jnp.stack([lax.psum(part, "seq") for part in parts]))
        totals = lax.psum(jnp.stack(small), ("batch", "seq"))
    outs = [o.astype(F32) for o in outs]
    d_gains = totals[:, :3]
    d_gate_params = totals[:, 3].reshape(LAYERS, 2, chan)
    return (block_out, dx.reshape(rows, length, width), *outs, d_gains, d_gate_params)


def solution(mesh):
    tok = P("batch", "seq", None)
    mat = P(None, "batch", None)
    return jax.shard_map(
        shards,
        mesh=mesh,
        in_specs=(tok, P("batch", None), mat, mat, mat, mat, P(), P(), tok),
        out_specs=(tok, tok, mat, mat, mat, mat, P(), P()),
        check_vma=False,
    )
```

```python
import functools

import jax
import jax.numpy as jnp
from jax import lax
from jax.experimental import pallas as pl
from jax.experimental.pallas import tpu as pltpu
from jax.sharding import PartitionSpec as P

EPS = 1e-06
F32 = jnp.float32
BF16 = jnp.bfloat16
LANES = 128
CHUNK = 768
MESH = pl.DeviceIdType.MESH


def sigmoid(values):
    return 1.0 / (1.0 + jnp.exp(-values))


def rms_scale(values):
    return lax.rsqrt(jnp.mean(values * values, axis=-1, keepdims=True) + EPS)


def dot(left, right):
    return jnp.dot(left, right, preferred_element_type=F32)


def dot_t(left, right):
    return lax.dot_general(left, right, (((1,), (1,)), ((), ())), preferred_element_type=F32)


def eight_sum(values):
    rows, cols = values.shape
    return jnp.sum(values.reshape(rows // 8, 8, cols), axis=0)


def wide(ref, first, last):
    return jnp.concatenate([ref[g] for g in range(first, last)], axis=-1)


def split_store(ref, first, values):
    for g in range(values.shape[1] // LANES):
        ref[first + g] = values[:, g * LANES : (g + 1) * LANES]


def lanes(values):
    return [values[:, g * LANES : (g + 1) * LANES] for g in range(values.shape[1] // LANES)]


LIMIT = 60 * 1024 * 1024


def whole(*shape):
    return pl.BlockSpec(shape, lambda *_: (0,) * len(shape), pipeline_mode=pl.Buffered(1))


def order_matrix(tokens, back):
    shape = (tokens, tokens)
    here = lax.broadcasted_iota(jnp.int32, shape, 1 if back else 0)
    there = lax.broadcasted_iota(jnp.int32, shape, 0 if back else 1)
    return jnp.where(there == (here & 7) * (tokens // 8) + (here >> 3), 1.0, 0.0).astype(BF16)


def reset_mask(rel_ref, row, first, tokens):
    here = lax.broadcasted_iota(jnp.int32, (tokens, LANES), 0)
    pos = (here & 7) * (tokens // 8) + (here >> 3) + first
    hit = pos == rel_ref[row, 0]
    for k in range(1, rel_ref.shape[1]):
        hit = hit | (pos == rel_ref[row, k])
    return hit


def retain(rel_ref, row, first, p_f, lower):
    tokens, chan = p_f.shape
    forget = sigmoid(p_f)
    lam = lower + (1.0 - lower) * forget
    keep = jnp.where(reset_mask(rel_ref, row, first, tokens), 0.0, 1.0)
    return lam * jnp.concatenate([keep] * (chan // LANES), axis=-1), forget, keep


def at_step(s):
    return pl.ds(pl.multiple_of(s * 8, 8), 8)


def enter_tile(rel_ref, row, tile, x, w_ref, gain_ref, gate_ref, proj_ref, pg_ref, normed_ref, h_ref, cum_ref,
               ends_ref, tot_ref, src, lam_ref):
    tokens, width = x.shape
    chan = width // 2
    seg = tokens // 8
    groups = chan // LANES
    normed = (x * rms_scale(x) * gain_ref[0:1, :]).astype(BF16)
    normed_ref[...] = normed
    proj = dot(normed, w_ref[...])
    proj_ref[...] = proj[:, : 3 * chan].astype(BF16)
    pg_ref[...] = proj[:, 3 * chan :].astype(BF16)
    cos, sin, lower = gate_ref[0:1, :], gate_ref[1:2, :], gate_ref[2:3, :]
    seg_cos, seg_sin = gate_ref[3:4, :], gate_ref[4:5, :]
    p_r, p_i, p_f = proj[:, :chan], proj[:, chan : 2 * chan], proj[:, 2 * chan : 3 * chan]
    lam, _, _ = retain(rel_ref, row, tile * tokens, p_f, lower)
    split_store(lam_ref, 0, lam)
    split_store(src, 0, (1.0 - lam) * (p_r * sigmoid(p_r)))
    split_store(src, groups, (1.0 - lam) * (p_i * sigmoid(p_i)))
    cos_l, sin_l = lanes(cos), lanes(sin)

    def step(s, state):
        at = at_step(s)
        after = []
        for k, (h_r, h_i, cum) in enumerate(state):
            lam_s = lam_ref[k, at, :]
            a_r, a_i = lam_s * cos_l[k], lam_s * sin_l[k]
            n_r = a_r * h_r - a_i * h_i + src[k, at, :]
            n_i = a_r * h_i + a_i * h_r + src[groups + k, at, :]
            cum = cum * lam_s
            h_ref[k, at, :] = n_r
            h_ref[groups + k, at, :] = n_i
            cum_ref[k, at, :] = cum
            after.append((n_r, n_i, cum))
        return tuple(after)

    zero = lam_ref[0, 0:8, :] * 0.0
    last = lax.fori_loop(0, seg, step, ((zero, zero, zero + 1.0),) * groups, unroll=8)
    e_r, e_i, e_c = (jnp.concatenate([v[i] for v in last], axis=-1) for i in range(3))
    ends_ref[0:8, :] = e_r
    ends_ref[8:16, :] = e_i
    ends_ref[16:24, :] = e_c

    @pl.when(tile == 0)
    def _():
        tot_ref[0:2, :] = jnp.zeros((2, chan), F32)
        tot_ref[2:3, :] = jnp.ones((1, chan), F32)

    c_r, c_i, c_l = tot_ref[0:1, :], tot_ref[1:2, :], tot_ref[2:3, :]
    for j in range(8):
        m = e_c[j : j + 1, :]
        a_r, a_i = m * seg_cos, m * seg_sin
        c_r, c_i = a_r * c_r - a_i * c_i + e_r[j : j + 1, :], a_r * c_i + a_i * c_r + e_i[j : j + 1, :]
        c_l = c_l * m
    tot_ref[0:1, :] = c_r
    tot_ref[1:2, :] = c_i
    tot_ref[2:3, :] = c_l


def leave_tile(tile, x, pg_ref, h_ref, cum_ref, ends_ref, carry_ref, wo_ref, wf_ref, wd_ref, gain_ref, gate_ref,
               starts_ref, state_ref, mixed_ref, mid_ref, normed_ref, gu_ref, hid_ref, run):
    tokens, width = x.shape
    chan = width // 2
    seg = tokens // 8
    groups = chan // LANES
    cos, sin = gate_ref[0:1, :], gate_ref[1:2, :]
    seg_cos, seg_sin = gate_ref[3:4, :], gate_ref[4:5, :]

    @pl.when(tile == 0)
    def _():
        run[0:2, :] = carry_ref[0:2, :]

    c_r, c_i = run[0:1, :], run[1:2, :]
    l_r, l_i = [], []
    for j in range(8):
        l_r.append(c_r)
        l_i.append(c_i)
        m = ends_ref[16 + j : 17 + j, :]
        a_r, a_i = m * seg_cos, m * seg_sin
        c_r, c_i = (
            a_r * c_r - a_i * c_i + ends_ref[j : j + 1, :],
            a_r * c_i + a_i * c_r + ends_ref[8 + j : 9 + j, :],
        )
    run[0:1, :] = c_r
    run[1:2, :] = c_i
    start_r, start_i = jnp.concatenate(l_r, axis=0), jnp.concatenate(l_i, axis=0)
    starts_ref[...] = jnp.concatenate([start_r, start_i], axis=-1)
    cos_l, sin_l = lanes(cos), lanes(sin)

    def step(s, state):
        at = at_step(s)
        after = []
        for k, (w_r, w_i) in enumerate(state):
            w_r, w_i = w_r * cos_l[k] - w_i * sin_l[k], w_r * sin_l[k] + w_i * cos_l[k]
            cum = cum_ref[k, at, :]
            h_ref[k, at, :] += cum * w_r
            h_ref[groups + k, at, :] += cum * w_i
            after.append((w_r, w_i))
        return tuple(after)

    lax.fori_loop(0, seg, step, tuple(zip(lanes(start_r), lanes(start_i))), unroll=8)
    state = wide(h_ref, 0, 2 * groups)
    state_ref[...] = state.astype(BF16)
    p_g = pg_ref[...].astype(F32)
    mixed = (state * rms_scale(state) * gain_ref[1:2, :] * (p_g * sigmoid(p_g))).astype(BF16)
    mixed_ref[...] = mixed
    mid = x + dot(mixed, wo_ref[...])
    mid_ref[...] = mid.astype(BF16)
    normed = (mid * rms_scale(mid) * gain_ref[2:3, :]).astype(BF16)
    normed_ref[...] = normed
    gu = dot(normed, wf_ref[...])
    gu_ref[...] = gu.astype(BF16)
    hidden = gu.shape[1] // 2
    gate = gu[:, :hidden]
    hid = (gate * sigmoid(gate) * gu[:, hidden:]).astype(BF16)
    hid_ref[...] = hid
    return mid + dot(hid, wd_ref[...])


def back_out_tile(rel_ref, row, tile, last, dx_ref, gu_ref, mid_ref, state_ref, pg_ref, pf_ref, wo_ref, wf_ref,
                  wd_ref, gain_ref, gate_ref, dz_ref, dgu_ref, dy_ref, dpg_ref, lam_ref, g_ref, cum_ref, ends_ref,
                  tot_ref, small_ref, grad):
    tokens, width = dx_ref.shape
    chan = width // 2
    seg = tokens // 8
    groups = chan // LANES
    cos, sin, lower = gate_ref[0:1, :], gate_ref[1:2, :], gate_ref[2:3, :]
    seg_cos, seg_sin = gate_ref[3:4, :], gate_ref[4:5, :]
    dx = dx_ref[...]
    dz = dx.astype(BF16)
    dz_ref[...] = dz
    d_hid = dot_t(dz, wd_ref[...])
    hidden = d_hid.shape[1]
    gate = gu_ref[:, :hidden].astype(F32)
    up = gu_ref[:, hidden:].astype(F32)
    sg = sigmoid(gate)
    silu = gate * sg
    d_gu = jnp.concatenate(
        [(d_hid * up * (sg + silu * (1.0 - sg))).astype(BF16), (d_hid * silu).astype(BF16)], axis=1
    )
    dgu_ref[...] = d_gu
    d_n = dot_t(d_gu, wf_ref[...])
    mid = mid_ref[...].astype(F32)
    scale = rms_scale(mid)
    hat = mid * scale
    d_hat = d_n * gain_ref[2:3, :]
    small_ref[16:24, :] += eight_sum(d_n * hat)
    d_mid = dx + scale * (d_hat - hat * jnp.mean(d_hat * hat, axis=-1, keepdims=True))
    dx_ref[...] = d_mid
    dy = d_mid.astype(BF16)
    dy_ref[...] = dy
    d_mixed = dot_t(dy, wo_ref[...])
    p_g = pg_ref[...].astype(F32)
    sg = sigmoid(p_g)
    silu = p_g * sg
    state = state_ref[...].astype(F32)
    scale = rms_scale(state)
    hat = state * scale
    g1 = gain_ref[1:2, :]
    dpg_ref[...] = (d_mixed * hat * g1 * (sg + silu * (1.0 - sg))).astype(BF16)
    d_n = d_mixed * silu
    small_ref[8:16, :] += eight_sum(d_n * hat)
    d_hat = d_n * g1
    split_store(grad, 0, scale * (d_hat - hat * jnp.mean(d_hat * hat, axis=-1, keepdims=True)))
    lam, _, _ = retain(rel_ref, row, tile * tokens, pf_ref[...].astype(F32), lower)
    split_store(lam_ref, 0, lam)
    cos_l, sin_l = lanes(cos), lanes(sin)

    def step(s, state):
        at = at_step(seg - 1 - s)
        after = []
        for k, (g_r, g_i, cum, lam_n) in enumerate(state):
            a_r, a_i = lam_n * cos_l[k], lam_n * sin_l[k]
            n_r = grad[k, at, :] + a_r * g_r + a_i * g_i
            n_i = grad[groups + k, at, :] + a_r * g_i - a_i * g_r
            cum = cum * lam_n
            g_ref[k, at, :] = n_r
            g_ref[groups + k, at, :] = n_i
            cum_ref[k, at, :] = cum
            after.append((n_r, n_i, cum, lam_ref[k, at, :]))
        return tuple(after)

    zero = lam_ref[0, 0:8, :] * 0.0
    final = lax.fori_loop(0, seg, step, ((zero, zero, zero + 1.0, zero + 1.0),) * groups, unroll=8)
    g_r, g_i, cum, lam_0 = (jnp.concatenate([v[i] for v in final], axis=-1) for i in range(4))
    e_r = lam_0 * (cos * g_r + sin * g_i)
    e_i = lam_0 * (cos * g_i - sin * g_r)
    e_c = lam_0 * cum
    ends_ref[0:8, :] = e_r
    ends_ref[8:16, :] = e_i
    ends_ref[16:24, :] = e_c

    @pl.when(tile == last)
    def _():
        tot_ref[0:2, :] = jnp.zeros((2, chan), F32)
        tot_ref[2:3, :] = jnp.ones((1, chan), F32)

    c_r, c_i, c_l = tot_ref[0:1, :], tot_ref[1:2, :], tot_ref[2:3, :]
    for j in reversed(range(8)):
        m = e_c[j : j + 1, :]
        a_r, a_i = m * seg_cos, m * seg_sin
        c_r, c_i = a_r * c_r + a_i * c_i + e_r[j : j + 1, :], a_r * c_i - a_i * c_r + e_i[j : j + 1, :]
        c_l = c_l * m
    tot_ref[0:1, :] = c_r
    tot_ref[1:2, :] = c_i
    tot_ref[2:3, :] = c_l


def back_in_tile(rel_ref, row, tile, last, dx_ref, x_ref, proj_ref, dpg_ref, lam_ref, starts_ref, state_ref, g_ref,
                 cum_ref, ends_ref, carry_ref, w_ref, gain_ref, gate_ref, dproj_ref, small_ref, run):
    tokens, width = dx_ref.shape
    chan = width // 2
    seg = tokens // 8
    groups = chan // LANES
    cos, sin, lower = gate_ref[0:1, :], gate_ref[1:2, :], gate_ref[2:3, :]
    seg_cos, seg_sin = gate_ref[3:4, :], gate_ref[4:5, :]

    @pl.when(tile == last)
    def _():
        run[0:2, :] = carry_ref[0:2, :]

    c_r, c_i = run[0:1, :], run[1:2, :]
    l_r, l_i = [None] * 8, [None] * 8
    for j in reversed(range(8)):
        l_r[j], l_i[j] = c_r, c_i
        m = ends_ref[16 + j : 17 + j, :]
        a_r, a_i = m * seg_cos, m * seg_sin
        c_r, c_i = (
            a_r * c_r + a_i * c_i + ends_ref[j : j + 1, :],
            a_r * c_i - a_i * c_r + ends_ref[8 + j : 9 + j, :],
        )
    run[0:1, :] = c_r
    run[1:2, :] = c_i
    cos_l, sin_l = lanes(cos), lanes(sin)

    def step(s, state):
        at = at_step(seg - 1 - s)
        after = []
        for k, (w_r, w_i) in enumerate(state):
            cum = cum_ref[k, at, :]
            g_ref[k, at, :] += cum * w_r
            g_ref[groups + k, at, :] += cum * w_i
            after.append((w_r * cos_l[k] + w_i * sin_l[k], w_i * cos_l[k] - w_r * sin_l[k]))
        return tuple(after)

    starts = (jnp.concatenate(l_r, axis=0), jnp.concatenate(l_i, axis=0))
    lax.fori_loop(0, seg, step, tuple(zip(lanes(starts[0]), lanes(starts[1]))), unroll=8)
    g_r, g_i = wide(g_ref, 0, groups), wide(g_ref, groups, 2 * groups)
    prior = jnp.concatenate([starts_ref[...], state_ref[...].astype(F32)[: tokens - 8, :]], axis=0)
    q_r, q_i = prior[:, :chan], prior[:, chan:]
    p_r = proj_ref[:, :chan].astype(F32)
    p_i = proj_ref[:, chan : 2 * chan].astype(F32)
    _, forget, keep = retain(rel_ref, row, tile * tokens, proj_ref[:, 2 * chan :].astype(F32), lower)
    lam = wide(lam_ref, 0, groups)
    d_ar = g_r * q_r + g_i * q_i
    d_ai = g_i * q_r - g_r * q_i
    s_r, s_i = sigmoid(p_r), sigmoid(p_i)
    in_r, in_i = p_r * s_r, p_i * s_i
    d_lam = d_ar * cos + d_ai * sin - (g_r * in_r + g_i * in_i)
    d_f = jnp.concatenate([keep] * groups, axis=-1) * d_lam * (1.0 - forget)
    small_ref[24:32, :] += jnp.concatenate(
        [eight_sum(lam * (d_ai * cos - d_ar * sin)), eight_sum(d_f)], axis=-1
    )
    rest = 1.0 - lam
    d_proj = jnp.concatenate(
        [
            (rest * g_r * (s_r + in_r * (1.0 - s_r))).astype(BF16),
            (rest * g_i * (s_i + in_i * (1.0 - s_i))).astype(BF16),
            (d_f * (1.0 - lower) * forget).astype(BF16),
            dpg_ref[...],
        ],
        axis=1,
    )
    dproj_ref[...] = d_proj
    d_n = dot_t(d_proj, w_ref[...])
    x = x_ref[...].astype(F32)
    scale = rms_scale(x)
    hat = x * scale
    small_ref[0:8, :] += eight_sum(d_n * hat)
    d_hat = d_n * gain_ref[0:1, :]
    dx_ref[...] = dx_ref[...] + scale * (d_hat - hat * jnp.mean(d_hat * hat, axis=-1, keepdims=True))


def combine(count, me, forward, buf, rot_ref, out_ref):
    cos, sin = rot_ref[0:1, :], rot_ref[1:2, :]
    for r in range(buf.shape[1]):
        c_r = jnp.zeros_like(cos)
        c_i = jnp.zeros_like(cos)
        for k in range(count - 1, 0, -1):
            slot = k - 1 if forward else count - k - 1
            valid = me >= k if forward else me + k < count
            e_r, e_i, m = buf[slot, r, 0:1, :], buf[slot, r, 1:2, :], buf[slot, r, 2:3, :]
            a_r = m * cos
            a_i = m * sin if forward else -m * sin
            n_r = a_r * c_r - a_i * c_i + e_r
            n_i = a_r * c_i + a_i * c_r + e_i
            keep = jnp.where(valid, 1.0, 0.0)
            c_r, c_i = n_r * keep, n_i * keep
        out_ref[r, 0:1, :] = c_r
        out_ref[r, 1:2, :] = c_i


def carry_copies(count, me, tot_ref, buf, send_sem, recv_sem):
    return [
        remote(tot_ref, buf.at[k - 1], send_sem.at[k - 1], recv_sem.at[k - 1], {"seq": lax.rem(me + k, count)})
        for k in range(1, count)
    ]


class Ring:
    def __init__(self, n):
        self.n = n
        self.batch, self.seq = lax.axis_index("batch"), lax.axis_index("seq")
        z, x = self.batch // 2, self.batch % 2
        self.pos = z + x * (n - 1 - 2 * z)
        self.core, self.y = self.seq % 2, self.seq // 2
        self.sign = 1 - 2 * self.core
        self.core_peer = self.seq + self.sign
        self.y_peer = self.seq + 2 * (1 - 2 * self.y)

    def at(self, distance):
        p = (self.pos + distance + 2 * self.n) % self.n
        h = p // (self.n // 2)
        return 2 * (p + h * (self.n - 1 - 2 * p)) + h

    def ahead(self, hops):
        return self.at(self.sign * hops)


def remote(src, dst, send, recv, device):
    return pltpu.make_async_remote_copy(
        src_ref=src, dst_ref=dst, send_sem=send, recv_sem=recv, device_id=device, device_id_type=MESH
    )


def meet(devices):
    barrier = pltpu.get_barrier_semaphore()
    for device in devices:
        pl.semaphore_signal(barrier, inc=1, device_id=device, device_id_type=MESH)
    pl.semaphore_wait(barrier, len(devices))


class Gather:
    def __init__(self, ring, jobs, sems):
        self.ring, self.jobs = ring, jobs
        (self.own_sem, self.ring_send, self.ring_recv, self.y_send, self.y_recv, self.core_send,
         self.core_recv) = sems
        n = ring.n
        self.hops = ((1, n // 2, 0), (-1, n - 1 - n // 2, n // 2))

    def rows(self, j, piece):
        src, dst, u = self.jobs[j]
        ring = self.ring
        base = ring.core * (3 * u)
        whole = piece * (6 * u)
        view = lambda first, rows: dst.at[pl.ds(pl.multiple_of(whole + base + first, 16), rows)]
        return view(ring.y * u, 2 * u), view(2 * ring.y * u, u), view(2 * (1 - ring.y) * u, u)

    def own_copy(self, j):
        src, dst, u = self.jobs[j]
        return pltpu.make_async_copy(
            src, dst.at[pl.ds(pl.multiple_of(self.ring.batch * (6 * u), 16), 6 * u)], self.own_sem.at[j]
        )

    def own(self, j):
        src, dst, u = self.jobs[j]
        ring = self.ring
        mine, _, _ = self.rows(j, ring.batch)
        piece = src.at[pl.ds(pl.multiple_of(ring.core * (3 * u) + ring.y * u, 16), 2 * u)]
        for way, hops, first in self.hops:
            remote(piece, mine, self.ring_send.at[j], self.ring_recv.at[j, first],
                   {"batch": ring.ahead(way)}).start()
        self.own_copy(j).start()

    def arrived(self, j, h):
        ring = self.ring
        for way, hops, first in self.hops:
            if h < hops:
                mine, give, _ = self.rows(j, ring.ahead(-way * (h + 1)))
                on = lambda slot: remote(mine, mine, self.ring_send.at[j], self.ring_recv.at[j, first + slot],
                                         {"batch": ring.ahead(way)})
                on(h).wait_recv()
                if h + 1 < hops:
                    on(h + 1).start()
                remote(give, give, self.y_send.at[j], self.y_recv.at[j, first + h], {"seq": ring.y_peer}).start()
                remote(mine, mine, self.core_send.at[j], self.core_recv.at[j], {"seq": ring.core_peer}).start()

    def crossed(self, j, h):
        ring = self.ring
        for way, hops, first in self.hops:
            if h < hops:
                _, _, take = self.rows(j, ring.ahead(-way * (h + 1)))
                remote(take, take, self.y_send.at[j], self.y_recv.at[j, first + h], {"seq": ring.y_peer}).wait_recv()
                remote(take, take, self.core_send.at[j], self.core_recv.at[j], {"seq": ring.core_peer}).start()

    def swapped(self, j):
        src, dst, u = self.jobs[j]
        view = dst.at[0 : (self.ring.n - 1) * 3 * u]
        remote(view, view, self.core_send.at[j], self.core_recv.at[j], {"seq": self.ring.core_peer}).wait_recv()
        self.own_copy(j).wait()

    def sent(self, j):
        src, dst, u = self.jobs[j]
        for rows, send in ((2 * u, self.ring_send), (u, self.y_send), (3 * u, self.core_send)):
            view = dst.at[0 : (self.ring.n - 1) * rows]
            remote(view, view, send.at[j], self.core_recv.at[j], {"seq": self.ring.core_peer}).wait_send()


class Agenda:
    def __init__(self):
        self.calls = {}

    def add(self, when, f, *args):
        self.calls.setdefault(when, []).append((f, args))

    def run(self, now):
        for when, calls in sorted(self.calls.items(), key=lambda item: item[0]):

            @pl.when(now == when)
            def _(calls=calls):
                for f, args in calls:
                    f(*args)


def plan_gather(agenda, net, layers, mats, count, load):
    far = net.ring.n // 2

    def hop(j, h):
        if h < far:
            net.arrived(j, h)
        if h >= 1:
            net.crossed(j, h - 1)

    def complete(j):
        net.swapped(j)
        load(j).start()

    agenda.add(0, net.own, 0)
    agenda.add(0, net.own, 1)
    for h in range(far + 1):
        agenda.add(0, hop, 0, h)
        if h == 0:
            agenda.add(0, net.own, 3)
        if h == 1:
            agenda.add(0, net.own, 2)
    agenda.add(0, complete, 0)
    for h in range(far + 1):
        for j in (1, 3, 2):
            agenda.add(min(1 + h, count), hop, j, h)
    for j in range(mats, layers * mats):
        agenda.add(max(count - 2, 0), net.own, j)
    for j in (1, 3, 2):
        agenda.add(count, complete, j)
    for k in range(1, layers):
        start = (2 * k - 1) * count
        for h in range(far + 1):
            for j in range(k * mats, k * mats + mats):
                agenda.add(start + 1 + min(h, count - 1), hop, j, h)
        agenda.add(start + count, complete, k * mats)
        for j in range(k * mats + 1, k * mats + mats):
            agenda.add(start + count + 1, complete, j)


def forward_kernel(n, n_seq, layers, rows, paired, *refs):
    rel_ref, tok_ref = refs[:2]
    mats = 4
    given, (gain_ref, gate_ref) = refs[2 : 2 + mats], refs[2 + mats : 4 + mats]
    refs = refs[4 + mats :]
    if paired:
        gathered, refs = refs[: layers * mats], refs[layers * mats :]
    (xin_ref, proj_ref, pg_ref, normed_ref, starts_ref, state_ref, mixed_ref, mid_ref, normed2_ref, gu_ref, hid_ref,
     out_ref) = refs[:12]
    (xs, hs, cum, pg, ends, tot, src, lam, run, carry, buf, *rest) = refs[12:]
    weights, (load_sem, carry_send, carry_recv), sems = rest[:mats], rest[mats : mats + 3], rest[mats + 3 :]
    layer, step = pl.program_id(0), pl.program_id(1)
    tokens = tok_ref.shape[0]
    count = xs.shape[0]
    tiles = count // rows
    now = layer * (2 * count) + step
    me = lax.axis_index("seq")
    peers = [{"seq": lax.rem(me + k, n_seq)} for k in range(1, n_seq)]
    agenda = Agenda()

    def load(j):
        source = gathered[j] if paired else given[j % mats].at[j // mats]
        return pltpu.make_async_copy(source, weights[j % mats], load_sem.at[j % mats])

    def ready(j):
        load(j).wait()

    def exchange():
        return carry_copies(n_seq, me, tot, buf.at[layer], carry_send.at[layer], carry_recv.at[layer])

    if paired:
        ring = Ring(n)
        jobs = [
            (given[m].at[k], gathered[k * mats + m], given[m].shape[1] // 6)
            for k in range(layers) for m in range(mats)
        ]
        net = Gather(ring, jobs, sems)
        agenda.add(0, meet, [{"batch": ring.ahead(1)}, {"batch": ring.ahead(-1)}] + peers)
        plan_gather(agenda, net, layers, mats, count, load)
    else:
        agenda.add(0, meet, peers)
        for k in range(layers):
            agenda.add(2 * count * k, lambda k=k: load(k * mats).start())
            for m in range(1, mats):
                agenda.add(2 * count * k + count - 1, lambda j=k * mats + m: load(j).start())
    for k in range(layers):
        agenda.add(2 * count * k, ready, k * mats)
        for m in range(1, mats):
            agenda.add(2 * count * k + count, ready, k * mats + m)
    agenda.run(now)

    tile = lax.rem(step, count)
    row, at_row = tile // tiles, lax.rem(tile, tiles)
    gains, gate = gain_ref.at[layer], gate_ref.at[layer]

    @pl.when((layer == 0) & (step < count))
    def _():
        xs[tile] = dot(order_matrix(tokens, False), tok_ref[...])

    @pl.when(step < count)
    def _():
        x = xs[tile]
        xin_ref[...] = x.astype(BF16)
        enter_tile(rel_ref, row, at_row, x, weights[0], gains, gate, proj_ref, pg.at[tile], normed_ref, hs.at[tile],
                   cum.at[tile], ends.at[tile], tot.at[row], src, lam)
        pg_ref[...] = pg[tile]

    @pl.when(step == count - 1)
    def _():
        for copy in exchange():
            copy.start()

    @pl.when(step == count)
    def _():
        for copy in exchange():
            copy.wait()
        combine(n_seq, me, True, buf.at[layer], gate.at[5:8], carry)

    @pl.when(step >= count)
    def _():
        out = leave_tile(at_row, xs[tile], pg.at[tile], hs.at[tile], cum.at[tile], ends.at[tile], carry.at[row],
                         weights[1], weights[2], weights[3], gains, gate, starts_ref, state_ref, mixed_ref, mid_ref,
                         normed2_ref, gu_ref, hid_ref, run)
        xs[tile] = out

        @pl.when(layer == layers - 1)
        def _():
            out_ref[...] = dot(order_matrix(tokens, True), out.astype(BF16)).astype(BF16)

    if paired:

        @pl.when(now == layers * 2 * count - 1)
        def _():
            for j in range(layers * mats):
                net.sent(j)


def tile_specs(tokens, layer):
    def flat(w, when, col=0):
        return pl.BlockSpec((None, tokens, w), lambda k, s: (layer(k), when(s), col))

    def few(r, w, when):
        return pl.BlockSpec((None, None, r, w), lambda k, s: (layer(k), when(s), 0, 0))

    return flat, few


def run_forward(n, n_seq, paired, rows, tokens, rel, x, sources, gain_rows, gate_rows):
    layers = sources[0].shape[0]
    total, width = x.shape
    chan = width // 2
    hidden = sources[2].shape[2] // 2
    count = total // tokens
    mats = len(sources)
    jobs = layers * mats if paired else 0
    shape = jax.ShapeDtypeStruct
    dma = pltpu.SemaphoreType.DMA
    any_ = pl.BlockSpec(memory_space=pl.ANY)

    def first(step):
        return jnp.minimum(step, count - 1)

    def second(step):
        return jnp.maximum(step - count, 0)

    flat, few = tile_specs(tokens, lambda k: k)

    def kept(w):
        return shape((layers, total, w), BF16)

    full = [((n if paired else 1) * w.shape[1], w.shape[2]) for w in sources]
    last = layers - 1
    outs = pl.pallas_call(
        functools.partial(forward_kernel, n, n_seq, layers, rows, paired),
        grid=(layers, 2 * count),
        in_specs=[
            pl.BlockSpec(memory_space=pltpu.SMEM),
            pl.BlockSpec((tokens, width), lambda k, s: (jnp.where(k == 0, first(s), count - 1), 0)),
        ]
        + [any_] * mats
        + [whole(layers, 8, width), whole(layers, 8, chan)],
        out_specs=[any_] * jobs
        + [
            flat(width, first),
            flat(3 * chan, first),
            flat(width, first),
            flat(width, first),
            few(8, width, second),
            flat(width, second),
            flat(width, second),
            flat(width, second),
            flat(width, second),
            flat(2 * hidden, second),
            flat(hidden, second),
            pl.BlockSpec((tokens, width), lambda k, s: (jnp.where(k == last, second(s), 0), 0)),
        ],
        out_shape=[shape(f, BF16) for _ in range(layers) for f in full][:jobs]
        + [
            kept(width),
            kept(3 * chan),
            kept(width),
            kept(width),
            shape((layers, count, 8, width), F32),
            kept(width),
            kept(width),
            kept(width),
            kept(width),
            kept(2 * hidden),
            kept(hidden),
            shape((total, width), BF16),
        ],
        scratch_shapes=[
            pltpu.VMEM((count, tokens, width), F32),
            pltpu.VMEM((count, width // LANES, tokens, LANES), F32),
            pltpu.VMEM((count, chan // LANES, tokens, LANES), F32),
            pltpu.VMEM((count, tokens, width), BF16),
            pltpu.VMEM((count, 24, chan), F32),
            pltpu.VMEM((rows, 8, chan), F32),
            pltpu.VMEM((width // LANES, tokens, LANES), F32),
            pltpu.VMEM((chan // LANES, tokens, LANES), F32),
            pltpu.VMEM((8, chan), F32),
            pltpu.VMEM((rows, 8, chan), F32),
            pltpu.VMEM((layers, n_seq - 1, rows, 8, chan), F32),
        ]
        + [pltpu.VMEM(f, BF16) for f in full]
        + [dma((mats,)), dma((layers, n_seq - 1)), dma((layers, n_seq - 1))]
        + [dma((s,)) if one else dma((s, n - 1)) for s in [max(jobs, 1)] for one in (1, 1, 0, 1, 0, 1, 1)],
        compiler_params=pltpu.CompilerParams(collective_id=3, has_side_effects=True, vmem_limit_bytes=LIMIT),
    )(rel, x, *sources, gain_rows, gate_rows)
    return outs[:jobs], outs[jobs:]


def backward_kernel(n_seq, layers, rows, mats, *refs):
    rel_ref, cot_ref = refs[:2]
    given, refs = refs[2 : 2 + layers * mats], refs[2 + layers * mats :]
    (gain_ref, gate_ref, gu_ref, mid_ref, state_ref, pg_ref, pf_ref, x_ref, proj_ref, starts_ref, prior_ref, dz_ref,
     dgu_ref, dy_ref, dproj_ref, dtok_ref, small_ref) = refs[:17]
    (dxs, gs, cum, lam, dpg, ends, tot, grad, run, carry, buf, *rest) = refs[17:]
    weights, (load_sem, carry_send, carry_recv) = rest[:mats], rest[mats:]
    turn, step = pl.program_id(0), pl.program_id(1)
    layer = layers - 1 - turn
    tokens = cot_ref.shape[0]
    count = dxs.shape[0]
    tiles = count // rows
    now = turn * (2 * count) + step
    me = lax.axis_index("seq")
    agenda = Agenda()

    def load(t, m):
        return pltpu.make_async_copy(given[(layers - 1 - t) * mats + m], weights[m], load_sem.at[m])

    def start(t, m):
        load(t, m).start()

    def ready(t, m):
        load(t, m).wait()

    def exchange():
        return carry_copies(n_seq, me, tot, buf.at[turn], carry_send.at[turn], carry_recv.at[turn])

    for m in (3, 2, 1):
        agenda.add(0, start, 0, m)
    agenda.add(0, meet, [{"seq": lax.rem(me + k, n_seq)} for k in range(1, n_seq)])
    for t in range(layers):
        begin = 2 * count * t
        agenda.add(begin, start, t, 0)
        for m in (3, 2, 1):
            agenda.add(begin, ready, t, m)
        agenda.add(begin + count, ready, t, 0)
        if t + 1 < layers:
            for m in (3, 2, 1):
                agenda.add(begin + count, start, t + 1, m)
    agenda.run(now)

    tile = count - 1 - lax.rem(step, count)
    row, at_row = tile // tiles, lax.rem(tile, tiles)
    gains, gate = gain_ref.at[layer], gate_ref.at[layer]

    @pl.when(step == 0)
    def _():
        small_ref[...] = jnp.zeros_like(small_ref)

    @pl.when((turn == 0) & (step < count))
    def _():
        dxs[tile] = dot(order_matrix(tokens, False), cot_ref[...])

    @pl.when(step < count)
    def _():
        back_out_tile(rel_ref, row, at_row, tiles - 1, dxs.at[tile], gu_ref, mid_ref, state_ref, pg_ref, pf_ref,
                      weights[1], weights[2], weights[3], gains, gate, dz_ref, dgu_ref, dy_ref, dpg.at[tile],
                      lam.at[tile], gs.at[tile], cum.at[tile], ends.at[tile], tot.at[row], small_ref, grad)

    @pl.when(step == count - 1)
    def _():
        for copy in exchange():
            copy.start()

    @pl.when(step == count)
    def _():
        for copy in exchange():
            copy.wait()
        combine(n_seq, me, False, buf.at[turn], gate.at[5:8], carry)

    @pl.when(step >= count)
    def _():
        back_in_tile(rel_ref, row, at_row, tiles - 1, dxs.at[tile], x_ref, proj_ref, dpg.at[tile], lam.at[tile],
                     starts_ref, prior_ref, gs.at[tile], cum.at[tile], ends.at[tile], carry.at[row], weights[0],
                     gains, gate, dproj_ref, small_ref, run)

        @pl.when(turn == layers - 1)
        def _():
            dx = dxs[tile]
            high = dx.astype(BF16)
            low = (dx - high.astype(F32)).astype(BF16)
            order = order_matrix(tokens, True)
            dtok_ref[...] = dot(order, high) + dot(order, low)


def run_backward(n_seq, rows, tokens, rel, cotangent, weights, gain_rows, gate_rows, kept):
    x, proj, p_g, starts, state, mid, gu = kept
    layers, total, width = x.shape
    chan = width // 2
    hidden = gu.shape[2] // 2
    count = total // tokens
    mats = len(weights) // layers
    shape = jax.ShapeDtypeStruct
    dma = pltpu.SemaphoreType.DMA
    any_ = pl.BlockSpec(memory_space=pl.ANY)
    last = layers - 1

    def first(step):
        return count - 1 - jnp.minimum(step, count - 1)

    def second(step):
        return count - 1 - jnp.maximum(step - count, 0)

    flat, few = tile_specs(tokens, lambda k: last - k)
    return pl.pallas_call(
        functools.partial(backward_kernel, n_seq, layers, rows, mats),
        grid=(layers, 2 * count),
        in_specs=[
            pl.BlockSpec(memory_space=pltpu.SMEM),
            pl.BlockSpec((tokens, width), lambda k, s: (jnp.where(k == 0, first(s), 0), 0)),
        ]
        + [any_] * len(weights)
        + [
            whole(layers, 8, width),
            whole(layers, 8, chan),
            flat(2 * hidden, first),
            flat(width, first),
            flat(width, first),
            flat(width, first),
            flat(chan, first, 2),
            flat(width, second),
            flat(3 * chan, second),
            few(8, width, second),
            flat(width, second),
        ],
        out_specs=[
            flat(width, first),
            flat(2 * hidden, first),
            flat(width, first),
            flat(3 * chan + width, second),
            pl.BlockSpec((tokens, width), lambda k, s: (jnp.where(k == last, second(s), count - 1), 0)),
            pl.BlockSpec((None, 32, width), lambda k, s: (last - k, 0, 0)),
        ],
        out_shape=[
            shape((layers, total, width), BF16),
            shape((layers, total, 2 * hidden), BF16),
            shape((layers, total, width), BF16),
            shape((layers, total, 3 * chan + width), BF16),
            shape((total, width), F32),
            shape((layers, 32, width), F32),
        ],
        scratch_shapes=[
            pltpu.VMEM((count, tokens, width), F32),
            pltpu.VMEM((count, width // LANES, tokens, LANES), F32),
            pltpu.VMEM((count, chan // LANES, tokens, LANES), F32),
            pltpu.VMEM((count, chan // LANES, tokens, LANES), F32),
            pltpu.VMEM((count, tokens, width), BF16),
            pltpu.VMEM((count, 24, chan), F32),
            pltpu.VMEM((rows, 8, chan), F32),
            pltpu.VMEM((width // LANES, tokens, LANES), F32),
            pltpu.VMEM((8, chan), F32),
            pltpu.VMEM((rows, 8, chan), F32),
            pltpu.VMEM((layers, n_seq - 1, rows, 8, chan), F32),
        ]
        + [pltpu.VMEM(w.shape, BF16) for w in weights[:mats]]
        + [dma((mats,)), dma((layers, n_seq - 1)), dma((layers, n_seq - 1))],
        compiler_params=pltpu.CompilerParams(collective_id=2, has_side_effects=True, vmem_limit_bytes=LIMIT),
    )(rel, cotangent, *weights, gain_rows, gate_rows, gu, mid, state, p_g, proj, x, proj, starts, state)


def add_rows(dst, dst_row, parts, rows):
    def block(i, _):
        step = pl.multiple_of(i * 16, 16)
        total = None
        for ref, first in parts:
            value = ref[pl.ds(pl.multiple_of(first + step, 16), 16), :].astype(F32)
            total = value if total is None else total + value
        dst[pl.ds(pl.multiple_of(dst_row + step, 16), 16), :] = total.astype(dst.dtype)
        return 0

    lax.fori_loop(0, rows // 16, block, 0)


def grads_kernel(n, plan, *refs):
    jobs = len(plan)
    lefts, rights, small = refs[:jobs], refs[jobs : 2 * jobs], refs[2 * jobs]
    outs_count = 1 + max(p[0] for p in plan)
    outs, small_out = refs[2 * jobs + 1 : 2 * jobs + 1 + outs_count], refs[2 * jobs + 1 + outs_count]
    rest = refs[2 * jobs + 2 + outs_count :]
    grads, core_buf, y_buf, ring_buf, fin_buf = (rest[i * jobs : (i + 1) * jobs] for i in range(5))
    (left_big, left_small, right_buf, small_buf, left_sem, right_sem, core_send, core_recv, y_send, y_recv,
     ring_send, ring_recv, end_send, end_recv, small_send, small_recv) = rest[5 * jobs :]
    ring = Ring(n)
    far, near = n // 2, n - 1 - n // 2
    core_dev, y_dev = {"seq": ring.core_peer}, {"seq": ring.y_peer}
    y, core = ring.y, ring.core
    rounds = [core_dev, y_dev]
    d = 1
    while d < n:
        rounds.append({"batch": ring.batch + d * (1 - 2 * ((ring.batch // d) % 2))})
        d *= 2
    us = [g.shape[0] // n // 6 for g in grads]
    split = [p[2] for p in plan]
    own_rows = [(2 if s else 3) * u for s, u in zip(split, us)]

    def left_copy(j):
        buf = (left_big, left_small)[j % 2]
        return pltpu.make_async_copy(lefts[j].at[plan[j][1]], buf.at[:, 0 : plan[j][3]], left_sem.at[j % 2])

    chunks = []
    for j, (_, _, _, rows, cols) in enumerate(plan):
        first = 0
        while first < cols:
            size = min(CHUNK, cols - first)
            chunks.append((j, first, size, first + size == cols))
            first += size

    def right_copy(i):
        j, first, size, _ = chunks[i]
        return pltpu.make_async_copy(
            rights[j].at[plan[j][1], :, first : first + size], right_buf.at[i % 2, :, 0:size], right_sem.at[i % 2]
        )

    left_copy(0).start()
    right_copy(0).start()
    right_copy(1).start()
    left_copy(1).start()
    meet([{"batch": ring.ahead(1)}, {"batch": ring.ahead(-1)}] + rounds)

    order = []
    for h in range(far):
        order.append((1, h, far - h))
        if h < near:
            order.append((-1, h, near - h))
    order.append((0, 0, 0))
    last = len(order)

    def rows_at(ref, first, rows):
        return ref.at[pl.ds(pl.multiple_of(first, 16), rows)]

    def core_copy(j, slot, piece):
        u = us[j]
        return remote(rows_at(grads[j], piece * (6 * u) + (1 - core) * (3 * u), 3 * u),
                      core_buf[j].at[slot], core_send.at[j], core_recv.at[j, slot], core_dev)

    def y_copy(j, slot, piece):
        u = us[j]
        src = rows_at(grads[j], piece * (6 * u) + core * (3 * u) + 2 * (1 - y) * u, u)
        return remote(src, y_buf[j].at[slot], y_send.at[j], y_recv.at[j, slot], y_dev)

    def mine(j, piece):
        u = us[j]
        return piece * (6 * u) + core * (3 * u) + (y * u if split[j] else 0)

    def ring_copy(j, slot, way, piece):
        return remote(rows_at(grads[j], mine(j, piece), own_rows[j]), ring_buf[j].at[slot], ring_send.at[j],
                      ring_recv.at[j, slot], {"batch": ring.ahead(way)})

    def small_round(r):
        return remote(small_buf.at[2 * r], small_buf.at[2 * r + 1], small_send.at[r], small_recv.at[r], rounds[r])

    small_buf[0] = small[...]
    small_round(0).start()

    def small_step(r):
        small_round(r).wait_recv()
        total = small_buf[2 * r] + small_buf[2 * r + 1]
        if r + 1 < len(rounds):
            small_buf[2 * r + 2] = total
            small_round(r + 1).start()
        else:
            small_out[...] = total

    def begin(j):
        for slot, (way, h, dist) in enumerate(order):
            core_copy(j, slot, ring.ahead(-way * dist)).start()

    def cross(j, slot):
        way, h, dist = order[slot]
        piece = ring.ahead(way * dist)
        u = us[j]
        core_copy(j, slot, piece).wait_recv()
        if not split[j]:
            return
        give = 2 * (1 - y) * u
        at = piece * (6 * u) + core * (3 * u) + give
        add_rows(grads[j], at, [(grads[j], at), (core_buf[j].at[slot], give)], u)
        y_copy(j, slot, piece).start()

    def hop(j, slot):
        way, h, dist = order[slot]
        piece = ring.ahead(way * dist)
        u = us[j]
        if split[j]:
            y_copy(j, slot, piece).wait_recv()
        if way == 0:
            prior = [i for i, o in enumerate(order) if o[2] == 1]
        elif h:
            prior = [i for i, o in enumerate(order) if o[0] == way and o[1] == h - 1]
        else:
            prior = []
        for i in prior:
            ring_copy(j, i, order[i][0], piece).wait_recv()
        at = mine(j, piece)
        base = [(grads[j], at), (core_buf[j].at[slot], y * u if split[j] else 0)]
        base += [(ring_buf[j].at[i], 0) for i in prior]
        if split[j]:
            for by, more in ((y * u, [(y_buf[j].at[slot], 0)]), ((1 - y) * u, [])):
                add_rows(grads[j], at + by, [(r, f + by) for r, f in base] + more, u)
        else:
            add_rows(grads[j], at, base, 3 * u)
        if way:
            ring_copy(j, slot, way, piece).start()

    def fin_copy(j):
        return remote(rows_at(grads[j], mine(j, ring.batch), own_rows[j]), fin_buf[j], end_send.at[j, 0],
                      end_recv.at[j, 0], y_dev)

    def half_copy(j):
        half = outs[plan[j][0]].at[plan[j][1], pl.ds(pl.multiple_of(core * (3 * us[j]), 16), 3 * us[j])]
        return remote(half, half, end_send.at[j, 1], end_recv.at[j, 1], core_dev)

    def finish(j):
        u = us[j]
        fin_copy(j).wait_recv()
        out = outs[plan[j][0]].at[plan[j][1]]
        at, to = mine(j, ring.batch), core * (3 * u)
        if split[j]:
            add_rows(out, to + 2 * y * u, [(grads[j], at + y * u)], u)
            add_rows(out, to + 2 * (1 - y) * u, [(fin_buf[j], (1 - y) * u)], u)
            add_rows(out, to + u, [(grads[j], at + (1 - y) * u), (fin_buf[j], y * u)], u)
        else:
            add_rows(out, to, [(grads[j], at), (fin_buf[j], 0)], 3 * u)
        half_copy(j).start()

    steps = far + 4

    def advance(j, t):
        now = [i for i, o in enumerate(order) if o[0] and o[1] == t]
        before = [i for i, o in enumerate(order) if o[0] and o[1] == t - 1]
        for slot in before:
            hop(j, slot)
        for slot in now:
            cross(j, slot)
        if t == far - 1:
            cross(j, last - 1)
        if t == far + 1:
            hop(j, last - 1)
            fin_copy(j).start()
        if t == far + 2:
            finish(j)
        if t == far + 3:
            half_copy(j).wait_recv()

    stage = {}

    def advance_all(turn):
        for j in list(stage):
            if j % 2 == turn:
                advance(j, stage[j])
                stage[j] += 1
                if stage[j] == steps:
                    del stage[j]

    small_at = 0
    for i, (j, first, size, done) in enumerate(chunks):
        if first == 0:
            left_copy(j).wait()
        right_copy(i).wait()
        left = (left_big, left_small)[j % 2]

        def multiply(b, _, i=i, j=j, first=first, size=size, left=left):
            at = pl.multiple_of(b * 256, 256)
            part = lax.dot_general(
                left[:, pl.ds(at, 256)], right_buf[i % 2, :, 0:size], (((0,), (0,)), ((), ())),
                preferred_element_type=F32,
            )
            grads[j][pl.ds(at, 256), first : first + size] = part.astype(BF16)
            return 0

        lax.fori_loop(0, plan[j][3] // 256, multiply, 0)
        if i + 2 < len(chunks):
            right_copy(i + 2).start()
        if done and j + 2 < jobs:
            left_copy(j + 2).start()
        advance_all(i % 2)
        if done:
            begin(j)
            stage[j] = 0
        if small_at < len(rounds):
            small_step(small_at)
            small_at += 1
    i = 0
    while stage:
        advance_all(i % 2)
        i += 1
    while small_at < len(rounds):
        small_step(small_at)
        small_at += 1
    for j in range(jobs):
        u = us[j]
        fin_copy(j).wait_send()
        half_copy(j).wait_send()
        remote(core_buf[j], core_buf[j], core_send.at[j], core_recv.at[j, 0], core_dev).wait_send()
        if split[j]:
            remote(y_buf[j], y_buf[j], y_send.at[j], y_recv.at[j, 0], y_dev).wait_send()
        remote(ring_buf[j], ring_buf[j], ring_send.at[j], ring_recv.at[j, 0], core_dev).wait_send()
    for r in range(len(rounds)):
        small_round(r).wait_send()


def grads_and_scatter(n, plan, lefts, rights, small):
    jobs = len(plan)
    plan = [p + (a.shape[2], b.shape[2]) for p, a, b in zip(plan, lefts, rights)]
    tokens = lefts[0].shape[1]
    layers = 1 + max(p[1] for p in plan)
    dma = pltpu.SemaphoreType.DMA
    rounds = 2 + (n - 1).bit_length()
    sizes = [(p[3] // n // 6, p[4], p[2]) for p in plan]
    outs = {p[0]: jax.ShapeDtypeStruct((layers, p[3] // n, p[4]), BF16) for p in plan}
    vm = pl.BlockSpec(memory_space=pltpu.VMEM)
    any_ = pl.BlockSpec(memory_space=pl.ANY)

    def bufs(f):
        return [pltpu.VMEM(f(u, w, s), BF16) for u, w, s in sizes]

    return pl.pallas_call(
        functools.partial(grads_kernel, n, plan),
        out_shape=[outs[m] for m in sorted(outs)] + [jax.ShapeDtypeStruct(small.shape, F32)],
        in_specs=[any_] * (2 * jobs) + [vm],
        out_specs=[vm] * (len(outs) + 1),
        scratch_shapes=bufs(lambda u, w, s: (6 * u * n, w))
        + bufs(lambda u, w, s: (n, 3 * u, w))
        + bufs(lambda u, w, s: (n if s else 1, u, w))
        + bufs(lambda u, w, s: (n - 1, 2 * u if s else 3 * u, w))
        + bufs(lambda u, w, s: (2 * u if s else 3 * u, w))
        + [
            pltpu.VMEM((tokens, max(p[3] for p in plan[0::2])), BF16),
            pltpu.VMEM((tokens, max(p[3] for p in plan[1::2])), BF16),
            pltpu.VMEM((2, tokens, CHUNK), BF16),
            pltpu.VMEM((2 * rounds,) + small.shape, F32),
            dma((2,)), dma((2,)), dma((jobs,)), dma((jobs, n)), dma((jobs,)), dma((jobs, n)), dma((jobs,)),
            dma((jobs, n)), dma((jobs, 2)), dma((jobs, 2)), dma((rounds,)), dma((rounds,)),
        ],
        compiler_params=pltpu.CompilerParams(
            collective_id=4, has_side_effects=True, vmem_limit_bytes=63 * 1024 * 1024
        ),
    )(*lefts, *rights, small)


def contract_rows(left, right):
    return lax.dot_general(
        left, right, (((0,), (0,)), ((), ())), preferred_element_type=F32
    ).astype(BF16)


def shards(
    tokens_in, doc_starts, mixer_in, mixer_out, ffn_in, ffn_out, gains, gate_params, cotangent
):
    rows, length, width = tokens_in.shape
    layers = gains.shape[0]
    chan = width // 2
    total = rows * length
    tokens = min(length, 256)
    seg = tokens // 8
    n, n_seq = lax.axis_size("batch"), lax.axis_size("seq")
    sources = (mixer_in, mixer_out, ffn_in, ffn_out)
    paired = n_seq == 4 and n % 4 == 0 and all(w.shape[1] % 96 == 0 for w in sources)
    rel = doc_starts - lax.axis_index("seq") * length
    gain_rows = jnp.pad(gains, ((0, 0), (0, 5), (0, 0)))
    theta, lower = gate_params[:, 0], gate_params[:, 1]
    turns = jnp.stack([theta, theta * seg, theta * length], axis=1)
    cos, sin = jnp.cos(turns), jnp.sin(turns)
    gate_rows = jnp.stack(
        [cos[:, 0], sin[:, 0], lower, cos[:, 1], sin[:, 1], cos[:, 2], sin[:, 2], lower], axis=1
    )
    x = tokens_in.reshape(total, width)
    if paired:
        weights, kept = run_forward(n, n_seq, True, rows, tokens, rel, x, sources, gain_rows, gate_rows)
    else:
        stacked = [lax.all_gather(w, "batch", axis=1, tiled=True) for w in sources]
        weights = [w[k] for k in range(layers) for w in stacked]
        _, kept = run_forward(n, n_seq, False, rows, tokens, rel, x, stacked, gain_rows, gate_rows)
    x_in, proj, p_g, normed, starts, state, mixed, mid, normed2, gu, hid, block_out = kept
    dz, d_gu, dy, d_proj, d_tokens, small = run_backward(
        n_seq, rows, tokens, rel, cotangent.reshape(total, width), weights, gain_rows, gate_rows,
        (x_in, proj, p_g, starts, state, mid, gu),
    )
    small = jnp.sum(small.reshape(layers, 4, 8, width), axis=2).reshape(layers * 4, width)
    pairs = ((normed, d_proj), (mixed, dy), (normed2, d_gu), (hid, dz))
    if paired:
        plan = []
        for k in reversed(range(layers)):
            plan += [(m, k, m != 0) for m in ((1, 2, 3, 0) if k == layers - 1 else (3, 2, 0, 1))]
        *outs, totals = grads_and_scatter(
            n, plan, [pairs[m][0] for m, _, _ in plan], [pairs[m][1] for m, _, _ in plan], small
        )
    else:
        outs = []
        for left, right in pairs:
            whole_grads = jnp.stack([contract_rows(left[k], right[k]) for k in range(layers)])
            part = lax.psum_scatter(whole_grads, "batch", scatter_dimension=1, tiled=True)
            outs.append(lax.psum(part, "seq"))
        totals = lax.psum(small, ("batch", "seq"))
    totals = totals.reshape(layers, 4, width)
    return (
        block_out.reshape(rows, length, width),
        d_tokens.reshape(rows, length, width),
        *[o.astype(F32) for o in outs],
        totals[:, :3],
        totals[:, 3].reshape(layers, 2, chan),
    )


def solution(mesh):
    tok = P("batch", "seq", None)
    mat = P(None, "batch", None)
    return jax.shard_map(
        shards,
        mesh=mesh,
        in_specs=(tok, P("batch", None), mat, mat, mat, mat, P(), P(), tok),
        out_specs=(tok, tok, mat, mat, mat, mat, P(), P()),
        check_vma=False,
    )
```

```python
import functools

import jax
import jax.numpy as jnp
from jax import lax
from jax.experimental import pallas as pl
from jax.experimental.pallas import tpu as pltpu
from jax.sharding import PartitionSpec as P

EPS = 1e-06
F32 = jnp.float32
BF16 = jnp.bfloat16
LANES = 128
CHUNK = 768
MESH = pl.DeviceIdType.MESH


def sigmoid(values):
    return 1.0 / (1.0 + jnp.exp(-values))


def rms_scale(values):
    return lax.rsqrt(jnp.mean(values * values, axis=-1, keepdims=True) + EPS)


def dot(left, right):
    return jnp.dot(left, right, preferred_element_type=F32)


def dot_t(left, right):
    return lax.dot_general(left, right, (((1,), (1,)), ((), ())), preferred_element_type=F32)


def eight_sum(values):
    rows, cols = values.shape
    return jnp.sum(values.reshape(rows // 8, 8, cols), axis=0)


def wide(ref, first, last):
    return jnp.concatenate([ref[g] for g in range(first, last)], axis=-1)


def split_store(ref, first, values):
    for g in range(values.shape[1] // LANES):
        ref[first + g] = values[:, g * LANES : (g + 1) * LANES]


def lanes(values):
    return [values[:, g * LANES : (g + 1) * LANES] for g in range(values.shape[1] // LANES)]


LIMIT = 60 * 1024 * 1024


def whole(*shape):
    return pl.BlockSpec(shape, lambda *_: (0,) * len(shape), pipeline_mode=pl.Buffered(1))


def order_matrix(tokens, back):
    shape = (tokens, tokens)
    here = lax.broadcasted_iota(jnp.int32, shape, 1 if back else 0)
    there = lax.broadcasted_iota(jnp.int32, shape, 0 if back else 1)
    return jnp.where(there == (here & 7) * (tokens // 8) + (here >> 3), 1.0, 0.0).astype(BF16)


def reset_mask(rel_ref, row, first, tokens):
    here = lax.broadcasted_iota(jnp.int32, (tokens, LANES), 0)
    pos = (here & 7) * (tokens // 8) + (here >> 3) + first
    hit = pos == rel_ref[row, 0]
    for k in range(1, rel_ref.shape[1]):
        hit = hit | (pos == rel_ref[row, k])
    return hit


def retain(rel_ref, row, first, p_f, lower):
    tokens, chan = p_f.shape
    forget = sigmoid(p_f)
    lam = lower + (1.0 - lower) * forget
    keep = jnp.where(reset_mask(rel_ref, row, first, tokens), 0.0, 1.0)
    return lam * jnp.concatenate([keep] * (chan // LANES), axis=-1), forget, keep


def pieces(total):
    size = 512 if total % 512 == 0 else total
    return [slice(first, first + size) for first in range(0, total, size)]


def moved(part, by):
    return slice(part.start + by, part.stop + by)


def at_step(s):
    return pl.ds(pl.multiple_of(s * 8, 8), 8)


def enter_tile(rel_ref, row, tile, x, w_ref, gain_ref, gate_ref, proj_ref, pg_ref, normed_ref, h_ref, cum_ref,
               ends_ref, tot_ref, src, lam_ref):
    tokens, width = x.shape
    chan = width // 2
    seg = tokens // 8
    groups = chan // LANES
    normed = (x * rms_scale(x) * gain_ref[0:1, :]).astype(BF16)
    normed_ref[...] = normed
    p_f = dot(normed, w_ref[:, 2 * chan : 3 * chan])
    p_c = dot(normed, w_ref[:, : 2 * chan])
    proj_ref[:, 2 * chan :] = p_f.astype(BF16)
    cos, sin, lower = gate_ref[0:1, :], gate_ref[1:2, :], gate_ref[2:3, :]
    seg_cos, seg_sin = gate_ref[3:4, :], gate_ref[4:5, :]
    lam, _, _ = retain(rel_ref, row, tile * tokens, p_f, lower)
    split_store(lam_ref, 0, lam)
    pg_ref[...] = dot(normed, w_ref[:, 3 * chan :]).astype(BF16)
    proj_ref[:, : 2 * chan] = p_c.astype(BF16)
    p_r, p_i = p_c[:, :chan], p_c[:, chan:]
    split_store(src, 0, (1.0 - lam) * (p_r * sigmoid(p_r)))
    split_store(src, groups, (1.0 - lam) * (p_i * sigmoid(p_i)))
    cos_l, sin_l = lanes(cos), lanes(sin)

    def step(s, state):
        at = at_step(s)
        after = []
        for k, (h_r, h_i, cum) in enumerate(state):
            lam_s = lam_ref[k, at, :]
            a_r, a_i = lam_s * cos_l[k], lam_s * sin_l[k]
            n_r = a_r * h_r - a_i * h_i + src[k, at, :]
            n_i = a_r * h_i + a_i * h_r + src[groups + k, at, :]
            cum = cum * lam_s
            h_ref[k, at, :] = n_r
            h_ref[groups + k, at, :] = n_i
            cum_ref[k, at, :] = cum
            after.append((n_r, n_i, cum))
        return tuple(after)

    zero = lam_ref[0, 0:8, :] * 0.0
    last = lax.fori_loop(0, seg, step, ((zero, zero, zero + 1.0),) * groups, unroll=8)
    e_r, e_i, e_c = (jnp.concatenate([v[i] for v in last], axis=-1) for i in range(3))
    ends_ref[0:8, :] = e_r
    ends_ref[8:16, :] = e_i
    ends_ref[16:24, :] = e_c

    @pl.when(tile == 0)
    def _():
        tot_ref[0:2, :] = jnp.zeros((2, chan), F32)
        tot_ref[2:3, :] = jnp.ones((1, chan), F32)

    c_r, c_i, c_l = tot_ref[0:1, :], tot_ref[1:2, :], tot_ref[2:3, :]
    for j in range(8):
        m = e_c[j : j + 1, :]
        a_r, a_i = m * seg_cos, m * seg_sin
        c_r, c_i = a_r * c_r - a_i * c_i + e_r[j : j + 1, :], a_r * c_i + a_i * c_r + e_i[j : j + 1, :]
        c_l = c_l * m
    tot_ref[0:1, :] = c_r
    tot_ref[1:2, :] = c_i
    tot_ref[2:3, :] = c_l


def leave_tile(tile, x, pg_ref, h_ref, cum_ref, ends_ref, carry_ref, wo_ref, wf_ref, wd_ref, gain_ref, gate_ref,
               starts_ref, state_ref, mixed_ref, mid_ref, normed_ref, gu_ref, hid_ref, run):
    tokens, width = x.shape
    chan = width // 2
    seg = tokens // 8
    groups = chan // LANES
    cos, sin = gate_ref[0:1, :], gate_ref[1:2, :]
    seg_cos, seg_sin = gate_ref[3:4, :], gate_ref[4:5, :]

    @pl.when(tile == 0)
    def _():
        run[0:2, :] = carry_ref[0:2, :]

    c_r, c_i = run[0:1, :], run[1:2, :]
    l_r, l_i = [], []
    for j in range(8):
        l_r.append(c_r)
        l_i.append(c_i)
        m = ends_ref[16 + j : 17 + j, :]
        a_r, a_i = m * seg_cos, m * seg_sin
        c_r, c_i = (
            a_r * c_r - a_i * c_i + ends_ref[j : j + 1, :],
            a_r * c_i + a_i * c_r + ends_ref[8 + j : 9 + j, :],
        )
    run[0:1, :] = c_r
    run[1:2, :] = c_i
    start_r, start_i = jnp.concatenate(l_r, axis=0), jnp.concatenate(l_i, axis=0)
    starts_ref[...] = jnp.concatenate([start_r, start_i], axis=-1)
    cos_l, sin_l = lanes(cos), lanes(sin)

    def step(s, state):
        at = at_step(s)
        after = []
        for k, (w_r, w_i) in enumerate(state):
            w_r, w_i = w_r * cos_l[k] - w_i * sin_l[k], w_r * sin_l[k] + w_i * cos_l[k]
            cum = cum_ref[k, at, :]
            h_ref[k, at, :] += cum * w_r
            h_ref[groups + k, at, :] += cum * w_i
            after.append((w_r, w_i))
        return tuple(after)

    lax.fori_loop(0, seg, step, tuple(zip(lanes(start_r), lanes(start_i))), unroll=8)
    state = wide(h_ref, 0, 2 * groups)
    state_ref[...] = state.astype(BF16)
    p_g = pg_ref[...].astype(F32)
    mixed = (state * rms_scale(state) * gain_ref[1:2, :] * (p_g * sigmoid(p_g))).astype(BF16)
    mixed_ref[...] = mixed
    mid = x + dot(mixed, wo_ref[...])
    mid_ref[...] = mid.astype(BF16)
    normed = (mid * rms_scale(mid) * gain_ref[2:3, :]).astype(BF16)
    normed_ref[...] = normed
    hidden = wd_ref.shape[0]
    parts = pieces(hidden)

    def gate_up(part):
        return dot(normed, wf_ref[:, part]), dot(normed, wf_ref[:, moved(part, hidden)])

    after = gate_up(parts[0])
    for i, part in enumerate(parts):
        gate, up = after
        if i + 1 < len(parts):
            after = gate_up(parts[i + 1])
        gu_ref[:, part] = gate.astype(BF16)
        gu_ref[:, moved(part, hidden)] = up.astype(BF16)
        hid_ref[:, part] = (gate * sigmoid(gate) * up).astype(BF16)
    return mid + dot(hid_ref[...], wd_ref[...])


def back_out_tile(rel_ref, row, tile, last, dx_ref, gu_ref, mid_ref, state_ref, pg_ref, pf_ref, wo_ref, wf_ref,
                  wd_ref, gain_ref, gate_ref, dz_ref, dgu_ref, dy_ref, dpg_ref, lam_ref, g_ref, cum_ref, ends_ref,
                  tot_ref, small_ref, grad):
    tokens, width = dx_ref.shape
    chan = width // 2
    seg = tokens // 8
    groups = chan // LANES
    cos, sin, lower = gate_ref[0:1, :], gate_ref[1:2, :], gate_ref[2:3, :]
    seg_cos, seg_sin = gate_ref[3:4, :], gate_ref[4:5, :]
    dx = dx_ref[...]
    dz = dx.astype(BF16)
    dz_ref[...] = dz
    hidden = wd_ref.shape[0]
    parts = pieces(hidden)
    d_next = dot_t(dz, wd_ref[parts[0], :])
    for i, part in enumerate(parts):
        d_hid = d_next
        if i + 1 < len(parts):
            d_next = dot_t(dz, wd_ref[parts[i + 1], :])
        gate = gu_ref[:, part].astype(F32)
        up = gu_ref[:, moved(part, hidden)].astype(F32)
        sg = sigmoid(gate)
        silu = gate * sg
        dgu_ref[:, part] = (d_hid * up * (sg + silu * (1.0 - sg))).astype(BF16)
        dgu_ref[:, moved(part, hidden)] = (d_hid * silu).astype(BF16)
    d_n = dot_t(dgu_ref[...], wf_ref[...])
    mid = mid_ref[...].astype(F32)
    scale = rms_scale(mid)
    hat = mid * scale
    d_hat = d_n * gain_ref[2:3, :]
    small_ref[16:24, :] += eight_sum(d_n * hat)
    d_mid = dx + scale * (d_hat - hat * jnp.mean(d_hat * hat, axis=-1, keepdims=True))
    dx_ref[...] = d_mid
    dy = d_mid.astype(BF16)
    dy_ref[...] = dy
    d_mixed = dot_t(dy, wo_ref[...])
    p_g = pg_ref[...].astype(F32)
    sg = sigmoid(p_g)
    silu = p_g * sg
    state = state_ref[...].astype(F32)
    scale = rms_scale(state)
    hat = state * scale
    g1 = gain_ref[1:2, :]
    dpg_ref[...] = (d_mixed * hat * g1 * (sg + silu * (1.0 - sg))).astype(BF16)
    d_n = d_mixed * silu
    small_ref[8:16, :] += eight_sum(d_n * hat)
    d_hat = d_n * g1
    split_store(grad, 0, scale * (d_hat - hat * jnp.mean(d_hat * hat, axis=-1, keepdims=True)))
    lam, _, _ = retain(rel_ref, row, tile * tokens, pf_ref[...].astype(F32), lower)
    split_store(lam_ref, 0, lam)
    cos_l, sin_l = lanes(cos), lanes(sin)

    def step(s, state):
        at = at_step(seg - 1 - s)
        after = []
        for k, (g_r, g_i, cum, lam_n) in enumerate(state):
            a_r, a_i = lam_n * cos_l[k], lam_n * sin_l[k]
            n_r = grad[k, at, :] + a_r * g_r + a_i * g_i
            n_i = grad[groups + k, at, :] + a_r * g_i - a_i * g_r
            cum = cum * lam_n
            g_ref[k, at, :] = n_r
            g_ref[groups + k, at, :] = n_i
            cum_ref[k, at, :] = cum
            after.append((n_r, n_i, cum, lam_ref[k, at, :]))
        return tuple(after)

    zero = lam_ref[0, 0:8, :] * 0.0
    final = lax.fori_loop(0, seg, step, ((zero, zero, zero + 1.0, zero + 1.0),) * groups, unroll=8)
    g_r, g_i, cum, lam_0 = (jnp.concatenate([v[i] for v in final], axis=-1) for i in range(4))
    e_r = lam_0 * (cos * g_r + sin * g_i)
    e_i = lam_0 * (cos * g_i - sin * g_r)
    e_c = lam_0 * cum
    ends_ref[0:8, :] = e_r
    ends_ref[8:16, :] = e_i
    ends_ref[16:24, :] = e_c

    @pl.when(tile == last)
    def _():
        tot_ref[0:2, :] = jnp.zeros((2, chan), F32)
        tot_ref[2:3, :] = jnp.ones((1, chan), F32)

    c_r, c_i, c_l = tot_ref[0:1, :], tot_ref[1:2, :], tot_ref[2:3, :]
    for j in reversed(range(8)):
        m = e_c[j : j + 1, :]
        a_r, a_i = m * seg_cos, m * seg_sin
        c_r, c_i = a_r * c_r + a_i * c_i + e_r[j : j + 1, :], a_r * c_i - a_i * c_r + e_i[j : j + 1, :]
        c_l = c_l * m
    tot_ref[0:1, :] = c_r
    tot_ref[1:2, :] = c_i
    tot_ref[2:3, :] = c_l


def back_in_tile(rel_ref, row, tile, last, dx_ref, x_ref, proj_ref, dpg_ref, lam_ref, starts_ref, state_ref, g_ref,
                 cum_ref, ends_ref, carry_ref, w_ref, gain_ref, gate_ref, dproj_ref, small_ref, run):
    tokens, width = dx_ref.shape
    chan = width // 2
    seg = tokens // 8
    groups = chan // LANES
    cos, sin, lower = gate_ref[0:1, :], gate_ref[1:2, :], gate_ref[2:3, :]
    seg_cos, seg_sin = gate_ref[3:4, :], gate_ref[4:5, :]

    @pl.when(tile == last)
    def _():
        run[0:2, :] = carry_ref[0:2, :]

    c_r, c_i = run[0:1, :], run[1:2, :]
    l_r, l_i = [None] * 8, [None] * 8
    for j in reversed(range(8)):
        l_r[j], l_i[j] = c_r, c_i
        m = ends_ref[16 + j : 17 + j, :]
        a_r, a_i = m * seg_cos, m * seg_sin
        c_r, c_i = (
            a_r * c_r + a_i * c_i + ends_ref[j : j + 1, :],
            a_r * c_i - a_i * c_r + ends_ref[8 + j : 9 + j, :],
        )
    run[0:1, :] = c_r
    run[1:2, :] = c_i
    cos_l, sin_l = lanes(cos), lanes(sin)

    def step(s, state):
        at = at_step(seg - 1 - s)
        after = []
        for k, (w_r, w_i) in enumerate(state):
            cum = cum_ref[k, at, :]
            g_ref[k, at, :] += cum * w_r
            g_ref[groups + k, at, :] += cum * w_i
            after.append((w_r * cos_l[k] + w_i * sin_l[k], w_i * cos_l[k] - w_r * sin_l[k]))
        return tuple(after)

    starts = (jnp.concatenate(l_r, axis=0), jnp.concatenate(l_i, axis=0))
    lax.fori_loop(0, seg, step, tuple(zip(lanes(starts[0]), lanes(starts[1]))), unroll=8)
    d_n = dot_t(dpg_ref[...], w_ref[:, 3 * chan :])
    g_r, g_i = wide(g_ref, 0, groups), wide(g_ref, groups, 2 * groups)
    prior = jnp.concatenate([starts_ref[...], state_ref[...].astype(F32)[: tokens - 8, :]], axis=0)
    q_r, q_i = prior[:, :chan], prior[:, chan:]
    p_r = proj_ref[:, :chan].astype(F32)
    p_i = proj_ref[:, chan : 2 * chan].astype(F32)
    _, forget, keep = retain(rel_ref, row, tile * tokens, proj_ref[:, 2 * chan :].astype(F32), lower)
    lam = wide(lam_ref, 0, groups)
    d_ar = g_r * q_r + g_i * q_i
    d_ai = g_i * q_r - g_r * q_i
    s_r, s_i = sigmoid(p_r), sigmoid(p_i)
    in_r, in_i = p_r * s_r, p_i * s_i
    d_lam = d_ar * cos + d_ai * sin - (g_r * in_r + g_i * in_i)
    d_f = jnp.concatenate([keep] * groups, axis=-1) * d_lam * (1.0 - forget)
    small_ref[24:32, :] += jnp.concatenate(
        [eight_sum(lam * (d_ai * cos - d_ar * sin)), eight_sum(d_f)], axis=-1
    )
    rest = 1.0 - lam
    d_proj = jnp.concatenate(
        [
            (rest * g_r * (s_r + in_r * (1.0 - s_r))).astype(BF16),
            (rest * g_i * (s_i + in_i * (1.0 - s_i))).astype(BF16),
            (d_f * (1.0 - lower) * forget).astype(BF16),
        ],
        axis=1,
    )
    dproj_ref[:, : 3 * chan] = d_proj
    dproj_ref[:, 3 * chan :] = dpg_ref[...]
    d_n = d_n + dot_t(d_proj, w_ref[:, : 3 * chan])
    x = x_ref[...].astype(F32)
    scale = rms_scale(x)
    hat = x * scale
    small_ref[0:8, :] += eight_sum(d_n * hat)
    d_hat = d_n * gain_ref[0:1, :]
    dx_ref[...] = dx_ref[...] + scale * (d_hat - hat * jnp.mean(d_hat * hat, axis=-1, keepdims=True))


def combine(count, me, forward, buf, rot_ref, out_ref):
    cos, sin = rot_ref[0:1, :], rot_ref[1:2, :]
    for r in range(buf.shape[1]):
        c_r = jnp.zeros_like(cos)
        c_i = jnp.zeros_like(cos)
        for k in range(count - 1, 0, -1):
            slot = k - 1 if forward else count - k - 1
            valid = me >= k if forward else me + k < count
            e_r, e_i, m = buf[slot, r, 0:1, :], buf[slot, r, 1:2, :], buf[slot, r, 2:3, :]
            a_r = m * cos
            a_i = m * sin if forward else -m * sin
            n_r = a_r * c_r - a_i * c_i + e_r
            n_i = a_r * c_i + a_i * c_r + e_i
            keep = jnp.where(valid, 1.0, 0.0)
            c_r, c_i = n_r * keep, n_i * keep
        out_ref[r, 0:1, :] = c_r
        out_ref[r, 1:2, :] = c_i


def carry_copies(count, me, tot_ref, buf, send_sem, recv_sem):
    return [
        remote(tot_ref, buf.at[k - 1], send_sem.at[k - 1], recv_sem.at[k - 1], {"seq": lax.rem(me + k, count)})
        for k in range(1, count)
    ]


class Ring:
    def __init__(self, n):
        self.n = n
        self.batch, self.seq = lax.axis_index("batch"), lax.axis_index("seq")
        z, x = self.batch // 2, self.batch % 2
        self.pos = z + x * (n - 1 - 2 * z)
        self.core, self.y = self.seq % 2, self.seq // 2
        self.sign = 1 - 2 * self.core
        self.core_peer = self.seq + self.sign
        self.y_peer = self.seq + 2 * (1 - 2 * self.y)

    def at(self, distance):
        p = (self.pos + distance + 2 * self.n) % self.n
        h = p // (self.n // 2)
        return 2 * (p + h * (self.n - 1 - 2 * p)) + h

    def ahead(self, hops):
        return self.at(self.sign * hops)


def remote(src, dst, send, recv, device):
    return pltpu.make_async_remote_copy(
        src_ref=src, dst_ref=dst, send_sem=send, recv_sem=recv, device_id=device, device_id_type=MESH
    )


def meet(devices):
    barrier = pltpu.get_barrier_semaphore()
    for device in devices:
        pl.semaphore_signal(barrier, inc=1, device_id=device, device_id_type=MESH)
    pl.semaphore_wait(barrier, len(devices))


class Gather:
    def __init__(self, ring, jobs, sems):
        self.ring, self.jobs = ring, jobs
        (self.own_sem, self.ring_send, self.ring_recv, self.y_send, self.y_recv, self.core_send,
         self.core_recv) = sems
        n = ring.n
        self.hops = ((1, n // 2, 0), (-1, n - 1 - n // 2, n // 2))

    def rows(self, j, piece):
        src, dst, u = self.jobs[j]
        ring = self.ring
        base = ring.core * (3 * u)
        whole = piece * (6 * u)
        view = lambda first, rows: dst.at[pl.ds(pl.multiple_of(whole + base + first, 16), rows)]
        return view(ring.y * u, 2 * u), view(2 * ring.y * u, u), view(2 * (1 - ring.y) * u, u)

    def own_copy(self, j):
        src, dst, u = self.jobs[j]
        return pltpu.make_async_copy(
            src, dst.at[pl.ds(pl.multiple_of(self.ring.batch * (6 * u), 16), 6 * u)], self.own_sem.at[j]
        )

    def own(self, j):
        src, dst, u = self.jobs[j]
        ring = self.ring
        mine, _, _ = self.rows(j, ring.batch)
        piece = src.at[pl.ds(pl.multiple_of(ring.core * (3 * u) + ring.y * u, 16), 2 * u)]
        for way, hops, first in self.hops:
            remote(piece, mine, self.ring_send.at[j], self.ring_recv.at[j, first],
                   {"batch": ring.ahead(way)}).start()
        self.own_copy(j).start()

    def arrived(self, j, h):
        ring = self.ring
        for way, hops, first in self.hops:
            if h < hops:
                mine, give, _ = self.rows(j, ring.ahead(-way * (h + 1)))
                on = lambda slot: remote(mine, mine, self.ring_send.at[j], self.ring_recv.at[j, first + slot],
                                         {"batch": ring.ahead(way)})
                on(h).wait_recv()
                if h + 1 < hops:
                    on(h + 1).start()
                remote(give, give, self.y_send.at[j], self.y_recv.at[j, first + h], {"seq": ring.y_peer}).start()
                remote(mine, mine, self.core_send.at[j], self.core_recv.at[j], {"seq": ring.core_peer}).start()

    def crossed(self, j, h):
        ring = self.ring
        for way, hops, first in self.hops:
            if h < hops:
                _, _, take = self.rows(j, ring.ahead(-way * (h + 1)))
                remote(take, take, self.y_send.at[j], self.y_recv.at[j, first + h], {"seq": ring.y_peer}).wait_recv()
                remote(take, take, self.core_send.at[j], self.core_recv.at[j], {"seq": ring.core_peer}).start()

    def swapped(self, j):
        src, dst, u = self.jobs[j]
        view = dst.at[0 : (self.ring.n - 1) * 3 * u]
        remote(view, view, self.core_send.at[j], self.core_recv.at[j], {"seq": self.ring.core_peer}).wait_recv()
        self.own_copy(j).wait()

    def sent(self, j):
        src, dst, u = self.jobs[j]
        for rows, send in ((2 * u, self.ring_send), (u, self.y_send), (3 * u, self.core_send)):
            view = dst.at[0 : (self.ring.n - 1) * rows]
            remote(view, view, send.at[j], self.core_recv.at[j], {"seq": self.ring.core_peer}).wait_send()


class Agenda:
    def __init__(self):
        self.calls = {}

    def add(self, when, f, *args):
        self.calls.setdefault(when, []).append((f, args))

    def run(self, now):
        for when, calls in sorted(self.calls.items(), key=lambda item: item[0]):

            @pl.when(now == when)
            def _(calls=calls):
                for f, args in calls:
                    f(*args)


OPENING = (((0, 0, 0), (0, 0, 1), (0, 0, 3), (0, 0, 2), (1, 0, 0), (1, 0, 1), (1, 0, 3), (1, 0, 2), (2, 0, 0), (2, 0, 1),
            (2, 0, 3), (2, 0, 2), (3, 0, 0), (3, 0, 1), (3, 0, 3), (4, 0, 0), (3, 0, 2), (0, 1, 0), (0, 1, 1), (0, 1, 3),
            (5, 0, 0)),)
FIRST = OPENING + (
    ((4, 0, 1), (4, 0, 3), (0, 1, 2)),
    ((4, 0, 2), (1, 1, 0)),
    ((5, 0, 1), (5, 0, 3), (1, 1, 1), (1, 1, 3)),
    ((5, 0, 2), (1, 1, 2)),
)
SECOND = (
    ((2, 1, 0), (2, 1, 1), (2, 1, 3)),
    ((2, 1, 2), (3, 1, 0)),
    ((3, 1, 1), (3, 1, 3), (4, 1, 0)),
)
LATER = (
    ((5, 0, 0), (3, 0, 2)),
    ((4, 0, 1), (4, 0, 3), (0, 1, 0)),
    ((4, 0, 2), (0, 1, 1), (0, 1, 3)),
    ((5, 0, 1), (5, 0, 3), (0, 1, 2)),
    ((5, 0, 2), (1, 1, 0), (1, 1, 1), (1, 1, 3), (1, 1, 2)),
)


def plan_gather(agenda, net, layers, mats, count, load):
    far = net.ring.n // 2

    def hops(j, quarter):
        for h in range(quarter * far // 4, (quarter + 1) * far // 4):
            net.arrived(j, h)
        cross(j, quarter - 1)

    def cross(j, quarter):
        for h in range(max(quarter, 0) * far // 4, (quarter + 1) * far // 4):
            net.crossed(j, h)

    def complete(j):
        cross(j, 3)
        net.swapped(j)
        load(j).start()

    for k in range(layers):
        for q, calls in enumerate((LATER if k else FIRST) + SECOND):
            for what, ahead, m in calls:
                if k + ahead < layers:
                    j = (k + ahead) * mats + m
                    when = 2 * count * k + q * count // 4
                    if what == 0:
                        agenda.add(when, net.own, j)
                    elif what == 5:
                        agenda.add(when, complete, j)
                    else:
                        agenda.add(when, hops, j, what - 1)


def forward_kernel(n, n_seq, layers, rows, paired, *refs):
    rel_ref, tok_ref = refs[:2]
    mats = 4
    given, (gain_ref, gate_ref) = refs[2 : 2 + mats], refs[2 + mats : 4 + mats]
    refs = refs[4 + mats :]
    if paired:
        gathered, refs = refs[: layers * mats], refs[layers * mats :]
    (xin_ref, proj_ref, pg_ref, normed_ref, starts_ref, state_ref, mixed_ref, mid_ref, normed2_ref, gu_ref, hid_ref,
     out_ref) = refs[:12]
    (xs, hs, cum, pg, ends, tot, src, lam, run, carry, buf, *rest) = refs[12:]
    weights, (load_sem, carry_send, carry_recv), sems = rest[:mats], rest[mats : mats + 3], rest[mats + 3 :]
    layer, step = pl.program_id(0), pl.program_id(1)
    tokens = tok_ref.shape[0]
    count = xs.shape[0]
    tiles = count // rows
    now = layer * (2 * count) + step
    me = lax.axis_index("seq")
    peers = [{"seq": lax.rem(me + k, n_seq)} for k in range(1, n_seq)]
    agenda = Agenda()

    def load(j):
        source = gathered[j] if paired else given[j % mats].at[j // mats]
        return pltpu.make_async_copy(source, weights[j % mats], load_sem.at[j % mats])

    def ready(j):
        load(j).wait()

    def exchange():
        return carry_copies(n_seq, me, tot, buf.at[layer], carry_send.at[layer], carry_recv.at[layer])

    if paired:
        ring = Ring(n)
        jobs = [
            (given[m].at[k], gathered[k * mats + m], given[m].shape[1] // 6)
            for k in range(layers) for m in range(mats)
        ]
        net = Gather(ring, jobs, sems)
        agenda.add(0, meet, [{"batch": ring.ahead(1)}, {"batch": ring.ahead(-1)}] + peers)
        plan_gather(agenda, net, layers, mats, count, load)
    else:
        agenda.add(0, meet, peers)
        for k in range(layers):
            agenda.add(2 * count * k, lambda k=k: load(k * mats).start())
            for m in range(1, mats):
                agenda.add(2 * count * k + count - 1, lambda j=k * mats + m: load(j).start())
    for k in range(layers):
        agenda.add(2 * count * k, ready, k * mats)
        for m in range(1, mats):
            agenda.add(2 * count * k + count, ready, k * mats + m)
    agenda.run(now)

    tile = lax.rem(step, count)
    row, at_row = tile // tiles, lax.rem(tile, tiles)
    gains, gate = gain_ref.at[layer], gate_ref.at[layer]

    @pl.when((layer == 0) & (step < count))
    def _():
        xs[tile] = dot(order_matrix(tokens, False), tok_ref[...])

    @pl.when(step < count)
    def _():
        x = xs[tile]
        xin_ref[...] = x.astype(BF16)
        enter_tile(rel_ref, row, at_row, x, weights[0], gains, gate, proj_ref, pg.at[tile], normed_ref, hs.at[tile],
                   cum.at[tile], ends.at[tile], tot.at[row], src, lam)
        pg_ref[...] = pg[tile]

    @pl.when(step == count - 1)
    def _():
        for copy in exchange():
            copy.start()

    @pl.when(step == count)
    def _():
        for copy in exchange():
            copy.wait()
        combine(n_seq, me, True, buf.at[layer], gate.at[5:8], carry)

    @pl.when(step >= count)
    def _():
        out = leave_tile(at_row, xs[tile], pg.at[tile], hs.at[tile], cum.at[tile], ends.at[tile], carry.at[row],
                         weights[1], weights[2], weights[3], gains, gate, starts_ref, state_ref, mixed_ref, mid_ref,
                         normed2_ref, gu_ref, hid_ref, run)
        xs[tile] = out

        @pl.when(layer == layers - 1)
        def _():
            out_ref[...] = dot(order_matrix(tokens, True), out.astype(BF16)).astype(BF16)

    if paired:

        @pl.when(now == layers * 2 * count - 1)
        def _():
            for j in range(layers * mats):
                net.sent(j)


def tile_specs(tokens, layer):
    def flat(w, when, col=0):
        return pl.BlockSpec((None, tokens, w), lambda k, s: (layer(k), when(s), col))

    def few(r, w, when):
        return pl.BlockSpec((None, None, r, w), lambda k, s: (layer(k), when(s), 0, 0))

    return flat, few


def run_forward(n, n_seq, paired, rows, tokens, rel, x, sources, gain_rows, gate_rows):
    layers = sources[0].shape[0]
    total, width = x.shape
    chan = width // 2
    hidden = sources[2].shape[2] // 2
    count = total // tokens
    mats = len(sources)
    jobs = layers * mats if paired else 0
    shape = jax.ShapeDtypeStruct
    dma = pltpu.SemaphoreType.DMA
    any_ = pl.BlockSpec(memory_space=pl.ANY)

    def first(step):
        return jnp.minimum(step, count - 1)

    def second(step):
        return jnp.maximum(step - count, 0)

    flat, few = tile_specs(tokens, lambda k: k)

    def kept(w):
        return shape((layers, total, w), BF16)

    full = [((n if paired else 1) * w.shape[1], w.shape[2]) for w in sources]
    last = layers - 1
    outs = pl.pallas_call(
        functools.partial(forward_kernel, n, n_seq, layers, rows, paired),
        grid=(layers, 2 * count),
        in_specs=[
            pl.BlockSpec(memory_space=pltpu.SMEM),
            pl.BlockSpec((tokens, width), lambda k, s: (jnp.where(k == 0, first(s), count - 1), 0)),
        ]
        + [any_] * mats
        + [whole(layers, 8, width), whole(layers, 8, chan)],
        out_specs=[any_] * jobs
        + [
            flat(width, first),
            flat(3 * chan, first),
            flat(width, first),
            flat(width, first),
            few(8, width, second),
            flat(width, second),
            flat(width, second),
            flat(width, second),
            flat(width, second),
            flat(2 * hidden, second),
            flat(hidden, second),
            pl.BlockSpec((tokens, width), lambda k, s: (jnp.where(k == last, second(s), 0), 0)),
        ],
        out_shape=[shape(f, BF16) for _ in range(layers) for f in full][:jobs]
        + [
            kept(width),
            kept(3 * chan),
            kept(width),
            kept(width),
            shape((layers, count, 8, width), F32),
            kept(width),
            kept(width),
            kept(width),
            kept(width),
            kept(2 * hidden),
            kept(hidden),
            shape((total, width), BF16),
        ],
        scratch_shapes=[
            pltpu.VMEM((count, tokens, width), F32),
            pltpu.VMEM((count, width // LANES, tokens, LANES), F32),
            pltpu.VMEM((count, chan // LANES, tokens, LANES), F32),
            pltpu.VMEM((count, tokens, width), BF16),
            pltpu.VMEM((count, 24, chan), F32),
            pltpu.VMEM((rows, 8, chan), F32),
            pltpu.VMEM((width // LANES, tokens, LANES), F32),
            pltpu.VMEM((chan // LANES, tokens, LANES), F32),
            pltpu.VMEM((8, chan), F32),
            pltpu.VMEM((rows, 8, chan), F32),
            pltpu.VMEM((layers, n_seq - 1, rows, 8, chan), F32),
        ]
        + [pltpu.VMEM(f, BF16) for f in full]
        + [dma((mats,)), dma((layers, n_seq - 1)), dma((layers, n_seq - 1))]
        + [dma((s,)) if one else dma((s, n - 1)) for s in [max(jobs, 1)] for one in (1, 1, 0, 1, 0, 1, 1)],
        compiler_params=pltpu.CompilerParams(collective_id=3, has_side_effects=True, vmem_limit_bytes=LIMIT),
    )(rel, x, *sources, gain_rows, gate_rows)
    return outs[:jobs], outs[jobs:]


def backward_kernel(n_seq, layers, rows, mats, *refs):
    rel_ref, cot_ref = refs[:2]
    given, refs = refs[2 : 2 + layers * mats], refs[2 + layers * mats :]
    (gain_ref, gate_ref, gu_ref, mid_ref, state_ref, pg_ref, pf_ref, x_ref, proj_ref, starts_ref, prior_ref, dz_ref,
     dgu_ref, dy_ref, dproj_ref, dtok_ref, small_ref) = refs[:17]
    (dxs, gs, cum, lam, dpg, ends, tot, grad, run, carry, buf, *rest) = refs[17:]
    weights, (load_sem, carry_send, carry_recv) = rest[:mats], rest[mats:]
    turn, step = pl.program_id(0), pl.program_id(1)
    layer = layers - 1 - turn
    tokens = cot_ref.shape[0]
    count = dxs.shape[0]
    tiles = count // rows
    now = turn * (2 * count) + step
    me = lax.axis_index("seq")
    agenda = Agenda()

    def load(t, m):
        return pltpu.make_async_copy(given[(layers - 1 - t) * mats + m], weights[m], load_sem.at[m])

    def start(t, m):
        load(t, m).start()

    def ready(t, m):
        load(t, m).wait()

    def exchange():
        return carry_copies(n_seq, me, tot, buf.at[turn], carry_send.at[turn], carry_recv.at[turn])

    for m in (3, 2, 1):
        agenda.add(0, start, 0, m)
    agenda.add(0, meet, [{"seq": lax.rem(me + k, n_seq)} for k in range(1, n_seq)])
    for t in range(layers):
        begin = 2 * count * t
        agenda.add(begin, start, t, 0)
        for m in (3, 2, 1):
            agenda.add(begin, ready, t, m)
        agenda.add(begin + count, ready, t, 0)
        if t + 1 < layers:
            for m in (3, 2, 1):
                agenda.add(begin + count, start, t + 1, m)
    agenda.run(now)

    tile = count - 1 - lax.rem(step, count)
    row, at_row = tile // tiles, lax.rem(tile, tiles)
    gains, gate = gain_ref.at[layer], gate_ref.at[layer]

    @pl.when(step == 0)
    def _():
        small_ref[...] = jnp.zeros_like(small_ref)

    @pl.when((turn == 0) & (step < count))
    def _():
        dxs[tile] = dot(order_matrix(tokens, False), cot_ref[...])

    @pl.when(step < count)
    def _():
        back_out_tile(rel_ref, row, at_row, tiles - 1, dxs.at[tile], gu_ref, mid_ref, state_ref, pg_ref, pf_ref,
                      weights[1], weights[2], weights[3], gains, gate, dz_ref, dgu_ref, dy_ref, dpg.at[tile],
                      lam.at[tile], gs.at[tile], cum.at[tile], ends.at[tile], tot.at[row], small_ref, grad)

    @pl.when(step == count - 1)
    def _():
        for copy in exchange():
            copy.start()

    @pl.when(step == count)
    def _():
        for copy in exchange():
            copy.wait()
        combine(n_seq, me, False, buf.at[turn], gate.at[5:8], carry)

    @pl.when(step >= count)
    def _():
        back_in_tile(rel_ref, row, at_row, tiles - 1, dxs.at[tile], x_ref, proj_ref, dpg.at[tile], lam.at[tile],
                     starts_ref, prior_ref, gs.at[tile], cum.at[tile], ends.at[tile], carry.at[row], weights[0],
                     gains, gate, dproj_ref, small_ref, run)

        @pl.when(turn == layers - 1)
        def _():
            dx = dxs[tile]
            high = dx.astype(BF16)
            low = (dx - high.astype(F32)).astype(BF16)
            order = order_matrix(tokens, True)
            dtok_ref[...] = dot(order, high) + dot(order, low)


def run_backward(n_seq, rows, tokens, rel, cotangent, weights, gain_rows, gate_rows, kept):
    x, proj, p_g, starts, state, mid, gu = kept
    layers, total, width = x.shape
    chan = width // 2
    hidden = gu.shape[2] // 2
    count = total // tokens
    mats = len(weights) // layers
    shape = jax.ShapeDtypeStruct
    dma = pltpu.SemaphoreType.DMA
    any_ = pl.BlockSpec(memory_space=pl.ANY)
    last = layers - 1

    def first(step):
        return count - 1 - jnp.minimum(step, count - 1)

    def second(step):
        return count - 1 - jnp.maximum(step - count, 0)

    flat, few = tile_specs(tokens, lambda k: last - k)
    return pl.pallas_call(
        functools.partial(backward_kernel, n_seq, layers, rows, mats),
        grid=(layers, 2 * count),
        in_specs=[
            pl.BlockSpec(memory_space=pltpu.SMEM),
            pl.BlockSpec((tokens, width), lambda k, s: (jnp.where(k == 0, first(s), 0), 0)),
        ]
        + [any_] * len(weights)
        + [
            whole(layers, 8, width),
            whole(layers, 8, chan),
            flat(2 * hidden, first),
            flat(width, first),
            flat(width, first),
            flat(width, first),
            flat(chan, first, 2),
            flat(width, second),
            flat(3 * chan, second),
            few(8, width, second),
            flat(width, second),
        ],
        out_specs=[
            flat(width, first),
            flat(2 * hidden, first),
            flat(width, first),
            flat(3 * chan + width, second),
            pl.BlockSpec((tokens, width), lambda k, s: (jnp.where(k == last, second(s), count - 1), 0)),
            pl.BlockSpec((None, 32, width), lambda k, s: (last - k, 0, 0)),
        ],
        out_shape=[
            shape((layers, total, width), BF16),
            shape((layers, total, 2 * hidden), BF16),
            shape((layers, total, width), BF16),
            shape((layers, total, 3 * chan + width), BF16),
            shape((total, width), F32),
            shape((layers, 32, width), F32),
        ],
        scratch_shapes=[
            pltpu.VMEM((count, tokens, width), F32),
            pltpu.VMEM((count, width // LANES, tokens, LANES), F32),
            pltpu.VMEM((count, chan // LANES, tokens, LANES), F32),
            pltpu.VMEM((count, chan // LANES, tokens, LANES), F32),
            pltpu.VMEM((count, tokens, width), BF16),
            pltpu.VMEM((count, 24, chan), F32),
            pltpu.VMEM((rows, 8, chan), F32),
            pltpu.VMEM((width // LANES, tokens, LANES), F32),
            pltpu.VMEM((8, chan), F32),
            pltpu.VMEM((rows, 8, chan), F32),
            pltpu.VMEM((layers, n_seq - 1, rows, 8, chan), F32),
        ]
        + [pltpu.VMEM(w.shape, BF16) for w in weights[:mats]]
        + [dma((mats,)), dma((layers, n_seq - 1)), dma((layers, n_seq - 1))],
        compiler_params=pltpu.CompilerParams(collective_id=2, has_side_effects=True, vmem_limit_bytes=LIMIT),
    )(rel, cotangent, *weights, gain_rows, gate_rows, gu, mid, state, p_g, proj, x, proj, starts, state)


def add_rows(dst, dst_row, parts, rows):
    def block(i, _):
        step = pl.multiple_of(i * 16, 16)
        total = None
        for ref, first in parts:
            value = ref[pl.ds(pl.multiple_of(first + step, 16), 16), :].astype(F32)
            total = value if total is None else total + value
        dst[pl.ds(pl.multiple_of(dst_row + step, 16), 16), :] = total.astype(dst.dtype)
        return 0

    lax.fori_loop(0, rows // 16, block, 0)


def grads_kernel(n, plan, *refs):
    jobs = len(plan)
    lefts, rights, small = refs[:jobs], refs[jobs : 2 * jobs], refs[2 * jobs]
    outs_count = 1 + max(p[0] for p in plan)
    outs, small_out = refs[2 * jobs + 1 : 2 * jobs + 1 + outs_count], refs[2 * jobs + 1 + outs_count]
    rest = refs[2 * jobs + 2 + outs_count :]
    grads, core_buf, y_buf, ring_buf, fin_buf = (rest[i * jobs : (i + 1) * jobs] for i in range(5))
    (left_big, left_small, right_buf, small_buf, left_sem, right_sem, core_send, core_recv, y_send, y_recv,
     ring_send, ring_recv, end_send, end_recv, small_send, small_recv) = rest[5 * jobs :]
    ring = Ring(n)
    far, near = n // 2, n - 1 - n // 2
    core_dev, y_dev = {"seq": ring.core_peer}, {"seq": ring.y_peer}
    y, core = ring.y, ring.core
    rounds = [core_dev, y_dev]
    d = 1
    while d < n:
        rounds.append({"batch": ring.batch + d * (1 - 2 * ((ring.batch // d) % 2))})
        d *= 2
    us = [g.shape[0] // n // 6 for g in grads]
    split = [p[2] for p in plan]
    own_rows = [(2 if s else 3) * u for s, u in zip(split, us)]

    def left_copy(j):
        buf = (left_big, left_small)[j % 2]
        return pltpu.make_async_copy(lefts[j].at[plan[j][1]], buf.at[:, 0 : plan[j][3]], left_sem.at[j % 2])

    chunks = []
    for j, (_, _, _, rows, cols) in enumerate(plan):
        first = 0
        while first < cols:
            size = min(CHUNK, cols - first)
            chunks.append((j, first, size, first + size == cols))
            first += size

    def right_copy(i):
        j, first, size, _ = chunks[i]
        return pltpu.make_async_copy(
            rights[j].at[plan[j][1], :, first : first + size], right_buf.at[i % 2, :, 0:size], right_sem.at[i % 2]
        )

    left_copy(0).start()
    right_copy(0).start()
    right_copy(1).start()
    left_copy(1).start()
    meet([{"batch": ring.ahead(1)}, {"batch": ring.ahead(-1)}] + rounds)

    order = []
    for h in range(far):
        order.append((1, h, far - h))
        if h < near:
            order.append((-1, h, near - h))
    order.append((0, 0, 0))
    last = len(order)

    def rows_at(ref, first, rows):
        return ref.at[pl.ds(pl.multiple_of(first, 16), rows)]

    def core_copy(j, slot, piece):
        u = us[j]
        return remote(rows_at(grads[j], piece * (6 * u) + (1 - core) * (3 * u), 3 * u),
                      core_buf[j].at[slot], core_send.at[j], core_recv.at[j, slot], core_dev)

    def y_copy(j, slot, piece):
        u = us[j]
        src = rows_at(grads[j], piece * (6 * u) + core * (3 * u) + 2 * (1 - y) * u, u)
        return remote(src, y_buf[j].at[slot], y_send.at[j], y_recv.at[j, slot], y_dev)

    def mine(j, piece):
        u = us[j]
        return piece * (6 * u) + core * (3 * u) + (y * u if split[j] else 0)

    def ring_copy(j, slot, way, piece):
        return remote(rows_at(grads[j], mine(j, piece), own_rows[j]), ring_buf[j].at[slot], ring_send.at[j],
                      ring_recv.at[j, slot], {"batch": ring.ahead(way)})

    def small_round(r):
        return remote(small_buf.at[2 * r], small_buf.at[2 * r + 1], small_send.at[r], small_recv.at[r], rounds[r])

    small_buf[0] = small[...]
    small_round(0).start()

    def small_step(r):
        small_round(r).wait_recv()
        total = small_buf[2 * r] + small_buf[2 * r + 1]
        if r + 1 < len(rounds):
            small_buf[2 * r + 2] = total
            small_round(r + 1).start()
        else:
            small_out[...] = total

    def begin(j):
        for slot, (way, h, dist) in enumerate(order):
            core_copy(j, slot, ring.ahead(-way * dist)).start()

    def cross(j, slot):
        way, h, dist = order[slot]
        piece = ring.ahead(way * dist)
        u = us[j]
        core_copy(j, slot, piece).wait_recv()
        if not split[j]:
            return
        give = 2 * (1 - y) * u
        at = piece * (6 * u) + core * (3 * u) + give
        add_rows(grads[j], at, [(grads[j], at), (core_buf[j].at[slot], give)], u)
        y_copy(j, slot, piece).start()

    def hop(j, slot):
        way, h, dist = order[slot]
        piece = ring.ahead(way * dist)
        u = us[j]
        if split[j]:
            y_copy(j, slot, piece).wait_recv()
        if way == 0:
            prior = [i for i, o in enumerate(order) if o[2] == 1]
        elif h:
            prior = [i for i, o in enumerate(order) if o[0] == way and o[1] == h - 1]
        else:
            prior = []
        for i in prior:
            ring_copy(j, i, order[i][0], piece).wait_recv()
        at = mine(j, piece)
        base = [(grads[j], at), (core_buf[j].at[slot], y * u if split[j] else 0)]
        base += [(ring_buf[j].at[i], 0) for i in prior]
        if split[j]:
            for by, more in ((y * u, [(y_buf[j].at[slot], 0)]), ((1 - y) * u, [])):
                add_rows(grads[j], at + by, [(r, f + by) for r, f in base] + more, u)
        else:
            add_rows(grads[j], at, base, 3 * u)
        if way:
            ring_copy(j, slot, way, piece).start()

    def fin_copy(j):
        return remote(rows_at(grads[j], mine(j, ring.batch), own_rows[j]), fin_buf[j], end_send.at[j, 0],
                      end_recv.at[j, 0], y_dev)

    def half_copy(j):
        half = outs[plan[j][0]].at[plan[j][1], pl.ds(pl.multiple_of(core * (3 * us[j]), 16), 3 * us[j])]
        return remote(half, half, end_send.at[j, 1], end_recv.at[j, 1], core_dev)

    def finish(j):
        u = us[j]
        fin_copy(j).wait_recv()
        out = outs[plan[j][0]].at[plan[j][1]]
        at, to = mine(j, ring.batch), core * (3 * u)
        if split[j]:
            add_rows(out, to + 2 * y * u, [(grads[j], at + y * u)], u)
            add_rows(out, to + 2 * (1 - y) * u, [(fin_buf[j], (1 - y) * u)], u)
            add_rows(out, to + u, [(grads[j], at + (1 - y) * u), (fin_buf[j], y * u)], u)
        else:
            add_rows(out, to, [(grads[j], at), (fin_buf[j], 0)], 3 * u)
        half_copy(j).start()

    steps = far + 4

    def advance(j, t):
        now = [i for i, o in enumerate(order) if o[0] and o[1] == t]
        before = [i for i, o in enumerate(order) if o[0] and o[1] == t - 1]
        for slot in before:
            hop(j, slot)
        for slot in now:
            cross(j, slot)
        if t == far - 1:
            cross(j, last - 1)
        if t == far + 1:
            hop(j, last - 1)
            fin_copy(j).start()
        if t == far + 2:
            finish(j)
        if t == far + 3:
            half_copy(j).wait_recv()

    stage = {}

    def advance_all(turn):
        for j in list(stage):
            if j % 2 == turn:
                advance(j, stage[j])
                stage[j] += 1
                if stage[j] == steps:
                    del stage[j]

    small_at = 0
    for i, (j, first, size, done) in enumerate(chunks):
        if first == 0:
            left_copy(j).wait()
        right_copy(i).wait()
        left = (left_big, left_small)[j % 2]

        def multiply(b, _, i=i, j=j, first=first, size=size, left=left):
            at = pl.multiple_of(b * 256, 256)
            part = lax.dot_general(
                left[:, pl.ds(at, 256)], right_buf[i % 2, :, 0:size], (((0,), (0,)), ((), ())),
                preferred_element_type=F32,
            )
            grads[j][pl.ds(at, 256), first : first + size] = part.astype(BF16)
            return 0

        lax.fori_loop(0, plan[j][3] // 256, multiply, 0)
        if i + 2 < len(chunks):
            right_copy(i + 2).start()
        if done and j + 2 < jobs:
            left_copy(j + 2).start()
        advance_all(i % 2)
        if done:
            begin(j)
            stage[j] = 0
        if small_at < len(rounds):
            small_step(small_at)
            small_at += 1
    i = 0
    while stage:
        advance_all(i % 2)
        i += 1
    while small_at < len(rounds):
        small_step(small_at)
        small_at += 1
    for j in range(jobs):
        u = us[j]
        fin_copy(j).wait_send()
        half_copy(j).wait_send()
        remote(core_buf[j], core_buf[j], core_send.at[j], core_recv.at[j, 0], core_dev).wait_send()
        if split[j]:
            remote(y_buf[j], y_buf[j], y_send.at[j], y_recv.at[j, 0], y_dev).wait_send()
        remote(ring_buf[j], ring_buf[j], ring_send.at[j], ring_recv.at[j, 0], core_dev).wait_send()
    for r in range(len(rounds)):
        small_round(r).wait_send()


def grads_and_scatter(n, plan, lefts, rights, small):
    jobs = len(plan)
    plan = [p + (a.shape[2], b.shape[2]) for p, a, b in zip(plan, lefts, rights)]
    tokens = lefts[0].shape[1]
    layers = 1 + max(p[1] for p in plan)
    dma = pltpu.SemaphoreType.DMA
    rounds = 2 + (n - 1).bit_length()
    sizes = [(p[3] // n // 6, p[4], p[2]) for p in plan]
    outs = {p[0]: jax.ShapeDtypeStruct((layers, p[3] // n, p[4]), BF16) for p in plan}
    vm = pl.BlockSpec(memory_space=pltpu.VMEM)
    any_ = pl.BlockSpec(memory_space=pl.ANY)

    def bufs(f):
        return [pltpu.VMEM(f(u, w, s), BF16) for u, w, s in sizes]

    return pl.pallas_call(
        functools.partial(grads_kernel, n, plan),
        out_shape=[outs[m] for m in sorted(outs)] + [jax.ShapeDtypeStruct(small.shape, F32)],
        in_specs=[any_] * (2 * jobs) + [vm],
        out_specs=[vm] * (len(outs) + 1),
        scratch_shapes=bufs(lambda u, w, s: (6 * u * n, w))
        + bufs(lambda u, w, s: (n, 3 * u, w))
        + bufs(lambda u, w, s: (n if s else 1, u, w))
        + bufs(lambda u, w, s: (n - 1, 2 * u if s else 3 * u, w))
        + bufs(lambda u, w, s: (2 * u if s else 3 * u, w))
        + [
            pltpu.VMEM((tokens, max(p[3] for p in plan[0::2])), BF16),
            pltpu.VMEM((tokens, max(p[3] for p in plan[1::2])), BF16),
            pltpu.VMEM((2, tokens, CHUNK), BF16),
            pltpu.VMEM((2 * rounds,) + small.shape, F32),
            dma((2,)), dma((2,)), dma((jobs,)), dma((jobs, n)), dma((jobs,)), dma((jobs, n)), dma((jobs,)),
            dma((jobs, n)), dma((jobs, 2)), dma((jobs, 2)), dma((rounds,)), dma((rounds,)),
        ],
        compiler_params=pltpu.CompilerParams(
            collective_id=4, has_side_effects=True, vmem_limit_bytes=63 * 1024 * 1024
        ),
    )(*lefts, *rights, small)


def contract_rows(left, right):
    return lax.dot_general(
        left, right, (((0,), (0,)), ((), ())), preferred_element_type=F32
    ).astype(BF16)


def shards(
    tokens_in, doc_starts, mixer_in, mixer_out, ffn_in, ffn_out, gains, gate_params, cotangent
):
    rows, length, width = tokens_in.shape
    layers = gains.shape[0]
    chan = width // 2
    total = rows * length
    tokens = min(length, 256)
    seg = tokens // 8
    n, n_seq = lax.axis_size("batch"), lax.axis_size("seq")
    sources = (mixer_in, mixer_out, ffn_in, ffn_out)
    paired = n_seq == 4 and n % 4 == 0 and all(w.shape[1] % 96 == 0 for w in sources)
    rel = doc_starts - lax.axis_index("seq") * length
    gain_rows = jnp.pad(gains, ((0, 0), (0, 5), (0, 0)))
    theta, lower = gate_params[:, 0], gate_params[:, 1]
    turns = jnp.stack([theta, theta * seg, theta * length], axis=1)
    cos, sin = jnp.cos(turns), jnp.sin(turns)
    gate_rows = jnp.stack(
        [cos[:, 0], sin[:, 0], lower, cos[:, 1], sin[:, 1], cos[:, 2], sin[:, 2], lower], axis=1
    )
    x = tokens_in.reshape(total, width)
    if paired:
        weights, kept = run_forward(n, n_seq, True, rows, tokens, rel, x, sources, gain_rows, gate_rows)
    else:
        stacked = [lax.all_gather(w, "batch", axis=1, tiled=True) for w in sources]
        weights = [w[k] for k in range(layers) for w in stacked]
        _, kept = run_forward(n, n_seq, False, rows, tokens, rel, x, stacked, gain_rows, gate_rows)
    x_in, proj, p_g, normed, starts, state, mixed, mid, normed2, gu, hid, block_out = kept
    dz, d_gu, dy, d_proj, d_tokens, small = run_backward(
        n_seq, rows, tokens, rel, cotangent.reshape(total, width), weights, gain_rows, gate_rows,
        (x_in, proj, p_g, starts, state, mid, gu),
    )
    small = jnp.sum(small.reshape(layers, 4, 8, width), axis=2).reshape(layers * 4, width)
    pairs = ((normed, d_proj), (mixed, dy), (normed2, d_gu), (hid, dz))
    if paired:
        plan = []
        for k in reversed(range(layers)):
            plan += [(m, k, m != 0) for m in ((1, 2, 3, 0) if k == layers - 1 else (3, 2, 0, 1))]
        *outs, totals = grads_and_scatter(
            n, plan, [pairs[m][0] for m, _, _ in plan], [pairs[m][1] for m, _, _ in plan], small
        )
    else:
        outs = []
        for left, right in pairs:
            whole_grads = jnp.stack([contract_rows(left[k], right[k]) for k in range(layers)])
            part = lax.psum_scatter(whole_grads, "batch", scatter_dimension=1, tiled=True)
            outs.append(lax.psum(part, "seq"))
        totals = lax.psum(small, ("batch", "seq"))
    totals = totals.reshape(layers, 4, width)
    return (
        block_out.reshape(rows, length, width),
        d_tokens.reshape(rows, length, width),
        *[o.astype(F32) for o in outs],
        totals[:, :3],
        totals[:, 3].reshape(layers, 2, chan),
    )


def solution(mesh):
    tok = P("batch", "seq", None)
    mat = P(None, "batch", None)
    return jax.shard_map(
        shards,
        mesh=mesh,
        in_specs=(tok, P("batch", None), mat, mat, mat, mat, P(), P(), tok),
        out_specs=(tok, tok, mat, mat, mat, mat, P(), P()),
        check_vma=False,
    )
```

```python
import functools
import math

import jax
import jax.numpy as jnp
from jax import lax
from jax.experimental import pallas as pl
from jax.experimental.pallas import tpu as pltpu
from jax.sharding import PartitionSpec as P

EPS = 1e-06
F32 = jnp.float32
BF16 = jnp.bfloat16
LANES = 128
CHUNK = 768
MESH = pl.DeviceIdType.MESH


def sigmoid(values):
    return 1.0 / (1.0 + jnp.exp(-values))


def rms_scale(values):
    return lax.rsqrt(jnp.mean(values * values, axis=-1, keepdims=True) + EPS)


def dot(left, right):
    return jnp.dot(left, right, preferred_element_type=F32)


def dot_t(left, right):
    return lax.dot_general(left, right, (((1,), (1,)), ((), ())), preferred_element_type=F32)


def eight_sum(values):
    rows, cols = values.shape
    return jnp.sum(values.reshape(rows // 8, 8, cols), axis=0)


def wide(ref, first, last):
    return jnp.concatenate([ref[g] for g in range(first, last)], axis=-1)


def split_store(ref, first, values):
    for g in range(values.shape[1] // LANES):
        ref[first + g] = values[:, g * LANES : (g + 1) * LANES]


def lanes(values):
    return [values[:, g * LANES : (g + 1) * LANES] for g in range(values.shape[1] // LANES)]


LIMIT = 60 * 1024 * 1024


def whole(*shape):
    return pl.BlockSpec(shape, lambda *_: (0,) * len(shape), pipeline_mode=pl.Buffered(1))


def order_matrix(tokens, back):
    shape = (tokens, tokens)
    here = lax.broadcasted_iota(jnp.int32, shape, 1 if back else 0)
    there = lax.broadcasted_iota(jnp.int32, shape, 0 if back else 1)
    return jnp.where(there == (here & 7) * (tokens // 8) + (here >> 3), 1.0, 0.0).astype(BF16)


def reset_mask(doc_ref, row, first, tokens):
    here = lax.broadcasted_iota(jnp.int32, (tokens, LANES), 0)
    pos = (here & 7) * (tokens // 8) + (here >> 3) + first
    hit = pos == doc_ref[row, 0]
    for k in range(1, doc_ref.shape[1]):
        hit = hit | (pos == doc_ref[row, k])
    return hit


def retain(doc_ref, row, first, p_f, lower):
    tokens, chan = p_f.shape
    forget = sigmoid(p_f)
    lam = lower + (1.0 - lower) * forget
    keep = jnp.where(reset_mask(doc_ref, row, first, tokens), 0.0, 1.0)
    return lam * jnp.concatenate([keep] * (chan // LANES), axis=-1), forget, keep


def pieces(total):
    size = 512 if total % 512 == 0 else total
    return [slice(first, first + size) for first in range(0, total, size)]


def moved(part, by):
    return slice(part.start + by, part.stop + by)


def at_step(s):
    return pl.ds(pl.multiple_of(s * 8, 8), 8)


def enter_tile(doc_ref, row, tile, start, x, w_ref, gain_ref, gate_ref, proj_ref, pg_ref, normed_ref, h_ref, cum_ref,
               ends_ref, tot_ref, src, lam_ref):
    tokens, width = x.shape
    chan = width // 2
    seg = tokens // 8
    groups = chan // LANES
    normed = (x * rms_scale(x) * gain_ref[0:1, :]).astype(BF16)
    normed_ref[...] = normed
    p_f = dot(normed, w_ref[:, 2 * chan : 3 * chan])
    p_c = dot(normed, w_ref[:, : 2 * chan])
    proj_ref[:, 2 * chan :] = p_f.astype(BF16)
    cos, sin, lower = gate_ref[0:1, :], gate_ref[1:2, :], gate_ref[2:3, :]
    seg_cos, seg_sin = gate_ref[3:4, :], gate_ref[4:5, :]
    lam, _, _ = retain(doc_ref, row, start, p_f, lower)
    split_store(lam_ref, 0, lam)
    pg_ref[...] = dot(normed, w_ref[:, 3 * chan :]).astype(BF16)
    proj_ref[:, : 2 * chan] = p_c.astype(BF16)
    p_r, p_i = p_c[:, :chan], p_c[:, chan:]
    split_store(src, 0, (1.0 - lam) * (p_r * sigmoid(p_r)))
    split_store(src, groups, (1.0 - lam) * (p_i * sigmoid(p_i)))
    cos_l, sin_l = lanes(cos), lanes(sin)

    def step(s, state):
        at = at_step(s)
        after = []
        for k, (h_r, h_i, cum) in enumerate(state):
            lam_s = lam_ref[k, at, :]
            a_r, a_i = lam_s * cos_l[k], lam_s * sin_l[k]
            n_r = a_r * h_r - a_i * h_i + src[k, at, :]
            n_i = a_r * h_i + a_i * h_r + src[groups + k, at, :]
            cum = cum * lam_s
            h_ref[k, at, :] = n_r
            h_ref[groups + k, at, :] = n_i
            cum_ref[k, at, :] = cum
            after.append((n_r, n_i, cum))
        return tuple(after)

    zero = lam_ref[0, 0:8, :] * 0.0
    last = lax.fori_loop(0, seg, step, ((zero, zero, zero + 1.0),) * groups, unroll=8)
    e_r, e_i, e_c = (jnp.concatenate([v[i] for v in last], axis=-1) for i in range(3))
    ends_ref[0:8, :] = e_r
    ends_ref[8:16, :] = e_i
    ends_ref[16:24, :] = e_c

    @pl.when(tile == 0)
    def _():
        tot_ref[0:2, :] = jnp.zeros((2, chan), F32)
        tot_ref[2:3, :] = jnp.ones((1, chan), F32)

    c_r, c_i, c_l = tot_ref[0:1, :], tot_ref[1:2, :], tot_ref[2:3, :]
    for j in range(8):
        m = e_c[j : j + 1, :]
        a_r, a_i = m * seg_cos, m * seg_sin
        c_r, c_i = a_r * c_r - a_i * c_i + e_r[j : j + 1, :], a_r * c_i + a_i * c_r + e_i[j : j + 1, :]
        c_l = c_l * m
    tot_ref[0:1, :] = c_r
    tot_ref[1:2, :] = c_i
    tot_ref[2:3, :] = c_l


def leave_tile(tile, x, pg_ref, h_ref, cum_ref, ends_ref, carry_ref, wo_ref, wf_ref, wd_ref, gain_ref, gate_ref,
               starts_ref, state_ref, mixed_ref, mid_ref, normed_ref, gu_ref, hid_ref, run):
    tokens, width = x.shape
    chan = width // 2
    seg = tokens // 8
    groups = chan // LANES
    cos, sin = gate_ref[0:1, :], gate_ref[1:2, :]
    seg_cos, seg_sin = gate_ref[3:4, :], gate_ref[4:5, :]

    @pl.when(tile == 0)
    def _():
        run[0:2, :] = carry_ref[0:2, :]

    c_r, c_i = run[0:1, :], run[1:2, :]
    l_r, l_i = [], []
    for j in range(8):
        l_r.append(c_r)
        l_i.append(c_i)
        m = ends_ref[16 + j : 17 + j, :]
        a_r, a_i = m * seg_cos, m * seg_sin
        c_r, c_i = (
            a_r * c_r - a_i * c_i + ends_ref[j : j + 1, :],
            a_r * c_i + a_i * c_r + ends_ref[8 + j : 9 + j, :],
        )
    run[0:1, :] = c_r
    run[1:2, :] = c_i
    start_r, start_i = jnp.concatenate(l_r, axis=0), jnp.concatenate(l_i, axis=0)
    starts_ref[...] = jnp.concatenate([start_r, start_i], axis=-1)
    cos_l, sin_l = lanes(cos), lanes(sin)

    def step(s, state):
        at = at_step(s)
        after = []
        for k, (w_r, w_i) in enumerate(state):
            w_r, w_i = w_r * cos_l[k] - w_i * sin_l[k], w_r * sin_l[k] + w_i * cos_l[k]
            cum = cum_ref[k, at, :]
            h_ref[k, at, :] += cum * w_r
            h_ref[groups + k, at, :] += cum * w_i
            after.append((w_r, w_i))
        return tuple(after)

    lax.fori_loop(0, seg, step, tuple(zip(lanes(start_r), lanes(start_i))), unroll=8)
    state = wide(h_ref, 0, 2 * groups)
    state_ref[...] = state.astype(BF16)
    p_g = pg_ref[...].astype(F32)
    mixed = (state * rms_scale(state) * gain_ref[1:2, :] * (p_g * sigmoid(p_g))).astype(BF16)
    mixed_ref[...] = mixed
    mid = x + dot(mixed, wo_ref[...])
    mid_ref[...] = mid.astype(BF16)
    normed = (mid * rms_scale(mid) * gain_ref[2:3, :]).astype(BF16)
    normed_ref[...] = normed
    hidden = wd_ref.shape[0]
    parts = pieces(hidden)

    def gate_up(part):
        return dot(normed, wf_ref[:, part]), dot(normed, wf_ref[:, moved(part, hidden)])

    after = gate_up(parts[0])
    for i, part in enumerate(parts):
        gate, up = after
        if i + 1 < len(parts):
            after = gate_up(parts[i + 1])
        gu_ref[:, part] = gate.astype(BF16)
        gu_ref[:, moved(part, hidden)] = up.astype(BF16)
        hid_ref[:, part] = (gate * sigmoid(gate) * up).astype(BF16)
    return mid + dot(hid_ref[...], wd_ref[...])


def back_out_tile(doc_ref, row, tile, start, last, dx_ref, gu_ref, mid_ref, state_ref, pg_ref, pf_ref, wo_ref, wf_ref,
                  wd_ref, gain_ref, gate_ref, dz_ref, dgu_ref, dy_ref, dpg_ref, lam_ref, g_ref, cum_ref, ends_ref,
                  tot_ref, small_ref, grad):
    tokens, width = dx_ref.shape
    chan = width // 2
    seg = tokens // 8
    groups = chan // LANES
    cos, sin, lower = gate_ref[0:1, :], gate_ref[1:2, :], gate_ref[2:3, :]
    seg_cos, seg_sin = gate_ref[3:4, :], gate_ref[4:5, :]
    dx = dx_ref[...]
    dz = dx.astype(BF16)
    dz_ref[...] = dz
    hidden = wd_ref.shape[0]
    parts = pieces(hidden)
    d_next = dot_t(dz, wd_ref[parts[0], :])
    for i, part in enumerate(parts):
        d_hid = d_next
        if i + 1 < len(parts):
            d_next = dot_t(dz, wd_ref[parts[i + 1], :])
        gate = gu_ref[:, part].astype(F32)
        up = gu_ref[:, moved(part, hidden)].astype(F32)
        sg = sigmoid(gate)
        silu = gate * sg
        dgu_ref[:, part] = (d_hid * up * (sg + silu * (1.0 - sg))).astype(BF16)
        dgu_ref[:, moved(part, hidden)] = (d_hid * silu).astype(BF16)
    d_n = dot_t(dgu_ref[...], wf_ref[...])
    mid = mid_ref[...].astype(F32)
    scale = rms_scale(mid)
    hat = mid * scale
    d_hat = d_n * gain_ref[2:3, :]
    small_ref[16:24, :] += eight_sum(d_n * hat)
    d_mid = dx + scale * (d_hat - hat * jnp.mean(d_hat * hat, axis=-1, keepdims=True))
    dx_ref[...] = d_mid
    dy = d_mid.astype(BF16)
    dy_ref[...] = dy
    d_mixed = dot_t(dy, wo_ref[...])
    p_g = pg_ref[...].astype(F32)
    sg = sigmoid(p_g)
    silu = p_g * sg
    state = state_ref[...].astype(F32)
    scale = rms_scale(state)
    hat = state * scale
    g1 = gain_ref[1:2, :]
    dpg_ref[...] = (d_mixed * hat * g1 * (sg + silu * (1.0 - sg))).astype(BF16)
    d_n = d_mixed * silu
    small_ref[8:16, :] += eight_sum(d_n * hat)
    d_hat = d_n * g1
    split_store(grad, 0, scale * (d_hat - hat * jnp.mean(d_hat * hat, axis=-1, keepdims=True)))
    lam, _, _ = retain(doc_ref, row, start, pf_ref[...].astype(F32), lower)
    split_store(lam_ref, 0, lam)
    cos_l, sin_l = lanes(cos), lanes(sin)

    def step(s, state):
        at = at_step(seg - 1 - s)
        after = []
        for k, (g_r, g_i, cum, lam_n) in enumerate(state):
            a_r, a_i = lam_n * cos_l[k], lam_n * sin_l[k]
            n_r = grad[k, at, :] + a_r * g_r + a_i * g_i
            n_i = grad[groups + k, at, :] + a_r * g_i - a_i * g_r
            cum = cum * lam_n
            g_ref[k, at, :] = n_r
            g_ref[groups + k, at, :] = n_i
            cum_ref[k, at, :] = cum
            after.append((n_r, n_i, cum, lam_ref[k, at, :]))
        return tuple(after)

    zero = lam_ref[0, 0:8, :] * 0.0
    final = lax.fori_loop(0, seg, step, ((zero, zero, zero + 1.0, zero + 1.0),) * groups, unroll=8)
    g_r, g_i, cum, lam_0 = (jnp.concatenate([v[i] for v in final], axis=-1) for i in range(4))
    e_r = lam_0 * (cos * g_r + sin * g_i)
    e_i = lam_0 * (cos * g_i - sin * g_r)
    e_c = lam_0 * cum
    ends_ref[0:8, :] = e_r
    ends_ref[8:16, :] = e_i
    ends_ref[16:24, :] = e_c

    @pl.when(tile == last)
    def _():
        tot_ref[0:2, :] = jnp.zeros((2, chan), F32)
        tot_ref[2:3, :] = jnp.ones((1, chan), F32)

    c_r, c_i, c_l = tot_ref[0:1, :], tot_ref[1:2, :], tot_ref[2:3, :]
    for j in reversed(range(8)):
        m = e_c[j : j + 1, :]
        a_r, a_i = m * seg_cos, m * seg_sin
        c_r, c_i = a_r * c_r + a_i * c_i + e_r[j : j + 1, :], a_r * c_i - a_i * c_r + e_i[j : j + 1, :]
        c_l = c_l * m
    tot_ref[0:1, :] = c_r
    tot_ref[1:2, :] = c_i
    tot_ref[2:3, :] = c_l


def back_in_tile(doc_ref, row, tile, start, last, dx_ref, x_ref, proj_ref, dpg_ref, lam_ref, starts_ref, state_ref, g_ref,
                 cum_ref, ends_ref, carry_ref, w_ref, gain_ref, gate_ref, dproj_ref, small_ref, run):
    tokens, width = dx_ref.shape
    chan = width // 2
    seg = tokens // 8
    groups = chan // LANES
    cos, sin, lower = gate_ref[0:1, :], gate_ref[1:2, :], gate_ref[2:3, :]
    seg_cos, seg_sin = gate_ref[3:4, :], gate_ref[4:5, :]

    @pl.when(tile == last)
    def _():
        run[0:2, :] = carry_ref[0:2, :]

    c_r, c_i = run[0:1, :], run[1:2, :]
    l_r, l_i = [None] * 8, [None] * 8
    for j in reversed(range(8)):
        l_r[j], l_i[j] = c_r, c_i
        m = ends_ref[16 + j : 17 + j, :]
        a_r, a_i = m * seg_cos, m * seg_sin
        c_r, c_i = (
            a_r * c_r + a_i * c_i + ends_ref[j : j + 1, :],
            a_r * c_i - a_i * c_r + ends_ref[8 + j : 9 + j, :],
        )
    run[0:1, :] = c_r
    run[1:2, :] = c_i
    cos_l, sin_l = lanes(cos), lanes(sin)

    def step(s, state):
        at = at_step(seg - 1 - s)
        after = []
        for k, (w_r, w_i) in enumerate(state):
            cum = cum_ref[k, at, :]
            g_ref[k, at, :] += cum * w_r
            g_ref[groups + k, at, :] += cum * w_i
            after.append((w_r * cos_l[k] + w_i * sin_l[k], w_i * cos_l[k] - w_r * sin_l[k]))
        return tuple(after)

    start_at = (jnp.concatenate(l_r, axis=0), jnp.concatenate(l_i, axis=0))
    lax.fori_loop(0, seg, step, tuple(zip(lanes(start_at[0]), lanes(start_at[1]))), unroll=8)
    d_n = dot_t(dpg_ref[...], w_ref[:, 3 * chan :])
    g_r, g_i = wide(g_ref, 0, groups), wide(g_ref, groups, 2 * groups)
    prior = jnp.concatenate([starts_ref[...], state_ref[...].astype(F32)[: tokens - 8, :]], axis=0)
    q_r, q_i = prior[:, :chan], prior[:, chan:]
    p_r = proj_ref[:, :chan].astype(F32)
    p_i = proj_ref[:, chan : 2 * chan].astype(F32)
    _, forget, keep = retain(doc_ref, row, start, proj_ref[:, 2 * chan :].astype(F32), lower)
    lam = wide(lam_ref, 0, groups)
    d_ar = g_r * q_r + g_i * q_i
    d_ai = g_i * q_r - g_r * q_i
    s_r, s_i = sigmoid(p_r), sigmoid(p_i)
    in_r, in_i = p_r * s_r, p_i * s_i
    d_lam = d_ar * cos + d_ai * sin - (g_r * in_r + g_i * in_i)
    d_f = jnp.concatenate([keep] * groups, axis=-1) * d_lam * (1.0 - forget)
    small_ref[24:32, :] += jnp.concatenate(
        [eight_sum(lam * (d_ai * cos - d_ar * sin)), eight_sum(d_f)], axis=-1
    )
    rest = 1.0 - lam
    d_proj = jnp.concatenate(
        [
            (rest * g_r * (s_r + in_r * (1.0 - s_r))).astype(BF16),
            (rest * g_i * (s_i + in_i * (1.0 - s_i))).astype(BF16),
            (d_f * (1.0 - lower) * forget).astype(BF16),
        ],
        axis=1,
    )
    dproj_ref[:, : 3 * chan] = d_proj
    dproj_ref[:, 3 * chan :] = dpg_ref[...]
    d_n = d_n + dot_t(d_proj, w_ref[:, : 3 * chan])
    x = x_ref[...].astype(F32)
    scale = rms_scale(x)
    hat = x * scale
    small_ref[0:8, :] += eight_sum(d_n * hat)
    d_hat = d_n * gain_ref[0:1, :]
    dx_ref[...] = dx_ref[...] + scale * (d_hat - hat * jnp.mean(d_hat * hat, axis=-1, keepdims=True))


def combine(count, me, forward, buf, rot_ref, out_ref):
    cos, sin = rot_ref[0:1, :], rot_ref[1:2, :]
    c_r = jnp.zeros_like(cos)
    c_i = jnp.zeros_like(cos)
    for k in range(count - 1, 0, -1):
        slot = k - 1 if forward else count - k - 1
        valid = me >= k if forward else me + k < count
        e_r, e_i, m = buf[slot, 0:1, :], buf[slot, 1:2, :], buf[slot, 2:3, :]
        a_r = m * cos
        a_i = m * sin if forward else -m * sin
        n_r = a_r * c_r - a_i * c_i + e_r
        n_i = a_r * c_i + a_i * c_r + e_i
        keep = jnp.where(valid, 1.0, 0.0)
        c_r, c_i = n_r * keep, n_i * keep
    out_ref[0:1, :] = c_r
    out_ref[1:2, :] = c_i


def carry_copies(count, me, tot_ref, buf, send_sem, recv_sem):
    return [
        remote(tot_ref, buf.at[k - 1], send_sem.at[k - 1], recv_sem.at[k - 1], {"seq": lax.rem(me + k, count)})
        for k in range(1, count)
    ]


class Ring:
    def __init__(self, n):
        self.n = n
        self.batch, self.seq = lax.axis_index("batch"), lax.axis_index("seq")
        z, x = self.batch // 2, self.batch % 2
        self.pos = z + x * (n - 1 - 2 * z)
        self.core, self.y = self.seq % 2, self.seq // 2
        self.sign = 1 - 2 * self.core
        self.core_peer = self.seq + self.sign
        self.y_peer = self.seq + 2 * (1 - 2 * self.y)

    def at(self, distance):
        p = (self.pos + distance + 2 * self.n) % self.n
        h = p // (self.n // 2)
        return 2 * (p + h * (self.n - 1 - 2 * p)) + h

    def ahead(self, hops):
        return self.at(self.sign * hops)


def remote(src, dst, send, recv, device):
    return pltpu.make_async_remote_copy(
        src_ref=src, dst_ref=dst, send_sem=send, recv_sem=recv, device_id=device, device_id_type=MESH
    )


def meet(devices):
    barrier = pltpu.get_barrier_semaphore()
    for device in devices:
        pl.semaphore_signal(barrier, inc=1, device_id=device, device_id_type=MESH)
    pl.semaphore_wait(barrier, len(devices))


class Gather:
    def __init__(self, ring, jobs, sems):
        self.ring, self.jobs = ring, jobs
        (self.own_sem, self.ring_send, self.ring_recv, self.y_send, self.y_recv, self.core_send,
         self.core_recv) = sems
        n = ring.n
        self.hops = ((1, n // 2, 0), (-1, n - 1 - n // 2, n // 2))

    def rows(self, j, piece):
        src, dst, u = self.jobs[j]
        ring = self.ring
        base = ring.core * (3 * u)
        whole = piece * (6 * u)
        view = lambda first, rows: dst.at[pl.ds(pl.multiple_of(whole + base + first, 16), rows)]
        return view(ring.y * u, 2 * u), view(2 * ring.y * u, u), view(2 * (1 - ring.y) * u, u)

    def own_copy(self, j):
        src, dst, u = self.jobs[j]
        return pltpu.make_async_copy(
            src, dst.at[pl.ds(pl.multiple_of(self.ring.batch * (6 * u), 16), 6 * u)], self.own_sem.at[j]
        )

    def own(self, j):
        src, dst, u = self.jobs[j]
        ring = self.ring
        mine, _, _ = self.rows(j, ring.batch)
        piece = src.at[pl.ds(pl.multiple_of(ring.core * (3 * u) + ring.y * u, 16), 2 * u)]
        for way, hops, first in self.hops:
            remote(piece, mine, self.ring_send.at[j], self.ring_recv.at[j, first],
                   {"batch": ring.ahead(way)}).start()
        self.own_copy(j).start()

    def arrived(self, j, h):
        ring = self.ring
        for way, hops, first in self.hops:
            if h < hops:
                mine, give, _ = self.rows(j, ring.ahead(-way * (h + 1)))
                on = lambda slot: remote(mine, mine, self.ring_send.at[j], self.ring_recv.at[j, first + slot],
                                         {"batch": ring.ahead(way)})
                on(h).wait_recv()
                if h + 1 < hops:
                    on(h + 1).start()
                remote(give, give, self.y_send.at[j], self.y_recv.at[j, first + h], {"seq": ring.y_peer}).start()
                remote(mine, mine, self.core_send.at[j], self.core_recv.at[j], {"seq": ring.core_peer}).start()

    def crossed(self, j, h):
        ring = self.ring
        for way, hops, first in self.hops:
            if h < hops:
                _, _, take = self.rows(j, ring.ahead(-way * (h + 1)))
                remote(take, take, self.y_send.at[j], self.y_recv.at[j, first + h], {"seq": ring.y_peer}).wait_recv()
                remote(take, take, self.core_send.at[j], self.core_recv.at[j], {"seq": ring.core_peer}).start()

    def swapped(self, j):
        src, dst, u = self.jobs[j]
        view = dst.at[0 : (self.ring.n - 1) * 3 * u]
        remote(view, view, self.core_send.at[j], self.core_recv.at[j], {"seq": self.ring.core_peer}).wait_recv()
        self.own_copy(j).wait()

    def sent(self, j):
        src, dst, u = self.jobs[j]
        for rows, send in ((2 * u, self.ring_send), (u, self.y_send), (3 * u, self.core_send)):
            view = dst.at[0 : (self.ring.n - 1) * rows]
            remote(view, view, send.at[j], self.core_recv.at[j], {"seq": self.ring.core_peer}).wait_send()


class Agenda:
    def __init__(self):
        self.calls = {}

    def add(self, when, f, *args):
        self.calls.setdefault(when, []).append((f, args))

    def run(self, now):
        for when, calls in sorted(self.calls.items(), key=lambda item: item[0]):

            @pl.when(now == when)
            def _(calls=calls):
                for f, args in calls:
                    f(*args)


OPENING = (((0, 0, 0), (0, 0, 1), (0, 0, 3), (0, 0, 2), (1, 0, 0), (1, 0, 1), (1, 0, 3), (1, 0, 2), (2, 0, 0), (2, 0, 1),
            (2, 0, 3), (2, 0, 2), (3, 0, 0), (3, 0, 1), (3, 0, 3), (4, 0, 0), (3, 0, 2), (0, 1, 0), (0, 1, 1), (0, 1, 3),
            (5, 0, 0)),)
FIRST = OPENING + (
    ((4, 0, 1), (4, 0, 3), (0, 1, 2)),
    ((4, 0, 2), (1, 1, 0)),
    ((5, 0, 1), (5, 0, 3), (1, 1, 1), (1, 1, 3)),
    ((5, 0, 2), (1, 1, 2)),
)
SECOND = (
    ((2, 1, 0), (2, 1, 1), (2, 1, 3)),
    ((2, 1, 2), (3, 1, 0)),
    ((3, 1, 1), (3, 1, 3), (4, 1, 0)),
)
LATER = (
    ((5, 0, 0), (3, 0, 2)),
    ((4, 0, 1), (4, 0, 3), (0, 1, 0)),
    ((4, 0, 2), (0, 1, 1), (0, 1, 3)),
    ((5, 0, 1), (5, 0, 3), (0, 1, 2)),
    ((5, 0, 2), (1, 1, 0), (1, 1, 1), (1, 1, 3), (1, 1, 2)),
)


def plan_gather(agenda, net, layers, mats, count, load):
    far = net.ring.n // 2

    def hops(j, quarter):
        for h in range(quarter * far // 4, (quarter + 1) * far // 4):
            net.arrived(j, h)
        cross(j, quarter - 1)

    def cross(j, quarter):
        for h in range(max(quarter, 0) * far // 4, (quarter + 1) * far // 4):
            net.crossed(j, h)

    def complete(j):
        cross(j, 3)
        net.swapped(j)
        load(j).start()

    for k in range(layers):
        for q, calls in enumerate((LATER if k else FIRST) + SECOND):
            for what, ahead, m in calls:
                if k + ahead < layers:
                    j = (k + ahead) * mats + m
                    when = 2 * count * k + q * count // 4
                    if what == 0:
                        agenda.add(when, net.own, j)
                    elif what == 5:
                        agenda.add(when, complete, j)
                    else:
                        agenda.add(when, hops, j, what - 1)


def forward_kernel(n, n_seq, layers, rows, paired, *refs):
    doc_ref, tok_ref = refs[:2]
    mats = 4
    given, table_ref, refs = refs[2 : 2 + mats], refs[2 + mats], refs[3 + mats :]
    if paired:
        gathered, refs = refs[: layers * mats], refs[layers * mats :]
    (xin_ref, proj_ref, pg_ref, normed_ref, starts_ref, state_ref, mixed_ref, mid_ref, normed2_ref, gu_ref, hid_ref,
     out_ref) = refs[:12]
    (xs, hs, cum, pg, ends, tot, src, lam, run, carry, buf, *rest) = refs[12:]
    weights, (load_sem, carry_send, carry_recv), sems = rest[:mats], rest[mats : mats + 3], rest[mats + 3 :]
    layer, step = pl.program_id(0), pl.program_id(1)
    tokens, width = tok_ref.shape
    count = xs.shape[0]
    tiles = count // rows
    now = layer * (2 * count) + step
    me = lax.axis_index("seq")
    peers = [{"seq": lax.rem(me + k, n_seq)} for k in range(1, n_seq)]
    agenda = Agenda()

    def load(j):
        source = gathered[j] if paired else given[j % mats].at[j // mats]
        return pltpu.make_async_copy(source, weights[j % mats], load_sem.at[j % mats])

    def ready(j):
        load(j).wait()

    if paired:
        ring = Ring(n)
        jobs = [
            (given[m].at[k], gathered[k * mats + m], given[m].shape[1] // 6)
            for k in range(layers) for m in range(mats)
        ]
        net = Gather(ring, jobs, sems)
        agenda.add(0, meet, [{"batch": ring.ahead(1)}, {"batch": ring.ahead(-1)}] + peers)
        plan_gather(agenda, net, layers, mats, count, load)
    else:
        agenda.add(0, meet, peers)
        for k in range(layers):
            agenda.add(2 * count * k, lambda k=k: load(k * mats).start())
            for m in range(1, mats):
                agenda.add(2 * count * k + count - 1, lambda j=k * mats + m: load(j).start())
    for k in range(layers):
        agenda.add(2 * count * k, ready, k * mats)
        for m in range(1, mats):
            agenda.add(2 * count * k + count, ready, k * mats + m)
    agenda.run(now)

    tile = lax.rem(step, count)
    row, at_row = tile // tiles, lax.rem(tile, tiles)
    start = (me * tiles + at_row) * tokens
    gains, gate = table_ref.at[layer, 0:8], table_ref.at[layer, 8:16, 0 : width // 2]

    @pl.when((layer == 0) & (step < count))
    def _():
        xs[tile] = dot(order_matrix(tokens, False), tok_ref[...])

    @pl.when(step < count)
    def _():
        x = xs[tile]
        xin_ref[...] = x.astype(BF16)
        enter_tile(doc_ref, row, at_row, start, x, weights[0], gains, gate, proj_ref, pg.at[tile], normed_ref, hs.at[tile],
                   cum.at[tile], ends.at[tile], tot.at[row], src, lam)
        pg_ref[...] = pg[tile]

    def exchange():
        return carry_copies(n_seq, me, tot.at[row], buf.at[layer, row], carry_send.at[layer, row], carry_recv.at[layer, row])

    @pl.when((step < count) & (lax.rem(step, tiles) == tiles - 1))
    def _():
        for copy in exchange():
            copy.start()

    @pl.when((step >= count) & (lax.rem(step, tiles) == 0))
    def _():
        for copy in exchange():
            copy.wait()
        combine(n_seq, me, True, buf.at[layer, row], gate.at[5:8], carry.at[row])

    @pl.when(step >= count)
    def _():
        out = leave_tile(at_row, xs[tile], pg.at[tile], hs.at[tile], cum.at[tile], ends.at[tile], carry.at[row],
                         weights[1], weights[2], weights[3], gains, gate, starts_ref, state_ref, mixed_ref, mid_ref,
                         normed2_ref, gu_ref, hid_ref, run)
        xs[tile] = out

        @pl.when(layer == layers - 1)
        def _():
            out_ref[...] = dot(order_matrix(tokens, True), out.astype(BF16)).astype(BF16)

    if paired:

        @pl.when(now == layers * 2 * count - 1)
        def _():
            for j in range(layers * mats):
                net.sent(j)


def tile_specs(tokens, layer):
    def flat(w, when, col=0):
        return pl.BlockSpec((None, tokens, w), lambda k, s: (layer(k), when(s), col))

    def few(r, w, when):
        return pl.BlockSpec((None, None, r, w), lambda k, s: (layer(k), when(s), 0, 0))

    return flat, few


def run_forward(n, n_seq, paired, rows, tokens, docs, x, sources, table):
    layers = sources[0].shape[0]
    total, width = x.shape
    chan = width // 2
    hidden = sources[2].shape[2] // 2
    count = total // tokens
    mats = len(sources)
    jobs = layers * mats if paired else 0
    shape = jax.ShapeDtypeStruct
    dma = pltpu.SemaphoreType.DMA
    any_ = pl.BlockSpec(memory_space=pl.ANY)

    def first(step):
        return jnp.minimum(step, count - 1)

    def second(step):
        return jnp.maximum(step - count, 0)

    flat, few = tile_specs(tokens, lambda k: k)

    def kept(w):
        return shape((layers, total, w), BF16)

    full = [((n if paired else 1) * w.shape[1], w.shape[2]) for w in sources]
    last = layers - 1
    outs = pl.pallas_call(
        functools.partial(forward_kernel, n, n_seq, layers, rows, paired),
        grid=(layers, 2 * count),
        in_specs=[
            pl.BlockSpec(memory_space=pltpu.SMEM),
            pl.BlockSpec((tokens, width), lambda k, s: (jnp.where(k == 0, first(s), count - 1), 0)),
        ]
        + [any_] * mats
        + [whole(*table.shape)],
        out_specs=[any_] * jobs
        + [
            flat(width, first),
            flat(3 * chan, first),
            flat(width, first),
            flat(width, first),
            few(8, width, second),
            flat(width, second),
            flat(width, second),
            flat(width, second),
            flat(width, second),
            flat(2 * hidden, second),
            flat(hidden, second),
            pl.BlockSpec((tokens, width), lambda k, s: (jnp.where(k == last, second(s), 0), 0)),
        ],
        out_shape=[shape(f, BF16) for _ in range(layers) for f in full][:jobs]
        + [
            kept(width),
            kept(3 * chan),
            kept(width),
            kept(width),
            shape((layers, count, 8, width), F32),
            kept(width),
            kept(width),
            kept(width),
            kept(width),
            kept(2 * hidden),
            kept(hidden),
            shape((total, width), BF16),
        ],
        scratch_shapes=[
            pltpu.VMEM((count, tokens, width), F32),
            pltpu.VMEM((count, width // LANES, tokens, LANES), F32),
            pltpu.VMEM((count, chan // LANES, tokens, LANES), F32),
            pltpu.VMEM((count, tokens, width), BF16),
            pltpu.VMEM((count, 24, chan), F32),
            pltpu.VMEM((rows, 8, chan), F32),
            pltpu.VMEM((width // LANES, tokens, LANES), F32),
            pltpu.VMEM((chan // LANES, tokens, LANES), F32),
            pltpu.VMEM((8, chan), F32),
            pltpu.VMEM((rows, 8, chan), F32),
            pltpu.VMEM((layers, rows, n_seq - 1, 8, chan), F32),
        ]
        + [pltpu.VMEM(f, BF16) for f in full]
        + [dma((mats,)), dma((layers, rows, n_seq - 1)), dma((layers, rows, n_seq - 1))]
        + [dma((s,)) if one else dma((s, n - 1)) for s in [max(jobs, 1)] for one in (1, 1, 0, 1, 0, 1, 1)],
        compiler_params=pltpu.CompilerParams(collective_id=3, has_side_effects=True, vmem_limit_bytes=LIMIT),
    )(docs, x, *sources, table)
    return outs[:jobs], outs[jobs:]


def backward_kernel(n_seq, layers, rows, mats, *refs):
    doc_ref, cot_ref = refs[:2]
    given, refs = refs[2 : 2 + layers * mats], refs[2 + layers * mats :]
    (table_ref, gu_ref, mid_ref, state_ref, pg_ref, pf_ref, x_ref, proj_ref, starts_ref, prior_ref, dz_ref,
     dgu_ref, dy_ref, dproj_ref, dtok_ref, small_ref) = refs[:16]
    (dxs, gs, cum, lam, dpg, ends, tot, grad, run, carry, buf, *rest) = refs[16:]
    weights, (load_sem, carry_send, carry_recv) = rest[:mats], rest[mats:]
    turn, step = pl.program_id(0), pl.program_id(1)
    layer = layers - 1 - turn
    tokens, width = cot_ref.shape
    count = dxs.shape[0]
    tiles = count // rows
    now = turn * (2 * count) + step
    me = lax.axis_index("seq")
    agenda = Agenda()

    def load(t, m):
        return pltpu.make_async_copy(given[(layers - 1 - t) * mats + m], weights[m], load_sem.at[m])

    def fetch(t, m):
        load(t, m).start()

    def ready(t, m):
        load(t, m).wait()

    for m in (3, 2, 1):
        agenda.add(0, fetch, 0, m)
    agenda.add(0, meet, [{"seq": lax.rem(me + k, n_seq)} for k in range(1, n_seq)])
    for t in range(layers):
        begin = 2 * count * t
        agenda.add(begin, fetch, t, 0)
        for m in (3, 2, 1):
            agenda.add(begin, ready, t, m)
        agenda.add(begin + count, ready, t, 0)
        if t + 1 < layers:
            for m in (3, 2, 1):
                agenda.add(begin + count, fetch, t + 1, m)
    agenda.run(now)

    tile = count - 1 - lax.rem(step, count)
    row, at_row = tile // tiles, lax.rem(tile, tiles)
    start = (me * tiles + at_row) * tokens
    gains, gate = table_ref.at[layer, 0:8], table_ref.at[layer, 8:16, 0 : width // 2]

    @pl.when(step == 0)
    def _():
        small_ref[...] = jnp.zeros_like(small_ref)

    @pl.when((turn == 0) & (step < count))
    def _():
        dxs[tile] = dot(order_matrix(tokens, False), cot_ref[...])

    @pl.when(step < count)
    def _():
        back_out_tile(doc_ref, row, at_row, start, tiles - 1, dxs.at[tile], gu_ref, mid_ref, state_ref, pg_ref, pf_ref,
                      weights[1], weights[2], weights[3], gains, gate, dz_ref, dgu_ref, dy_ref, dpg.at[tile],
                      lam.at[tile], gs.at[tile], cum.at[tile], ends.at[tile], tot.at[row], small_ref, grad)

    def exchange():
        return carry_copies(n_seq, me, tot.at[row], buf.at[turn, row], carry_send.at[turn, row], carry_recv.at[turn, row])

    @pl.when((step < count) & (lax.rem(step, tiles) == tiles - 1))
    def _():
        for copy in exchange():
            copy.start()

    @pl.when((step >= count) & (lax.rem(step, tiles) == 0))
    def _():
        for copy in exchange():
            copy.wait()
        combine(n_seq, me, False, buf.at[turn, row], gate.at[5:8], carry.at[row])

    @pl.when(step >= count)
    def _():
        back_in_tile(doc_ref, row, at_row, start, tiles - 1, dxs.at[tile], x_ref, proj_ref, dpg.at[tile], lam.at[tile],
                     starts_ref, prior_ref, gs.at[tile], cum.at[tile], ends.at[tile], carry.at[row], weights[0],
                     gains, gate, dproj_ref, small_ref, run)

        @pl.when(turn == layers - 1)
        def _():
            dx = dxs[tile]
            high = dx.astype(BF16)
            low = (dx - high.astype(F32)).astype(BF16)
            order = order_matrix(tokens, True)
            dtok_ref[...] = dot(order, high) + dot(order, low)


def run_backward(n_seq, rows, tokens, docs, cotangent, weights, table, kept):
    x, proj, p_g, starts, state, mid, gu = kept
    layers, total, width = x.shape
    chan = width // 2
    hidden = gu.shape[2] // 2
    count = total // tokens
    mats = len(weights) // layers
    shape = jax.ShapeDtypeStruct
    dma = pltpu.SemaphoreType.DMA
    any_ = pl.BlockSpec(memory_space=pl.ANY)
    last = layers - 1

    def first(step):
        return count - 1 - jnp.minimum(step, count - 1)

    def second(step):
        return count - 1 - jnp.maximum(step - count, 0)

    flat, few = tile_specs(tokens, lambda k: last - k)
    return pl.pallas_call(
        functools.partial(backward_kernel, n_seq, layers, rows, mats),
        grid=(layers, 2 * count),
        in_specs=[
            pl.BlockSpec(memory_space=pltpu.SMEM),
            pl.BlockSpec((tokens, width), lambda k, s: (jnp.where(k == 0, first(s), 0), 0)),
        ]
        + [any_] * len(weights)
        + [
            whole(*table.shape),
            flat(2 * hidden, first),
            flat(width, first),
            flat(width, first),
            flat(width, first),
            flat(chan, first, 2),
            flat(width, second),
            flat(3 * chan, second),
            few(8, width, second),
            flat(width, second),
        ],
        out_specs=[
            flat(width, first),
            flat(2 * hidden, first),
            flat(width, first),
            flat(3 * chan + width, second),
            pl.BlockSpec((tokens, width), lambda k, s: (jnp.where(k == last, second(s), count - 1), 0)),
            pl.BlockSpec((None, 32, width), lambda k, s: (last - k, 0, 0)),
        ],
        out_shape=[
            shape((layers, total, width), BF16),
            shape((layers, total, 2 * hidden), BF16),
            shape((layers, total, width), BF16),
            shape((layers, total, 3 * chan + width), BF16),
            shape((total, width), F32),
            shape((layers, 32, width), F32),
        ],
        scratch_shapes=[
            pltpu.VMEM((count, tokens, width), F32),
            pltpu.VMEM((count, width // LANES, tokens, LANES), F32),
            pltpu.VMEM((count, chan // LANES, tokens, LANES), F32),
            pltpu.VMEM((count, chan // LANES, tokens, LANES), F32),
            pltpu.VMEM((count, tokens, width), BF16),
            pltpu.VMEM((count, 24, chan), F32),
            pltpu.VMEM((rows, 8, chan), F32),
            pltpu.VMEM((width // LANES, tokens, LANES), F32),
            pltpu.VMEM((8, chan), F32),
            pltpu.VMEM((rows, 8, chan), F32),
            pltpu.VMEM((layers, rows, n_seq - 1, 8, chan), F32),
        ]
        + [pltpu.VMEM(w.shape, BF16) for w in weights[:mats]]
        + [dma((mats,)), dma((layers, rows, n_seq - 1)), dma((layers, rows, n_seq - 1))],
        compiler_params=pltpu.CompilerParams(collective_id=2, has_side_effects=True, vmem_limit_bytes=LIMIT),
    )(docs, cotangent, *weights, table, gu, mid, state, p_g, proj, x, proj, starts, state)


def add_rows(dst, dst_row, parts, rows):
    def block(i, _):
        step = pl.multiple_of(i * 16, 16)
        total = None
        for ref, first in parts:
            value = ref[pl.ds(pl.multiple_of(first + step, 16), 16), :].astype(F32)
            total = value if total is None else total + value
        dst[pl.ds(pl.multiple_of(dst_row + step, 16), 16), :] = total.astype(dst.dtype)
        return 0

    lax.fori_loop(0, rows // 16, block, 0)


def grads_kernel(n, plan, *refs):
    jobs = len(plan)
    lefts, rights, small = refs[:jobs], refs[jobs : 2 * jobs], refs[2 * jobs]
    outs_count = 1 + max(p[0] for p in plan)
    outs, rest = refs[2 * jobs + 1 : 2 * jobs + 1 + outs_count], refs[2 * jobs + 1 + outs_count :]
    gains_out, gate_out, rest = rest[0], rest[1], rest[2:]
    grads, core_buf, y_buf, ring_buf, fin_buf = (rest[i * jobs : (i + 1) * jobs] for i in range(5))
    (left_big, left_small, right_buf, small_buf, left_sem, right_sem, core_send, core_recv, y_send, y_recv,
     ring_send, ring_recv, end_send, end_recv, small_send, small_recv) = rest[5 * jobs :]
    ring = Ring(n)
    far, near = n // 2, n - 1 - n // 2
    core_dev, y_dev = {"seq": ring.core_peer}, {"seq": ring.y_peer}
    y, core = ring.y, ring.core
    rounds = [core_dev, y_dev]
    d = 1
    while d < n:
        rounds.append({"batch": ring.batch + d * (1 - 2 * ((ring.batch // d) % 2))})
        d *= 2
    us = [g.shape[0] // n // 6 for g in grads]
    split = [p[2] for p in plan]
    own_rows = [(2 if s else 3) * u for s, u in zip(split, us)]

    def left_copy(j):
        buf = (left_big, left_small)[j % 2]
        return pltpu.make_async_copy(lefts[j].at[plan[j][1]], buf.at[:, 0 : plan[j][3]], left_sem.at[j % 2])

    chunks = []
    for j, (_, _, _, rows, cols) in enumerate(plan):
        first = 0
        while first < cols:
            size = min(CHUNK, cols - first)
            chunks.append((j, first, size, first + size == cols))
            first += size

    def right_copy(i):
        j, first, size, _ = chunks[i]
        return pltpu.make_async_copy(
            rights[j].at[plan[j][1], :, first : first + size], right_buf.at[i % 2, :, 0:size], right_sem.at[i % 2]
        )

    left_copy(0).start()
    right_copy(0).start()
    right_copy(1).start()
    left_copy(1).start()
    meet([{"batch": ring.ahead(1)}, {"batch": ring.ahead(-1)}] + rounds)

    order = []
    for h in range(far):
        order.append((1, h, far - h))
        if h < near:
            order.append((-1, h, near - h))
    order.append((0, 0, 0))
    last = len(order)

    def rows_at(ref, first, rows):
        return ref.at[pl.ds(pl.multiple_of(first, 16), rows)]

    def core_copy(j, slot, piece):
        u = us[j]
        return remote(rows_at(grads[j], piece * (6 * u) + (1 - core) * (3 * u), 3 * u),
                      core_buf[j].at[slot], core_send.at[j], core_recv.at[j, slot], core_dev)

    def y_copy(j, slot, piece):
        u = us[j]
        src = rows_at(grads[j], piece * (6 * u) + core * (3 * u) + 2 * (1 - y) * u, u)
        return remote(src, y_buf[j].at[slot], y_send.at[j], y_recv.at[j, slot], y_dev)

    def mine(j, piece):
        u = us[j]
        return piece * (6 * u) + core * (3 * u) + (y * u if split[j] else 0)

    def ring_copy(j, slot, way, piece):
        return remote(rows_at(grads[j], mine(j, piece), own_rows[j]), ring_buf[j].at[slot], ring_send.at[j],
                      ring_recv.at[j, slot], {"batch": ring.ahead(way)})

    def small_round(r):
        return remote(small_buf.at[2 * r], small_buf.at[2 * r + 1], small_send.at[r], small_recv.at[r], rounds[r])

    layers = small.shape[0]
    for k in range(layers):
        for i in range(4):
            small_buf[0, 4 * k + i : 4 * k + i + 1, :] = jnp.sum(small[k, 8 * i : 8 * i + 8, :], axis=0, keepdims=True)
    small_round(0).start()

    def small_step(r):
        small_round(r).wait_recv()
        total = small_buf[2 * r] + small_buf[2 * r + 1]
        if r + 1 < len(rounds):
            small_buf[2 * r + 2] = total
            small_round(r + 1).start()
        else:
            chan = gate_out.shape[2]
            for k in range(layers):
                gains_out[k] = total[4 * k : 4 * k + 3, :]
                gate_out[k, 0:1, :] = total[4 * k + 3 : 4 * k + 4, :chan]
                gate_out[k, 1:2, :] = total[4 * k + 3 : 4 * k + 4, chan:]

    def begin(j):
        for slot, (way, h, dist) in enumerate(order):
            core_copy(j, slot, ring.ahead(-way * dist)).start()

    def cross(j, slot):
        way, h, dist = order[slot]
        piece = ring.ahead(way * dist)
        u = us[j]
        core_copy(j, slot, piece).wait_recv()
        if not split[j]:
            return
        give = 2 * (1 - y) * u
        at = piece * (6 * u) + core * (3 * u) + give
        add_rows(grads[j], at, [(grads[j], at), (core_buf[j].at[slot], give)], u)
        y_copy(j, slot, piece).start()

    def hop(j, slot):
        way, h, dist = order[slot]
        piece = ring.ahead(way * dist)
        u = us[j]
        if split[j]:
            y_copy(j, slot, piece).wait_recv()
        if way == 0:
            prior = [i for i, o in enumerate(order) if o[2] == 1]
        elif h:
            prior = [i for i, o in enumerate(order) if o[0] == way and o[1] == h - 1]
        else:
            prior = []
        for i in prior:
            ring_copy(j, i, order[i][0], piece).wait_recv()
        at = mine(j, piece)
        base = [(grads[j], at), (core_buf[j].at[slot], y * u if split[j] else 0)]
        base += [(ring_buf[j].at[i], 0) for i in prior]
        if split[j]:
            for by, more in ((y * u, [(y_buf[j].at[slot], 0)]), ((1 - y) * u, [])):
                add_rows(grads[j], at + by, [(r, f + by) for r, f in base] + more, u)
        else:
            add_rows(grads[j], at, base, 3 * u)
        if way:
            ring_copy(j, slot, way, piece).start()

    def fin_copy(j):
        return remote(rows_at(grads[j], mine(j, ring.batch), own_rows[j]), fin_buf[j], end_send.at[j, 0],
                      end_recv.at[j, 0], y_dev)

    def half_copy(j):
        half = outs[plan[j][0]].at[plan[j][1], pl.ds(pl.multiple_of(core * (3 * us[j]), 16), 3 * us[j])]
        return remote(half, half, end_send.at[j, 1], end_recv.at[j, 1], core_dev)

    def finish(j):
        u = us[j]
        fin_copy(j).wait_recv()
        out = outs[plan[j][0]].at[plan[j][1]]
        at, to = mine(j, ring.batch), core * (3 * u)
        if split[j]:
            add_rows(out, to + 2 * y * u, [(grads[j], at + y * u)], u)
            add_rows(out, to + 2 * (1 - y) * u, [(fin_buf[j], (1 - y) * u)], u)
            add_rows(out, to + u, [(grads[j], at + (1 - y) * u), (fin_buf[j], y * u)], u)
        else:
            add_rows(out, to, [(grads[j], at), (fin_buf[j], 0)], 3 * u)
        half_copy(j).start()

    steps = far + 4

    def advance(j, t):
        now = [i for i, o in enumerate(order) if o[0] and o[1] == t]
        before = [i for i, o in enumerate(order) if o[0] and o[1] == t - 1]
        for slot in before:
            hop(j, slot)
        for slot in now:
            cross(j, slot)
        if t == far - 1:
            cross(j, last - 1)
        if t == far + 1:
            hop(j, last - 1)
            fin_copy(j).start()
        if t == far + 2:
            finish(j)
        if t == far + 3:
            half_copy(j).wait_recv()

    stage = {}

    def advance_all(turn):
        for j in list(stage):
            if j % 2 == turn:
                advance(j, stage[j])
                stage[j] += 1
                if stage[j] == steps:
                    del stage[j]

    small_at = 0
    for i, (j, first, size, done) in enumerate(chunks):
        if first == 0:
            left_copy(j).wait()
        right_copy(i).wait()
        left = (left_big, left_small)[j % 2]

        def multiply(b, _, i=i, j=j, first=first, size=size, left=left):
            at = pl.multiple_of(b * 256, 256)
            part = lax.dot_general(
                left[:, pl.ds(at, 256)], right_buf[i % 2, :, 0:size], (((0,), (0,)), ((), ())),
                preferred_element_type=F32,
            )
            grads[j][pl.ds(at, 256), first : first + size] = part.astype(BF16)
            return 0

        lax.fori_loop(0, plan[j][3] // 256, multiply, 0)
        if i + 2 < len(chunks):
            right_copy(i + 2).start()
        if done and j + 2 < jobs:
            left_copy(j + 2).start()
        advance_all(i % 2)
        if done:
            begin(j)
            stage[j] = 0
        if small_at < len(rounds):
            small_step(small_at)
            small_at += 1
    i = 0
    while stage:
        advance_all(i % 2)
        i += 1
    while small_at < len(rounds):
        small_step(small_at)
        small_at += 1
    for j in range(jobs):
        u = us[j]
        fin_copy(j).wait_send()
        half_copy(j).wait_send()
        remote(core_buf[j], core_buf[j], core_send.at[j], core_recv.at[j, 0], core_dev).wait_send()
        if split[j]:
            remote(y_buf[j], y_buf[j], y_send.at[j], y_recv.at[j, 0], y_dev).wait_send()
        remote(ring_buf[j], ring_buf[j], ring_send.at[j], ring_recv.at[j, 0], core_dev).wait_send()
    for r in range(len(rounds)):
        small_round(r).wait_send()


def grads_and_scatter(n, plan, lefts, rights, small):
    jobs = len(plan)
    plan = [p + (a.shape[2], b.shape[2]) for p, a, b in zip(plan, lefts, rights)]
    tokens = lefts[0].shape[1]
    layers, _, width = small.shape
    dma = pltpu.SemaphoreType.DMA
    rounds = 2 + (n - 1).bit_length()
    sizes = [(p[3] // n // 6, p[4], p[2]) for p in plan]
    outs = {p[0]: jax.ShapeDtypeStruct((layers, p[3] // n, p[4]), BF16) for p in plan}
    vm = pl.BlockSpec(memory_space=pltpu.VMEM)
    any_ = pl.BlockSpec(memory_space=pl.ANY)

    def bufs(f):
        return [pltpu.VMEM(f(u, w, s), BF16) for u, w, s in sizes]

    return pl.pallas_call(
        functools.partial(grads_kernel, n, plan),
        out_shape=[outs[m] for m in sorted(outs)]
        + [jax.ShapeDtypeStruct((layers, 3, width), F32), jax.ShapeDtypeStruct((layers, 2, width // 2), F32)],
        in_specs=[any_] * (2 * jobs) + [vm],
        out_specs=[vm] * (len(outs) + 2),
        scratch_shapes=bufs(lambda u, w, s: (6 * u * n, w))
        + bufs(lambda u, w, s: (n, 3 * u, w))
        + bufs(lambda u, w, s: (n if s else 1, u, w))
        + bufs(lambda u, w, s: (n - 1, 2 * u if s else 3 * u, w))
        + bufs(lambda u, w, s: (2 * u if s else 3 * u, w))
        + [
            pltpu.VMEM((tokens, max(p[3] for p in plan[0::2])), BF16),
            pltpu.VMEM((tokens, max(p[3] for p in plan[1::2])), BF16),
            pltpu.VMEM((2, tokens, CHUNK), BF16),
            pltpu.VMEM((2 * rounds, 4 * layers, width), F32),
            dma((2,)), dma((2,)), dma((jobs,)), dma((jobs, n)), dma((jobs,)), dma((jobs, n)), dma((jobs,)),
            dma((jobs, n)), dma((jobs, 2)), dma((jobs, 2)), dma((rounds,)), dma((rounds,)),
        ],
        compiler_params=pltpu.CompilerParams(
            collective_id=4, has_side_effects=True, vmem_limit_bytes=63 * 1024 * 1024
        ),
    )(*lefts, *rights, small)


def contract_rows(left, right):
    return lax.dot_general(
        left, right, (((0,), (0,)), ((), ())), preferred_element_type=F32
    ).astype(BF16)


def shards(
    tokens_in, doc_starts, mixer_in, mixer_out, ffn_in, ffn_out, gains, gate_params, cotangent
):
    rows, length, width = tokens_in.shape
    layers = gains.shape[0]
    chan = width // 2
    total = rows * length
    tokens = min(length, 256)
    seg = tokens // 8
    n, n_seq = lax.axis_size("batch"), lax.axis_size("seq")
    sources = (mixer_in, mixer_out, ffn_in, ffn_out)
    paired = n_seq == 4 and n % 4 == 0 and all(w.shape[1] % 96 == 0 for w in sources)
    theta, lower = gate_params[:, 0:1], gate_params[:, 1:2]
    at = lax.broadcasted_iota(jnp.int32, (layers, 8, chan), 1)
    times = jnp.where(at < 3, 1, jnp.where(at < 5, seg, length)).astype(F32)
    quarter = jnp.where((at == 1) | (at == 4) | (at == 6), math.pi / 2, 0.0)
    gate_rows = jnp.where(at == 2, lower, jnp.cos(theta * times - quarter))
    table = jnp.concatenate(
        [jnp.pad(gains, ((0, 0), (0, 5), (0, 0))), jnp.pad(gate_rows, ((0, 0), (0, 0), (0, width - chan)))], axis=1
    )
    x = tokens_in.reshape(total, width)
    if paired:
        weights, kept = run_forward(n, n_seq, True, rows, tokens, doc_starts, x, sources, table)
    else:
        stacked = [lax.all_gather(w, "batch", axis=1, tiled=True) for w in sources]
        weights = [w[k] for k in range(layers) for w in stacked]
        _, kept = run_forward(n, n_seq, False, rows, tokens, doc_starts, x, stacked, table)
    x_in, proj, p_g, normed, starts, state, mixed, mid, normed2, gu, hid, block_out = kept
    dz, d_gu, dy, d_proj, d_tokens, small = run_backward(
        n_seq, rows, tokens, doc_starts, cotangent.reshape(total, width), weights, table,
        (x_in, proj, p_g, starts, state, mid, gu),
    )
    pairs = ((normed, d_proj), (mixed, dy), (normed2, d_gu), (hid, dz))
    if paired:
        plan = []
        for k in reversed(range(layers)):
            plan += [(m, k, m != 0) for m in ((1, 2, 3, 0) if k == layers - 1 else (3, 2, 0, 1))]
        *outs, d_gains, d_gate = grads_and_scatter(
            n, plan, [pairs[m][0] for m, _, _ in plan], [pairs[m][1] for m, _, _ in plan], small
        )
    else:
        outs = []
        for left, right in pairs:
            whole_grads = jnp.stack([contract_rows(left[k], right[k]) for k in range(layers)])
            part = lax.psum_scatter(whole_grads, "batch", scatter_dimension=1, tiled=True)
            outs.append(lax.psum(part, "seq"))
        totals = lax.psum(jnp.sum(small.reshape(layers, 4, 8, width), axis=2), ("batch", "seq"))
        d_gains, d_gate = totals[:, :3], totals[:, 3].reshape(layers, 2, chan)
    return (
        block_out.reshape(rows, length, width),
        d_tokens.reshape(rows, length, width),
        *[o.astype(F32) for o in outs],
        d_gains,
        d_gate,
    )


def solution(mesh):
    tok = P("batch", "seq", None)
    mat = P(None, "batch", None)
    return jax.shard_map(
        shards,
        mesh=mesh,
        in_specs=(tok, P("batch", None), mat, mat, mat, mat, P(), P(), tok),
        out_specs=(tok, tok, mat, mat, mat, mat, P(), P()),
        check_vma=False,
    )
```

```python
import functools
import math

import jax
import jax.numpy as jnp
from jax import lax
from jax.experimental import pallas as pl
from jax.experimental.pallas import tpu as pltpu
from jax.sharding import PartitionSpec as P

EPS = 1e-06
F32 = jnp.float32
BF16 = jnp.bfloat16
LANES = 128
CHUNK = 768
ORDERS = (((1, 0, 1), (2, 0, 2), (3, 0, 1), (2, 1, 2), (0, 0, 1)), ((2, 0, 2), (3, 0, 1), (2, 1, 2), (0, 0, 1), (1, 0, 1)))
MESH = pl.DeviceIdType.MESH


def sigmoid(values):
    return 1.0 / (1.0 + jnp.exp(-values))


def rms_scale(values):
    return lax.rsqrt(jnp.mean(values * values, axis=-1, keepdims=True) + EPS)


def dot(left, right):
    return jnp.dot(left, right, preferred_element_type=F32)


def dot_t(left, right):
    return lax.dot_general(left, right, (((1,), (1,)), ((), ())), preferred_element_type=F32)


def eight_sum(values):
    rows, cols = values.shape
    return jnp.sum(values.reshape(rows // 8, 8, cols), axis=0)


def wide(ref, first, last):
    return jnp.concatenate([ref[g] for g in range(first, last)], axis=-1)


def split_store(ref, first, values):
    for g in range(values.shape[1] // LANES):
        ref[first + g] = values[:, g * LANES : (g + 1) * LANES]


def lanes(values):
    return [values[:, g * LANES : (g + 1) * LANES] for g in range(values.shape[1] // LANES)]


LIMIT = 60 * 1024 * 1024


def whole(*shape):
    return pl.BlockSpec(shape, lambda *_: (0,) * len(shape), pipeline_mode=pl.Buffered(1))


def order_matrix(tokens, back):
    shape = (tokens, tokens)
    here = lax.broadcasted_iota(jnp.int32, shape, 1 if back else 0)
    there = lax.broadcasted_iota(jnp.int32, shape, 0 if back else 1)
    return jnp.where(there == (here & 7) * (tokens // 8) + (here >> 3), 1.0, 0.0).astype(BF16)


def reset_mask(doc_ref, row, first, tokens):
    here = lax.broadcasted_iota(jnp.int32, (tokens, LANES), 0)
    pos = (here & 7) * (tokens // 8) + (here >> 3) + first
    hit = pos == doc_ref[row, 0]
    for k in range(1, doc_ref.shape[1]):
        hit = hit | (pos == doc_ref[row, k])
    return hit


def retain(doc_ref, row, first, p_f, lower):
    tokens, chan = p_f.shape
    forget = sigmoid(p_f)
    lam = lower + (1.0 - lower) * forget
    keep = jnp.where(reset_mask(doc_ref, row, first, tokens), 0.0, 1.0)
    return lam * jnp.concatenate([keep] * (chan // LANES), axis=-1), forget, keep


def pieces(total):
    size = 512 if total % 512 == 0 else total
    return [slice(first, first + size) for first in range(0, total, size)]


def moved(part, by):
    return slice(part.start + by, part.stop + by)


def at_step(s):
    return pl.ds(pl.multiple_of(s * 8, 8), 8)


def enter_tile(doc_ref, row, tile, start, x, w_ref, gain_ref, gate_ref, proj_ref, pg_ref, normed_ref, h_ref, cum_ref,
               ends_ref, tot_ref, src, lam_ref):
    tokens, width = x.shape
    chan = width // 2
    seg = tokens // 8
    groups = chan // LANES
    normed = (x * rms_scale(x) * gain_ref[0:1, :]).astype(BF16)
    normed_ref[...] = normed
    p_f = dot(normed, w_ref[:, 2 * chan : 3 * chan])
    p_c = dot(normed, w_ref[:, : 2 * chan])
    proj_ref[:, 2 * chan :] = p_f.astype(BF16)
    cos, sin, lower = gate_ref[0:1, :], gate_ref[1:2, :], gate_ref[2:3, :]
    seg_cos, seg_sin = gate_ref[3:4, :], gate_ref[4:5, :]
    lam, _, _ = retain(doc_ref, row, start, p_f, lower)
    split_store(lam_ref, 0, lam)
    pg_ref[...] = dot(normed, w_ref[:, 3 * chan :]).astype(BF16)
    proj_ref[:, : 2 * chan] = p_c.astype(BF16)
    p_r, p_i = p_c[:, :chan], p_c[:, chan:]
    split_store(src, 0, (1.0 - lam) * (p_r * sigmoid(p_r)))
    split_store(src, groups, (1.0 - lam) * (p_i * sigmoid(p_i)))
    cos_l, sin_l = lanes(cos), lanes(sin)

    def step(s, state):
        at = at_step(s)
        after = []
        for k, (h_r, h_i, cum) in enumerate(state):
            lam_s = lam_ref[k, at, :]
            a_r, a_i = lam_s * cos_l[k], lam_s * sin_l[k]
            n_r = a_r * h_r - a_i * h_i + src[k, at, :]
            n_i = a_r * h_i + a_i * h_r + src[groups + k, at, :]
            cum = cum * lam_s
            h_ref[k, at, :] = n_r
            h_ref[groups + k, at, :] = n_i
            cum_ref[k, at, :] = cum
            after.append((n_r, n_i, cum))
        return tuple(after)

    zero = lam_ref[0, 0:8, :] * 0.0
    last = lax.fori_loop(0, seg, step, ((zero, zero, zero + 1.0),) * groups, unroll=8)
    e_r, e_i, e_c = (jnp.concatenate([v[i] for v in last], axis=-1) for i in range(3))
    ends_ref[0:8, :] = e_r
    ends_ref[8:16, :] = e_i
    ends_ref[16:24, :] = e_c

    @pl.when(tile == 0)
    def _():
        tot_ref[0:2, :] = jnp.zeros((2, chan), F32)
        tot_ref[2:3, :] = jnp.ones((1, chan), F32)

    c_r, c_i, c_l = tot_ref[0:1, :], tot_ref[1:2, :], tot_ref[2:3, :]
    for j in range(8):
        m = e_c[j : j + 1, :]
        a_r, a_i = m * seg_cos, m * seg_sin
        c_r, c_i = a_r * c_r - a_i * c_i + e_r[j : j + 1, :], a_r * c_i + a_i * c_r + e_i[j : j + 1, :]
        c_l = c_l * m
    tot_ref[0:1, :] = c_r
    tot_ref[1:2, :] = c_i
    tot_ref[2:3, :] = c_l


def leave_tile(tile, x, pg_ref, h_ref, cum_ref, ends_ref, carry_ref, wo_ref, wf_ref, wd_ref, gain_ref, gate_ref,
               starts_ref, state_ref, mixed_ref, mid_ref, normed_ref, gu_ref, hid_ref, run):
    tokens, width = x.shape
    chan = width // 2
    seg = tokens // 8
    groups = chan // LANES
    cos, sin = gate_ref[0:1, :], gate_ref[1:2, :]
    seg_cos, seg_sin = gate_ref[3:4, :], gate_ref[4:5, :]

    @pl.when(tile == 0)
    def _():
        run[0:2, :] = carry_ref[0:2, :]

    c_r, c_i = run[0:1, :], run[1:2, :]
    l_r, l_i = [], []
    for j in range(8):
        l_r.append(c_r)
        l_i.append(c_i)
        m = ends_ref[16 + j : 17 + j, :]
        a_r, a_i = m * seg_cos, m * seg_sin
        c_r, c_i = (
            a_r * c_r - a_i * c_i + ends_ref[j : j + 1, :],
            a_r * c_i + a_i * c_r + ends_ref[8 + j : 9 + j, :],
        )
    run[0:1, :] = c_r
    run[1:2, :] = c_i
    start_r, start_i = jnp.concatenate(l_r, axis=0), jnp.concatenate(l_i, axis=0)
    starts_ref[...] = jnp.concatenate([start_r, start_i], axis=-1)
    cos_l, sin_l = lanes(cos), lanes(sin)

    def step(s, state):
        at = at_step(s)
        after = []
        for k, (w_r, w_i) in enumerate(state):
            w_r, w_i = w_r * cos_l[k] - w_i * sin_l[k], w_r * sin_l[k] + w_i * cos_l[k]
            cum = cum_ref[k, at, :]
            h_ref[k, at, :] += cum * w_r
            h_ref[groups + k, at, :] += cum * w_i
            after.append((w_r, w_i))
        return tuple(after)

    lax.fori_loop(0, seg, step, tuple(zip(lanes(start_r), lanes(start_i))), unroll=8)
    state = wide(h_ref, 0, 2 * groups)
    state_ref[...] = state.astype(BF16)
    p_g = pg_ref[...].astype(F32)
    mixed = (state * rms_scale(state) * gain_ref[1:2, :] * (p_g * sigmoid(p_g))).astype(BF16)
    mixed_ref[...] = mixed
    mid = x + dot(mixed, wo_ref[...])
    mid_ref[...] = mid.astype(BF16)
    normed = (mid * rms_scale(mid) * gain_ref[2:3, :]).astype(BF16)
    normed_ref[...] = normed
    hidden = wd_ref.shape[0]
    parts = pieces(hidden)

    def gate_up(part):
        return dot(normed, wf_ref[:, part]), dot(normed, wf_ref[:, moved(part, hidden)])

    after = gate_up(parts[0])
    for i, part in enumerate(parts):
        gate, up = after
        if i + 1 < len(parts):
            after = gate_up(parts[i + 1])
        gu_ref[:, part] = gate.astype(BF16)
        gu_ref[:, moved(part, hidden)] = up.astype(BF16)
        hid_ref[:, part] = (gate * sigmoid(gate) * up).astype(BF16)
    return mid + dot(hid_ref[...], wd_ref[...])


def back_out_tile(doc_ref, row, tile, start, last, dx_ref, gu_ref, mid_ref, state_ref, pg_ref, pf_ref, wo_ref, wf_ref,
                  wd_ref, gain_ref, gate_ref, dz_ref, dgu_ref, dy_ref, dpg_ref, lam_ref, g_ref, cum_ref, ends_ref,
                  tot_ref, small_ref, grad):
    tokens, width = dx_ref.shape
    chan = width // 2
    seg = tokens // 8
    groups = chan // LANES
    cos, sin, lower = gate_ref[0:1, :], gate_ref[1:2, :], gate_ref[2:3, :]
    seg_cos, seg_sin = gate_ref[3:4, :], gate_ref[4:5, :]
    dx = dx_ref[...]
    dz = dx.astype(BF16)
    dz_ref[...] = dz
    hidden = wd_ref.shape[0]
    parts = pieces(hidden)
    d_next = dot_t(dz, wd_ref[parts[0], :])
    for i, part in enumerate(parts):
        d_hid = d_next
        if i + 1 < len(parts):
            d_next = dot_t(dz, wd_ref[parts[i + 1], :])
        gate = gu_ref[:, part].astype(F32)
        up = gu_ref[:, moved(part, hidden)].astype(F32)
        sg = sigmoid(gate)
        silu = gate * sg
        dgu_ref[:, part] = (d_hid * up * (sg + silu * (1.0 - sg))).astype(BF16)
        dgu_ref[:, moved(part, hidden)] = (d_hid * silu).astype(BF16)
    d_n = dot_t(dgu_ref[...], wf_ref[...])
    mid = mid_ref[...].astype(F32)
    scale = rms_scale(mid)
    hat = mid * scale
    d_hat = d_n * gain_ref[2:3, :]
    small_ref[16:24, :] += eight_sum(d_n * hat)
    d_mid = dx + scale * (d_hat - hat * jnp.mean(d_hat * hat, axis=-1, keepdims=True))
    dx_ref[...] = d_mid
    dy = d_mid.astype(BF16)
    dy_ref[...] = dy
    d_mixed = dot_t(dy, wo_ref[...])
    p_g = pg_ref[...].astype(F32)
    sg = sigmoid(p_g)
    silu = p_g * sg
    state = state_ref[...].astype(F32)
    scale = rms_scale(state)
    hat = state * scale
    g1 = gain_ref[1:2, :]
    dpg_ref[...] = (d_mixed * hat * g1 * (sg + silu * (1.0 - sg))).astype(BF16)
    d_n = d_mixed * silu
    small_ref[8:16, :] += eight_sum(d_n * hat)
    d_hat = d_n * g1
    split_store(grad, 0, scale * (d_hat - hat * jnp.mean(d_hat * hat, axis=-1, keepdims=True)))
    lam, _, _ = retain(doc_ref, row, start, pf_ref[...].astype(F32), lower)
    split_store(lam_ref, 0, lam)
    cos_l, sin_l = lanes(cos), lanes(sin)

    def step(s, state):
        at = at_step(seg - 1 - s)
        after = []
        for k, (g_r, g_i, cum, lam_n) in enumerate(state):
            a_r, a_i = lam_n * cos_l[k], lam_n * sin_l[k]
            n_r = grad[k, at, :] + a_r * g_r + a_i * g_i
            n_i = grad[groups + k, at, :] + a_r * g_i - a_i * g_r
            cum = cum * lam_n
            g_ref[k, at, :] = n_r
            g_ref[groups + k, at, :] = n_i
            cum_ref[k, at, :] = cum
            after.append((n_r, n_i, cum, lam_ref[k, at, :]))
        return tuple(after)

    zero = lam_ref[0, 0:8, :] * 0.0
    final = lax.fori_loop(0, seg, step, ((zero, zero, zero + 1.0, zero + 1.0),) * groups, unroll=8)
    g_r, g_i, cum, lam_0 = (jnp.concatenate([v[i] for v in final], axis=-1) for i in range(4))
    e_r = lam_0 * (cos * g_r + sin * g_i)
    e_i = lam_0 * (cos * g_i - sin * g_r)
    e_c = lam_0 * cum
    ends_ref[0:8, :] = e_r
    ends_ref[8:16, :] = e_i
    ends_ref[16:24, :] = e_c

    @pl.when(tile == last)
    def _():
        tot_ref[0:2, :] = jnp.zeros((2, chan), F32)
        tot_ref[2:3, :] = jnp.ones((1, chan), F32)

    c_r, c_i, c_l = tot_ref[0:1, :], tot_ref[1:2, :], tot_ref[2:3, :]
    for j in reversed(range(8)):
        m = e_c[j : j + 1, :]
        a_r, a_i = m * seg_cos, m * seg_sin
        c_r, c_i = a_r * c_r + a_i * c_i + e_r[j : j + 1, :], a_r * c_i - a_i * c_r + e_i[j : j + 1, :]
        c_l = c_l * m
    tot_ref[0:1, :] = c_r
    tot_ref[1:2, :] = c_i
    tot_ref[2:3, :] = c_l


def back_in_tile(doc_ref, row, tile, start, last, dx_ref, x_ref, proj_ref, dpg_ref, lam_ref, starts_ref, state_ref, g_ref,
                 cum_ref, ends_ref, carry_ref, w_ref, gain_ref, gate_ref, dproj_ref, small_ref, run):
    tokens, width = dx_ref.shape
    chan = width // 2
    seg = tokens // 8
    groups = chan // LANES
    cos, sin, lower = gate_ref[0:1, :], gate_ref[1:2, :], gate_ref[2:3, :]
    seg_cos, seg_sin = gate_ref[3:4, :], gate_ref[4:5, :]

    @pl.when(tile == last)
    def _():
        run[0:2, :] = carry_ref[0:2, :]

    c_r, c_i = run[0:1, :], run[1:2, :]
    l_r, l_i = [None] * 8, [None] * 8
    for j in reversed(range(8)):
        l_r[j], l_i[j] = c_r, c_i
        m = ends_ref[16 + j : 17 + j, :]
        a_r, a_i = m * seg_cos, m * seg_sin
        c_r, c_i = (
            a_r * c_r + a_i * c_i + ends_ref[j : j + 1, :],
            a_r * c_i - a_i * c_r + ends_ref[8 + j : 9 + j, :],
        )
    run[0:1, :] = c_r
    run[1:2, :] = c_i
    cos_l, sin_l = lanes(cos), lanes(sin)

    def step(s, state):
        at = at_step(seg - 1 - s)
        after = []
        for k, (w_r, w_i) in enumerate(state):
            cum = cum_ref[k, at, :]
            g_ref[k, at, :] += cum * w_r
            g_ref[groups + k, at, :] += cum * w_i
            after.append((w_r * cos_l[k] + w_i * sin_l[k], w_i * cos_l[k] - w_r * sin_l[k]))
        return tuple(after)

    start_at = (jnp.concatenate(l_r, axis=0), jnp.concatenate(l_i, axis=0))
    lax.fori_loop(0, seg, step, tuple(zip(lanes(start_at[0]), lanes(start_at[1]))), unroll=8)
    d_n = dot_t(dpg_ref[...], w_ref[:, 3 * chan :])
    g_r, g_i = wide(g_ref, 0, groups), wide(g_ref, groups, 2 * groups)
    prior = jnp.concatenate([starts_ref[...], state_ref[...].astype(F32)[: tokens - 8, :]], axis=0)
    q_r, q_i = prior[:, :chan], prior[:, chan:]
    p_r = proj_ref[:, :chan].astype(F32)
    p_i = proj_ref[:, chan : 2 * chan].astype(F32)
    _, forget, keep = retain(doc_ref, row, start, proj_ref[:, 2 * chan :].astype(F32), lower)
    lam = wide(lam_ref, 0, groups)
    d_ar = g_r * q_r + g_i * q_i
    d_ai = g_i * q_r - g_r * q_i
    s_r, s_i = sigmoid(p_r), sigmoid(p_i)
    in_r, in_i = p_r * s_r, p_i * s_i
    d_lam = d_ar * cos + d_ai * sin - (g_r * in_r + g_i * in_i)
    d_f = jnp.concatenate([keep] * groups, axis=-1) * d_lam * (1.0 - forget)
    small_ref[24:32, :] += jnp.concatenate(
        [eight_sum(lam * (d_ai * cos - d_ar * sin)), eight_sum(d_f)], axis=-1
    )
    rest = 1.0 - lam
    d_proj = jnp.concatenate(
        [
            (rest * g_r * (s_r + in_r * (1.0 - s_r))).astype(BF16),
            (rest * g_i * (s_i + in_i * (1.0 - s_i))).astype(BF16),
            (d_f * (1.0 - lower) * forget).astype(BF16),
        ],
        axis=1,
    )
    dproj_ref[:, : 3 * chan] = d_proj
    dproj_ref[:, 3 * chan :] = dpg_ref[...]
    d_n = d_n + dot_t(d_proj, w_ref[:, : 3 * chan])
    x = x_ref[...].astype(F32)
    scale = rms_scale(x)
    hat = x * scale
    small_ref[0:8, :] += eight_sum(d_n * hat)
    d_hat = d_n * gain_ref[0:1, :]
    dx_ref[...] = dx_ref[...] + scale * (d_hat - hat * jnp.mean(d_hat * hat, axis=-1, keepdims=True))


def combine(count, me, forward, buf, rot_ref, out_ref):
    cos, sin = rot_ref[0:1, :], rot_ref[1:2, :]
    c_r = jnp.zeros_like(cos)
    c_i = jnp.zeros_like(cos)
    for k in range(count - 1, 0, -1):
        slot = k - 1 if forward else count - k - 1
        valid = me >= k if forward else me + k < count
        e_r, e_i, m = buf[slot, 0:1, :], buf[slot, 1:2, :], buf[slot, 2:3, :]
        a_r = m * cos
        a_i = m * sin if forward else -m * sin
        n_r = a_r * c_r - a_i * c_i + e_r
        n_i = a_r * c_i + a_i * c_r + e_i
        keep = jnp.where(valid, 1.0, 0.0)
        c_r, c_i = n_r * keep, n_i * keep
    out_ref[0:1, :] = c_r
    out_ref[1:2, :] = c_i


def carry_copies(count, me, tot_ref, buf, send_sem, recv_sem):
    return [
        remote(tot_ref, buf.at[k - 1], send_sem.at[k - 1], recv_sem.at[k - 1], {"seq": lax.rem(me + k, count)})
        for k in range(1, count)
    ]


class Ring:
    def __init__(self, n):
        self.n = n
        self.batch, self.seq = lax.axis_index("batch"), lax.axis_index("seq")
        z, x = self.batch // 2, self.batch % 2
        self.pos = z + x * (n - 1 - 2 * z)
        self.core, self.y = self.seq % 2, self.seq // 2
        self.sign = 1 - 2 * self.core
        self.core_peer = self.seq + self.sign
        self.y_peer = self.seq + 2 * (1 - 2 * self.y)

    def at(self, distance):
        p = (self.pos + distance + 2 * self.n) % self.n
        h = p // (self.n // 2)
        return 2 * (p + h * (self.n - 1 - 2 * p)) + h

    def ahead(self, hops):
        return self.at(self.sign * hops)


def remote(src, dst, send, recv, device):
    return pltpu.make_async_remote_copy(
        src_ref=src, dst_ref=dst, send_sem=send, recv_sem=recv, device_id=device, device_id_type=MESH
    )


def meet(devices):
    barrier = pltpu.get_barrier_semaphore()
    for device in devices:
        pl.semaphore_signal(barrier, inc=1, device_id=device, device_id_type=MESH)
    pl.semaphore_wait(barrier, len(devices))


class Gather:
    def __init__(self, ring, jobs, sems):
        self.ring, self.jobs = ring, jobs
        (self.own_sem, self.ring_send, self.ring_recv, self.y_send, self.y_recv, self.core_send,
         self.core_recv) = sems
        n = ring.n
        self.hops = ((1, n // 2, 0), (-1, n - 1 - n // 2, n // 2))

    def rows(self, j, piece):
        src, dst, u = self.jobs[j]
        ring = self.ring
        base = ring.core * (3 * u)
        whole = piece * (6 * u)
        view = lambda first, rows: dst.at[pl.ds(pl.multiple_of(whole + base + first, 16), rows)]
        return view(ring.y * u, 2 * u), view(2 * ring.y * u, u), view(2 * (1 - ring.y) * u, u)

    def own_copy(self, j):
        src, dst, u = self.jobs[j]
        return pltpu.make_async_copy(
            src, dst.at[pl.ds(pl.multiple_of(self.ring.batch * (6 * u), 16), 6 * u)], self.own_sem.at[j]
        )

    def own(self, j):
        src, dst, u = self.jobs[j]
        ring = self.ring
        mine, _, _ = self.rows(j, ring.batch)
        piece = src.at[pl.ds(pl.multiple_of(ring.core * (3 * u) + ring.y * u, 16), 2 * u)]
        for way, hops, first in self.hops:
            remote(piece, mine, self.ring_send.at[j], self.ring_recv.at[j, first],
                   {"batch": ring.ahead(way)}).start()
        self.own_copy(j).start()

    def arrived(self, j, h):
        ring = self.ring
        for way, hops, first in self.hops:
            if h < hops:
                mine, give, _ = self.rows(j, ring.ahead(-way * (h + 1)))
                on = lambda slot: remote(mine, mine, self.ring_send.at[j], self.ring_recv.at[j, first + slot],
                                         {"batch": ring.ahead(way)})
                on(h).wait_recv()
                if h + 1 < hops:
                    on(h + 1).start()
                remote(give, give, self.y_send.at[j], self.y_recv.at[j, first + h], {"seq": ring.y_peer}).start()
                remote(mine, mine, self.core_send.at[j], self.core_recv.at[j], {"seq": ring.core_peer}).start()

    def crossed(self, j, h):
        ring = self.ring
        for way, hops, first in self.hops:
            if h < hops:
                _, _, take = self.rows(j, ring.ahead(-way * (h + 1)))
                remote(take, take, self.y_send.at[j], self.y_recv.at[j, first + h], {"seq": ring.y_peer}).wait_recv()
                remote(take, take, self.core_send.at[j], self.core_recv.at[j], {"seq": ring.core_peer}).start()

    def swapped(self, j):
        src, dst, u = self.jobs[j]
        view = dst.at[0 : (self.ring.n - 1) * 3 * u]
        remote(view, view, self.core_send.at[j], self.core_recv.at[j], {"seq": self.ring.core_peer}).wait_recv()
        self.own_copy(j).wait()

    def sent(self, j):
        src, dst, u = self.jobs[j]
        for rows, send in ((2 * u, self.ring_send), (u, self.y_send), (3 * u, self.core_send)):
            view = dst.at[0 : (self.ring.n - 1) * rows]
            remote(view, view, send.at[j], self.core_recv.at[j], {"seq": self.ring.core_peer}).wait_send()


class Agenda:
    def __init__(self):
        self.calls = {}

    def add(self, when, f, *args):
        self.calls.setdefault(when, []).append((f, args))

    def run(self, now):
        for when, calls in sorted(self.calls.items(), key=lambda item: item[0]):

            @pl.when(now == when)
            def _(calls=calls):
                for f, args in calls:
                    f(*args)


OPENING = (((0, 0, 0), (0, 0, 1), (0, 0, 3), (0, 0, 2), (1, 0, 0), (1, 0, 1), (1, 0, 3), (1, 0, 2), (2, 0, 0), (2, 0, 1),
            (2, 0, 3), (2, 0, 2), (3, 0, 0), (3, 0, 1), (3, 0, 3), (4, 0, 0), (3, 0, 2), (0, 1, 0), (0, 1, 1), (0, 1, 3),
            (5, 0, 0)),)
FIRST = OPENING + (
    ((4, 0, 1), (4, 0, 3), (0, 1, 2)),
    ((4, 0, 2), (1, 1, 0)),
    ((5, 0, 1), (5, 0, 3), (1, 1, 1), (1, 1, 3)),
    ((5, 0, 2), (1, 1, 2)),
)
SECOND = (
    ((2, 1, 0), (2, 1, 1), (2, 1, 3)),
    ((2, 1, 2), (3, 1, 0)),
    ((3, 1, 1), (3, 1, 3), (4, 1, 0)),
)
LATER = (
    ((5, 0, 0), (3, 0, 2)),
    ((4, 0, 1), (4, 0, 3), (0, 1, 0)),
    ((4, 0, 2), (0, 1, 1), (0, 1, 3)),
    ((5, 0, 1), (5, 0, 3), (0, 1, 2)),
    ((5, 0, 2), (1, 1, 0), (1, 1, 1), (1, 1, 3), (1, 1, 2)),
)


def plan_gather(agenda, net, layers, mats, count, load):
    far = net.ring.n // 2

    def hops(j, quarter):
        for h in range(quarter * far // 4, (quarter + 1) * far // 4):
            net.arrived(j, h)
        cross(j, quarter - 1)

    def cross(j, quarter):
        for h in range(max(quarter, 0) * far // 4, (quarter + 1) * far // 4):
            net.crossed(j, h)

    def complete(j):
        cross(j, 3)
        net.swapped(j)
        load(j).start()

    for k in range(layers):
        for q, calls in enumerate((LATER if k else FIRST) + SECOND):
            for what, ahead, m in calls:
                if k + ahead < layers:
                    j = (k + ahead) * mats + m
                    when = 2 * count * k + q * count // 4
                    if what == 0:
                        agenda.add(when, net.own, j)
                    elif what == 5:
                        agenda.add(when, complete, j)
                    else:
                        agenda.add(when, hops, j, what - 1)


def forward_kernel(n, n_seq, layers, rows, paired, *refs):
    doc_ref, tok_ref = refs[:2]
    mats = 4
    given, table_ref, refs = refs[2 : 2 + mats], refs[2 + mats], refs[3 + mats :]
    if paired:
        gathered, refs = refs[: layers * mats], refs[layers * mats :]
    (xin_ref, proj_ref, pg_ref, normed_ref, starts_ref, state_ref, mixed_ref, mid_ref, normed2_ref, gu_ref, hid_ref,
     out_ref) = refs[:12]
    (xs, hs, cum, pg, ends, tot, src, lam, run, carry, buf, *rest) = refs[12:]
    weights, (load_sem, carry_send, carry_recv), sems = rest[:mats], rest[mats : mats + 3], rest[mats + 3 :]
    layer, step = pl.program_id(0), pl.program_id(1)
    tokens, width = tok_ref.shape
    count = xs.shape[0]
    tiles = count // rows
    now = layer * (2 * count) + step
    me = lax.axis_index("seq")
    peers = [{"seq": lax.rem(me + k, n_seq)} for k in range(1, n_seq)]
    agenda = Agenda()

    def load(j):
        source = gathered[j] if paired else given[j % mats].at[j // mats]
        return pltpu.make_async_copy(source, weights[j % mats], load_sem.at[j % mats])

    def ready(j):
        load(j).wait()

    if paired:
        ring = Ring(n)
        jobs = [
            (given[m].at[k], gathered[k * mats + m], given[m].shape[1] // 6)
            for k in range(layers) for m in range(mats)
        ]
        net = Gather(ring, jobs, sems)
        agenda.add(0, meet, [{"batch": ring.ahead(1)}, {"batch": ring.ahead(-1)}] + peers)
        plan_gather(agenda, net, layers, mats, count, load)
    else:
        agenda.add(0, meet, peers)
        for k in range(layers):
            agenda.add(2 * count * k, lambda k=k: load(k * mats).start())
            for m in range(1, mats):
                agenda.add(2 * count * k + count - 1, lambda j=k * mats + m: load(j).start())
    for k in range(layers):
        agenda.add(2 * count * k, ready, k * mats)
        for m in range(1, mats):
            agenda.add(2 * count * k + count, ready, k * mats + m)
    agenda.run(now)

    tile = lax.rem(step, count)
    row, at_row = tile // tiles, lax.rem(tile, tiles)
    start = (me * tiles + at_row) * tokens
    gains, gate = table_ref.at[layer, 0:8], table_ref.at[layer, 8:16, 0 : width // 2]

    @pl.when((layer == 0) & (step < count))
    def _():
        xs[tile] = dot(order_matrix(tokens, False), tok_ref[...])

    @pl.when(step < count)
    def _():
        x = xs[tile]
        xin_ref[...] = x.astype(BF16)
        enter_tile(doc_ref, row, at_row, start, x, weights[0], gains, gate, proj_ref, pg.at[tile], normed_ref, hs.at[tile],
                   cum.at[tile], ends.at[tile], tot.at[row], src, lam)
        pg_ref[...] = pg[tile]

    def exchange():
        return carry_copies(n_seq, me, tot.at[row], buf.at[layer, row], carry_send.at[layer, row], carry_recv.at[layer, row])

    @pl.when((step < count) & (lax.rem(step, tiles) == tiles - 1))
    def _():
        for copy in exchange():
            copy.start()

    @pl.when((step >= count) & (lax.rem(step, tiles) == 0))
    def _():
        for copy in exchange():
            copy.wait()
        combine(n_seq, me, True, buf.at[layer, row], gate.at[5:8], carry.at[row])

    @pl.when(step >= count)
    def _():
        out = leave_tile(at_row, xs[tile], pg.at[tile], hs.at[tile], cum.at[tile], ends.at[tile], carry.at[row],
                         weights[1], weights[2], weights[3], gains, gate, starts_ref, state_ref, mixed_ref, mid_ref,
                         normed2_ref, gu_ref, hid_ref, run)
        xs[tile] = out

        @pl.when(layer == layers - 1)
        def _():
            out_ref[...] = out.astype(BF16)

    if paired:

        @pl.when(now == layers * 2 * count - 1)
        def _():
            for j in range(layers * mats):
                net.sent(j)


def tile_specs(tokens, layer):
    def flat(w, when, col=0):
        return pl.BlockSpec((None, tokens, w), lambda k, s: (layer(k), when(s), col))

    def few(r, w, when):
        return pl.BlockSpec((None, None, r, w), lambda k, s: (layer(k), when(s), 0, 0))

    return flat, few


def run_forward(n, n_seq, paired, rows, tokens, docs, x, sources, table):
    layers = sources[0].shape[0]
    total, width = x.shape
    chan = width // 2
    hidden = sources[2].shape[2] // 2
    count = total // tokens
    mats = len(sources)
    jobs = layers * mats if paired else 0
    shape = jax.ShapeDtypeStruct
    dma = pltpu.SemaphoreType.DMA
    any_ = pl.BlockSpec(memory_space=pl.ANY)

    def first(step):
        return jnp.minimum(step, count - 1)

    def second(step):
        return jnp.maximum(step - count, 0)

    flat, few = tile_specs(tokens, lambda k: k)

    def kept(w):
        return shape((layers, total, w), BF16)

    full = [((n if paired else 1) * w.shape[1], w.shape[2]) for w in sources]
    last = layers - 1
    outs = pl.pallas_call(
        functools.partial(forward_kernel, n, n_seq, layers, rows, paired),
        grid=(layers, 2 * count),
        in_specs=[
            pl.BlockSpec(memory_space=pltpu.SMEM),
            pl.BlockSpec((tokens, width), lambda k, s: (jnp.where(k == 0, first(s), count - 1), 0)),
        ]
        + [any_] * mats
        + [whole(*table.shape)],
        out_specs=[any_] * jobs
        + [
            flat(width, first),
            flat(3 * chan, first),
            flat(width, first),
            flat(width, first),
            few(8, width, second),
            flat(width, second),
            flat(width, second),
            flat(width, second),
            flat(width, second),
            flat(2 * hidden, second),
            flat(hidden, second),
            pl.BlockSpec((tokens, width), lambda k, s: (jnp.where(k == last, second(s), 0), 0)),
        ],
        out_shape=[shape(f, BF16) for _ in range(layers) for f in full][:jobs]
        + [
            kept(width),
            kept(3 * chan),
            kept(width),
            kept(width),
            shape((layers, count, 8, width), F32),
            kept(width),
            kept(width),
            kept(width),
            kept(width),
            kept(2 * hidden),
            kept(hidden),
            shape((total, width), BF16),
        ],
        scratch_shapes=[
            pltpu.VMEM((count, tokens, width), F32),
            pltpu.VMEM((count, width // LANES, tokens, LANES), F32),
            pltpu.VMEM((count, chan // LANES, tokens, LANES), F32),
            pltpu.VMEM((count, tokens, width), BF16),
            pltpu.VMEM((count, 24, chan), F32),
            pltpu.VMEM((rows, 8, chan), F32),
            pltpu.VMEM((width // LANES, tokens, LANES), F32),
            pltpu.VMEM((chan // LANES, tokens, LANES), F32),
            pltpu.VMEM((8, chan), F32),
            pltpu.VMEM((rows, 8, chan), F32),
            pltpu.VMEM((layers, rows, n_seq - 1, 8, chan), F32),
        ]
        + [pltpu.VMEM(f, BF16) for f in full]
        + [dma((mats,)), dma((layers, rows, n_seq - 1)), dma((layers, rows, n_seq - 1))]
        + [dma((s,)) if one else dma((s, n - 1)) for s in [max(jobs, 1)] for one in (1, 1, 0, 1, 0, 1, 1)],
        compiler_params=pltpu.CompilerParams(collective_id=3, has_side_effects=True, vmem_limit_bytes=LIMIT),
    )(docs, x, *sources, table)
    return outs[:jobs], outs[jobs:]


def backward_kernel(n_seq, layers, rows, mats, *refs):
    doc_ref, cot_ref = refs[:2]
    given, refs = refs[2 : 2 + layers * mats], refs[2 + layers * mats :]
    (table_ref, gu_ref, mid_ref, state_ref, pg_ref, pf_ref, x_ref, proj_ref, starts_ref, prior_ref, dz_ref,
     dgu_ref, dy_ref, dproj_ref, dtok_ref, small_ref) = refs[:16]
    (dxs, gs, cum, lam, dpg, ends, tot, grad, run, carry, buf, *rest) = refs[16:]
    weights, (load_sem, carry_send, carry_recv) = rest[:mats], rest[mats:]
    turn, step = pl.program_id(0), pl.program_id(1)
    layer = layers - 1 - turn
    tokens, width = cot_ref.shape
    count = dxs.shape[0]
    tiles = count // rows
    now = turn * (2 * count) + step
    me = lax.axis_index("seq")
    agenda = Agenda()

    def load(t, m):
        return pltpu.make_async_copy(given[(layers - 1 - t) * mats + m], weights[m], load_sem.at[m])

    def fetch(t, m):
        load(t, m).start()

    def ready(t, m):
        load(t, m).wait()

    for m in (3, 2, 1):
        agenda.add(0, fetch, 0, m)
    agenda.add(0, meet, [{"seq": lax.rem(me + k, n_seq)} for k in range(1, n_seq)])
    for t in range(layers):
        begin = 2 * count * t
        agenda.add(begin, fetch, t, 0)
        for m in (3, 2, 1):
            agenda.add(begin, ready, t, m)
        agenda.add(begin + count, ready, t, 0)
        if t + 1 < layers:
            for m in (3, 2, 1):
                agenda.add(begin + count, fetch, t + 1, m)
    agenda.run(now)

    tile = count - 1 - lax.rem(step, count)
    row, at_row = tile // tiles, lax.rem(tile, tiles)
    start = (me * tiles + at_row) * tokens
    gains, gate = table_ref.at[layer, 0:8], table_ref.at[layer, 8:16, 0 : width // 2]

    @pl.when(step == 0)
    def _():
        small_ref[...] = jnp.zeros_like(small_ref)

    @pl.when((turn == 0) & (step < count))
    def _():
        dxs[tile] = dot(order_matrix(tokens, False), cot_ref[...])

    @pl.when(step < count)
    def _():
        back_out_tile(doc_ref, row, at_row, start, tiles - 1, dxs.at[tile], gu_ref, mid_ref, state_ref, pg_ref, pf_ref,
                      weights[1], weights[2], weights[3], gains, gate, dz_ref, dgu_ref, dy_ref, dpg.at[tile],
                      lam.at[tile], gs.at[tile], cum.at[tile], ends.at[tile], tot.at[row], small_ref, grad)

    def exchange():
        return carry_copies(n_seq, me, tot.at[row], buf.at[turn, row], carry_send.at[turn, row], carry_recv.at[turn, row])

    @pl.when((step < count) & (lax.rem(step, tiles) == tiles - 1))
    def _():
        for copy in exchange():
            copy.start()

    @pl.when((step >= count) & (lax.rem(step, tiles) == 0))
    def _():
        for copy in exchange():
            copy.wait()
        combine(n_seq, me, False, buf.at[turn, row], gate.at[5:8], carry.at[row])

    @pl.when(step >= count)
    def _():
        back_in_tile(doc_ref, row, at_row, start, tiles - 1, dxs.at[tile], x_ref, proj_ref, dpg.at[tile], lam.at[tile],
                     starts_ref, prior_ref, gs.at[tile], cum.at[tile], ends.at[tile], carry.at[row], weights[0],
                     gains, gate, dproj_ref, small_ref, run)

        @pl.when(turn == layers - 1)
        def _():
            dtok_ref[...] = dxs[tile]


def run_backward(n_seq, rows, tokens, docs, cotangent, weights, table, kept):
    x, proj, p_g, starts, state, mid, gu = kept
    layers, total, width = x.shape
    chan = width // 2
    hidden = gu.shape[2] // 2
    count = total // tokens
    mats = len(weights) // layers
    shape = jax.ShapeDtypeStruct
    dma = pltpu.SemaphoreType.DMA
    any_ = pl.BlockSpec(memory_space=pl.ANY)
    last = layers - 1

    def first(step):
        return count - 1 - jnp.minimum(step, count - 1)

    def second(step):
        return count - 1 - jnp.maximum(step - count, 0)

    flat, few = tile_specs(tokens, lambda k: last - k)
    return pl.pallas_call(
        functools.partial(backward_kernel, n_seq, layers, rows, mats),
        grid=(layers, 2 * count),
        in_specs=[
            pl.BlockSpec(memory_space=pltpu.SMEM),
            pl.BlockSpec((tokens, width), lambda k, s: (jnp.where(k == 0, first(s), 0), 0)),
        ]
        + [any_] * len(weights)
        + [
            whole(*table.shape),
            flat(2 * hidden, first),
            flat(width, first),
            flat(width, first),
            flat(width, first),
            flat(chan, first, 2),
            flat(width, second),
            flat(3 * chan, second),
            few(8, width, second),
            flat(width, second),
        ],
        out_specs=[
            flat(width, first),
            flat(2 * hidden, first),
            flat(width, first),
            flat(3 * chan + width, second),
            pl.BlockSpec((tokens, width), lambda k, s: (jnp.where(k == last, second(s), count - 1), 0)),
            pl.BlockSpec((None, 32, width), lambda k, s: (last - k, 0, 0)),
        ],
        out_shape=[
            shape((layers, total, width), BF16),
            shape((layers, total, 2 * hidden), BF16),
            shape((layers, total, width), BF16),
            shape((layers, total, 3 * chan + width), BF16),
            shape((total, width), F32),
            shape((layers, 32, width), F32),
        ],
        scratch_shapes=[
            pltpu.VMEM((count, tokens, width), F32),
            pltpu.VMEM((count, width // LANES, tokens, LANES), F32),
            pltpu.VMEM((count, chan // LANES, tokens, LANES), F32),
            pltpu.VMEM((count, chan // LANES, tokens, LANES), F32),
            pltpu.VMEM((count, tokens, width), BF16),
            pltpu.VMEM((count, 24, chan), F32),
            pltpu.VMEM((rows, 8, chan), F32),
            pltpu.VMEM((width // LANES, tokens, LANES), F32),
            pltpu.VMEM((8, chan), F32),
            pltpu.VMEM((rows, 8, chan), F32),
            pltpu.VMEM((layers, rows, n_seq - 1, 8, chan), F32),
        ]
        + [pltpu.VMEM(w.shape, BF16) for w in weights[:mats]]
        + [dma((mats,)), dma((layers, rows, n_seq - 1)), dma((layers, rows, n_seq - 1))],
        compiler_params=pltpu.CompilerParams(collective_id=2, has_side_effects=True, vmem_limit_bytes=LIMIT),
    )(docs, cotangent, *weights, table, gu, mid, state, p_g, proj, x, proj, starts, state)


def add_rows(dst, dst_row, parts, rows):
    def block(i, _):
        step = pl.multiple_of(i * 16, 16)
        total = None
        for ref, first in parts:
            value = ref[pl.ds(pl.multiple_of(first + step, 16), 16), :].astype(F32)
            total = value if total is None else total + value
        dst[pl.ds(pl.multiple_of(dst_row + step, 16), 16), :] = total.astype(dst.dtype)
        return 0

    lax.fori_loop(0, rows // 16, block, 0)


def grads_kernel(n, plan, *refs):
    jobs = len(plan)
    lefts, rights, small = refs[:jobs], refs[jobs : 2 * jobs], refs[2 * jobs]
    outs_count = 1 + max(p[0] for p in plan)
    outs, rest = refs[2 * jobs + 1 : 2 * jobs + 1 + outs_count], refs[2 * jobs + 1 + outs_count :]
    gains_out, gate_out, rest = rest[0], rest[1], rest[2:]
    grads, core_buf, y_buf, ring_buf, fin_buf = (rest[i * jobs : (i + 1) * jobs] for i in range(5))
    (left_big, left_small, right_buf, small_buf, left_sem, right_sem, core_send, core_recv, y_send, y_recv,
     ring_send, ring_recv, end_send, end_recv, small_send, small_recv) = rest[5 * jobs :]
    ring = Ring(n)
    far, near = n // 2, n - 1 - n // 2
    core_dev, y_dev = {"seq": ring.core_peer}, {"seq": ring.y_peer}
    y, core = ring.y, ring.core
    rounds = [core_dev, y_dev]
    d = 1
    while d < n:
        rounds.append({"batch": ring.batch + d * (1 - 2 * ((ring.batch // d) % 2))})
        d *= 2
    us = [g.shape[0] // n // 6 for g in grads]
    split = [p[2] for p in plan]
    own_rows = [(2 if s else 3) * u for s, u in zip(split, us)]

    def left_copy(j):
        buf = (left_big, left_small)[j % 2]
        return pltpu.make_async_copy(lefts[j].at[plan[j][1]], buf.at[:, 0 : plan[j][3]], left_sem.at[j % 2])

    chunks = []
    for j, (_, _, _, rows, cols, _, _) in enumerate(plan):
        first = 0
        while first < cols:
            size = min(CHUNK, cols - first)
            chunks.append((j, first, size, first + size == cols))
            first += size

    def right_copy(i):
        j, first, size, _ = chunks[i]
        return pltpu.make_async_copy(
            rights[j].at[plan[j][1], :, plan[j][5] + first : plan[j][5] + first + size], right_buf.at[i % 2, :, 0:size], right_sem.at[i % 2]
        )

    left_copy(0).start()
    right_copy(0).start()
    right_copy(1).start()
    left_copy(1).start()
    meet([{"batch": ring.ahead(1)}, {"batch": ring.ahead(-1)}] + rounds)

    order = []
    for h in range(far):
        order.append((1, h, far - h))
        if h < near:
            order.append((-1, h, near - h))
    order.append((0, 0, 0))
    last = len(order)

    def rows_at(ref, first, rows):
        return ref.at[pl.ds(pl.multiple_of(first, 16), rows)]

    def core_copy(j, slot, piece):
        u = us[j]
        return remote(rows_at(grads[j], piece * (6 * u) + (1 - core) * (3 * u), 3 * u),
                      core_buf[j].at[slot], core_send.at[j], core_recv.at[j, slot], core_dev)

    def y_copy(j, slot, piece):
        u = us[j]
        src = rows_at(grads[j], piece * (6 * u) + core * (3 * u) + 2 * (1 - y) * u, u)
        return remote(src, y_buf[j].at[slot], y_send.at[j], y_recv.at[j, slot], y_dev)

    def mine(j, piece):
        u = us[j]
        return piece * (6 * u) + core * (3 * u) + (y * u if split[j] else 0)

    def ring_copy(j, slot, way, piece):
        return remote(rows_at(grads[j], mine(j, piece), own_rows[j]), ring_buf[j].at[slot], ring_send.at[j],
                      ring_recv.at[j, slot], {"batch": ring.ahead(way)})

    def small_round(r):
        return remote(small_buf.at[2 * r], small_buf.at[2 * r + 1], small_send.at[r], small_recv.at[r], rounds[r])

    layers = small.shape[0]
    for k in range(layers):
        for i in range(4):
            small_buf[0, 4 * k + i : 4 * k + i + 1, :] = jnp.sum(small[k, 8 * i : 8 * i + 8, :], axis=0, keepdims=True)
    small_round(0).start()

    def small_step(r):
        small_round(r).wait_recv()
        total = small_buf[2 * r] + small_buf[2 * r + 1]
        if r + 1 < len(rounds):
            small_buf[2 * r + 2] = total
            small_round(r + 1).start()
        else:
            chan = gate_out.shape[2]
            for k in range(layers):
                gains_out[k] = total[4 * k : 4 * k + 3, :]
                gate_out[k, 0:1, :] = total[4 * k + 3 : 4 * k + 4, :chan]
                gate_out[k, 1:2, :] = total[4 * k + 3 : 4 * k + 4, chan:]

    def begin(j):
        for slot, (way, h, dist) in enumerate(order):
            core_copy(j, slot, ring.ahead(-way * dist)).start()

    def cross(j, slot):
        way, h, dist = order[slot]
        piece = ring.ahead(way * dist)
        u = us[j]
        core_copy(j, slot, piece).wait_recv()
        if not split[j]:
            return
        give = 2 * (1 - y) * u
        at = piece * (6 * u) + core * (3 * u) + give
        add_rows(grads[j], at, [(grads[j], at), (core_buf[j].at[slot], give)], u)
        y_copy(j, slot, piece).start()

    def hop(j, slot):
        way, h, dist = order[slot]
        piece = ring.ahead(way * dist)
        u = us[j]
        if split[j]:
            y_copy(j, slot, piece).wait_recv()
        if way == 0:
            prior = [i for i, o in enumerate(order) if o[2] == 1]
        elif h:
            prior = [i for i, o in enumerate(order) if o[0] == way and o[1] == h - 1]
        else:
            prior = []
        for i in prior:
            ring_copy(j, i, order[i][0], piece).wait_recv()
        at = mine(j, piece)
        base = [(grads[j], at), (core_buf[j].at[slot], y * u if split[j] else 0)]
        base += [(ring_buf[j].at[i], 0) for i in prior]
        if split[j]:
            for by, more in ((y * u, [(y_buf[j].at[slot], 0)]), ((1 - y) * u, [])):
                add_rows(grads[j], at + by, [(r, f + by) for r, f in base] + more, u)
        else:
            add_rows(grads[j], at, base, 3 * u)
        if way:
            ring_copy(j, slot, way, piece).start()

    def fin_copy(j):
        return remote(rows_at(grads[j], mine(j, ring.batch), own_rows[j]), fin_buf[j], end_send.at[j, 0],
                      end_recv.at[j, 0], y_dev)

    def out_of(j):
        return outs[plan[j][0]].at[plan[j][1], :, plan[j][5] : plan[j][5] + plan[j][4]]

    def half_copy(j):
        half = out_of(j).at[pl.ds(pl.multiple_of(core * (3 * us[j]), 16), 3 * us[j])]
        return remote(half, half, end_send.at[j, 1], end_recv.at[j, 1], core_dev)

    def finish(j):
        u = us[j]
        fin_copy(j).wait_recv()
        out = out_of(j)
        at, to = mine(j, ring.batch), core * (3 * u)
        if split[j]:
            add_rows(out, to + 2 * y * u, [(grads[j], at + y * u)], u)
            add_rows(out, to + 2 * (1 - y) * u, [(fin_buf[j], (1 - y) * u)], u)
            add_rows(out, to + u, [(grads[j], at + (1 - y) * u), (fin_buf[j], y * u)], u)
        else:
            add_rows(out, to, [(grads[j], at), (fin_buf[j], 0)], 3 * u)
        half_copy(j).start()

    steps = far + 4

    def advance(j, t):
        now = [i for i, o in enumerate(order) if o[0] and o[1] == t]
        before = [i for i, o in enumerate(order) if o[0] and o[1] == t - 1]
        for slot in before:
            hop(j, slot)
        for slot in now:
            cross(j, slot)
        if t == far - 1:
            cross(j, last - 1)
        if t == far + 1:
            hop(j, last - 1)
            fin_copy(j).start()
        if t == far + 2:
            finish(j)
        if t == far + 3:
            half_copy(j).wait_recv()

    stage = {}

    def advance_all(turn):
        for j in list(stage):
            if j % 2 == turn:
                advance(j, stage[j])
                stage[j] += 1
                if stage[j] == steps:
                    del stage[j]

    small_at = 0
    for i, (j, first, size, done) in enumerate(chunks):
        if first == 0:
            left_copy(j).wait()
        right_copy(i).wait()
        left = (left_big, left_small)[j % 2]

        def multiply(b, _, i=i, j=j, first=first, size=size, left=left):
            at = pl.multiple_of(b * 256, 256)
            part = lax.dot_general(
                left[:, pl.ds(at, 256)], right_buf[i % 2, :, 0:size], (((0,), (0,)), ((), ())),
                preferred_element_type=F32,
            )
            grads[j][pl.ds(at, 256), first : first + size] = part.astype(BF16)
            return 0

        lax.fori_loop(0, plan[j][3] // 256, multiply, 0)
        if i + 2 < len(chunks):
            right_copy(i + 2).start()
        if done and j + 2 < jobs:
            left_copy(j + 2).start()
        advance_all(i % 2)
        if done:
            begin(j)
            stage[j] = 0
        if small_at < len(rounds):
            small_step(small_at)
            small_at += 1
    i = 0
    while stage:
        advance_all(i % 2)
        i += 1
    while small_at < len(rounds):
        small_step(small_at)
        small_at += 1
    for j in range(jobs):
        u = us[j]
        fin_copy(j).wait_send()
        half_copy(j).wait_send()
        remote(core_buf[j], core_buf[j], core_send.at[j], core_recv.at[j, 0], core_dev).wait_send()
        if split[j]:
            remote(y_buf[j], y_buf[j], y_send.at[j], y_recv.at[j, 0], y_dev).wait_send()
        remote(ring_buf[j], ring_buf[j], ring_send.at[j], ring_recv.at[j, 0], core_dev).wait_send()
    for r in range(len(rounds)):
        small_round(r).wait_send()


def grads_and_scatter(n, plan, lefts, rights, small):
    jobs = len(plan)
    full = []
    for (m, k, crosses, part, of), a, b in zip(plan, lefts, rights):
        cols = b.shape[2] // of
        full.append((m, k, crosses, a.shape[2], cols, part * cols, b.shape[2]))
    plan = full
    tokens = lefts[0].shape[1]
    layers, _, width = small.shape
    dma = pltpu.SemaphoreType.DMA
    rounds = 2 + (n - 1).bit_length()
    sizes = [(p[3] // n // 6, p[4], p[2]) for p in plan]
    outs = {p[0]: jax.ShapeDtypeStruct((layers, p[3] // n, p[6]), BF16) for p in plan}
    vm = pl.BlockSpec(memory_space=pltpu.VMEM)
    any_ = pl.BlockSpec(memory_space=pl.ANY)

    def bufs(f):
        return [pltpu.VMEM(f(u, w, s), BF16) for u, w, s in sizes]

    return pl.pallas_call(
        functools.partial(grads_kernel, n, plan),
        out_shape=[outs[m] for m in sorted(outs)]
        + [jax.ShapeDtypeStruct((layers, 3, width), F32), jax.ShapeDtypeStruct((layers, 2, width // 2), F32)],
        in_specs=[any_] * (2 * jobs) + [vm],
        out_specs=[vm] * (len(outs) + 2),
        scratch_shapes=bufs(lambda u, w, s: (6 * u * n, w))
        + bufs(lambda u, w, s: (n, 3 * u, w))
        + bufs(lambda u, w, s: (n if s else 1, u, w))
        + bufs(lambda u, w, s: (n - 1, 2 * u if s else 3 * u, w))
        + bufs(lambda u, w, s: (2 * u if s else 3 * u, w))
        + [
            pltpu.VMEM((tokens, max(p[3] for p in plan[0::2])), BF16),
            pltpu.VMEM((tokens, max(p[3] for p in plan[1::2])), BF16),
            pltpu.VMEM((2, tokens, CHUNK), BF16),
            pltpu.VMEM((2 * rounds, 4 * layers, width), F32),
            dma((2,)), dma((2,)), dma((jobs,)), dma((jobs, n)), dma((jobs,)), dma((jobs, n)), dma((jobs,)),
            dma((jobs, n)), dma((jobs, 2)), dma((jobs, 2)), dma((rounds,)), dma((rounds,)),
        ],
        compiler_params=pltpu.CompilerParams(
            collective_id=4, has_side_effects=True, vmem_limit_bytes=63 * 1024 * 1024
        ),
    )(*lefts, *rights, small)


def finish_kernel(mats, *refs):
    grads, (out_ref, dtok_ref) = refs[:mats], refs[mats : mats + 2]
    wide_refs, (out_to, dtok_to) = refs[mats + 2 : 2 * mats + 2], refs[2 * mats + 2 :]
    for grad, to in zip(grads, wide_refs):
        to[...] = grad[...].astype(F32)
    order = order_matrix(out_ref.shape[0], True)
    out_to[...] = dot(order, out_ref[...]).astype(BF16)
    dx = dtok_ref[...]
    high = dx.astype(BF16)
    dtok_to[...] = dot(order, high) + dot(order, (dx - high.astype(F32)).astype(BF16))


def finish(tokens, grads, block_out, d_tokens):
    total, width = block_out.shape
    count = total // tokens
    if grads[0].shape[0] * 2 != count:
        def ordered(values):
            return values.reshape(count, tokens // 8, 8, width).swapaxes(1, 2).reshape(total, width)

        return [g.astype(F32) for g in grads], ordered(block_out), ordered(d_tokens)
    halves = [
        pl.BlockSpec((1, g.shape[1] // 2, g.shape[2]), lambda i: (i // 2, i % 2, 0)) for g in grads
    ]
    tile = pl.BlockSpec((tokens, width), lambda i: (i, 0))
    outs = pl.pallas_call(
        functools.partial(finish_kernel, len(grads)),
        grid=(count,),
        in_specs=halves + [tile, tile],
        out_specs=halves + [tile, tile],
        out_shape=[jax.ShapeDtypeStruct(g.shape, F32) for g in grads]
        + [jax.ShapeDtypeStruct(v.shape, v.dtype) for v in (block_out, d_tokens)],
        compiler_params=pltpu.CompilerParams(vmem_limit_bytes=LIMIT),
    )(*grads, block_out, d_tokens)
    return outs[:-2], outs[-2], outs[-1]


def contract_rows(left, right):
    return lax.dot_general(
        left, right, (((0,), (0,)), ((), ())), preferred_element_type=F32
    ).astype(BF16)


def shards(
    tokens_in, doc_starts, mixer_in, mixer_out, ffn_in, ffn_out, gains, gate_params, cotangent
):
    rows, length, width = tokens_in.shape
    layers = gains.shape[0]
    chan = width // 2
    total = rows * length
    tokens = min(length, 256)
    seg = tokens // 8
    n, n_seq = lax.axis_size("batch"), lax.axis_size("seq")
    sources = (mixer_in, mixer_out, ffn_in, ffn_out)
    paired = n_seq == 4 and n % 4 == 0 and all(w.shape[1] % 96 == 0 for w in sources)
    theta, lower = gate_params[:, 0:1], gate_params[:, 1:2]
    at = lax.broadcasted_iota(jnp.int32, (layers, 8, chan), 1)
    times = jnp.where(at < 3, 1, jnp.where(at < 5, seg, length)).astype(F32)
    quarter = jnp.where((at == 1) | (at == 4) | (at == 6), math.pi / 2, 0.0)
    gate_rows = jnp.where(at == 2, lower, jnp.cos(theta * times - quarter))
    table = jnp.concatenate(
        [jnp.pad(gains, ((0, 0), (0, 5), (0, 0))), jnp.pad(gate_rows, ((0, 0), (0, 0), (0, width - chan)))], axis=1
    )
    x = tokens_in.reshape(total, width)
    if paired:
        weights, kept = run_forward(n, n_seq, True, rows, tokens, doc_starts, x, sources, table)
    else:
        stacked = [lax.all_gather(w, "batch", axis=1, tiled=True) for w in sources]
        weights = [w[k] for k in range(layers) for w in stacked]
        _, kept = run_forward(n, n_seq, False, rows, tokens, doc_starts, x, stacked, table)
    x_in, proj, p_g, normed, starts, state, mixed, mid, normed2, gu, hid, block_out = kept
    dz, d_gu, dy, d_proj, d_tokens, small = run_backward(
        n_seq, rows, tokens, doc_starts, cotangent.reshape(total, width), weights, table,
        (x_in, proj, p_g, starts, state, mid, gu),
    )
    pairs = ((normed, d_proj), (mixed, dy), (normed2, d_gu), (hid, dz))
    if paired:
        plan = []
        for k in reversed(range(layers)):
            jobs = ORDERS[0] if k == layers - 1 else ORDERS[1]
            plan += [(m, k, m != 0, part, of) for m, part, of in jobs]
        *outs, d_gains, d_gate = grads_and_scatter(
            n, plan, [pairs[p[0]][0] for p in plan], [pairs[p[0]][1] for p in plan], small
        )
    else:
        outs = []
        for left, right in pairs:
            whole_grads = jnp.stack([contract_rows(left[k], right[k]) for k in range(layers)])
            part = lax.psum_scatter(whole_grads, "batch", scatter_dimension=1, tiled=True)
            outs.append(lax.psum(part, "seq"))
        totals = lax.psum(jnp.sum(small.reshape(layers, 4, 8, width), axis=2), ("batch", "seq"))
        d_gains, d_gate = totals[:, :3], totals[:, 3].reshape(layers, 2, chan)
    outs, block_out, d_tokens = finish(tokens, outs, block_out, d_tokens)
    return (
        block_out.reshape(rows, length, width),
        d_tokens.reshape(rows, length, width),
        *outs,
        d_gains,
        d_gate,
    )


def solution(mesh):
    tok = P("batch", "seq", None)
    mat = P(None, "batch", None)
    return jax.shard_map(
        shards,
        mesh=mesh,
        in_specs=(tok, P("batch", None), mat, mat, mat, mat, P(), P(), tok),
        out_specs=(tok, tok, mat, mat, mat, mat, P(), P()),
        check_vma=False,
    )
```

```python
import functools
import math

import jax
import jax.numpy as jnp
from jax import lax
from jax.experimental import pallas as pl
from jax.experimental.pallas import tpu as pltpu
from jax.sharding import PartitionSpec as P

EPS = 1e-06
F32 = jnp.float32
BF16 = jnp.bfloat16
LANES = 128
CHUNK = 768
ORDERS = (((1, 0, 1), (2, 0, 2), (3, 0, 1), (2, 1, 2), (0, 0, 1)), ((2, 0, 2), (3, 0, 1), (2, 1, 2), (0, 0, 1), (1, 0, 1)))
MESH = pl.DeviceIdType.MESH


def sigmoid(values):
    return 1.0 / (1.0 + jnp.exp(-values))


def rms_scale(values):
    return lax.rsqrt(jnp.mean(values * values, axis=-1, keepdims=True) + EPS)


def dot(left, right):
    return jnp.dot(left, right, preferred_element_type=F32)


def dot_t(left, right):
    return lax.dot_general(left, right, (((1,), (1,)), ((), ())), preferred_element_type=F32)


def eight_sum(values):
    rows, cols = values.shape
    return jnp.sum(values.reshape(rows // 8, 8, cols), axis=0)


def wide(ref, first, last):
    return jnp.concatenate([ref[g] for g in range(first, last)], axis=-1)


def split_store(ref, first, values):
    for g in range(values.shape[1] // LANES):
        ref[first + g] = values[:, g * LANES : (g + 1) * LANES]


def lanes(values):
    return [values[:, g * LANES : (g + 1) * LANES] for g in range(values.shape[1] // LANES)]


LIMIT = 60 * 1024 * 1024


def whole(*shape):
    return pl.BlockSpec(shape, lambda *_: (0,) * len(shape), pipeline_mode=pl.Buffered(1))


def order_matrix(tokens, back):
    shape = (tokens, tokens)
    here = lax.broadcasted_iota(jnp.int32, shape, 1 if back else 0)
    there = lax.broadcasted_iota(jnp.int32, shape, 0 if back else 1)
    return jnp.where(there == (here & 7) * (tokens // 8) + (here >> 3), 1.0, 0.0).astype(BF16)


def reset_mask(doc_ref, row, first, tokens):
    here = lax.broadcasted_iota(jnp.int32, (tokens, LANES), 0)
    pos = (here & 7) * (tokens // 8) + (here >> 3) + first
    hit = pos == doc_ref[row, 0]
    for k in range(1, doc_ref.shape[1]):
        hit = hit | (pos == doc_ref[row, k])
    return hit


def retain(doc_ref, row, first, p_f, lower):
    tokens, chan = p_f.shape
    forget = sigmoid(p_f)
    lam = lower + (1.0 - lower) * forget
    keep = jnp.where(reset_mask(doc_ref, row, first, tokens), 0.0, 1.0)
    return lam * jnp.concatenate([keep] * (chan // LANES), axis=-1), forget, keep


def pieces(total):
    size = 512 if total % 512 == 0 else total
    return [slice(first, first + size) for first in range(0, total, size)]


def moved(part, by):
    return slice(part.start + by, part.stop + by)


def at_step(s):
    return pl.ds(pl.multiple_of(s * 8, 8), 8)


def enter_tile(doc_ref, row, tile, start, x, w_ref, gain_ref, gate_ref, proj_ref, pg_ref, normed_ref, h_ref, cum_ref,
               ends_ref, tot_ref, src, lam_ref):
    tokens, width = x.shape
    chan = width // 2
    seg = tokens // 8
    groups = chan // LANES
    normed = (x * rms_scale(x) * gain_ref[0:1, :]).astype(BF16)
    normed_ref[...] = normed
    p_f = dot(normed, w_ref[:, 2 * chan : 3 * chan])
    p_c = dot(normed, w_ref[:, : 2 * chan])
    proj_ref[:, 2 * chan :] = p_f.astype(BF16)
    cos, sin, lower = gate_ref[0:1, :], gate_ref[1:2, :], gate_ref[2:3, :]
    seg_cos, seg_sin = gate_ref[3:4, :], gate_ref[4:5, :]
    lam, _, _ = retain(doc_ref, row, start, p_f, lower)
    split_store(lam_ref, 0, lam)
    pg_ref[...] = dot(normed, w_ref[:, 3 * chan :]).astype(BF16)
    proj_ref[:, : 2 * chan] = p_c.astype(BF16)
    p_r, p_i = p_c[:, :chan], p_c[:, chan:]
    split_store(src, 0, (1.0 - lam) * (p_r * sigmoid(p_r)))
    split_store(src, groups, (1.0 - lam) * (p_i * sigmoid(p_i)))
    cos_l, sin_l = lanes(cos), lanes(sin)

    def step(s, state):
        at = at_step(s)
        after = []
        for k, (h_r, h_i, cum) in enumerate(state):
            lam_s = lam_ref[k, at, :]
            a_r, a_i = lam_s * cos_l[k], lam_s * sin_l[k]
            n_r = a_r * h_r - a_i * h_i + src[k, at, :]
            n_i = a_r * h_i + a_i * h_r + src[groups + k, at, :]
            cum = cum * lam_s
            h_ref[k, at, :] = n_r
            h_ref[groups + k, at, :] = n_i
            cum_ref[k, at, :] = cum
            after.append((n_r, n_i, cum))
        return tuple(after)

    zero = lam_ref[0, 0:8, :] * 0.0
    last = lax.fori_loop(0, seg, step, ((zero, zero, zero + 1.0),) * groups, unroll=8)
    e_r, e_i, e_c = (jnp.concatenate([v[i] for v in last], axis=-1) for i in range(3))
    ends_ref[0:8, :] = e_r
    ends_ref[8:16, :] = e_i
    ends_ref[16:24, :] = e_c

    @pl.when(tile == 0)
    def _():
        tot_ref[0:2, :] = jnp.zeros((2, chan), F32)
        tot_ref[2:3, :] = jnp.ones((1, chan), F32)

    c_r, c_i, c_l = tot_ref[0:1, :], tot_ref[1:2, :], tot_ref[2:3, :]
    for j in range(8):
        m = e_c[j : j + 1, :]
        a_r, a_i = m * seg_cos, m * seg_sin
        c_r, c_i = a_r * c_r - a_i * c_i + e_r[j : j + 1, :], a_r * c_i + a_i * c_r + e_i[j : j + 1, :]
        c_l = c_l * m
    tot_ref[0:1, :] = c_r
    tot_ref[1:2, :] = c_i
    tot_ref[2:3, :] = c_l


def leave_tile(tile, x, pg_ref, h_ref, cum_ref, ends_ref, carry_ref, wo_ref, wf_ref, wd_ref, gain_ref, gate_ref,
               starts_ref, state_ref, mixed_ref, mid_ref, normed_ref, gu_ref, hid_ref, run):
    tokens, width = x.shape
    chan = width // 2
    seg = tokens // 8
    groups = chan // LANES
    cos, sin = gate_ref[0:1, :], gate_ref[1:2, :]
    seg_cos, seg_sin = gate_ref[3:4, :], gate_ref[4:5, :]

    @pl.when(tile == 0)
    def _():
        run[0:2, :] = carry_ref[0:2, :]

    c_r, c_i = run[0:1, :], run[1:2, :]
    l_r, l_i = [], []
    for j in range(8):
        l_r.append(c_r)
        l_i.append(c_i)
        m = ends_ref[16 + j : 17 + j, :]
        a_r, a_i = m * seg_cos, m * seg_sin
        c_r, c_i = (
            a_r * c_r - a_i * c_i + ends_ref[j : j + 1, :],
            a_r * c_i + a_i * c_r + ends_ref[8 + j : 9 + j, :],
        )
    run[0:1, :] = c_r
    run[1:2, :] = c_i
    start_r, start_i = jnp.concatenate(l_r, axis=0), jnp.concatenate(l_i, axis=0)
    starts_ref[...] = jnp.concatenate([start_r, start_i], axis=-1)
    cos_l, sin_l = lanes(cos), lanes(sin)

    def step(s, state):
        at = at_step(s)
        after = []
        for k, (w_r, w_i) in enumerate(state):
            w_r, w_i = w_r * cos_l[k] - w_i * sin_l[k], w_r * sin_l[k] + w_i * cos_l[k]
            cum = cum_ref[k, at, :]
            h_ref[k, at, :] += cum * w_r
            h_ref[groups + k, at, :] += cum * w_i
            after.append((w_r, w_i))
        return tuple(after)

    lax.fori_loop(0, seg, step, tuple(zip(lanes(start_r), lanes(start_i))), unroll=8)
    state = wide(h_ref, 0, 2 * groups)
    state_ref[...] = state.astype(BF16)
    p_g = pg_ref[...].astype(F32)
    mixed = (state * rms_scale(state) * gain_ref[1:2, :] * (p_g * sigmoid(p_g))).astype(BF16)
    mixed_ref[...] = mixed
    mid = x + dot(mixed, wo_ref[...])
    mid_ref[...] = mid.astype(BF16)
    normed = (mid * rms_scale(mid) * gain_ref[2:3, :]).astype(BF16)
    normed_ref[...] = normed
    hidden = wd_ref.shape[0]
    parts = pieces(hidden)

    def gate_up(part):
        return dot(normed, wf_ref[:, part]), dot(normed, wf_ref[:, moved(part, hidden)])

    after = gate_up(parts[0])
    for i, part in enumerate(parts):
        gate, up = after
        if i + 1 < len(parts):
            after = gate_up(parts[i + 1])
        gu_ref[:, part] = gate.astype(BF16)
        gu_ref[:, moved(part, hidden)] = up.astype(BF16)
        hid_ref[:, part] = (gate * sigmoid(gate) * up).astype(BF16)
    return mid + dot(hid_ref[...], wd_ref[...])


def back_out_tile(doc_ref, row, tile, start, last, dx_ref, gu_ref, mid_ref, state_ref, pg_ref, pf_ref, wo_ref, wf_ref,
                  wd_ref, gain_ref, gate_ref, dz_ref, dgu_ref, dy_ref, dpg_ref, lam_ref, g_ref, cum_ref, ends_ref,
                  tot_ref, small_ref, grad):
    tokens, width = dx_ref.shape
    chan = width // 2
    seg = tokens // 8
    groups = chan // LANES
    cos, sin, lower = gate_ref[0:1, :], gate_ref[1:2, :], gate_ref[2:3, :]
    seg_cos, seg_sin = gate_ref[3:4, :], gate_ref[4:5, :]
    dx = dx_ref[...]
    dz = dx.astype(BF16)
    dz_ref[...] = dz
    hidden = wd_ref.shape[0]
    parts = pieces(hidden)
    d_next = dot_t(dz, wd_ref[parts[0], :])
    for i, part in enumerate(parts):
        d_hid = d_next
        if i + 1 < len(parts):
            d_next = dot_t(dz, wd_ref[parts[i + 1], :])
        gate = gu_ref[:, part].astype(F32)
        up = gu_ref[:, moved(part, hidden)].astype(F32)
        sg = sigmoid(gate)
        silu = gate * sg
        dgu_ref[:, part] = (d_hid * up * (sg + silu * (1.0 - sg))).astype(BF16)
        dgu_ref[:, moved(part, hidden)] = (d_hid * silu).astype(BF16)
    d_n = dot_t(dgu_ref[...], wf_ref[...])
    mid = mid_ref[...].astype(F32)
    scale = rms_scale(mid)
    hat = mid * scale
    d_hat = d_n * gain_ref[2:3, :]
    small_ref[16:24, :] += eight_sum(d_n * hat)
    d_mid = dx + scale * (d_hat - hat * jnp.mean(d_hat * hat, axis=-1, keepdims=True))
    dx_ref[...] = d_mid
    dy = d_mid.astype(BF16)
    dy_ref[...] = dy
    d_mixed = dot_t(dy, wo_ref[...])
    p_g = pg_ref[...].astype(F32)
    sg = sigmoid(p_g)
    silu = p_g * sg
    state = state_ref[...].astype(F32)
    scale = rms_scale(state)
    hat = state * scale
    g1 = gain_ref[1:2, :]
    dpg_ref[...] = (d_mixed * hat * g1 * (sg + silu * (1.0 - sg))).astype(BF16)
    d_n = d_mixed * silu
    small_ref[8:16, :] += eight_sum(d_n * hat)
    d_hat = d_n * g1
    split_store(grad, 0, scale * (d_hat - hat * jnp.mean(d_hat * hat, axis=-1, keepdims=True)))
    lam, _, _ = retain(doc_ref, row, start, pf_ref[...].astype(F32), lower)
    split_store(lam_ref, 0, lam)
    cos_l, sin_l = lanes(cos), lanes(sin)

    def step(s, state):
        at = at_step(seg - 1 - s)
        after = []
        for k, (g_r, g_i, cum, lam_n) in enumerate(state):
            a_r, a_i = lam_n * cos_l[k], lam_n * sin_l[k]
            n_r = grad[k, at, :] + a_r * g_r + a_i * g_i
            n_i = grad[groups + k, at, :] + a_r * g_i - a_i * g_r
            cum = cum * lam_n
            g_ref[k, at, :] = n_r
            g_ref[groups + k, at, :] = n_i
            cum_ref[k, at, :] = cum
            after.append((n_r, n_i, cum, lam_ref[k, at, :]))
        return tuple(after)

    zero = lam_ref[0, 0:8, :] * 0.0
    final = lax.fori_loop(0, seg, step, ((zero, zero, zero + 1.0, zero + 1.0),) * groups, unroll=8)
    g_r, g_i, cum, lam_0 = (jnp.concatenate([v[i] for v in final], axis=-1) for i in range(4))
    e_r = lam_0 * (cos * g_r + sin * g_i)
    e_i = lam_0 * (cos * g_i - sin * g_r)
    e_c = lam_0 * cum
    ends_ref[0:8, :] = e_r
    ends_ref[8:16, :] = e_i
    ends_ref[16:24, :] = e_c

    @pl.when(tile == last)
    def _():
        tot_ref[0:2, :] = jnp.zeros((2, chan), F32)
        tot_ref[2:3, :] = jnp.ones((1, chan), F32)

    c_r, c_i, c_l = tot_ref[0:1, :], tot_ref[1:2, :], tot_ref[2:3, :]
    for j in reversed(range(8)):
        m = e_c[j : j + 1, :]
        a_r, a_i = m * seg_cos, m * seg_sin
        c_r, c_i = a_r * c_r + a_i * c_i + e_r[j : j + 1, :], a_r * c_i - a_i * c_r + e_i[j : j + 1, :]
        c_l = c_l * m
    tot_ref[0:1, :] = c_r
    tot_ref[1:2, :] = c_i
    tot_ref[2:3, :] = c_l


def back_in_tile(doc_ref, row, tile, start, last, dx_ref, x_ref, proj_ref, dpg_ref, lam_ref, starts_ref, state_ref, g_ref,
                 cum_ref, ends_ref, carry_ref, w_ref, gain_ref, gate_ref, dproj_ref, small_ref, run):
    tokens, width = dx_ref.shape
    chan = width // 2
    seg = tokens // 8
    groups = chan // LANES
    cos, sin, lower = gate_ref[0:1, :], gate_ref[1:2, :], gate_ref[2:3, :]
    seg_cos, seg_sin = gate_ref[3:4, :], gate_ref[4:5, :]

    @pl.when(tile == last)
    def _():
        run[0:2, :] = carry_ref[0:2, :]

    c_r, c_i = run[0:1, :], run[1:2, :]
    l_r, l_i = [None] * 8, [None] * 8
    for j in reversed(range(8)):
        l_r[j], l_i[j] = c_r, c_i
        m = ends_ref[16 + j : 17 + j, :]
        a_r, a_i = m * seg_cos, m * seg_sin
        c_r, c_i = (
            a_r * c_r + a_i * c_i + ends_ref[j : j + 1, :],
            a_r * c_i - a_i * c_r + ends_ref[8 + j : 9 + j, :],
        )
    run[0:1, :] = c_r
    run[1:2, :] = c_i
    cos_l, sin_l = lanes(cos), lanes(sin)

    def step(s, state):
        at = at_step(seg - 1 - s)
        after = []
        for k, (w_r, w_i) in enumerate(state):
            cum = cum_ref[k, at, :]
            g_ref[k, at, :] += cum * w_r
            g_ref[groups + k, at, :] += cum * w_i
            after.append((w_r * cos_l[k] + w_i * sin_l[k], w_i * cos_l[k] - w_r * sin_l[k]))
        return tuple(after)

    start_at = (jnp.concatenate(l_r, axis=0), jnp.concatenate(l_i, axis=0))
    lax.fori_loop(0, seg, step, tuple(zip(lanes(start_at[0]), lanes(start_at[1]))), unroll=8)
    d_n = dot_t(dpg_ref[...], w_ref[:, 3 * chan :])
    g_r, g_i = wide(g_ref, 0, groups), wide(g_ref, groups, 2 * groups)
    prior = jnp.concatenate([starts_ref[...], state_ref[...].astype(F32)[: tokens - 8, :]], axis=0)
    q_r, q_i = prior[:, :chan], prior[:, chan:]
    p_r = proj_ref[:, :chan].astype(F32)
    p_i = proj_ref[:, chan : 2 * chan].astype(F32)
    _, forget, keep = retain(doc_ref, row, start, proj_ref[:, 2 * chan :].astype(F32), lower)
    lam = wide(lam_ref, 0, groups)
    d_ar = g_r * q_r + g_i * q_i
    d_ai = g_i * q_r - g_r * q_i
    s_r, s_i = sigmoid(p_r), sigmoid(p_i)
    in_r, in_i = p_r * s_r, p_i * s_i
    d_lam = d_ar * cos + d_ai * sin - (g_r * in_r + g_i * in_i)
    d_f = jnp.concatenate([keep] * groups, axis=-1) * d_lam * (1.0 - forget)
    small_ref[24:32, :] += jnp.concatenate(
        [eight_sum(lam * (d_ai * cos - d_ar * sin)), eight_sum(d_f)], axis=-1
    )
    rest = 1.0 - lam
    d_proj = jnp.concatenate(
        [
            (rest * g_r * (s_r + in_r * (1.0 - s_r))).astype(BF16),
            (rest * g_i * (s_i + in_i * (1.0 - s_i))).astype(BF16),
            (d_f * (1.0 - lower) * forget).astype(BF16),
        ],
        axis=1,
    )
    dproj_ref[:, : 3 * chan] = d_proj
    dproj_ref[:, 3 * chan :] = dpg_ref[...]
    d_n = d_n + dot_t(d_proj, w_ref[:, : 3 * chan])
    x = x_ref[...].astype(F32)
    scale = rms_scale(x)
    hat = x * scale
    small_ref[0:8, :] += eight_sum(d_n * hat)
    d_hat = d_n * gain_ref[0:1, :]
    dx_ref[...] = dx_ref[...] + scale * (d_hat - hat * jnp.mean(d_hat * hat, axis=-1, keepdims=True))


def combine(count, me, forward, buf, rot_ref, out_ref):
    cos, sin = rot_ref[0:1, :], rot_ref[1:2, :]
    c_r = jnp.zeros_like(cos)
    c_i = jnp.zeros_like(cos)
    for k in range(count - 1, 0, -1):
        slot = k - 1 if forward else count - k - 1
        valid = me >= k if forward else me + k < count
        e_r, e_i, m = buf[slot, 0:1, :], buf[slot, 1:2, :], buf[slot, 2:3, :]
        a_r = m * cos
        a_i = m * sin if forward else -m * sin
        n_r = a_r * c_r - a_i * c_i + e_r
        n_i = a_r * c_i + a_i * c_r + e_i
        keep = jnp.where(valid, 1.0, 0.0)
        c_r, c_i = n_r * keep, n_i * keep
    out_ref[0:1, :] = c_r
    out_ref[1:2, :] = c_i


def carry_copies(count, me, tot_ref, buf, send_sem, recv_sem):
    return [
        remote(tot_ref, buf.at[k - 1], send_sem.at[k - 1], recv_sem.at[k - 1], {"seq": lax.rem(me + k, count)})
        for k in range(1, count)
    ]


class Ring:
    def __init__(self, n):
        self.n = n
        self.batch, self.seq = lax.axis_index("batch"), lax.axis_index("seq")
        z, x = self.batch // 2, self.batch % 2
        self.pos = z + x * (n - 1 - 2 * z)
        self.core, self.y = self.seq % 2, self.seq // 2
        self.sign = 1 - 2 * self.core
        self.core_peer = self.seq + self.sign
        self.y_peer = self.seq + 2 * (1 - 2 * self.y)

    def at(self, distance):
        p = (self.pos + distance + 2 * self.n) % self.n
        h = p // (self.n // 2)
        return 2 * (p + h * (self.n - 1 - 2 * p)) + h

    def ahead(self, hops):
        return self.at(self.sign * hops)


def remote(src, dst, send, recv, device):
    return pltpu.make_async_remote_copy(
        src_ref=src, dst_ref=dst, send_sem=send, recv_sem=recv, device_id=device, device_id_type=MESH
    )


def meet(devices):
    barrier = pltpu.get_barrier_semaphore()
    for device in devices:
        pl.semaphore_signal(barrier, inc=1, device_id=device, device_id_type=MESH)
    pl.semaphore_wait(barrier, len(devices))


class Gather:
    def __init__(self, ring, jobs, sems):
        self.ring, self.jobs = ring, jobs
        (self.own_sem, self.ring_send, self.ring_recv, self.y_send, self.y_recv, self.core_send,
         self.core_recv) = sems
        n = ring.n
        self.hops = ((1, n // 2, 0), (-1, n - 1 - n // 2, n // 2))

    def rows(self, j, piece):
        src, dst, u = self.jobs[j]
        ring = self.ring
        base = ring.core * (3 * u)
        whole = piece * (6 * u)
        view = lambda first, rows: dst.at[pl.ds(pl.multiple_of(whole + base + first, 16), rows)]
        return view(ring.y * u, 2 * u), view(2 * ring.y * u, u), view(2 * (1 - ring.y) * u, u)

    def own_copy(self, j):
        src, dst, u = self.jobs[j]
        return pltpu.make_async_copy(
            src, dst.at[pl.ds(pl.multiple_of(self.ring.batch * (6 * u), 16), 6 * u)], self.own_sem.at[j]
        )

    def own(self, j):
        src, dst, u = self.jobs[j]
        ring = self.ring
        mine, _, _ = self.rows(j, ring.batch)
        piece = src.at[pl.ds(pl.multiple_of(ring.core * (3 * u) + ring.y * u, 16), 2 * u)]
        for way, hops, first in self.hops:
            remote(piece, mine, self.ring_send.at[j], self.ring_recv.at[j, first],
                   {"batch": ring.ahead(way)}).start()
        self.own_copy(j).start()

    def arrived(self, j, h):
        ring = self.ring
        for way, hops, first in self.hops:
            if h < hops:
                mine, give, _ = self.rows(j, ring.ahead(-way * (h + 1)))
                on = lambda slot: remote(mine, mine, self.ring_send.at[j], self.ring_recv.at[j, first + slot],
                                         {"batch": ring.ahead(way)})
                on(h).wait_recv()
                if h + 1 < hops:
                    on(h + 1).start()
                remote(give, give, self.y_send.at[j], self.y_recv.at[j, first + h], {"seq": ring.y_peer}).start()
                remote(mine, mine, self.core_send.at[j], self.core_recv.at[j], {"seq": ring.core_peer}).start()

    def crossed(self, j, h):
        ring = self.ring
        for way, hops, first in self.hops:
            if h < hops:
                _, _, take = self.rows(j, ring.ahead(-way * (h + 1)))
                remote(take, take, self.y_send.at[j], self.y_recv.at[j, first + h], {"seq": ring.y_peer}).wait_recv()
                remote(take, take, self.core_send.at[j], self.core_recv.at[j], {"seq": ring.core_peer}).start()

    def swapped(self, j):
        src, dst, u = self.jobs[j]
        view = dst.at[0 : (self.ring.n - 1) * 3 * u]
        remote(view, view, self.core_send.at[j], self.core_recv.at[j], {"seq": self.ring.core_peer}).wait_recv()
        self.own_copy(j).wait()

    def sent(self, j):
        src, dst, u = self.jobs[j]
        for rows, send in ((2 * u, self.ring_send), (u, self.y_send), (3 * u, self.core_send)):
            view = dst.at[0 : (self.ring.n - 1) * rows]
            remote(view, view, send.at[j], self.core_recv.at[j], {"seq": self.ring.core_peer}).wait_send()


class Agenda:
    def __init__(self):
        self.calls = {}

    def add(self, when, f, *args):
        self.calls.setdefault(when, []).append((f, args))

    def run(self, now):
        for when, calls in sorted(self.calls.items(), key=lambda item: item[0]):

            @pl.when(now == when)
            def _(calls=calls):
                for f, args in calls:
                    f(*args)


OPENING = (((0, 0, 0), (0, 0, 1), (0, 0, 3), (0, 0, 2), (1, 0, 0), (1, 0, 1), (1, 0, 3), (1, 0, 2), (2, 0, 0), (2, 0, 1),
            (2, 0, 3), (2, 0, 2), (3, 0, 0), (3, 0, 1), (3, 0, 3), (4, 0, 0), (3, 0, 2), (0, 1, 0), (0, 1, 1), (0, 1, 3),
            (5, 0, 0)),)
FIRST = OPENING + (
    ((4, 0, 1), (4, 0, 3), (0, 1, 2)),
    ((4, 0, 2), (1, 1, 0)),
    ((5, 0, 1), (5, 0, 3), (1, 1, 1), (1, 1, 3)),
    ((5, 0, 2), (1, 1, 2)),
)
SECOND = (
    ((2, 1, 0), (2, 1, 1), (2, 1, 3)),
    ((2, 1, 2), (3, 1, 0)),
    ((3, 1, 1), (3, 1, 3), (4, 1, 0)),
)
LATER = (
    ((5, 0, 0), (3, 0, 2)),
    ((4, 0, 1), (4, 0, 3), (0, 1, 0)),
    ((4, 0, 2), (0, 1, 1), (0, 1, 3)),
    ((5, 0, 1), (5, 0, 3), (5, 0, 2), (0, 1, 2)),
    ((1, 1, 0), (1, 1, 1), (1, 1, 3), (1, 1, 2)),
)


def plan_gather(agenda, net, layers, mats, count, load, save):
    far = net.ring.n // 2

    def hops(j, quarter):
        for h in range(quarter * far // 4, (quarter + 1) * far // 4):
            net.arrived(j, h)
        cross(j, quarter - 1)

    def cross(j, quarter):
        for h in range(max(quarter, 0) * far // 4, (quarter + 1) * far // 4):
            net.crossed(j, h)

    def complete(j):
        cross(j, 3)
        net.swapped(j)
        if j < mats:
            save(j).start()
        else:
            if j < 2 * mats:
                save(j - mats).wait()
                net.sent(j - mats)
            load(j).start()

    for k in range(layers):
        for q, calls in enumerate((LATER if k else FIRST) + SECOND):
            for what, ahead, m in calls:
                if k + ahead < layers:
                    j = (k + ahead) * mats + m
                    when = 2 * count * k + q * count // 4
                    if what == 0:
                        agenda.add(when, net.own, j)
                    elif what == 5:
                        agenda.add(when, complete, j)
                    else:
                        agenda.add(when, hops, j, what - 1)


def forward_kernel(n, n_seq, layers, rows, paired, *refs):
    doc_ref, tok_ref = refs[:2]
    mats = 4
    given, table_ref, refs = refs[2 : 2 + mats], refs[2 + mats], refs[3 + mats :]
    if paired:
        gathered, refs = refs[: layers * mats], refs[layers * mats :]
    (xin_ref, proj_ref, pg_ref, normed_ref, starts_ref, state_ref, mixed_ref, mid_ref, normed2_ref, gu_ref, hid_ref,
     out_ref) = refs[:12]
    (xs, hs, cum, pg, ends, tot, src, lam, run, carry, buf, *rest) = refs[12:]
    weights, (load_sem, save_sem, carry_send, carry_recv), sems = rest[:mats], rest[mats : mats + 4], rest[mats + 4 :]
    layer, step = pl.program_id(0), pl.program_id(1)
    tokens, width = tok_ref.shape
    count = xs.shape[0]
    tiles = count // rows
    now = layer * (2 * count) + step
    me = lax.axis_index("seq")
    peers = [{"seq": lax.rem(me + k, n_seq)} for k in range(1, n_seq)]
    agenda = Agenda()

    def load(j):
        source = gathered[j] if paired else given[j % mats].at[j // mats]
        return pltpu.make_async_copy(source, weights[j % mats], load_sem.at[j % mats])

    def ready(j):
        load(j).wait()

    if paired:
        ring = Ring(n)
        jobs = [
            (given[m].at[k], gathered[k * mats + m] if k else weights[m], given[m].shape[1] // 6)
            for k in range(layers) for m in range(mats)
        ]
        net = Gather(ring, jobs, sems)

        def save(j):
            return pltpu.make_async_copy(weights[j], gathered[j], save_sem.at[j])

        agenda.add(0, meet, [{"batch": ring.ahead(1)}, {"batch": ring.ahead(-1)}] + peers)
        plan_gather(agenda, net, layers, mats, count, load, save)
    else:
        agenda.add(0, meet, peers)
        for k in range(layers):
            agenda.add(2 * count * k, lambda k=k: load(k * mats).start())
            for m in range(1, mats):
                agenda.add(2 * count * k + count - 1, lambda j=k * mats + m: load(j).start())
    for k in range(1 if paired else 0, layers):
        agenda.add(2 * count * k, ready, k * mats)
        for m in range(1, mats):
            agenda.add(2 * count * k + count, ready, k * mats + m)
    agenda.run(now)

    tile = lax.rem(step, count)
    row, at_row = tile // tiles, lax.rem(tile, tiles)
    start = (me * tiles + at_row) * tokens
    gains, gate = table_ref.at[layer, 0:8], table_ref.at[layer, 8:16, 0 : width // 2]

    @pl.when((layer == 0) & (step < count))
    def _():
        xs[tile] = dot(order_matrix(tokens, False), tok_ref[...])

    @pl.when(step < count)
    def _():
        x = xs[tile]
        xin_ref[...] = x.astype(BF16)
        enter_tile(doc_ref, row, at_row, start, x, weights[0], gains, gate, proj_ref, pg.at[tile], normed_ref, hs.at[tile],
                   cum.at[tile], ends.at[tile], tot.at[row], src, lam)
        pg_ref[...] = pg[tile]

    def exchange():
        return carry_copies(n_seq, me, tot.at[row], buf.at[layer, row], carry_send.at[layer, row], carry_recv.at[layer, row])

    @pl.when((step < count) & (lax.rem(step, tiles) == tiles - 1))
    def _():
        for copy in exchange():
            copy.start()

    @pl.when((step >= count) & (lax.rem(step, tiles) == 0))
    def _():
        for copy in exchange():
            copy.wait()
        combine(n_seq, me, True, buf.at[layer, row], gate.at[5:8], carry.at[row])

    @pl.when(step >= count)
    def _():
        out = leave_tile(at_row, xs[tile], pg.at[tile], hs.at[tile], cum.at[tile], ends.at[tile], carry.at[row],
                         weights[1], weights[2], weights[3], gains, gate, starts_ref, state_ref, mixed_ref, mid_ref,
                         normed2_ref, gu_ref, hid_ref, run)
        xs[tile] = out

        @pl.when(layer == layers - 1)
        def _():
            out_ref[...] = out.astype(BF16)

    if paired:

        @pl.when(now == layers * 2 * count - 1)
        def _():
            for j in range(layers * mats):
                if j < mats and layers == 1:
                    save(j).wait()
                if j >= mats or layers == 1:
                    net.sent(j)


def tile_specs(tokens, layer):
    def flat(w, when, col=0):
        return pl.BlockSpec((None, tokens, w), lambda k, s: (layer(k), when(s), col))

    def few(r, w, when):
        return pl.BlockSpec((None, None, r, w), lambda k, s: (layer(k), when(s), 0, 0))

    return flat, few


def run_forward(n, n_seq, paired, rows, tokens, docs, x, sources, table):
    layers = sources[0].shape[0]
    total, width = x.shape
    chan = width // 2
    hidden = sources[2].shape[2] // 2
    count = total // tokens
    mats = len(sources)
    jobs = layers * mats if paired else 0
    shape = jax.ShapeDtypeStruct
    dma = pltpu.SemaphoreType.DMA
    any_ = pl.BlockSpec(memory_space=pl.ANY)

    def first(step):
        return jnp.minimum(step, count - 1)

    def second(step):
        return jnp.maximum(step - count, 0)

    flat, few = tile_specs(tokens, lambda k: k)

    def kept(w):
        return shape((layers, total, w), BF16)

    full = [((n if paired else 1) * w.shape[1], w.shape[2]) for w in sources]
    last = layers - 1
    outs = pl.pallas_call(
        functools.partial(forward_kernel, n, n_seq, layers, rows, paired),
        grid=(layers, 2 * count),
        in_specs=[
            pl.BlockSpec(memory_space=pltpu.SMEM),
            pl.BlockSpec((tokens, width), lambda k, s: (jnp.where(k == 0, first(s), count - 1), 0)),
        ]
        + [any_] * mats
        + [whole(*table.shape)],
        out_specs=[any_] * jobs
        + [
            flat(width, first),
            flat(3 * chan, first),
            flat(width, first),
            flat(width, first),
            few(8, width, second),
            flat(width, second),
            flat(width, second),
            flat(width, second),
            flat(width, second),
            flat(2 * hidden, second),
            flat(hidden, second),
            pl.BlockSpec((tokens, width), lambda k, s: (jnp.where(k == last, second(s), 0), 0)),
        ],
        out_shape=[shape(f, BF16) for _ in range(layers) for f in full][:jobs]
        + [
            kept(width),
            kept(3 * chan),
            kept(width),
            kept(width),
            shape((layers, count, 8, width), F32),
            kept(width),
            kept(width),
            kept(width),
            kept(width),
            kept(2 * hidden),
            kept(hidden),
            shape((total, width), BF16),
        ],
        scratch_shapes=[
            pltpu.VMEM((count, tokens, width), F32),
            pltpu.VMEM((count, width // LANES, tokens, LANES), F32),
            pltpu.VMEM((count, chan // LANES, tokens, LANES), F32),
            pltpu.VMEM((count, tokens, width), BF16),
            pltpu.VMEM((count, 24, chan), F32),
            pltpu.VMEM((rows, 8, chan), F32),
            pltpu.VMEM((width // LANES, tokens, LANES), F32),
            pltpu.VMEM((chan // LANES, tokens, LANES), F32),
            pltpu.VMEM((8, chan), F32),
            pltpu.VMEM((rows, 8, chan), F32),
            pltpu.VMEM((layers, rows, n_seq - 1, 8, chan), F32),
        ]
        + [pltpu.VMEM(f, BF16) for f in full]
        + [dma((mats,)), dma((mats,)), dma((layers, rows, n_seq - 1)), dma((layers, rows, n_seq - 1))]
        + [dma((s,)) if one else dma((s, n - 1)) for s in [max(jobs, 1)] for one in (1, 1, 0, 1, 0, 1, 1)],
        compiler_params=pltpu.CompilerParams(collective_id=3, has_side_effects=True, vmem_limit_bytes=LIMIT),
    )(docs, x, *sources, table)
    return outs[:jobs], outs[jobs:]


def backward_kernel(n_seq, layers, rows, mats, *refs):
    doc_ref, cot_ref = refs[:2]
    given, refs = refs[2 : 2 + layers * mats], refs[2 + layers * mats :]
    (table_ref, gu_ref, mid_ref, state_ref, pg_ref, pf_ref, x_ref, proj_ref, starts_ref, prior_ref, dz_ref,
     dgu_ref, dy_ref, dproj_ref, dtok_ref, small_ref) = refs[:16]
    (dxs, gs, cum, lam, dpg, ends, tot, grad, run, carry, buf, *rest) = refs[16:]
    weights, (load_sem, carry_send, carry_recv) = rest[:mats], rest[mats:]
    turn, step = pl.program_id(0), pl.program_id(1)
    layer = layers - 1 - turn
    tokens, width = cot_ref.shape
    count = dxs.shape[0]
    tiles = count // rows
    now = turn * (2 * count) + step
    me = lax.axis_index("seq")
    agenda = Agenda()

    def load(t, m):
        return pltpu.make_async_copy(given[(layers - 1 - t) * mats + m], weights[m], load_sem.at[m])

    def fetch(t, m):
        load(t, m).start()

    def ready(t, m):
        load(t, m).wait()

    for m in (3, 2, 1):
        agenda.add(0, fetch, 0, m)
    agenda.add(0, meet, [{"seq": lax.rem(me + k, n_seq)} for k in range(1, n_seq)])
    for t in range(layers):
        begin = 2 * count * t
        agenda.add(begin, fetch, t, 0)
        for m in (3, 2, 1):
            agenda.add(begin, ready, t, m)
        agenda.add(begin + count, ready, t, 0)
        if t + 1 < layers:
            for m in (3, 2, 1):
                agenda.add(begin + count, fetch, t + 1, m)
    agenda.run(now)

    tile = count - 1 - lax.rem(step, count)
    row, at_row = tile // tiles, lax.rem(tile, tiles)
    start = (me * tiles + at_row) * tokens
    gains, gate = table_ref.at[layer, 0:8], table_ref.at[layer, 8:16, 0 : width // 2]

    @pl.when(step == 0)
    def _():
        small_ref[...] = jnp.zeros_like(small_ref)

    @pl.when((turn == 0) & (step < count))
    def _():
        dxs[tile] = dot(order_matrix(tokens, False), cot_ref[...])

    @pl.when(step < count)
    def _():
        back_out_tile(doc_ref, row, at_row, start, tiles - 1, dxs.at[tile], gu_ref, mid_ref, state_ref, pg_ref, pf_ref,
                      weights[1], weights[2], weights[3], gains, gate, dz_ref, dgu_ref, dy_ref, dpg.at[tile],
                      lam.at[tile], gs.at[tile], cum.at[tile], ends.at[tile], tot.at[row], small_ref, grad)

    def exchange():
        return carry_copies(n_seq, me, tot.at[row], buf.at[turn, row], carry_send.at[turn, row], carry_recv.at[turn, row])

    @pl.when((step < count) & (lax.rem(step, tiles) == tiles - 1))
    def _():
        for copy in exchange():
            copy.start()

    @pl.when((step >= count) & (lax.rem(step, tiles) == 0))
    def _():
        for copy in exchange():
            copy.wait()
        combine(n_seq, me, False, buf.at[turn, row], gate.at[5:8], carry.at[row])

    @pl.when(step >= count)
    def _():
        back_in_tile(doc_ref, row, at_row, start, tiles - 1, dxs.at[tile], x_ref, proj_ref, dpg.at[tile], lam.at[tile],
                     starts_ref, prior_ref, gs.at[tile], cum.at[tile], ends.at[tile], carry.at[row], weights[0],
                     gains, gate, dproj_ref, small_ref, run)

        @pl.when(turn == layers - 1)
        def _():
            dtok_ref[...] = dxs[tile]


def run_backward(n_seq, rows, tokens, docs, cotangent, weights, table, kept):
    x, proj, p_g, starts, state, mid, gu = kept
    layers, total, width = x.shape
    chan = width // 2
    hidden = gu.shape[2] // 2
    count = total // tokens
    mats = len(weights) // layers
    shape = jax.ShapeDtypeStruct
    dma = pltpu.SemaphoreType.DMA
    any_ = pl.BlockSpec(memory_space=pl.ANY)
    last = layers - 1

    def first(step):
        return count - 1 - jnp.minimum(step, count - 1)

    def second(step):
        return count - 1 - jnp.maximum(step - count, 0)

    flat, few = tile_specs(tokens, lambda k: last - k)
    return pl.pallas_call(
        functools.partial(backward_kernel, n_seq, layers, rows, mats),
        grid=(layers, 2 * count),
        in_specs=[
            pl.BlockSpec(memory_space=pltpu.SMEM),
            pl.BlockSpec((tokens, width), lambda k, s: (jnp.where(k == 0, first(s), 0), 0)),
        ]
        + [any_] * len(weights)
        + [
            whole(*table.shape),
            flat(2 * hidden, first),
            flat(width, first),
            flat(width, first),
            flat(width, first),
            flat(chan, first, 2),
            flat(width, second),
            flat(3 * chan, second),
            few(8, width, second),
            flat(width, second),
        ],
        out_specs=[
            flat(width, first),
            flat(2 * hidden, first),
            flat(width, first),
            flat(3 * chan + width, second),
            pl.BlockSpec((tokens, width), lambda k, s: (jnp.where(k == last, second(s), count - 1), 0)),
            pl.BlockSpec((None, 32, width), lambda k, s: (last - k, 0, 0)),
        ],
        out_shape=[
            shape((layers, total, width), BF16),
            shape((layers, total, 2 * hidden), BF16),
            shape((layers, total, width), BF16),
            shape((layers, total, 3 * chan + width), BF16),
            shape((total, width), F32),
            shape((layers, 32, width), F32),
        ],
        scratch_shapes=[
            pltpu.VMEM((count, tokens, width), F32),
            pltpu.VMEM((count, width // LANES, tokens, LANES), F32),
            pltpu.VMEM((count, chan // LANES, tokens, LANES), F32),
            pltpu.VMEM((count, chan // LANES, tokens, LANES), F32),
            pltpu.VMEM((count, tokens, width), BF16),
            pltpu.VMEM((count, 24, chan), F32),
            pltpu.VMEM((rows, 8, chan), F32),
            pltpu.VMEM((width // LANES, tokens, LANES), F32),
            pltpu.VMEM((8, chan), F32),
            pltpu.VMEM((rows, 8, chan), F32),
            pltpu.VMEM((layers, rows, n_seq - 1, 8, chan), F32),
        ]
        + [pltpu.VMEM(w.shape, BF16) for w in weights[:mats]]
        + [dma((mats,)), dma((layers, rows, n_seq - 1)), dma((layers, rows, n_seq - 1))],
        compiler_params=pltpu.CompilerParams(collective_id=2, has_side_effects=True, vmem_limit_bytes=LIMIT),
    )(docs, cotangent, *weights, table, gu, mid, state, p_g, proj, x, proj, starts, state)


def add_rows(dst, dst_row, parts, rows):
    def block(i, _):
        step = pl.multiple_of(i * 16, 16)
        total = None
        for ref, first in parts:
            value = ref[pl.ds(pl.multiple_of(first + step, 16), 16), :].astype(F32)
            total = value if total is None else total + value
        dst[pl.ds(pl.multiple_of(dst_row + step, 16), 16), :] = total.astype(dst.dtype)
        return 0

    lax.fori_loop(0, rows // 16, block, 0)


def grads_kernel(n, plan, *refs):
    jobs = len(plan)
    lefts, rights, small = refs[:jobs], refs[jobs : 2 * jobs], refs[2 * jobs]
    outs_count = 1 + max(p[0] for p in plan)
    outs, rest = refs[2 * jobs + 1 : 2 * jobs + 1 + outs_count], refs[2 * jobs + 1 + outs_count :]
    gains_out, gate_out, rest = rest[0], rest[1], rest[2:]
    grads, core_buf, y_buf, ring_buf, fin_buf = (rest[i * jobs : (i + 1) * jobs] for i in range(5))
    (left_big, left_small, right_buf, small_buf, left_sem, right_sem, core_send, core_recv, y_send, y_recv,
     ring_send, ring_recv, end_send, end_recv, small_send, small_recv) = rest[5 * jobs :]
    ring = Ring(n)
    far, near = n // 2, n - 1 - n // 2
    core_dev, y_dev = {"seq": ring.core_peer}, {"seq": ring.y_peer}
    y, core = ring.y, ring.core
    rounds = [core_dev, y_dev]
    d = 1
    while d < n:
        rounds.append({"batch": ring.batch + d * (1 - 2 * ((ring.batch // d) % 2))})
        d *= 2
    us = [g.shape[0] // n // 6 for g in grads]
    split = [p[2] for p in plan]
    own_rows = [(2 if s else 3) * u for s, u in zip(split, us)]

    def left_copy(j):
        buf = (left_big, left_small)[j % 2]
        return pltpu.make_async_copy(lefts[j].at[plan[j][1]], buf.at[:, 0 : plan[j][3]], left_sem.at[j % 2])

    chunks = []
    for j, (_, _, _, rows, cols, _, _) in enumerate(plan):
        first = 0
        while first < cols:
            size = min(CHUNK, cols - first)
            chunks.append((j, first, size, first + size == cols))
            first += size

    def right_copy(i):
        j, first, size, _ = chunks[i]
        return pltpu.make_async_copy(
            rights[j].at[plan[j][1], :, plan[j][5] + first : plan[j][5] + first + size], right_buf.at[i % 2, :, 0:size], right_sem.at[i % 2]
        )

    left_copy(0).start()
    right_copy(0).start()
    right_copy(1).start()
    left_copy(1).start()
    meet([{"batch": ring.ahead(1)}, {"batch": ring.ahead(-1)}] + rounds)

    order = []
    for h in range(far):
        order.append((1, h, far - h))
        if h < near:
            order.append((-1, h, near - h))
    order.append((0, 0, 0))
    last = len(order)

    def rows_at(ref, first, rows):
        return ref.at[pl.ds(pl.multiple_of(first, 16), rows)]

    def core_copy(j, slot, piece):
        u = us[j]
        return remote(rows_at(grads[j], piece * (6 * u) + (1 - core) * (3 * u), 3 * u),
                      core_buf[j].at[slot], core_send.at[j], core_recv.at[j, slot], core_dev)

    def y_copy(j, slot, piece):
        u = us[j]
        src = rows_at(grads[j], piece * (6 * u) + core * (3 * u) + 2 * (1 - y) * u, u)
        return remote(src, y_buf[j].at[slot], y_send.at[j], y_recv.at[j, slot], y_dev)

    def mine(j, piece):
        u = us[j]
        return piece * (6 * u) + core * (3 * u) + (y * u if split[j] else 0)

    def ring_copy(j, slot, way, piece):
        return remote(rows_at(grads[j], mine(j, piece), own_rows[j]), ring_buf[j].at[slot], ring_send.at[j],
                      ring_recv.at[j, slot], {"batch": ring.ahead(way)})

    def small_round(r):
        return remote(small_buf.at[2 * r], small_buf.at[2 * r + 1], small_send.at[r], small_recv.at[r], rounds[r])

    layers = small.shape[0]
    for k in range(layers):
        for i in range(4):
            small_buf[0, 4 * k + i : 4 * k + i + 1, :] = jnp.sum(small[k, 8 * i : 8 * i + 8, :], axis=0, keepdims=True)
    small_round(0).start()

    def small_step(r):
        small_round(r).wait_recv()
        total = small_buf[2 * r] + small_buf[2 * r + 1]
        if r + 1 < len(rounds):
            small_buf[2 * r + 2] = total
            small_round(r + 1).start()
        else:
            chan = gate_out.shape[2]
            for k in range(layers):
                gains_out[k] = total[4 * k : 4 * k + 3, :]
                gate_out[k, 0:1, :] = total[4 * k + 3 : 4 * k + 4, :chan]
                gate_out[k, 1:2, :] = total[4 * k + 3 : 4 * k + 4, chan:]

    def begin(j):
        for slot, (way, h, dist) in enumerate(order):
            core_copy(j, slot, ring.ahead(-way * dist)).start()

    def cross(j, slot):
        way, h, dist = order[slot]
        piece = ring.ahead(way * dist)
        u = us[j]
        core_copy(j, slot, piece).wait_recv()
        if not split[j]:
            return
        give = 2 * (1 - y) * u
        at = piece * (6 * u) + core * (3 * u) + give
        add_rows(grads[j], at, [(grads[j], at), (core_buf[j].at[slot], give)], u)
        y_copy(j, slot, piece).start()

    def hop(j, slot):
        way, h, dist = order[slot]
        piece = ring.ahead(way * dist)
        u = us[j]
        if split[j]:
            y_copy(j, slot, piece).wait_recv()
        if way == 0:
            prior = [i for i, o in enumerate(order) if o[2] == 1]
        elif h:
            prior = [i for i, o in enumerate(order) if o[0] == way and o[1] == h - 1]
        else:
            prior = []
        for i in prior:
            ring_copy(j, i, order[i][0], piece).wait_recv()
        at = mine(j, piece)
        base = [(grads[j], at), (core_buf[j].at[slot], y * u if split[j] else 0)]
        base += [(ring_buf[j].at[i], 0) for i in prior]
        if split[j]:
            for by, more in ((y * u, [(y_buf[j].at[slot], 0)]), ((1 - y) * u, [])):
                add_rows(grads[j], at + by, [(r, f + by) for r, f in base] + more, u)
        else:
            add_rows(grads[j], at, base, 3 * u)
        if way:
            ring_copy(j, slot, way, piece).start()

    def fin_copy(j):
        return remote(rows_at(grads[j], mine(j, ring.batch), own_rows[j]), fin_buf[j], end_send.at[j, 0],
                      end_recv.at[j, 0], y_dev)

    def out_of(j):
        return outs[plan[j][0]].at[plan[j][1], :, plan[j][5] : plan[j][5] + plan[j][4]]

    def half_copy(j):
        half = out_of(j).at[pl.ds(pl.multiple_of(core * (3 * us[j]), 16), 3 * us[j])]
        return remote(half, half, end_send.at[j, 1], end_recv.at[j, 1], core_dev)

    def finish(j):
        u = us[j]
        fin_copy(j).wait_recv()
        out = out_of(j)
        at, to = mine(j, ring.batch), core * (3 * u)
        if split[j]:
            add_rows(out, to + 2 * y * u, [(grads[j], at + y * u)], u)
            add_rows(out, to + 2 * (1 - y) * u, [(fin_buf[j], (1 - y) * u)], u)
            add_rows(out, to + u, [(grads[j], at + (1 - y) * u), (fin_buf[j], y * u)], u)
        else:
            add_rows(out, to, [(grads[j], at), (fin_buf[j], 0)], 3 * u)
        half_copy(j).start()

    steps = far + 4

    def advance(j, t):
        now = [i for i, o in enumerate(order) if o[0] and o[1] == t]
        before = [i for i, o in enumerate(order) if o[0] and o[1] == t - 1]
        for slot in before:
            hop(j, slot)
        for slot in now:
            cross(j, slot)
        if t == far - 1:
            cross(j, last - 1)
        if t == far + 1:
            hop(j, last - 1)
            fin_copy(j).start()
        if t == far + 2:
            finish(j)
        if t == far + 3:
            half_copy(j).wait_recv()

    stage = {}

    def advance_all(turn):
        for j in list(stage):
            if j % 2 == turn:
                advance(j, stage[j])
                stage[j] += 1
                if stage[j] == steps:
                    del stage[j]

    small_at = 0
    for i, (j, first, size, done) in enumerate(chunks):
        if first == 0:
            left_copy(j).wait()
        right_copy(i).wait()
        left = (left_big, left_small)[j % 2]

        def multiply(b, _, i=i, j=j, first=first, size=size, left=left):
            at = pl.multiple_of(b * 256, 256)
            part = lax.dot_general(
                left[:, pl.ds(at, 256)], right_buf[i % 2, :, 0:size], (((0,), (0,)), ((), ())),
                preferred_element_type=F32,
            )
            grads[j][pl.ds(at, 256), first : first + size] = part.astype(BF16)
            return 0

        lax.fori_loop(0, plan[j][3] // 256, multiply, 0)
        if i + 2 < len(chunks):
            right_copy(i + 2).start()
        if done and j + 2 < jobs:
            left_copy(j + 2).start()
        advance_all(i % 2)
        if done:
            begin(j)
            stage[j] = 0
        if small_at < len(rounds):
            small_step(small_at)
            small_at += 1
    i = 0
    while stage:
        advance_all(i % 2)
        i += 1
    while small_at < len(rounds):
        small_step(small_at)
        small_at += 1
    for j in range(jobs):
        u = us[j]
        fin_copy(j).wait_send()
        half_copy(j).wait_send()
        remote(core_buf[j], core_buf[j], core_send.at[j], core_recv.at[j, 0], core_dev).wait_send()
        if split[j]:
            remote(y_buf[j], y_buf[j], y_send.at[j], y_recv.at[j, 0], y_dev).wait_send()
        remote(ring_buf[j], ring_buf[j], ring_send.at[j], ring_recv.at[j, 0], core_dev).wait_send()
    for r in range(len(rounds)):
        small_round(r).wait_send()


def grads_and_scatter(n, plan, lefts, rights, small):
    jobs = len(plan)
    full = []
    for (m, k, crosses, part, of), a, b in zip(plan, lefts, rights):
        cols = b.shape[2] // of
        full.append((m, k, crosses, a.shape[2], cols, part * cols, b.shape[2]))
    plan = full
    tokens = lefts[0].shape[1]
    layers, _, width = small.shape
    dma = pltpu.SemaphoreType.DMA
    rounds = 2 + (n - 1).bit_length()
    sizes = [(p[3] // n // 6, p[4], p[2]) for p in plan]
    outs = {p[0]: jax.ShapeDtypeStruct((layers, p[3] // n, p[6]), BF16) for p in plan}
    vm = pl.BlockSpec(memory_space=pltpu.VMEM)
    any_ = pl.BlockSpec(memory_space=pl.ANY)

    def bufs(f):
        return [pltpu.VMEM(f(u, w, s), BF16) for u, w, s in sizes]

    return pl.pallas_call(
        functools.partial(grads_kernel, n, plan),
        out_shape=[outs[m] for m in sorted(outs)]
        + [jax.ShapeDtypeStruct((layers, 3, width), F32), jax.ShapeDtypeStruct((layers, 2, width // 2), F32)],
        in_specs=[any_] * (2 * jobs) + [vm],
        out_specs=[vm] * (len(outs) + 2),
        scratch_shapes=bufs(lambda u, w, s: (6 * u * n, w))
        + bufs(lambda u, w, s: (n, 3 * u, w))
        + bufs(lambda u, w, s: (n if s else 1, u, w))
        + bufs(lambda u, w, s: (n - 1, 2 * u if s else 3 * u, w))
        + bufs(lambda u, w, s: (2 * u if s else 3 * u, w))
        + [
            pltpu.VMEM((tokens, max(p[3] for p in plan[0::2])), BF16),
            pltpu.VMEM((tokens, max(p[3] for p in plan[1::2])), BF16),
            pltpu.VMEM((2, tokens, CHUNK), BF16),
            pltpu.VMEM((2 * rounds, 4 * layers, width), F32),
            dma((2,)), dma((2,)), dma((jobs,)), dma((jobs, n)), dma((jobs,)), dma((jobs, n)), dma((jobs,)),
            dma((jobs, n)), dma((jobs, 2)), dma((jobs, 2)), dma((rounds,)), dma((rounds,)),
        ],
        compiler_params=pltpu.CompilerParams(
            collective_id=4, has_side_effects=True, vmem_limit_bytes=63 * 1024 * 1024
        ),
    )(*lefts, *rights, small)


def finish_kernel(mats, *refs):
    grads, (out_ref, dtok_ref) = refs[:mats], refs[mats : mats + 2]
    wide_refs, (out_to, dtok_to) = refs[mats + 2 : 2 * mats + 2], refs[2 * mats + 2 :]
    for grad, to in zip(grads, wide_refs):
        to[...] = grad[...].astype(F32)
    order = order_matrix(out_ref.shape[0], True)
    out_to[...] = dot(order, out_ref[...]).astype(BF16)
    dx = dtok_ref[...]
    high = dx.astype(BF16)
    dtok_to[...] = dot(order, high) + dot(order, (dx - high.astype(F32)).astype(BF16))


def finish(tokens, grads, block_out, d_tokens):
    total, width = block_out.shape
    count = total // tokens
    if grads[0].shape[0] * 2 != count:
        def ordered(values):
            return values.reshape(count, tokens // 8, 8, width).swapaxes(1, 2).reshape(total, width)

        return [g.astype(F32) for g in grads], ordered(block_out), ordered(d_tokens)
    halves = [
        pl.BlockSpec((1, g.shape[1] // 2, g.shape[2]), lambda i: (i // 2, i % 2, 0)) for g in grads
    ]
    tile = pl.BlockSpec((tokens, width), lambda i: (i, 0))
    outs = pl.pallas_call(
        functools.partial(finish_kernel, len(grads)),
        grid=(count,),
        in_specs=halves + [tile, tile],
        out_specs=halves + [tile, tile],
        out_shape=[jax.ShapeDtypeStruct(g.shape, F32) for g in grads]
        + [jax.ShapeDtypeStruct(v.shape, v.dtype) for v in (block_out, d_tokens)],
        compiler_params=pltpu.CompilerParams(vmem_limit_bytes=LIMIT),
    )(*grads, block_out, d_tokens)
    return outs[:-2], outs[-2], outs[-1]


def contract_rows(left, right):
    return lax.dot_general(
        left, right, (((0,), (0,)), ((), ())), preferred_element_type=F32
    ).astype(BF16)


def shards(
    tokens_in, doc_starts, mixer_in, mixer_out, ffn_in, ffn_out, gains, gate_params, cotangent
):
    rows, length, width = tokens_in.shape
    layers = gains.shape[0]
    chan = width // 2
    total = rows * length
    tokens = min(length, 256)
    seg = tokens // 8
    n, n_seq = lax.axis_size("batch"), lax.axis_size("seq")
    sources = (mixer_in, mixer_out, ffn_in, ffn_out)
    paired = n_seq == 4 and n % 4 == 0 and all(w.shape[1] % 96 == 0 for w in sources)
    theta, lower = gate_params[:, 0:1], gate_params[:, 1:2]
    at = lax.broadcasted_iota(jnp.int32, (layers, 8, chan), 1)
    times = jnp.where(at < 3, 1, jnp.where(at < 5, seg, length)).astype(F32)
    quarter = jnp.where((at == 1) | (at == 4) | (at == 6), math.pi / 2, 0.0)
    gate_rows = jnp.where(at == 2, lower, jnp.cos(theta * times - quarter))
    table = jnp.concatenate(
        [jnp.pad(gains, ((0, 0), (0, 5), (0, 0))), jnp.pad(gate_rows, ((0, 0), (0, 0), (0, width - chan)))], axis=1
    )
    x = tokens_in.reshape(total, width)
    if paired:
        weights, kept = run_forward(n, n_seq, True, rows, tokens, doc_starts, x, sources, table)
    else:
        stacked = [lax.all_gather(w, "batch", axis=1, tiled=True) for w in sources]
        weights = [w[k] for k in range(layers) for w in stacked]
        _, kept = run_forward(n, n_seq, False, rows, tokens, doc_starts, x, stacked, table)
    x_in, proj, p_g, normed, starts, state, mixed, mid, normed2, gu, hid, block_out = kept
    dz, d_gu, dy, d_proj, d_tokens, small = run_backward(
        n_seq, rows, tokens, doc_starts, cotangent.reshape(total, width), weights, table,
        (x_in, proj, p_g, starts, state, mid, gu),
    )
    pairs = ((normed, d_proj), (mixed, dy), (normed2, d_gu), (hid, dz))
    if paired:
        plan = []
        for k in reversed(range(layers)):
            jobs = ORDERS[0] if k == layers - 1 else ORDERS[1]
            plan += [(m, k, m != 0, part, of) for m, part, of in jobs]
        *outs, d_gains, d_gate = grads_and_scatter(
            n, plan, [pairs[p[0]][0] for p in plan], [pairs[p[0]][1] for p in plan], small
        )
    else:
        outs = []
        for left, right in pairs:
            whole_grads = jnp.stack([contract_rows(left[k], right[k]) for k in range(layers)])
            part = lax.psum_scatter(whole_grads, "batch", scatter_dimension=1, tiled=True)
            outs.append(lax.psum(part, "seq"))
        totals = lax.psum(jnp.sum(small.reshape(layers, 4, 8, width), axis=2), ("batch", "seq"))
        d_gains, d_gate = totals[:, :3], totals[:, 3].reshape(layers, 2, chan)
    outs, block_out, d_tokens = finish(tokens, outs, block_out, d_tokens)
    return (
        block_out.reshape(rows, length, width),
        d_tokens.reshape(rows, length, width),
        *outs,
        d_gains,
        d_gate,
    )


def solution(mesh):
    tok = P("batch", "seq", None)
    mat = P(None, "batch", None)
    return jax.shard_map(
        shards,
        mesh=mesh,
        in_specs=(tok, P("batch", None), mat, mat, mat, mat, P(), P(), tok),
        out_specs=(tok, tok, mat, mat, mat, mat, P(), P()),
        check_vma=False,
    )
```

```python
import functools
import math

import jax
import jax.numpy as jnp
from jax import lax
from jax.experimental import pallas as pl
from jax.experimental.pallas import tpu as pltpu
from jax.sharding import PartitionSpec as P

EPS = 1e-06
F32 = jnp.float32
BF16 = jnp.bfloat16
LANES = 128
CHUNK = 1024
ORDERS = (((1, 0, 1), (2, 0, 2), (3, 0, 1), (2, 1, 2), (0, 0, 1)), ((2, 0, 2), (3, 0, 1), (2, 1, 2), (0, 0, 1), (1, 0, 1)))
MESH = pl.DeviceIdType.MESH


def sigmoid(values):
    return 1.0 / (1.0 + jnp.exp(-values))


def rms_scale(values):
    return lax.rsqrt(jnp.mean(values * values, axis=-1, keepdims=True) + EPS)


def dot(left, right):
    return jnp.dot(left, right, preferred_element_type=F32)


def dot_t(left, right):
    return lax.dot_general(left, right, (((1,), (1,)), ((), ())), preferred_element_type=F32)


def eight_sum(values):
    rows, cols = values.shape
    return jnp.sum(values.reshape(rows // 8, 8, cols), axis=0)


def wide(ref, first, last):
    return jnp.concatenate([ref[g] for g in range(first, last)], axis=-1)


def split_store(ref, first, values):
    for g in range(values.shape[1] // LANES):
        ref[first + g] = values[:, g * LANES : (g + 1) * LANES]


def lanes(values):
    return [values[:, g * LANES : (g + 1) * LANES] for g in range(values.shape[1] // LANES)]


LIMIT = 60 * 1024 * 1024


def whole(*shape):
    return pl.BlockSpec(shape, lambda *_: (0,) * len(shape), pipeline_mode=pl.Buffered(1))


def order_matrix(tokens, back):
    shape = (tokens, tokens)
    here = lax.broadcasted_iota(jnp.int32, shape, 1 if back else 0)
    there = lax.broadcasted_iota(jnp.int32, shape, 0 if back else 1)
    return jnp.where(there == (here & 7) * (tokens // 8) + (here >> 3), 1.0, 0.0).astype(BF16)


def reset_mask(doc_ref, row, first, tokens):
    here = lax.broadcasted_iota(jnp.int32, (tokens, LANES), 0)
    pos = (here & 7) * (tokens // 8) + (here >> 3) + first
    hit = pos == doc_ref[row, 0]
    for k in range(1, doc_ref.shape[1]):
        hit = hit | (pos == doc_ref[row, k])
    return hit


def retain(doc_ref, row, first, p_f, lower):
    tokens, chan = p_f.shape
    forget = sigmoid(p_f)
    lam = lower + (1.0 - lower) * forget
    keep = jnp.where(reset_mask(doc_ref, row, first, tokens), 0.0, 1.0)
    return lam * jnp.concatenate([keep] * (chan // LANES), axis=-1), forget, keep


def pieces(total):
    size = 512 if total % 512 == 0 else total
    return [slice(first, first + size) for first in range(0, total, size)]


def moved(part, by):
    return slice(part.start + by, part.stop + by)


def at_step(s):
    return pl.ds(pl.multiple_of(s * 8, 8), 8)


def enter_tile(doc_ref, row, tile, start, x, w_ref, gain_ref, gate_ref, proj_ref, pg_ref, normed_ref, h_ref, cum_ref,
               ends_ref, tot_ref, src, lam_ref):
    tokens, width = x.shape
    chan = width // 2
    seg = tokens // 8
    groups = chan // LANES
    normed = (x * rms_scale(x) * gain_ref[0:1, :]).astype(BF16)
    normed_ref[...] = normed
    p_f = dot(normed, w_ref[:, 2 * chan : 3 * chan])
    p_c = dot(normed, w_ref[:, : 2 * chan])
    proj_ref[:, 2 * chan :] = p_f.astype(BF16)
    cos, sin, lower = gate_ref[0:1, :], gate_ref[1:2, :], gate_ref[2:3, :]
    seg_cos, seg_sin = gate_ref[3:4, :], gate_ref[4:5, :]
    lam, _, _ = retain(doc_ref, row, start, p_f, lower)
    split_store(lam_ref, 0, lam)
    pg_ref[...] = dot(normed, w_ref[:, 3 * chan :]).astype(BF16)
    proj_ref[:, : 2 * chan] = p_c.astype(BF16)
    p_r, p_i = p_c[:, :chan], p_c[:, chan:]
    split_store(src, 0, (1.0 - lam) * (p_r * sigmoid(p_r)))
    split_store(src, groups, (1.0 - lam) * (p_i * sigmoid(p_i)))
    cos_l, sin_l = lanes(cos), lanes(sin)

    def step(s, state):
        at = at_step(s)
        after = []
        for k, (h_r, h_i, cum) in enumerate(state):
            lam_s = lam_ref[k, at, :]
            a_r, a_i = lam_s * cos_l[k], lam_s * sin_l[k]
            n_r = a_r * h_r - a_i * h_i + src[k, at, :]
            n_i = a_r * h_i + a_i * h_r + src[groups + k, at, :]
            cum = cum * lam_s
            h_ref[k, at, :] = n_r
            h_ref[groups + k, at, :] = n_i
            cum_ref[k, at, :] = cum
            after.append((n_r, n_i, cum))
        return tuple(after)

    zero = lam_ref[0, 0:8, :] * 0.0
    last = lax.fori_loop(0, seg, step, ((zero, zero, zero + 1.0),) * groups, unroll=8)
    e_r, e_i, e_c = (jnp.concatenate([v[i] for v in last], axis=-1) for i in range(3))
    ends_ref[0:8, :] = e_r
    ends_ref[8:16, :] = e_i
    ends_ref[16:24, :] = e_c

    @pl.when(tile == 0)
    def _():
        tot_ref[0:2, :] = jnp.zeros((2, chan), F32)
        tot_ref[2:3, :] = jnp.ones((1, chan), F32)

    c_r, c_i, c_l = tot_ref[0:1, :], tot_ref[1:2, :], tot_ref[2:3, :]
    for j in range(8):
        m = e_c[j : j + 1, :]
        a_r, a_i = m * seg_cos, m * seg_sin
        c_r, c_i = a_r * c_r - a_i * c_i + e_r[j : j + 1, :], a_r * c_i + a_i * c_r + e_i[j : j + 1, :]
        c_l = c_l * m
    tot_ref[0:1, :] = c_r
    tot_ref[1:2, :] = c_i
    tot_ref[2:3, :] = c_l


def leave_tile(tile, x, pg_ref, h_ref, cum_ref, ends_ref, carry_ref, wo_ref, wf_ref, wd_ref, gain_ref, gate_ref,
               starts_ref, state_ref, mixed_ref, mid_ref, normed_ref, gu_ref, hid_ref, run):
    tokens, width = x.shape
    chan = width // 2
    seg = tokens // 8
    groups = chan // LANES
    cos, sin = gate_ref[0:1, :], gate_ref[1:2, :]
    seg_cos, seg_sin = gate_ref[3:4, :], gate_ref[4:5, :]

    @pl.when(tile == 0)
    def _():
        run[0:2, :] = carry_ref[0:2, :]

    c_r, c_i = run[0:1, :], run[1:2, :]
    l_r, l_i = [], []
    for j in range(8):
        l_r.append(c_r)
        l_i.append(c_i)
        m = ends_ref[16 + j : 17 + j, :]
        a_r, a_i = m * seg_cos, m * seg_sin
        c_r, c_i = (
            a_r * c_r - a_i * c_i + ends_ref[j : j + 1, :],
            a_r * c_i + a_i * c_r + ends_ref[8 + j : 9 + j, :],
        )
    run[0:1, :] = c_r
    run[1:2, :] = c_i
    start_r, start_i = jnp.concatenate(l_r, axis=0), jnp.concatenate(l_i, axis=0)
    starts_ref[...] = jnp.concatenate([start_r, start_i], axis=-1)
    cos_l, sin_l = lanes(cos), lanes(sin)

    def step(s, state):
        at = at_step(s)
        after = []
        for k, (w_r, w_i) in enumerate(state):
            w_r, w_i = w_r * cos_l[k] - w_i * sin_l[k], w_r * sin_l[k] + w_i * cos_l[k]
            cum = cum_ref[k, at, :]
            h_ref[k, at, :] += cum * w_r
            h_ref[groups + k, at, :] += cum * w_i
            after.append((w_r, w_i))
        return tuple(after)

    lax.fori_loop(0, seg, step, tuple(zip(lanes(start_r), lanes(start_i))), unroll=8)
    state = wide(h_ref, 0, 2 * groups)
    state_ref[...] = state.astype(BF16)
    p_g = pg_ref[...].astype(F32)
    mixed = (state * rms_scale(state) * gain_ref[1:2, :] * (p_g * sigmoid(p_g))).astype(BF16)
    mixed_ref[...] = mixed
    mid = x + dot(mixed, wo_ref[...])
    mid_ref[...] = mid.astype(BF16)
    normed = (mid * rms_scale(mid) * gain_ref[2:3, :]).astype(BF16)
    normed_ref[...] = normed
    hidden = wd_ref.shape[0]
    parts = pieces(hidden)

    def gate_up(part):
        return dot(normed, wf_ref[:, part]), dot(normed, wf_ref[:, moved(part, hidden)])

    after = gate_up(parts[0])
    for i, part in enumerate(parts):
        gate, up = after
        if i + 1 < len(parts):
            after = gate_up(parts[i + 1])
        gu_ref[:, part] = gate.astype(BF16)
        gu_ref[:, moved(part, hidden)] = up.astype(BF16)
        hid_ref[:, part] = (gate * sigmoid(gate) * up).astype(BF16)
    return mid + dot(hid_ref[...], wd_ref[...])


def back_out_tile(doc_ref, row, tile, start, last, dx_ref, gu_ref, mid_ref, state_ref, pg_ref, pf_ref, wo_ref, wf_ref,
                  wd_ref, gain_ref, gate_ref, dz_ref, dgu_ref, dy_ref, dpg_ref, lam_ref, g_ref, cum_ref, ends_ref,
                  tot_ref, small_ref, grad):
    tokens, width = dx_ref.shape
    chan = width // 2
    seg = tokens // 8
    groups = chan // LANES
    cos, sin, lower = gate_ref[0:1, :], gate_ref[1:2, :], gate_ref[2:3, :]
    seg_cos, seg_sin = gate_ref[3:4, :], gate_ref[4:5, :]
    dx = dx_ref[...]
    dz = dx.astype(BF16)
    dz_ref[...] = dz
    hidden = wd_ref.shape[0]
    parts = pieces(hidden)
    d_next = dot_t(dz, wd_ref[parts[0], :])
    for i, part in enumerate(parts):
        d_hid = d_next
        if i + 1 < len(parts):
            d_next = dot_t(dz, wd_ref[parts[i + 1], :])
        gate = gu_ref[:, part].astype(F32)
        up = gu_ref[:, moved(part, hidden)].astype(F32)
        sg = sigmoid(gate)
        silu = gate * sg
        dgu_ref[:, part] = (d_hid * up * (sg + silu * (1.0 - sg))).astype(BF16)
        dgu_ref[:, moved(part, hidden)] = (d_hid * silu).astype(BF16)
    d_n = dot_t(dgu_ref[...], wf_ref[...])
    mid = mid_ref[...].astype(F32)
    scale = rms_scale(mid)
    hat = mid * scale
    d_hat = d_n * gain_ref[2:3, :]
    small_ref[16:24, :] += eight_sum(d_n * hat)
    d_mid = dx + scale * (d_hat - hat * jnp.mean(d_hat * hat, axis=-1, keepdims=True))
    dx_ref[...] = d_mid
    dy = d_mid.astype(BF16)
    dy_ref[...] = dy
    d_mixed = dot_t(dy, wo_ref[...])
    p_g = pg_ref[...].astype(F32)
    sg = sigmoid(p_g)
    silu = p_g * sg
    state = state_ref[...].astype(F32)
    scale = rms_scale(state)
    hat = state * scale
    g1 = gain_ref[1:2, :]
    dpg_ref[...] = (d_mixed * hat * g1 * (sg + silu * (1.0 - sg))).astype(BF16)
    d_n = d_mixed * silu
    small_ref[8:16, :] += eight_sum(d_n * hat)
    d_hat = d_n * g1
    split_store(grad, 0, scale * (d_hat - hat * jnp.mean(d_hat * hat, axis=-1, keepdims=True)))
    lam, _, _ = retain(doc_ref, row, start, pf_ref[...].astype(F32), lower)
    split_store(lam_ref, 0, lam)
    cos_l, sin_l = lanes(cos), lanes(sin)

    def step(s, state):
        at = at_step(seg - 1 - s)
        after = []
        for k, (g_r, g_i, cum, lam_n) in enumerate(state):
            a_r, a_i = lam_n * cos_l[k], lam_n * sin_l[k]
            n_r = grad[k, at, :] + a_r * g_r + a_i * g_i
            n_i = grad[groups + k, at, :] + a_r * g_i - a_i * g_r
            cum = cum * lam_n
            g_ref[k, at, :] = n_r
            g_ref[groups + k, at, :] = n_i
            cum_ref[k, at, :] = cum
            after.append((n_r, n_i, cum, lam_ref[k, at, :]))
        return tuple(after)

    zero = lam_ref[0, 0:8, :] * 0.0
    final = lax.fori_loop(0, seg, step, ((zero, zero, zero + 1.0, zero + 1.0),) * groups, unroll=8)
    g_r, g_i, cum, lam_0 = (jnp.concatenate([v[i] for v in final], axis=-1) for i in range(4))
    e_r = lam_0 * (cos * g_r + sin * g_i)
    e_i = lam_0 * (cos * g_i - sin * g_r)
    e_c = lam_0 * cum
    ends_ref[0:8, :] = e_r
    ends_ref[8:16, :] = e_i
    ends_ref[16:24, :] = e_c

    @pl.when(tile == last)
    def _():
        tot_ref[0:2, :] = jnp.zeros((2, chan), F32)
        tot_ref[2:3, :] = jnp.ones((1, chan), F32)

    c_r, c_i, c_l = tot_ref[0:1, :], tot_ref[1:2, :], tot_ref[2:3, :]
    for j in reversed(range(8)):
        m = e_c[j : j + 1, :]
        a_r, a_i = m * seg_cos, m * seg_sin
        c_r, c_i = a_r * c_r + a_i * c_i + e_r[j : j + 1, :], a_r * c_i - a_i * c_r + e_i[j : j + 1, :]
        c_l = c_l * m
    tot_ref[0:1, :] = c_r
    tot_ref[1:2, :] = c_i
    tot_ref[2:3, :] = c_l


def back_in_tile(doc_ref, row, tile, start, last, dx_ref, x_ref, proj_ref, dpg_ref, lam_ref, starts_ref, state_ref, g_ref,
                 cum_ref, ends_ref, carry_ref, w_ref, gain_ref, gate_ref, dproj_ref, small_ref, run):
    tokens, width = dx_ref.shape
    chan = width // 2
    seg = tokens // 8
    groups = chan // LANES
    cos, sin, lower = gate_ref[0:1, :], gate_ref[1:2, :], gate_ref[2:3, :]
    seg_cos, seg_sin = gate_ref[3:4, :], gate_ref[4:5, :]

    @pl.when(tile == last)
    def _():
        run[0:2, :] = carry_ref[0:2, :]

    c_r, c_i = run[0:1, :], run[1:2, :]
    l_r, l_i = [None] * 8, [None] * 8
    for j in reversed(range(8)):
        l_r[j], l_i[j] = c_r, c_i
        m = ends_ref[16 + j : 17 + j, :]
        a_r, a_i = m * seg_cos, m * seg_sin
        c_r, c_i = (
            a_r * c_r + a_i * c_i + ends_ref[j : j + 1, :],
            a_r * c_i - a_i * c_r + ends_ref[8 + j : 9 + j, :],
        )
    run[0:1, :] = c_r
    run[1:2, :] = c_i
    cos_l, sin_l = lanes(cos), lanes(sin)

    def step(s, state):
        at = at_step(seg - 1 - s)
        after = []
        for k, (w_r, w_i) in enumerate(state):
            cum = cum_ref[k, at, :]
            g_ref[k, at, :] += cum * w_r
            g_ref[groups + k, at, :] += cum * w_i
            after.append((w_r * cos_l[k] + w_i * sin_l[k], w_i * cos_l[k] - w_r * sin_l[k]))
        return tuple(after)

    start_at = (jnp.concatenate(l_r, axis=0), jnp.concatenate(l_i, axis=0))
    lax.fori_loop(0, seg, step, tuple(zip(lanes(start_at[0]), lanes(start_at[1]))), unroll=8)
    d_n = dot_t(dpg_ref[...], w_ref[:, 3 * chan :])
    g_r, g_i = wide(g_ref, 0, groups), wide(g_ref, groups, 2 * groups)
    prior = jnp.concatenate([starts_ref[...], state_ref[...].astype(F32)[: tokens - 8, :]], axis=0)
    q_r, q_i = prior[:, :chan], prior[:, chan:]
    p_r = proj_ref[:, :chan].astype(F32)
    p_i = proj_ref[:, chan : 2 * chan].astype(F32)
    _, forget, keep = retain(doc_ref, row, start, proj_ref[:, 2 * chan :].astype(F32), lower)
    lam = wide(lam_ref, 0, groups)
    d_ar = g_r * q_r + g_i * q_i
    d_ai = g_i * q_r - g_r * q_i
    s_r, s_i = sigmoid(p_r), sigmoid(p_i)
    in_r, in_i = p_r * s_r, p_i * s_i
    d_lam = d_ar * cos + d_ai * sin - (g_r * in_r + g_i * in_i)
    d_f = jnp.concatenate([keep] * groups, axis=-1) * d_lam * (1.0 - forget)
    small_ref[24:32, :] += jnp.concatenate(
        [eight_sum(lam * (d_ai * cos - d_ar * sin)), eight_sum(d_f)], axis=-1
    )
    rest = 1.0 - lam
    d_proj = jnp.concatenate(
        [
            (rest * g_r * (s_r + in_r * (1.0 - s_r))).astype(BF16),
            (rest * g_i * (s_i + in_i * (1.0 - s_i))).astype(BF16),
            (d_f * (1.0 - lower) * forget).astype(BF16),
        ],
        axis=1,
    )
    dproj_ref[:, : 3 * chan] = d_proj
    dproj_ref[:, 3 * chan :] = dpg_ref[...]
    d_n = d_n + dot_t(d_proj, w_ref[:, : 3 * chan])
    x = x_ref[...].astype(F32)
    scale = rms_scale(x)
    hat = x * scale
    small_ref[0:8, :] += eight_sum(d_n * hat)
    d_hat = d_n * gain_ref[0:1, :]
    dx_ref[...] = dx_ref[...] + scale * (d_hat - hat * jnp.mean(d_hat * hat, axis=-1, keepdims=True))


def combine(count, me, forward, buf, rot_ref, out_ref):
    cos, sin = rot_ref[0:1, :], rot_ref[1:2, :]
    c_r = jnp.zeros_like(cos)
    c_i = jnp.zeros_like(cos)
    for k in range(count - 1, 0, -1):
        slot = k - 1 if forward else count - k - 1
        valid = me >= k if forward else me + k < count
        e_r, e_i, m = buf[slot, 0:1, :], buf[slot, 1:2, :], buf[slot, 2:3, :]
        a_r = m * cos
        a_i = m * sin if forward else -m * sin
        n_r = a_r * c_r - a_i * c_i + e_r
        n_i = a_r * c_i + a_i * c_r + e_i
        keep = jnp.where(valid, 1.0, 0.0)
        c_r, c_i = n_r * keep, n_i * keep
    out_ref[0:1, :] = c_r
    out_ref[1:2, :] = c_i


def carry_copies(count, me, tot_ref, buf, send_sem, recv_sem):
    return [
        remote(tot_ref, buf.at[k - 1], send_sem.at[k - 1], recv_sem.at[k - 1], {"seq": lax.rem(me + k, count)})
        for k in range(1, count)
    ]


class Ring:
    def __init__(self, n):
        self.n = n
        self.batch, self.seq = lax.axis_index("batch"), lax.axis_index("seq")
        z, x = self.batch // 2, self.batch % 2
        self.pos = z + x * (n - 1 - 2 * z)
        self.core, self.y = self.seq % 2, self.seq // 2
        self.sign = 1 - 2 * self.core
        self.core_peer = self.seq + self.sign
        self.y_peer = self.seq + 2 * (1 - 2 * self.y)

    def at(self, distance):
        p = (self.pos + distance + 2 * self.n) % self.n
        h = p // (self.n // 2)
        return 2 * (p + h * (self.n - 1 - 2 * p)) + h

    def ahead(self, hops):
        return self.at(self.sign * hops)


def remote(src, dst, send, recv, device):
    return pltpu.make_async_remote_copy(
        src_ref=src, dst_ref=dst, send_sem=send, recv_sem=recv, device_id=device, device_id_type=MESH
    )


def meet(devices):
    barrier = pltpu.get_barrier_semaphore()
    for device in devices:
        pl.semaphore_signal(barrier, inc=1, device_id=device, device_id_type=MESH)
    pl.semaphore_wait(barrier, len(devices))


class Gather:
    def __init__(self, ring, jobs, sems):
        self.ring, self.jobs = ring, jobs
        (self.own_sem, self.ring_send, self.ring_recv, self.y_send, self.y_recv, self.core_send,
         self.core_recv) = sems
        n = ring.n
        self.hops = ((1, n // 2, 0), (-1, n - 1 - n // 2, n // 2))

    def rows(self, j, piece):
        src, dst, u = self.jobs[j]
        ring = self.ring
        base = ring.core * (3 * u)
        whole = piece * (6 * u)
        view = lambda first, rows: dst.at[pl.ds(pl.multiple_of(whole + base + first, 16), rows)]
        return view(ring.y * u, 2 * u), view(2 * ring.y * u, u), view(2 * (1 - ring.y) * u, u)

    def own_copy(self, j):
        src, dst, u = self.jobs[j]
        return pltpu.make_async_copy(
            src, dst.at[pl.ds(pl.multiple_of(self.ring.batch * (6 * u), 16), 6 * u)], self.own_sem.at[j]
        )

    def own(self, j):
        src, dst, u = self.jobs[j]
        ring = self.ring
        mine, _, _ = self.rows(j, ring.batch)
        piece = src.at[pl.ds(pl.multiple_of(ring.core * (3 * u) + ring.y * u, 16), 2 * u)]
        for way, hops, first in self.hops:
            remote(piece, mine, self.ring_send.at[j], self.ring_recv.at[j, first],
                   {"batch": ring.ahead(way)}).start()
        self.own_copy(j).start()

    def arrived(self, j, h):
        ring = self.ring
        for way, hops, first in self.hops:
            if h < hops:
                mine, give, _ = self.rows(j, ring.ahead(-way * (h + 1)))
                on = lambda slot: remote(mine, mine, self.ring_send.at[j], self.ring_recv.at[j, first + slot],
                                         {"batch": ring.ahead(way)})
                on(h).wait_recv()
                if h + 1 < hops:
                    on(h + 1).start()
                remote(give, give, self.y_send.at[j], self.y_recv.at[j, first + h], {"seq": ring.y_peer}).start()
                remote(mine, mine, self.core_send.at[j], self.core_recv.at[j], {"seq": ring.core_peer}).start()

    def crossed(self, j, h):
        ring = self.ring
        for way, hops, first in self.hops:
            if h < hops:
                _, _, take = self.rows(j, ring.ahead(-way * (h + 1)))
                remote(take, take, self.y_send.at[j], self.y_recv.at[j, first + h], {"seq": ring.y_peer}).wait_recv()
                remote(take, take, self.core_send.at[j], self.core_recv.at[j], {"seq": ring.core_peer}).start()

    def swapped(self, j):
        src, dst, u = self.jobs[j]
        view = dst.at[0 : (self.ring.n - 1) * 3 * u]
        remote(view, view, self.core_send.at[j], self.core_recv.at[j], {"seq": self.ring.core_peer}).wait_recv()
        self.own_copy(j).wait()

    def sent(self, j):
        src, dst, u = self.jobs[j]
        for rows, send in ((2 * u, self.ring_send), (u, self.y_send), (3 * u, self.core_send)):
            view = dst.at[0 : (self.ring.n - 1) * rows]
            remote(view, view, send.at[j], self.core_recv.at[j], {"seq": self.ring.core_peer}).wait_send()


class Agenda:
    def __init__(self):
        self.calls = {}

    def add(self, when, f, *args):
        self.calls.setdefault(when, []).append((f, args))

    def run(self, now):
        for when, calls in sorted(self.calls.items(), key=lambda item: item[0]):

            @pl.when(now == when)
            def _(calls=calls):
                for f, args in calls:
                    f(*args)


OPENING = (((0, 0, 0), (0, 0, 1), (0, 0, 3), (0, 0, 2), (1, 0, 0), (1, 0, 1), (1, 0, 3), (1, 0, 2), (2, 0, 0), (2, 0, 1),
            (2, 0, 3), (2, 0, 2), (3, 0, 0), (3, 0, 1), (3, 0, 3), (4, 0, 0), (3, 0, 2), (0, 1, 0), (0, 1, 1), (0, 1, 3),
            (5, 0, 0)),)
FIRST = OPENING + (
    ((4, 0, 1), (4, 0, 3), (0, 1, 2)),
    ((4, 0, 2), (1, 1, 0)),
    ((5, 0, 1), (5, 0, 3), (1, 1, 1), (1, 1, 3)),
    ((5, 0, 2), (1, 1, 2)),
)
SECOND = (
    ((2, 1, 0), (2, 1, 1), (2, 1, 3)),
    ((2, 1, 2), (3, 1, 0)),
    ((3, 1, 1), (3, 1, 3), (4, 1, 0)),
)
LATER = (
    ((5, 0, 0), (3, 0, 2)),
    ((4, 0, 1), (4, 0, 3), (0, 1, 0)),
    ((4, 0, 2), (0, 1, 1), (0, 1, 3)),
    ((5, 0, 1), (5, 0, 3), (5, 0, 2), (0, 1, 2)),
    ((1, 1, 0), (1, 1, 1), (1, 1, 3), (1, 1, 2)),
)


def plan_gather(agenda, net, layers, mats, count, load, save):
    far = net.ring.n // 2

    def hops(j, quarter):
        for h in range(quarter * far // 4, (quarter + 1) * far // 4):
            net.arrived(j, h)
        cross(j, quarter - 1)

    def cross(j, quarter):
        for h in range(max(quarter, 0) * far // 4, (quarter + 1) * far // 4):
            net.crossed(j, h)

    def complete(j):
        cross(j, 3)
        net.swapped(j)
        if j < mats:
            save(j).start()
        else:
            if j < 2 * mats:
                save(j - mats).wait()
                net.sent(j - mats)
            load(j).start()

    for k in range(layers):
        for q, calls in enumerate((LATER if k else FIRST) + SECOND):
            for what, ahead, m in calls:
                if k + ahead < layers:
                    j = (k + ahead) * mats + m
                    when = 2 * count * k + q * count // 4
                    if what == 0:
                        agenda.add(when, net.own, j)
                    elif what == 5:
                        agenda.add(when, complete, j)
                    else:
                        agenda.add(when, hops, j, what - 1)


def forward_kernel(n, n_seq, layers, rows, paired, *refs):
    doc_ref, tok_ref = refs[:2]
    mats = 4
    given, table_ref, refs = refs[2 : 2 + mats], refs[2 + mats], refs[3 + mats :]
    if paired:
        gathered, refs = refs[: layers * mats], refs[layers * mats :]
    (xin_ref, proj_ref, pg_ref, normed_ref, starts_ref, state_ref, mixed_ref, mid_ref, normed2_ref, gu_ref, hid_ref,
     out_ref) = refs[:12]
    (xs, hs, cum, pg, ends, tot, src, lam, run, carry, buf, *rest) = refs[12:]
    weights, (load_sem, save_sem, carry_send, carry_recv), sems = rest[:mats], rest[mats : mats + 4], rest[mats + 4 :]
    layer, step = pl.program_id(0), pl.program_id(1)
    tokens, width = tok_ref.shape
    count = xs.shape[0]
    tiles = count // rows
    now = layer * (2 * count) + step
    me = lax.axis_index("seq")
    peers = [{"seq": lax.rem(me + k, n_seq)} for k in range(1, n_seq)]
    agenda = Agenda()

    def load(j):
        source = gathered[j] if paired else given[j % mats].at[j // mats]
        return pltpu.make_async_copy(source, weights[j % mats], load_sem.at[j % mats])

    def ready(j):
        load(j).wait()

    if paired:
        ring = Ring(n)
        jobs = [
            (given[m].at[k], gathered[k * mats + m] if k else weights[m], given[m].shape[1] // 6)
            for k in range(layers) for m in range(mats)
        ]
        net = Gather(ring, jobs, sems)

        def save(j):
            return pltpu.make_async_copy(weights[j], gathered[j], save_sem.at[j])

        agenda.add(0, meet, [{"batch": ring.ahead(1)}, {"batch": ring.ahead(-1)}] + peers)
        plan_gather(agenda, net, layers, mats, count, load, save)
    else:
        agenda.add(0, meet, peers)
        for k in range(layers):
            agenda.add(2 * count * k, lambda k=k: load(k * mats).start())
            for m in range(1, mats):
                agenda.add(2 * count * k + count - 1, lambda j=k * mats + m: load(j).start())
    for k in range(1 if paired else 0, layers):
        agenda.add(2 * count * k, ready, k * mats)
        for m in range(1, mats):
            agenda.add(2 * count * k + count, ready, k * mats + m)
    agenda.run(now)

    tile = lax.rem(step, count)
    row, at_row = tile // tiles, lax.rem(tile, tiles)
    start = (me * tiles + at_row) * tokens
    gains, gate = table_ref.at[layer, 0:8], table_ref.at[layer, 8:16, 0 : width // 2]

    @pl.when((layer == 0) & (step < count))
    def _():
        xs[tile] = dot(order_matrix(tokens, False), tok_ref[...])

    @pl.when(step < count)
    def _():
        x = xs[tile]
        xin_ref[...] = x.astype(BF16)
        enter_tile(doc_ref, row, at_row, start, x, weights[0], gains, gate, proj_ref, pg.at[tile], normed_ref, hs.at[tile],
                   cum.at[tile], ends.at[tile], tot.at[row], src, lam)
        pg_ref[...] = pg[tile]

    def exchange():
        return carry_copies(n_seq, me, tot.at[row], buf.at[layer, row], carry_send.at[layer, row], carry_recv.at[layer, row])

    @pl.when((step < count) & (lax.rem(step, tiles) == tiles - 1))
    def _():
        for copy in exchange():
            copy.start()

    @pl.when((step >= count) & (lax.rem(step, tiles) == 0))
    def _():
        for copy in exchange():
            copy.wait()
        combine(n_seq, me, True, buf.at[layer, row], gate.at[5:8], carry.at[row])

    @pl.when(step >= count)
    def _():
        out = leave_tile(at_row, xs[tile], pg.at[tile], hs.at[tile], cum.at[tile], ends.at[tile], carry.at[row],
                         weights[1], weights[2], weights[3], gains, gate, starts_ref, state_ref, mixed_ref, mid_ref,
                         normed2_ref, gu_ref, hid_ref, run)
        xs[tile] = out

        @pl.when(layer == layers - 1)
        def _():
            out_ref[...] = out.astype(BF16)

    if paired:

        @pl.when(now == layers * 2 * count - 1)
        def _():
            for j in range(layers * mats):
                if j < mats and layers == 1:
                    save(j).wait()
                if j >= mats or layers == 1:
                    net.sent(j)


def tile_specs(tokens, layer):
    def flat(w, when, col=0):
        return pl.BlockSpec((None, tokens, w), lambda k, s: (layer(k), when(s), col))

    def few(r, w, when):
        return pl.BlockSpec((None, None, r, w), lambda k, s: (layer(k), when(s), 0, 0))

    return flat, few


def run_forward(n, n_seq, paired, rows, tokens, docs, x, sources, table):
    layers = sources[0].shape[0]
    total, width = x.shape
    chan = width // 2
    hidden = sources[2].shape[2] // 2
    count = total // tokens
    mats = len(sources)
    jobs = layers * mats if paired else 0
    shape = jax.ShapeDtypeStruct
    dma = pltpu.SemaphoreType.DMA
    any_ = pl.BlockSpec(memory_space=pl.ANY)

    def first(step):
        return jnp.minimum(step, count - 1)

    def second(step):
        return jnp.maximum(step - count, 0)

    flat, few = tile_specs(tokens, lambda k: k)

    def kept(w):
        return shape((layers, total, w), BF16)

    full = [((n if paired else 1) * w.shape[1], w.shape[2]) for w in sources]
    last = layers - 1
    outs = pl.pallas_call(
        functools.partial(forward_kernel, n, n_seq, layers, rows, paired),
        grid=(layers, 2 * count),
        in_specs=[
            pl.BlockSpec(memory_space=pltpu.SMEM),
            pl.BlockSpec((tokens, width), lambda k, s: (jnp.where(k == 0, first(s), count - 1), 0)),
        ]
        + [any_] * mats
        + [whole(*table.shape)],
        out_specs=[any_] * jobs
        + [
            flat(width, first),
            flat(3 * chan, first),
            flat(width, first),
            flat(width, first),
            few(8, width, second),
            flat(width, second),
            flat(width, second),
            flat(width, second),
            flat(width, second),
            flat(2 * hidden, second),
            flat(hidden, second),
            pl.BlockSpec((tokens, width), lambda k, s: (jnp.where(k == last, second(s), 0), 0)),
        ],
        out_shape=[shape(f, BF16) for _ in range(layers) for f in full][:jobs]
        + [
            kept(width),
            kept(3 * chan),
            kept(width),
            kept(width),
            shape((layers, count, 8, width), F32),
            kept(width),
            kept(width),
            kept(width),
            kept(width),
            kept(2 * hidden),
            kept(hidden),
            shape((total, width), BF16),
        ],
        scratch_shapes=[
            pltpu.VMEM((count, tokens, width), F32),
            pltpu.VMEM((count, width // LANES, tokens, LANES), F32),
            pltpu.VMEM((count, chan // LANES, tokens, LANES), F32),
            pltpu.VMEM((count, tokens, width), BF16),
            pltpu.VMEM((count, 24, chan), F32),
            pltpu.VMEM((rows, 8, chan), F32),
            pltpu.VMEM((width // LANES, tokens, LANES), F32),
            pltpu.VMEM((chan // LANES, tokens, LANES), F32),
            pltpu.VMEM((8, chan), F32),
            pltpu.VMEM((rows, 8, chan), F32),
            pltpu.VMEM((layers, rows, n_seq - 1, 8, chan), F32),
        ]
        + [pltpu.VMEM(f, BF16) for f in full]
        + [dma((mats,)), dma((mats,)), dma((layers, rows, n_seq - 1)), dma((layers, rows, n_seq - 1))]
        + [dma((s,)) if one else dma((s, n - 1)) for s in [max(jobs, 1)] for one in (1, 1, 0, 1, 0, 1, 1)],
        compiler_params=pltpu.CompilerParams(collective_id=3, has_side_effects=True, vmem_limit_bytes=LIMIT),
    )(docs, x, *sources, table)
    return outs[:jobs], outs[jobs:]


def backward_kernel(n_seq, layers, rows, mats, *refs):
    doc_ref, cot_ref = refs[:2]
    given, refs = refs[2 : 2 + layers * mats], refs[2 + layers * mats :]
    (table_ref, gu_ref, mid_ref, state_ref, pg_ref, pf_ref, x_ref, proj_ref, starts_ref, prior_ref, dz_ref,
     dgu_ref, dy_ref, dproj_ref, dtok_ref, small_ref) = refs[:16]
    (dxs, gs, cum, lam, dpg, ends, tot, grad, run, carry, buf, *rest) = refs[16:]
    weights, (load_sem, carry_send, carry_recv) = rest[:mats], rest[mats:]
    turn, step = pl.program_id(0), pl.program_id(1)
    layer = layers - 1 - turn
    tokens, width = cot_ref.shape
    count = dxs.shape[0]
    tiles = count // rows
    now = turn * (2 * count) + step
    me = lax.axis_index("seq")
    agenda = Agenda()

    def load(t, m):
        return pltpu.make_async_copy(given[(layers - 1 - t) * mats + m], weights[m], load_sem.at[m])

    def fetch(t, m):
        load(t, m).start()

    def ready(t, m):
        load(t, m).wait()

    for m in (3, 2, 1):
        agenda.add(0, fetch, 0, m)
    agenda.add(0, meet, [{"seq": lax.rem(me + k, n_seq)} for k in range(1, n_seq)])
    for t in range(layers):
        begin = 2 * count * t
        agenda.add(begin, fetch, t, 0)
        for m in (3, 2, 1):
            agenda.add(begin, ready, t, m)
        agenda.add(begin + count, ready, t, 0)
        if t + 1 < layers:
            for m in (3, 2, 1):
                agenda.add(begin + count, fetch, t + 1, m)
    agenda.run(now)

    tile = count - 1 - lax.rem(step, count)
    row, at_row = tile // tiles, lax.rem(tile, tiles)
    start = (me * tiles + at_row) * tokens
    gains, gate = table_ref.at[layer, 0:8], table_ref.at[layer, 8:16, 0 : width // 2]

    @pl.when(step == 0)
    def _():
        small_ref[...] = jnp.zeros_like(small_ref)

    @pl.when((turn == 0) & (step < count))
    def _():
        dxs[tile] = dot(order_matrix(tokens, False), cot_ref[...])

    @pl.when(step < count)
    def _():
        back_out_tile(doc_ref, row, at_row, start, tiles - 1, dxs.at[tile], gu_ref, mid_ref, state_ref, pg_ref, pf_ref,
                      weights[1], weights[2], weights[3], gains, gate, dz_ref, dgu_ref, dy_ref, dpg.at[tile],
                      lam.at[tile], gs.at[tile], cum.at[tile], ends.at[tile], tot.at[row], small_ref, grad)

    def exchange():
        return carry_copies(n_seq, me, tot.at[row], buf.at[turn, row], carry_send.at[turn, row], carry_recv.at[turn, row])

    @pl.when((step < count) & (lax.rem(step, tiles) == tiles - 1))
    def _():
        for copy in exchange():
            copy.start()

    @pl.when((step >= count) & (lax.rem(step, tiles) == 0))
    def _():
        for copy in exchange():
            copy.wait()
        combine(n_seq, me, False, buf.at[turn, row], gate.at[5:8], carry.at[row])

    @pl.when(step >= count)
    def _():
        back_in_tile(doc_ref, row, at_row, start, tiles - 1, dxs.at[tile], x_ref, proj_ref, dpg.at[tile], lam.at[tile],
                     starts_ref, prior_ref, gs.at[tile], cum.at[tile], ends.at[tile], carry.at[row], weights[0],
                     gains, gate, dproj_ref, small_ref, run)

        @pl.when(turn == layers - 1)
        def _():
            dtok_ref[...] = dxs[tile]


def run_backward(n_seq, rows, tokens, docs, cotangent, weights, table, kept):
    x, proj, p_g, starts, state, mid, gu = kept
    layers, total, width = x.shape
    chan = width // 2
    hidden = gu.shape[2] // 2
    count = total // tokens
    mats = len(weights) // layers
    shape = jax.ShapeDtypeStruct
    dma = pltpu.SemaphoreType.DMA
    any_ = pl.BlockSpec(memory_space=pl.ANY)
    last = layers - 1

    def first(step):
        return count - 1 - jnp.minimum(step, count - 1)

    def second(step):
        return count - 1 - jnp.maximum(step - count, 0)

    flat, few = tile_specs(tokens, lambda k: last - k)
    return pl.pallas_call(
        functools.partial(backward_kernel, n_seq, layers, rows, mats),
        grid=(layers, 2 * count),
        in_specs=[
            pl.BlockSpec(memory_space=pltpu.SMEM),
            pl.BlockSpec((tokens, width), lambda k, s: (jnp.where(k == 0, first(s), 0), 0)),
        ]
        + [any_] * len(weights)
        + [
            whole(*table.shape),
            flat(2 * hidden, first),
            flat(width, first),
            flat(width, first),
            flat(width, first),
            flat(chan, first, 2),
            flat(width, second),
            flat(3 * chan, second),
            few(8, width, second),
            flat(width, second),
        ],
        out_specs=[
            flat(width, first),
            flat(2 * hidden, first),
            flat(width, first),
            flat(3 * chan + width, second),
            pl.BlockSpec((tokens, width), lambda k, s: (jnp.where(k == last, second(s), count - 1), 0)),
            pl.BlockSpec((None, 32, width), lambda k, s: (last - k, 0, 0)),
        ],
        out_shape=[
            shape((layers, total, width), BF16),
            shape((layers, total, 2 * hidden), BF16),
            shape((layers, total, width), BF16),
            shape((layers, total, 3 * chan + width), BF16),
            shape((total, width), F32),
            shape((layers, 32, width), F32),
        ],
        scratch_shapes=[
            pltpu.VMEM((count, tokens, width), F32),
            pltpu.VMEM((count, width // LANES, tokens, LANES), F32),
            pltpu.VMEM((count, chan // LANES, tokens, LANES), F32),
            pltpu.VMEM((count, chan // LANES, tokens, LANES), F32),
            pltpu.VMEM((count, tokens, width), BF16),
            pltpu.VMEM((count, 24, chan), F32),
            pltpu.VMEM((rows, 8, chan), F32),
            pltpu.VMEM((width // LANES, tokens, LANES), F32),
            pltpu.VMEM((8, chan), F32),
            pltpu.VMEM((rows, 8, chan), F32),
            pltpu.VMEM((layers, rows, n_seq - 1, 8, chan), F32),
        ]
        + [pltpu.VMEM(w.shape, BF16) for w in weights[:mats]]
        + [dma((mats,)), dma((layers, rows, n_seq - 1)), dma((layers, rows, n_seq - 1))],
        compiler_params=pltpu.CompilerParams(collective_id=2, has_side_effects=True, vmem_limit_bytes=LIMIT),
    )(docs, cotangent, *weights, table, gu, mid, state, p_g, proj, x, proj, starts, state)


def add_rows(dst, dst_row, parts, rows):
    def block(i, _):
        step = pl.multiple_of(i * 16, 16)
        total = None
        for ref, first in parts:
            value = ref[pl.ds(pl.multiple_of(first + step, 16), 16), :].astype(F32)
            total = value if total is None else total + value
        dst[pl.ds(pl.multiple_of(dst_row + step, 16), 16), :] = total.astype(dst.dtype)
        return 0

    lax.fori_loop(0, rows // 16, block, 0)


def grads_kernel(n, plan, *refs):
    jobs = len(plan)
    lefts, rights, small = refs[:jobs], refs[jobs : 2 * jobs], refs[2 * jobs]
    outs_count = 1 + max(p[0] for p in plan)
    outs, rest = refs[2 * jobs + 1 : 2 * jobs + 1 + outs_count], refs[2 * jobs + 1 + outs_count :]
    gains_out, gate_out, rest = rest[0], rest[1], rest[2:]
    grads, core_buf, y_buf, ring_buf, fin_buf = (rest[i * jobs : (i + 1) * jobs] for i in range(5))
    (left_big, left_small, right_buf, small_buf, left_sem, right_sem, core_send, core_recv, y_send, y_recv,
     ring_send, ring_recv, end_send, end_recv, small_send, small_recv) = rest[5 * jobs :]
    ring = Ring(n)
    far, near = n // 2, n - 1 - n // 2
    core_dev, y_dev = {"seq": ring.core_peer}, {"seq": ring.y_peer}
    y, core = ring.y, ring.core
    rounds = [core_dev, y_dev]
    d = 1
    while d < n:
        rounds.append({"batch": ring.batch + d * (1 - 2 * ((ring.batch // d) % 2))})
        d *= 2
    us = [g.shape[0] // n // 6 for g in grads]
    split = [p[2] for p in plan]
    own_rows = [(2 if s else 3) * u for s, u in zip(split, us)]

    def left_copy(j):
        buf = (left_big, left_small)[j % 2]
        return pltpu.make_async_copy(lefts[j].at[plan[j][1]], buf.at[:, 0 : plan[j][3]], left_sem.at[j % 2])

    chunks = []
    for j, (_, _, _, rows, cols, _, _) in enumerate(plan):
        first = 0
        while first < cols:
            size = min(CHUNK, cols - first)
            chunks.append((j, first, size, first + size == cols))
            first += size

    def right_copy(i):
        j, first, size, _ = chunks[i]
        return pltpu.make_async_copy(
            rights[j].at[plan[j][1], :, plan[j][5] + first : plan[j][5] + first + size], right_buf.at[i % 2, :, 0:size], right_sem.at[i % 2]
        )

    left_copy(0).start()
    right_copy(0).start()
    right_copy(1).start()
    left_copy(1).start()
    meet([{"batch": ring.ahead(1)}, {"batch": ring.ahead(-1)}] + rounds)

    order = []
    for h in range(far):
        order.append((1, h, far - h))
        if h < near:
            order.append((-1, h, near - h))
    order.append((0, 0, 0))
    last = len(order)

    def rows_at(ref, first, rows):
        return ref.at[pl.ds(pl.multiple_of(first, 16), rows)]

    def core_copy(j, slot, piece):
        u = us[j]
        return remote(rows_at(grads[j], piece * (6 * u) + (1 - core) * (3 * u), 3 * u),
                      core_buf[j].at[slot], core_send.at[j], core_recv.at[j, slot], core_dev)

    def y_copy(j, slot, piece):
        u = us[j]
        src = rows_at(grads[j], piece * (6 * u) + core * (3 * u) + 2 * (1 - y) * u, u)
        return remote(src, y_buf[j].at[slot], y_send.at[j], y_recv.at[j, slot], y_dev)

    def mine(j, piece):
        u = us[j]
        return piece * (6 * u) + core * (3 * u) + (y * u if split[j] else 0)

    def ring_copy(j, slot, way, piece):
        return remote(rows_at(grads[j], mine(j, piece), own_rows[j]), ring_buf[j].at[slot], ring_send.at[j],
                      ring_recv.at[j, slot], {"batch": ring.ahead(way)})

    def small_round(r):
        return remote(small_buf.at[2 * r], small_buf.at[2 * r + 1], small_send.at[r], small_recv.at[r], rounds[r])

    layers = small.shape[0]
    for k in range(layers):
        for i in range(4):
            small_buf[0, 4 * k + i : 4 * k + i + 1, :] = jnp.sum(small[k, 8 * i : 8 * i + 8, :], axis=0, keepdims=True)
    small_round(0).start()

    def small_step(r):
        small_round(r).wait_recv()
        total = small_buf[2 * r] + small_buf[2 * r + 1]
        if r + 1 < len(rounds):
            small_buf[2 * r + 2] = total
            small_round(r + 1).start()
        else:
            chan = gate_out.shape[2]
            for k in range(layers):
                gains_out[k] = total[4 * k : 4 * k + 3, :]
                gate_out[k, 0:1, :] = total[4 * k + 3 : 4 * k + 4, :chan]
                gate_out[k, 1:2, :] = total[4 * k + 3 : 4 * k + 4, chan:]

    def begin(j):
        for slot, (way, h, dist) in enumerate(order):
            core_copy(j, slot, ring.ahead(-way * dist)).start()

    def cross(j, slot):
        way, h, dist = order[slot]
        piece = ring.ahead(way * dist)
        u = us[j]
        core_copy(j, slot, piece).wait_recv()
        if not split[j]:
            return
        give = 2 * (1 - y) * u
        at = piece * (6 * u) + core * (3 * u) + give
        add_rows(grads[j], at, [(grads[j], at), (core_buf[j].at[slot], give)], u)
        y_copy(j, slot, piece).start()

    def hop(j, slot):
        way, h, dist = order[slot]
        piece = ring.ahead(way * dist)
        u = us[j]
        if split[j]:
            y_copy(j, slot, piece).wait_recv()
        if way == 0:
            prior = [i for i, o in enumerate(order) if o[2] == 1]
        elif h:
            prior = [i for i, o in enumerate(order) if o[0] == way and o[1] == h - 1]
        else:
            prior = []
        for i in prior:
            ring_copy(j, i, order[i][0], piece).wait_recv()
        at = mine(j, piece)
        base = [(grads[j], at), (core_buf[j].at[slot], y * u if split[j] else 0)]
        base += [(ring_buf[j].at[i], 0) for i in prior]
        if split[j]:
            for by, more in ((y * u, [(y_buf[j].at[slot], 0)]), ((1 - y) * u, [])):
                add_rows(grads[j], at + by, [(r, f + by) for r, f in base] + more, u)
        else:
            add_rows(grads[j], at, base, 3 * u)
        if way:
            ring_copy(j, slot, way, piece).start()

    def fin_copy(j):
        return remote(rows_at(grads[j], mine(j, ring.batch), own_rows[j]), fin_buf[j], end_send.at[j, 0],
                      end_recv.at[j, 0], y_dev)

    def out_of(j):
        return outs[plan[j][0]].at[plan[j][1], :, plan[j][5] : plan[j][5] + plan[j][4]]

    def half_copy(j):
        half = out_of(j).at[pl.ds(pl.multiple_of(core * (3 * us[j]), 16), 3 * us[j])]
        return remote(half, half, end_send.at[j, 1], end_recv.at[j, 1], core_dev)

    def finish(j):
        u = us[j]
        fin_copy(j).wait_recv()
        out = out_of(j)
        at, to = mine(j, ring.batch), core * (3 * u)
        if split[j]:
            add_rows(out, to + 2 * y * u, [(grads[j], at + y * u)], u)
            add_rows(out, to + 2 * (1 - y) * u, [(fin_buf[j], (1 - y) * u)], u)
            add_rows(out, to + u, [(grads[j], at + (1 - y) * u), (fin_buf[j], y * u)], u)
        else:
            add_rows(out, to, [(grads[j], at), (fin_buf[j], 0)], 3 * u)
        half_copy(j).start()

    steps = far + 4

    def advance(j, t):
        now = [i for i, o in enumerate(order) if o[0] and o[1] == t]
        before = [i for i, o in enumerate(order) if o[0] and o[1] == t - 1]
        for slot in before:
            hop(j, slot)
        for slot in now:
            cross(j, slot)
        if t == far - 1:
            cross(j, last - 1)
        if t == far + 1:
            hop(j, last - 1)
            fin_copy(j).start()
        if t == far + 2:
            finish(j)
        if t == far + 3:
            half_copy(j).wait_recv()

    stage = {}

    def advance_all(turn):
        for j in list(stage):
            if j % 2 == turn:
                advance(j, stage[j])
                stage[j] += 1
                if stage[j] == steps:
                    del stage[j]

    small_at = 0
    for i, (j, first, size, done) in enumerate(chunks):
        if first == 0:
            left_copy(j).wait()
        right_copy(i).wait()
        left = (left_big, left_small)[j % 2]

        def multiply(b, _, i=i, j=j, first=first, size=size, left=left):
            at = pl.multiple_of(b * 256, 256)
            part = lax.dot_general(
                left[:, pl.ds(at, 256)], right_buf[i % 2, :, 0:size], (((0,), (0,)), ((), ())),
                preferred_element_type=F32,
            )
            grads[j][pl.ds(at, 256), first : first + size] = part.astype(BF16)
            return 0

        lax.fori_loop(0, plan[j][3] // 256, multiply, 0)
        if i + 2 < len(chunks):
            right_copy(i + 2).start()
        if done and j + 2 < jobs:
            left_copy(j + 2).start()
        advance_all(i % 2)
        if done:
            begin(j)
            stage[j] = 0
        if small_at < len(rounds):
            small_step(small_at)
            small_at += 1
    i = 0
    while stage:
        advance_all(i % 2)
        i += 1
    while small_at < len(rounds):
        small_step(small_at)
        small_at += 1
    for j in range(jobs):
        u = us[j]
        fin_copy(j).wait_send()
        half_copy(j).wait_send()
        remote(core_buf[j], core_buf[j], core_send.at[j], core_recv.at[j, 0], core_dev).wait_send()
        if split[j]:
            remote(y_buf[j], y_buf[j], y_send.at[j], y_recv.at[j, 0], y_dev).wait_send()
        remote(ring_buf[j], ring_buf[j], ring_send.at[j], ring_recv.at[j, 0], core_dev).wait_send()
    for r in range(len(rounds)):
        small_round(r).wait_send()


def grads_and_scatter(n, plan, lefts, rights, small):
    jobs = len(plan)
    full = []
    for (m, k, crosses, part, of), a, b in zip(plan, lefts, rights):
        cols = b.shape[2] // of
        full.append((m, k, crosses, a.shape[2], cols, part * cols, b.shape[2]))
    plan = full
    tokens = lefts[0].shape[1]
    layers, _, width = small.shape
    dma = pltpu.SemaphoreType.DMA
    rounds = 2 + (n - 1).bit_length()
    sizes = [(p[3] // n // 6, p[4], p[2]) for p in plan]
    outs = {p[0]: jax.ShapeDtypeStruct((layers, p[3] // n, p[6]), BF16) for p in plan}
    vm = pl.BlockSpec(memory_space=pltpu.VMEM)
    any_ = pl.BlockSpec(memory_space=pl.ANY)

    def bufs(f):
        return [pltpu.VMEM(f(u, w, s), BF16) for u, w, s in sizes]

    return pl.pallas_call(
        functools.partial(grads_kernel, n, plan),
        out_shape=[outs[m] for m in sorted(outs)]
        + [jax.ShapeDtypeStruct((layers, 3, width), F32), jax.ShapeDtypeStruct((layers, 2, width // 2), F32)],
        in_specs=[any_] * (2 * jobs) + [vm],
        out_specs=[vm] * (len(outs) + 2),
        scratch_shapes=bufs(lambda u, w, s: (6 * u * n, w))
        + bufs(lambda u, w, s: (n, 3 * u, w))
        + bufs(lambda u, w, s: (n if s else 1, u, w))
        + bufs(lambda u, w, s: (n - 1, 2 * u if s else 3 * u, w))
        + bufs(lambda u, w, s: (2 * u if s else 3 * u, w))
        + [
            pltpu.VMEM((tokens, max(p[3] for p in plan[0::2])), BF16),
            pltpu.VMEM((tokens, max(p[3] for p in plan[1::2])), BF16),
            pltpu.VMEM((2, tokens, CHUNK), BF16),
            pltpu.VMEM((2 * rounds, 4 * layers, width), F32),
            dma((2,)), dma((2,)), dma((jobs,)), dma((jobs, n)), dma((jobs,)), dma((jobs, n)), dma((jobs,)),
            dma((jobs, n)), dma((jobs, 2)), dma((jobs, 2)), dma((rounds,)), dma((rounds,)),
        ],
        compiler_params=pltpu.CompilerParams(
            collective_id=4, has_side_effects=True, vmem_limit_bytes=63 * 1024 * 1024
        ),
    )(*lefts, *rights, small)


def finish_kernel(mats, *refs):
    grads, (out_ref, dtok_ref) = refs[:mats], refs[mats : mats + 2]
    wide_refs, (out_to, dtok_to) = refs[mats + 2 : 2 * mats + 2], refs[2 * mats + 2 :]
    for grad, to in zip(grads, wide_refs):
        to[...] = grad[...].astype(F32)
    order = order_matrix(out_ref.shape[0], True)
    out_to[...] = dot(order, out_ref[...]).astype(BF16)
    dx = dtok_ref[...]
    high = dx.astype(BF16)
    dtok_to[...] = dot(order, high) + dot(order, (dx - high.astype(F32)).astype(BF16))


def finish(tokens, grads, block_out, d_tokens):
    total, width = block_out.shape
    count = total // tokens
    if grads[0].shape[0] * 2 != count:
        def ordered(values):
            return values.reshape(count, tokens // 8, 8, width).swapaxes(1, 2).reshape(total, width)

        return [g.astype(F32) for g in grads], ordered(block_out), ordered(d_tokens)
    halves = [
        pl.BlockSpec((1, g.shape[1] // 2, g.shape[2]), lambda i: (i // 2, i % 2, 0)) for g in grads
    ]
    tile = pl.BlockSpec((tokens, width), lambda i: (i, 0))
    outs = pl.pallas_call(
        functools.partial(finish_kernel, len(grads)),
        grid=(count,),
        in_specs=halves + [tile, tile],
        out_specs=halves + [tile, tile],
        out_shape=[jax.ShapeDtypeStruct(g.shape, F32) for g in grads]
        + [jax.ShapeDtypeStruct(v.shape, v.dtype) for v in (block_out, d_tokens)],
        compiler_params=pltpu.CompilerParams(vmem_limit_bytes=LIMIT),
    )(*grads, block_out, d_tokens)
    return outs[:-2], outs[-2], outs[-1]


def contract_rows(left, right):
    return lax.dot_general(
        left, right, (((0,), (0,)), ((), ())), preferred_element_type=F32
    ).astype(BF16)


def shards(
    tokens_in, doc_starts, mixer_in, mixer_out, ffn_in, ffn_out, gains, gate_params, cotangent
):
    rows, length, width = tokens_in.shape
    layers = gains.shape[0]
    chan = width // 2
    total = rows * length
    tokens = min(length, 256)
    seg = tokens // 8
    n, n_seq = lax.axis_size("batch"), lax.axis_size("seq")
    sources = (mixer_in, mixer_out, ffn_in, ffn_out)
    paired = n_seq == 4 and n % 4 == 0 and all(w.shape[1] % 96 == 0 for w in sources)
    theta, lower = gate_params[:, 0:1], gate_params[:, 1:2]
    at = lax.broadcasted_iota(jnp.int32, (layers, 8, chan), 1)
    times = jnp.where(at < 3, 1, jnp.where(at < 5, seg, length)).astype(F32)
    quarter = jnp.where((at == 1) | (at == 4) | (at == 6), math.pi / 2, 0.0)
    gate_rows = jnp.where(at == 2, lower, jnp.cos(theta * times - quarter))
    table = jnp.concatenate(
        [jnp.pad(gains, ((0, 0), (0, 5), (0, 0))), jnp.pad(gate_rows, ((0, 0), (0, 0), (0, width - chan)))], axis=1
    )
    x = tokens_in.reshape(total, width)
    if paired:
        weights, kept = run_forward(n, n_seq, True, rows, tokens, doc_starts, x, sources, table)
    else:
        stacked = [lax.all_gather(w, "batch", axis=1, tiled=True) for w in sources]
        weights = [w[k] for k in range(layers) for w in stacked]
        _, kept = run_forward(n, n_seq, False, rows, tokens, doc_starts, x, stacked, table)
    x_in, proj, p_g, normed, starts, state, mixed, mid, normed2, gu, hid, block_out = kept
    dz, d_gu, dy, d_proj, d_tokens, small = run_backward(
        n_seq, rows, tokens, doc_starts, cotangent.reshape(total, width), weights, table,
        (x_in, proj, p_g, starts, state, mid, gu),
    )
    pairs = ((normed, d_proj), (mixed, dy), (normed2, d_gu), (hid, dz))
    if paired:
        plan = []
        for k in reversed(range(layers)):
            jobs = ORDERS[0] if k == layers - 1 else ORDERS[1]
            plan += [(m, k, m != 0, part, of) for m, part, of in jobs]
        *outs, d_gains, d_gate = grads_and_scatter(
            n, plan, [pairs[p[0]][0] for p in plan], [pairs[p[0]][1] for p in plan], small
        )
    else:
        outs = []
        for left, right in pairs:
            whole_grads = jnp.stack([contract_rows(left[k], right[k]) for k in range(layers)])
            part = lax.psum_scatter(whole_grads, "batch", scatter_dimension=1, tiled=True)
            outs.append(lax.psum(part, "seq"))
        totals = lax.psum(jnp.sum(small.reshape(layers, 4, 8, width), axis=2), ("batch", "seq"))
        d_gains, d_gate = totals[:, :3], totals[:, 3].reshape(layers, 2, chan)
    outs, block_out, d_tokens = finish(tokens, outs, block_out, d_tokens)
    return (
        block_out.reshape(rows, length, width),
        d_tokens.reshape(rows, length, width),
        *outs,
        d_gains,
        d_gate,
    )


def solution(mesh):
    tok = P("batch", "seq", None)
    mat = P(None, "batch", None)
    return jax.shard_map(
        shards,
        mesh=mesh,
        in_specs=(tok, P("batch", None), mat, mat, mat, mat, P(), P(), tok),
        out_specs=(tok, tok, mat, mat, mat, mat, P(), P()),
        check_vma=False,
    )
```
